32 devices in a mesh: row: 8 (over z, x), col: 4 (over y, core).
Axes of the slice: x: 2, y: 2, z: 4, core: 2. Of those that a mesh axis runs over, the one named last changes fastest.
Arguments:
- tokens: bfloat16 [64, 320, 768], P(('row', 'col')), may hold values from -6 to 6
- w_in_x: bfloat16 [768, 1536], P('row', 'col'), may hold values from -0.21875 to 0.21875
- w_in_z: bfloat16 [768, 1536], P('row', 'col'), may hold values from -0.21875 to 0.21875
- conv_w: bfloat16 [4, 1536], P(None, ('row', 'col')), may hold values from -3 to 3
- conv_b: bfloat16 [1536], P(('row', 'col')), may hold values from -0.5 to 0.5
- w_xproj: bfloat16 [1536, 80], P('row', 'col'), may hold values from -0.15625 to 0.15625
- w_dt: bfloat16 [48, 1536], P('row', 'col'), may hold values from -0.875 to 0.875
- dt_bias: bfloat16 [1536], P(('row', 'col')), may hold values from -7 to -3
- a_log: bfloat16 [16, 1536], P(None, ('row', 'col')), may hold values from 0 to 2.765625
- d_skip: bfloat16 [1536], P(('row', 'col')), may hold values from 0.5 to 1.5
- w_out: bfloat16 [1536, 768], P('row', 'col'), may hold values from -0.15625 to 0.15625
- gain_mix: bfloat16 [768], P(('row', 'col')), may hold values from 0.5 to 1.5
- gain_moe: bfloat16 [768], P(('row', 'col')), may hold values from 0.5 to 1.5
- w_router: bfloat16 [768, 32], P('row', 'col'), may hold values from -0.109375 to 0.109375
- w_up: bfloat16 [32, 768, 3072], P('row', None, 'col'), may hold values from -0.21875 to 0.21875
- w_down: bfloat16 [32, 3072, 768], P('row', 'col'), may hold values from -3.5 to 3.5
- routes: int32 [64, 320, 1], P(('row', 'col')), may hold values from 0 to 31
- lengths: int32 [64], P(('row', 'col')), may hold values from 128 to 320, as said below
- cotangent: float32 [64, 320, 768], P(('row', 'col')), may hold values from -6 to 6
Outputs:
- mixed_out: bfloat16 [64, 320, 768], P(('row', 'col'))
- grad_tokens: float32 [64, 320, 768], P(('row', 'col'))
- grad_w_in_x: float32 [768, 1536], P('row', 'col')
- grad_w_in_z: float32 [768, 1536], P('row', 'col')
- grad_conv_w: float32 [4, 1536], P(None, ('row', 'col'))
- grad_conv_b: float32 [1536], P(('row', 'col'))
- grad_w_xproj: float32 [1536, 80], P('row', 'col')
- grad_w_dt: float32 [48, 1536], P('row', 'col')
- grad_dt_bias: float32 [1536], P(('row', 'col'))
- grad_a_log: float32 [16, 1536], P(None, ('row', 'col'))
- grad_d_skip: float32 [1536], P(('row', 'col'))
- grad_w_out: float32 [1536, 768], P('row', 'col')
- grad_gain_mix: float32 [768], P(('row', 'col'))
- grad_gain_moe: float32 [768], P(('row', 'col'))
- grad_w_router: float32 [768, 32], P('row', 'col')
- grad_w_up: float32 [32, 768, 3072], P('row', None, 'col')
- grad_w_down: float32 [32, 3072, 768], P('row', 'col')
The draws below stay inside these ranges and needn't reach their ends.
Inputs may be any that keep to these rules, and one draw needn't show every extreme that they name: `lengths`: each sequence's number of real tokens; the slots after them are padding.
All inputs are finite; a program needn't handle non-finite values.
Results may differ from the reference program's by a relative error of at most 0.014.
Values may be sent and summed in bfloat16 or wider, within the bound.
No kernel may reach another device: no remote copies, remote signals or barrier semaphores. Data moves between devices by JAX's collectives and lax.ppermute only.
A program may use at most 320 MiB of HBM per device.

```python
import jax
import jax.numpy as jnp
from jax import lax

D = 768
DI = 1536
NS = 16
R = 48
KC = 4
FF = 3072
E = 32
XP = 80
L = 320
LMIN = 128
QB = 64
SEQ_MB = 1
CAP = 13
SEQS = 64


def draw_lengths(key, part):
    key_values, key_long, key_short = jax.random.split(key, 3)
    values = jax.random.randint(key_values, (SEQS,), LMIN, L + 1, dtype=jnp.int32)
    longest = jax.random.randint(key_long, (), 0, SEQS, dtype=jnp.int32)
    values = values.at[longest].set(L)
    shortest = (longest + 1 + jax.random.randint(key_short, (), 0, SEQS - 1, dtype=jnp.int32)) % SEQS
    values = values.at[shortest].set(LMIN)
    return values.astype(jnp.int32)


def steps_of(stream_key, extent, cuts, smallest, high):
    level = 1.0
    for position, parts in cuts:
        draws = jax.random.uniform(jax.random.fold_in(jax.random.fold_in(stream_key, 6), position), (parts,), jnp.float32, smallest / len(cuts), high / len(cuts))
        level = level * jnp.repeat(jnp.exp(draws), extent[position] // parts).reshape((-1,) + (1,) * (len(extent) - 1 - position))
    return level


def different_ones(stream_key, rows, number_of, top, lift):
    sequence = jax.random.permutation(jax.random.fold_in(stream_key, 1), number_of)
    boost = sequence
    for power in range(3):
        boost = boost * boost // number_of
    boost = boost * lift // number_of
    tickets = jax.random.randint(jax.random.fold_in(stream_key, 2), (rows, number_of), 0, 4096) + boost
    holders = jax.random.permutation(jax.random.fold_in(stream_key, 3), rows)[jnp.arange(number_of) % rows]
    tickets = jnp.where(jnp.arange(rows)[:, None] == holders[None, :], 1 << 14, tickets)
    priority = tickets * number_of + jnp.arange(number_of)
    return lax.top_k(priority.astype(jnp.int32), top)[1].astype(jnp.int32)


def scatter_about(rng, extent, spread, most, cuts=(), kind=jnp.bfloat16):
    gain = steps_of(rng, extent, cuts, -0.22, 0.18) if cuts else 1.0
    entries = jax.random.normal(rng, extent, jnp.float32) * spread * gain
    return jnp.minimum(jnp.maximum(entries, -most), most).astype(kind)


def setup_inputs(seed: int = 0) -> dict:
    splits = jax.random.split(jax.random.key(seed), 20)
    return {
        "tokens": scatter_about(splits[0], (SEQS, L, D), 1.0, 6.0, ((0, 32),)),
        "w_in_x": scatter_about(splits[1], (D, DI), D ** -0.5, 0.21875, ((0, 8), (1, 4))),
        "w_in_z": scatter_about(splits[2], (D, DI), D ** -0.5, 0.21875, ((0, 8), (1, 4))),
        "conv_w": scatter_about(splits[3], (KC, DI), 0.5, 3.0, ((1, 32),)),
        "conv_b": jnp.clip(jax.random.uniform(splits[4], (DI,), jnp.float32, -0.5, 0.5) * steps_of(splits[4], (DI,), ((0, 32),), -0.4, 0.0), -0.5, 0.5).astype(jnp.bfloat16),
        "w_xproj": scatter_about(splits[5], (DI, XP), DI ** -0.5, 0.15625, ((0, 8), (1, 4))),
        "w_dt": scatter_about(splits[6], (R, DI), R ** -0.5, 0.875, ((0, 8), (1, 4))),
        "dt_bias": jnp.clip(-7.0 + 4.0 * jax.random.uniform(splits[7], (DI,), jnp.float32) ** steps_of(splits[7], (DI,), ((0, 32),), -0.2, 0.2), -7.0, -3.0).astype(jnp.bfloat16),
        "a_log": jnp.clip(2.765625 * jax.random.uniform(splits[8], (NS, DI), jnp.float32) ** steps_of(splits[8], (NS, DI), ((1, 32),), -0.2, 0.2), 0.0, 2.765625).astype(jnp.bfloat16),
        "d_skip": jnp.clip(0.5 + 1.0 * jax.random.uniform(splits[9], (DI,), jnp.float32) ** steps_of(splits[9], (DI,), ((0, 32),), -0.2, 0.2), 0.5, 1.5).astype(jnp.bfloat16),
        "w_out": scatter_about(splits[10], (DI, D), DI ** -0.5, 0.15625, ((0, 8), (1, 4))),
        "gain_mix": jnp.clip(1.0 + 0.1 * jax.random.normal(splits[11], (D,), jnp.float32), 0.5, 1.5).astype(jnp.bfloat16),
        "gain_moe": jnp.clip(1.0 + 0.1 * jax.random.normal(splits[12], (D,), jnp.float32), 0.5, 1.5).astype(jnp.bfloat16),
        "w_router": scatter_about(splits[13], (D, E), (4 * D) ** -0.5, 0.109375, ((0, 8), (1, 4))),
        "w_up": scatter_about(splits[14], (E, D, FF), D ** -0.5, 0.21875, ((0, 8), (2, 4))),
        "w_down": scatter_about(splits[15], (E, FF, D), (max(1, FF // 1024)) ** -0.5, 3.5, ((0, 8), (1, 4))),
        "routes": different_ones(splits[16], SEQS * L, E, 1, 256).reshape((SEQS, L, 1)),
        "lengths": draw_lengths(jax.random.fold_in(splits[19], 71), 0),
        "cotangent": scatter_about(splits[18], (SEQS, L, D), 1.0, 6.0, ((0, 32),), jnp.float32),
    }


epsilon = 1e-05
highest = lax.Precision.HIGHEST

@jax.custom_vjp
def low(v):
    return lax.optimization_barrier(v.astype(jnp.bfloat16)).astype(jnp.float32)

@jax.custom_vjp
def low_back(v):
    return v

def low_keep(v):
    return (low(v), None)

def low_pass(kept, grad):
    return (grad,)

def back_keep(v):
    return (v, None)

def back_low(kept, grad):
    return (low(grad),)
low.defvjp(low_keep, low_pass)
low_back.defvjp(back_keep, back_low)

def matmul(left, right):
    return jnp.dot(left, right, precision=highest, preferred_element_type=jnp.float32)

def rms_scale(values, gain_vec):
    inv_rms = lax.rsqrt(lax.optimization_barrier(jnp.mean(values * values, axis=-1, keepdims=True)) + epsilon)
    return values * inv_rms * gain_vec

def conv_silu(inner_x, conv_weight, conv_bias):
    tap_count = conv_weight.shape[0]
    length = inner_x.shape[1]
    padded = jnp.pad(inner_x, ((0, 0), (tap_count - 1, 0), (0, 0)))
    summed = conv_bias + conv_weight[0] * padded[:, 0:length]
    for offset in range(1, tap_count):
        summed = summed + conv_weight[offset] * padded[:, offset:offset + length]
    return jax.nn.silu(summed)

def selective(u_value, delta_t, b_mat, c_mat, a_neg, block_len):
    seq_count, length, width = u_value.shape
    state_count = a_neg.shape[0]
    blocks = length // block_len

    def to_blocks(array_in):
        shaped = array_in.reshape(seq_count, blocks, block_len, array_in.shape[-1])
        return jnp.moveaxis(shaped, (1, 2), (0, 1))

    def one_position(state_now, inputs):
        u_pos, d_pos, b_pos, c_pos = inputs
        decay_now = jnp.exp(d_pos[:, None, :] * a_neg)
        state_now = decay_now * state_now + b_pos[:, :, None] * (d_pos * u_pos)[:, None, :]
        return (state_now, lax.optimization_barrier(jnp.sum(state_now * c_pos[:, :, None], axis=1)))

    def one_block(state_now, inputs):
        return lax.scan(one_position, state_now, inputs)
    start_state = jnp.zeros((seq_count, state_count, width), jnp.float32)
    pieces = tuple((to_blocks(member) for member in (u_value, delta_t, b_mat, c_mat)))
    last_state, outputs = lax.scan(jax.checkpoint(one_block), start_state, pieces)
    outputs = jnp.moveaxis(outputs, (0, 1), (1, 2))
    return outputs.reshape(seq_count, length, width)

def group_forward(x_float, weights, live_rows, live_int, route_block):
    w_in_x, w_in_z, conv_w, conv_b, w_xproj, w_dt, dt_bias, a_log, d_skip, w_out, gain_mix, gain_moe, w_router, w_up, w_down = weights
    normed_mix = low(rms_scale(x_float, gain_mix))
    inner_x = low_back(matmul(normed_mix, w_in_x))
    gate_z = low_back(matmul(normed_mix, w_in_z))
    u_value = conv_silu(inner_x, conv_w, conv_b)
    projected = low_back(matmul(low(u_value), w_xproj))
    dt_pre = low_back(matmul(low(projected[..., :R]), w_dt))
    delta_t = jax.nn.softplus(dt_pre + dt_bias)
    a_neg = -jnp.exp(a_log)
    ssm_out = selective(u_value, delta_t, projected[..., R:R + NS], projected[..., R + NS:], a_neg, QB) + d_skip * u_value
    gated = low(ssm_out * jax.nn.silu(gate_z))
    hidden = x_float + low_back(matmul(gated, w_out))
    normed_moe = rms_scale(hidden, gain_moe)
    route_probs = jax.nn.softmax(matmul(normed_moe, w_router), axis=-1)
    expert_iota = jnp.arange(E, dtype=jnp.int32)
    route_onehot = (route_block[..., None] == expert_iota).astype(jnp.float32)
    gate_prob = lax.optimization_barrier(jnp.sum(route_probs * route_onehot, axis=-1))
    flat_route = route_block.reshape(-1)
    flat_live = live_int.reshape(-1)
    hit_table = (flat_route[:, None] == expert_iota[None, :]).astype(jnp.int32) * flat_live[:, None]
    earlier = jnp.cumsum(hit_table, axis=0, dtype=jnp.int32) - hit_table
    slot_index = lax.optimization_barrier(jnp.sum(earlier * hit_table, axis=-1, dtype=jnp.int32))
    kept_rows = (flat_live > 0) & (slot_index < CAP)
    target = jnp.where(kept_rows, flat_route * CAP + slot_index, E * CAP)
    dispatch = (target[:, None] == jnp.arange(E * CAP, dtype=jnp.int32)[None, :]).astype(jnp.float32)
    send_rows = low_back(low(normed_moe)).reshape(-1, D)
    expert_in = jnp.einsum('tk,td->kd', dispatch, send_rows, precision=highest, preferred_element_type=jnp.float32).reshape(E, CAP, D)
    pre_act = low_back(jnp.einsum('ecd,edf->ecf', expert_in, w_up, precision=highest, preferred_element_type=jnp.float32))
    activ = low(jax.nn.gelu(pre_act, approximate=False))
    expert_out = low(low_back(jnp.einsum('ecf,efd->ecd', activ, w_down, precision=highest, preferred_element_type=jnp.float32)))
    expert_tok = matmul(dispatch, expert_out.reshape(E * CAP, D)).reshape(hidden.shape)
    return live_rows[..., None] * (hidden + gate_prob[..., None] * expert_tok)

def reference(tokens, w_in_x, w_in_z, conv_w, conv_b, w_xproj, w_dt, dt_bias, a_log, d_skip, w_out, gain_mix, gain_moe, w_router, w_up, w_down, routes, lengths, cotangent):
    weights = tuple((member.astype(jnp.float32) for member in (w_in_x, w_in_z, conv_w, conv_b, w_xproj, w_dt, dt_bias, a_log, d_skip, w_out, gain_mix, gain_moe, w_router, w_up, w_down)))
    groups = tokens.shape[0] // SEQ_MB
    x_groups = tokens.astype(jnp.float32).reshape(groups, SEQ_MB, L, D)
    route_groups = routes[..., 0].reshape(groups, SEQ_MB, L)
    length_groups = lengths.reshape(groups, SEQ_MB)
    grad_groups = cotangent.astype(jnp.float32).reshape(groups, SEQ_MB, L, D)
    position_iota = jnp.arange(L, dtype=jnp.int32)

    def group_step(totals, inputs):
        x_group, route_group, length_group, grad_group = inputs
        live_int = (position_iota[None, :] < length_group[:, None]).astype(jnp.int32)
        live_rows = live_int.astype(jnp.float32)

        def forward(x_float, params):
            return group_forward(x_float, params, live_rows, live_int, route_group)
        result, pullback = jax.vjp(forward, x_group, weights)
        grad_x, grad_params = pullback(grad_group)
        totals = jax.tree.map(jnp.add, totals, grad_params)
        return (totals, (result.astype(jnp.bfloat16), grad_x))
    zero_grads = jax.tree.map(jnp.zeros_like, weights)
    totals, (mixed_out, grad_tokens) = lax.scan(group_step, zero_grads, (x_groups, route_groups, length_groups, grad_groups))
    return (mixed_out.reshape(tokens.shape), grad_tokens.reshape(tokens.shape), totals[0], totals[1], totals[2], totals[3], totals[4], totals[5], totals[6], totals[7], totals[8], totals[9], totals[10], totals[11], totals[12], totals[13], totals[14])
```

```python
import functools
import jax
import jax.numpy as jnp
from jax import lax
from jax.sharding import PartitionSpec as P
from jax.experimental import pallas as pl
from jax.experimental.pallas import tpu as pltpu
NS=16
F32=jnp.float32
SLOT_OF=[4*((i>>2)&1)+2*(1-((i>>1)&1))+(1-(i&1)) for i in range(8)]
def merge8(rows):
    idx=lax.broadcasted_iota(jnp.int32,(8,128),0)
    m4=idx<4; m2=(idx&2)!=0; m1=(idx&1)!=0
    p=[None]*8
    for i in range(8): p[SLOT_OF[i]]=rows[i]
    r=[jnp.where(m4,p[k],p[k+4])+pltpu.roll(jnp.where(m4,p[k+4],p[k]),4,0) for k in range(4)]
    def half(x,y,m,d):
        return jnp.where(m,x+pltpu.roll(x,d,0),y+pltpu.roll(y,8-d,0))
    v=[half(r[k],r[k+2],m2,2) for k in range(2)]
    return half(v[0],v[1],m1,1)
def softplus(v):
    e=jnp.exp(-jnp.abs(v))
    return jnp.maximum(v,0.)+jnp.log1p(e)
def spread(dst,src,T):
    for j in range(T):
        dst[j]=jnp.broadcast_to(src[0,0,:,j:j+1],(NS,128))
def fold(x): return x[0:8]+x[8:16]

def fwd_kernel(T,Q,u_ref,dtp_ref,bT_ref,cT_ref,bias_ref,a2_ref,skip_ref,y_ref,st_ref,state,bx,cx,dl,du):
    DI=u_ref.shape[-1]
    @pl.when(pl.program_id(1)==0)
    def _(): state[...]=jnp.zeros_like(state)
    st_ref[0,0]=state[...]
    spread(bx,bT_ref,T); spread(cx,cT_ref,T)
    d=softplus(dtp_ref[0]+bias_ref[...][None])
    dl[...]=d
    du[...]=d*u_ref[0]
    def grp(g,_):
        base=pl.multiple_of(g*(Q*128),128)
        lanes=[pl.ds(base+q*128,128) for q in range(Q)]
        a=[a2_ref[:,ln] for ln in lanes]
        sk=[skip_ref[:,ln] for ln in lanes]
        def tb(i,s):
            s=list(s)
            rows=[[] for _ in range(Q)]
            for k in range(8):
                t=i*8+k
                b=bx[t]; c=cx[t]
                for q in range(Q):
                    dd=dl[i,k:k+1,lanes[q]]; dub=du[i,k:k+1,lanes[q]]
                    s[q]=jnp.exp2(dd*a[q])*s[q]+b*dub
                    rows[q].append(fold(s[q]*c))
            for q in range(Q):
                y_ref[0,i,:,lanes[q]]=merge8(rows[q])+sk[q]*u_ref[0,i,:,lanes[q]]
            return tuple(s)
        s=lax.fori_loop(0,T//8,tb,tuple(state[:,ln] for ln in lanes))
        for q in range(Q): state[:,lanes[q]]=s[q]
        return 0
    lax.fori_loop(0,DI//(Q*128),grp,0)

def rows8(x):
    S,L,DI=x.shape
    return x.reshape(S,L//8,8,DI)
def scan_fwd(u,dtp,bT,cT,bias,a2,skip,Q=3):
    S,L,DI=u.shape
    C,T=bT.shape[1],bT.shape[3]
    row=lambda s,c:(s,c,0,0)
    big=pl.BlockSpec((1,T//8,8,DI),row)
    small=pl.BlockSpec((1,1,NS,T),row)
    par=lambda n:pl.BlockSpec((n,DI),lambda s,c:(0,0))
    y,st=pl.pallas_call(functools.partial(fwd_kernel,T,Q),
        grid=(S,C),
        in_specs=[big,big,small,small,par(1),par(NS),par(1)],
        out_specs=[big,pl.BlockSpec((1,1,NS,DI),row)],
        out_shape=[jax.ShapeDtypeStruct((S,L//8,8,DI),F32),jax.ShapeDtypeStruct((S,C,NS,DI),F32)],
        scratch_shapes=[pltpu.VMEM((NS,DI),F32),pltpu.VMEM((T,NS,128),F32),pltpu.VMEM((T,NS,128),F32),
                        pltpu.VMEM((T//8,8,DI),F32),pltpu.VMEM((T//8,8,DI),F32)],
        compiler_params=pltpu.CompilerParams(vmem_limit_bytes=32<<20),
    )(rows8(u),rows8(dtp),bT,cT,bias,a2,skip)
    return y.reshape(S,L,DI),st

def bwd_kernel(T,Q,Q2,u_ref,dtp_ref,gs_ref,bT_ref,cT_ref,st_ref,bias_ref,an_ref,skip_ref,
               guc_ref,gdt_ref,gb_ref,gc_ref,gal_ref,gbias_ref,gskip_ref,
               carry,bx,cx,dl,du,hs,ds,gbp,gcp):
    DI=u_ref.shape[-1]
    s_id,c_id=pl.program_id(0),pl.program_id(1)
    @pl.when(c_id==0)
    def _(): carry[...]=jnp.zeros_like(carry)
    @pl.when((c_id==0)&(s_id==0))
    def _():
        gal_ref[...]=jnp.zeros_like(gal_ref)
        gbias_ref[...]=jnp.zeros_like(gbias_ref)
        gskip_ref[...]=jnp.zeros_like(gskip_ref)
    spread(bx,bT_ref,T); spread(cx,cT_ref,T)
    d=softplus(dtp_ref[0]+bias_ref[...][None])
    dl[...]=d
    du[...]=d*u_ref[0]
    gbp[...]=jnp.zeros_like(gbp)
    gcp[...]=jnp.zeros_like(gcp)
    W=Q*128
    def grp(g,_):
        base=pl.multiple_of(g*W,128)
        lanes=[pl.ds(base+q*128,128) for q in range(Q)]
        loc=[slice(q*128,q*128+128) for q in range(Q)]
        an=[an_ref[:,ln] for ln in lanes]
        a2=[x*1.4426950408889634 for x in an]
        def tb(i,s):
            s=list(s)
            for k in range(8):
                t=i*8+k
                b=bx[t]; gc=gcp[t]
                for q in range(Q):
                    dd=dl[i,k:k+1,lanes[q]]; dub=du[i,k:k+1,lanes[q]]; gsr=gs_ref[0,i,k:k+1,lanes[q]]
                    dec=jnp.exp2(dd*a2[q])
                    h=dec*s[q]
                    ds[t,:,loc[q]]=dec
                    hs[t,:,loc[q]]=h
                    s[q]=h+b*dub
                    gc=gc+s[q]*gsr
                gcp[t]=gc
            return tuple(s)
        lax.fori_loop(0,T//8,tb,tuple(st_ref[0,0,:,ln] for ln in lanes))
        for q0 in range(0,Q,Q2):
            qs=range(q0,q0+Q2)
            sk={q:skip_ref[:,lanes[q]] for q in qs}
            def rb(j,cr):
                i=T//8-1-j
                g_,ga={q:cr[0][q-q0] for q in qs},{q:cr[1][q-q0] for q in qs}
                gbs,gsk=cr[2],cr[3]
                m1={q:[None]*8 for q in qs}; m2={q:[None]*8 for q in qs}
                for k in range(7,-1,-1):
                    t=i*8+k
                    b=bx[t]; c=cx[t]; gb=gbp[t]
                    for q in qs:
                        dd=dl[i,k:k+1,lanes[q]]; dub=du[i,k:k+1,lanes[q]]; gsr=gs_ref[0,i,k:k+1,lanes[q]]
                        dec=ds[t,:,loc[q]]; h=hs[t,:,loc[q]]
                        gg=gsr*c+g_[q]
                        g_[q]=gg*dec
                        qq=gg*h
                        m1[q][k]=fold(gg*b)
                        m2[q][k]=fold(qq*an[q])
                        ga[q]=ga[q]+qq*dd
                        gb=gb+gg*dub
                    gbp[t]=gb
                for q in qs:
                    s1=merge8(m1[q]); s2=merge8(m2[q])
                    u8=u_ref[0,i,:,lanes[q]]; d8=dl[i,:,lanes[q]]; gs8=gs_ref[0,i,:,lanes[q]]
                    guc_ref[0,i,:,lanes[q]]=d8*s1+sk[q]*gs8
                    gd=(s2+u8*s1)*jax.nn.sigmoid(dtp_ref[0,i,:,lanes[q]]+bias_ref[:,lanes[q]])
                    gdt_ref[0,i,:,lanes[q]]=gd
                    gbs=gbs[:q-q0]+(gbs[q-q0]+gd,)+gbs[q-q0+1:]
                    gsk=gsk[:q-q0]+(gsk[q-q0]+gs8*u8,)+gsk[q-q0+1:]
                return (tuple(g_[q] for q in qs),tuple(ga[q] for q in qs),gbs,gsk)
            z8=tuple(jnp.zeros((8,128),F32) for q in qs)
            cr=lax.fori_loop(0,T//8,rb,(tuple(carry[:,lanes[q]] for q in qs),tuple(jnp.zeros((NS,128),F32) for q in qs),z8,z8))
            for q in qs:
                carry[:,lanes[q]]=cr[0][q-q0]
                gal_ref[:,lanes[q]]+=cr[1][q-q0]*an[q]
                gbias_ref[:,lanes[q]]+=cr[2][q-q0]
                gskip_ref[:,lanes[q]]+=cr[3][q-q0]
        return 0
    lax.fori_loop(0,DI//W,grp,0)
    ones=jnp.ones((8,128),F32)
    nt=(((1,),(1,)),((),()))
    gb_ref[0,0]=lax.dot_general(ones,gbp[...].reshape(T*NS,128),nt,precision=lax.Precision.HIGHEST,preferred_element_type=F32)
    gc_ref[0,0]=lax.dot_general(ones,gcp[...].reshape(T*NS,128),nt,precision=lax.Precision.HIGHEST,preferred_element_type=F32)

def scan_bwd(u,dtp,gs,bT,cT,st,bias,an,skip,Q=3,Q2=1):
    S,L,DI=u.shape
    C,T=bT.shape[1],bT.shape[3]
    row=lambda s,c:(s,C-1-c,0,0)
    big=pl.BlockSpec((1,T//8,8,DI),row)
    small=pl.BlockSpec((1,1,NS,T),row)
    par=lambda n:pl.BlockSpec((n,DI),lambda s,c:(0,0))
    red=pl.BlockSpec((1,1,8,T*NS),row)
    guc,gdt,gb,gc,gal,gbias,gskip=pl.pallas_call(functools.partial(bwd_kernel,T,Q,Q2),
        grid=(S,C),
        in_specs=[big,big,big,small,small,pl.BlockSpec((1,1,NS,DI),row),par(1),par(NS),par(1)],
        out_specs=[big,big,red,red,par(NS),par(8),par(8)],
        out_shape=[jax.ShapeDtypeStruct((S,L//8,8,DI),F32)]*2+[jax.ShapeDtypeStruct((S,C,8,T*NS),F32)]*2+
                  [jax.ShapeDtypeStruct((NS,DI),F32)]+[jax.ShapeDtypeStruct((8,DI),F32)]*2,
        scratch_shapes=[pltpu.VMEM((NS,DI),F32),pltpu.VMEM((T,NS,128),F32),pltpu.VMEM((T,NS,128),F32),
                        pltpu.VMEM((T//8,8,DI),F32),pltpu.VMEM((T//8,8,DI),F32),
                        pltpu.VMEM((T,NS,Q*128),F32),pltpu.VMEM((T,NS,Q*128),F32),
                        pltpu.VMEM((T,NS,128),F32),pltpu.VMEM((T,NS,128),F32)],
        compiler_params=pltpu.CompilerParams(vmem_limit_bytes=40<<20),
    )(rows8(u),rows8(dtp),rows8(gs),bT,cT,st,bias,an,skip)
    gb=gb[:,:,0].reshape(S,L,NS); gc=gc[:,:,0].reshape(S,L,NS)
    return guc.reshape(S,L,DI),gdt.reshape(S,L,DI),gb,gc,gal,jnp.sum(gbias,0),jnp.sum(gskip,0)


R = 48
QB = 64
CAP = 13
BF = jnp.bfloat16
epsilon = 1e-05
highest = lax.Precision.HIGHEST
root_half = 0.7071067811865476
inv_root_two_pi = 0.3989422804014327
log2e = 1.4426950408889634


def mm(a, b, dims=((1,), (0,)), **kw):
    return lax.dot_general(a, b, (dims, ((), ())), preferred_element_type=F32, **kw)


def swap(x, axis, bit):
    n = lax.axis_size(axis)
    return lax.ppermute(x, axis, [(i, i ^ bit) for i in range(n)])


def bits_of(axis):
    n = lax.axis_size(axis)
    return [1 << k for k in range(n.bit_length() - 1)]


def gather_steps():
    row, col = bits_of("row"), bits_of("col")
    return [("row", b) for b in row[1:] + row[:1]] + [("col", b) for b in col[::-1]]


def bit_set(axis, bit):
    return (lax.axis_index(axis) & bit) != 0


def gather_blocks(x):
    rows, cols = lax.axis_size("row"), lax.axis_size("col")
    dims = {}
    out = x
    order = []
    for axis, bit in gather_steps():
        other = swap(out, axis, bit)
        up = bit_set(axis, bit)
        out = jnp.where(up, jnp.stack([other, out]), jnp.stack([out, other]))
        order.insert(0, (axis, bit))
    n = len(order)
    wanted = [("row", b) for b in bits_of("row")[::-1]] + [("col", b) for b in bits_of("col")[::-1]]
    perm = [order.index(w) for w in wanted] + list(range(n, n + x.ndim))
    out = out.reshape((2,) * n + x.shape).transpose(perm)
    return out.reshape((rows, cols) + x.shape)


def reduce_blocks(x):
    block = x.shape[2:]
    row, col = bits_of("row"), bits_of("col")
    names = [("row", b) for b in row[::-1]] + [("col", b) for b in col[::-1]]
    x = x.reshape((2,) * len(names) + block)
    for axis, bit in gather_steps()[::-1]:
        d = names.index((axis, bit))
        names.pop(d)
        mine = bit_set(axis, bit).astype(jnp.int32)
        keep = lax.dynamic_index_in_dim(x, mine, d, keepdims=False)
        give = lax.dynamic_index_in_dim(x, 1 - mine, d, keepdims=False).astype(BF)
        x = keep + swap(give, axis, bit).astype(F32)
    return x


def gelu_parts(v):
    phi = 0.5 * (1.0 + lax.erf(v * root_half))
    return v * phi, phi + v * jnp.exp(-0.5 * v * v) * inv_root_two_pi


def to_chunks(b):
    s, length, n = b.shape
    return b.reshape(s, length // QB, QB, n).swapaxes(2, 3)


def on_device(tokens, w_in_x, w_in_z, conv_w, conv_b, w_xproj, w_dt, dt_bias, a_log, d_skip, w_out,
              gain_mix, gain_moe, w_router, w_up, w_down, routes, lengths, cotangent):
    rows, cols = lax.axis_size("row"), lax.axis_size("col")
    parts = rows * cols
    my_row = lax.axis_index("row")
    seqs, length, width = tokens.shape
    experts_here = w_up.shape[0]
    experts_all = experts_here * rows
    inner = w_in_x.shape[1] * cols
    count = seqs * length
    xp = w_xproj.shape[1] * cols
    share = inner // parts

    small = jnp.concatenate([conv_w, conv_b[None], dt_bias[None], a_log, d_skip[None],
                             jnp.concatenate([gain_mix, gain_moe])[None]], axis=0)
    flat = [w_xproj.reshape(-1), w_dt.reshape(-1), w_router.reshape(-1), small.reshape(-1)]
    sizes = [f.shape[0] for f in flat]
    lanes = w_in_x.shape[1]
    extra = -(-sum(sizes) // (8 * lanes)) * 8
    flat = jnp.pad(jnp.concatenate(flat), (0, extra * lanes - sum(sizes))).reshape(extra, lanes)
    here = w_in_x.shape[0]
    first = gather_blocks(jnp.concatenate([w_in_x, flat], axis=0))
    second = gather_blocks(jnp.concatenate([w_in_z.reshape(-1, lanes), w_out.reshape(-1, lanes)], axis=0))
    def whole(blocks):
        return blocks.transpose(0, 2, 1, 3).reshape(blocks.shape[0] * blocks.shape[2], -1)
    full_x = whole(first[:, :, :here])
    rest = first[:, :, here:].reshape(rows, cols, extra * lanes)
    cut = [0]
    for n in sizes:
        cut.append(cut[-1] + n)
    full_xproj = whole(rest[:, :, cut[0]:cut[1]].reshape((rows, cols) + w_xproj.shape))
    full_dt = whole(rest[:, :, cut[1]:cut[2]].reshape((rows, cols) + w_dt.shape))
    full_router = whole(rest[:, :, cut[2]:cut[3]].reshape((rows, cols) + w_router.shape))
    small = rest[:, :, cut[3]:cut[4]].reshape((parts,) + small.shape).transpose(1, 0, 2).astype(F32)
    chan = small[:-1].reshape(-1, inner)
    taps = conv_w.shape[0]
    conv_w_f, conv_b_f, dt_bias_f = chan[:taps], chan[taps], chan[taps + 1]
    a_log_f, d_skip_f = chan[taps + 2:taps + 2 + NS], chan[taps + 2 + NS]
    gain_mix_f = small[-1, :, :gain_mix.shape[0]].reshape(width)
    gain_moe_f = small[-1, :, gain_mix.shape[0]:].reshape(width)
    full_z = whole(second[:, :, :w_in_z.shape[0]])
    full_out = whole(second[:, :, w_in_z.shape[0]:].reshape((rows, cols) + w_out.shape))
    a_neg = -jnp.exp(a_log_f)

    flat_route = routes.reshape(count)
    live = (jnp.arange(length, dtype=jnp.int32)[None, :] < lengths[:, None]).reshape(count)
    live_f = live.astype(F32)[:, None]
    route_onehot = flat_route[:, None] == jnp.arange(experts_all, dtype=jnp.int32)
    hits = (route_onehot & live[:, None]).astype(BF).reshape(seqs, length, experts_all)
    before = jnp.arange(length)[:, None] > jnp.arange(length)[None, :]
    earlier = jnp.einsum("pq,sqe->spe", before.astype(BF), hits, preferred_element_type=F32)
    slot = jnp.sum(earlier * hits.astype(F32), axis=-1).astype(jnp.int32).reshape(count)
    kept = live & (slot < CAP)
    seq_of = jnp.arange(count, dtype=jnp.int32) // length
    per_row = experts_here * seqs * CAP
    target = (((flat_route // experts_here) ^ my_row) * per_row
              + (flat_route % experts_here) * (seqs * CAP) + seq_of * CAP + slot)
    target = jnp.where(kept, target, rows * per_row)
    route_f = route_onehot.astype(F32)

    x = tokens.astype(F32).reshape(count, width)
    rms1 = lax.rsqrt(jnp.mean(x * x, axis=-1, keepdims=True) + epsilon)
    hat1 = x * rms1
    normed_mix = (hat1 * gain_mix_f).astype(BF)
    inner_x = mm(normed_mix, full_x).reshape(seqs, length, inner)
    padded = jnp.pad(inner_x, ((0, 0), (taps - 1, 0), (0, 0)))
    conv_out = conv_b_f
    for k in range(taps):
        conv_out = conv_out + conv_w_f[k] * padded[:, k:k + length]
    conv_sig = jax.nn.sigmoid(conv_out)
    u_value = conv_out * conv_sig
    u_low = u_value.astype(BF).reshape(count, inner)
    projected = mm(u_low, full_xproj)
    dt_low = projected[:, :R].astype(BF)
    dt_pre = mm(dt_low, full_dt).reshape(seqs, length, inner)
    bT = to_chunks(projected[:, R:R + NS].reshape(seqs, length, NS))
    cT = to_chunks(projected[:, R + NS:].reshape(seqs, length, NS))
    ssm_out, starts = scan_fwd(u_value, dt_pre, bT, cT, dt_bias_f[None], a_neg * log2e, d_skip_f[None])
    ssm_out = ssm_out.reshape(count, inner)
    gate_z = mm(normed_mix, full_z)
    gate_sig = jax.nn.sigmoid(gate_z)
    gate_silu = gate_z * gate_sig
    gated = (ssm_out * gate_silu).astype(BF)
    hidden = x + mm(gated, full_out)

    rms2 = lax.rsqrt(jnp.mean(hidden * hidden, axis=-1, keepdims=True) + epsilon)
    hat2 = hidden * rms2
    normed_moe = hat2 * gain_moe_f
    router_f = full_router.astype(F32)
    route_probs = jax.nn.softmax(mm(normed_moe, router_f, precision=highest), axis=-1)
    gate_prob = jnp.sum(route_probs * route_f, axis=-1, keepdims=True)

    grad_y = live_f * cotangent.reshape(count, width)
    both = jnp.concatenate([normed_moe.astype(BF), (grad_y * gate_prob).astype(BF)], axis=1)
    place = jnp.arange(rows * per_row, dtype=jnp.int32)[:, None] == target[None, :]
    place = place.astype(BF)
    outgoing = mm(place, both).astype(BF)
    arrived = [outgoing[:per_row]]
    for k in range(1, rows):
        arrived.append(swap(outgoing[k * per_row:(k + 1) * per_row], "row", k))
    arrived = jnp.stack(arrived)
    for bit in bits_of("col")[::-1]:
        arrived = jnp.concatenate([arrived, swap(arrived, "col", bit)], axis=0)
    sources = rows * cols
    arrived = arrived.reshape(sources, experts_here, seqs * CAP, 2 * width).transpose(1, 0, 2, 3)
    arrived = arrived.reshape(experts_here, sources * seqs * CAP, 2 * width)
    expert_in, grad_eo = arrived[..., :width], arrived[..., width:]

    def bmm(a, b, da, db):
        return lax.dot_general(a, b, (((da,), (db,)), ((0,), (0,))), preferred_element_type=F32)
    pre_act = bmm(expert_in, w_up, 2, 1)
    act, slope = gelu_parts(pre_act)
    act = act.astype(BF)
    expert_out = bmm(act, w_down, 2, 1)
    grad_pre = (bmm(grad_eo, w_down, 2, 2) * slope).astype(BF)
    grad_ei = bmm(grad_pre, w_up, 2, 2)
    grad_w_up = bmm(expert_in, grad_pre, 1, 1)
    grad_w_down = bmm(act, grad_eo, 1, 1)
    back = jnp.concatenate([expert_out, grad_ei], axis=-1)
    back = back.reshape(experts_here, sources, seqs * CAP, 2 * width).transpose(1, 0, 2, 3)
    back = back.reshape(sources, per_row, 2 * width)
    for bit in bits_of("col"):
        half = back.shape[0] // 2
        back = back[:half] + swap(back[half:].astype(BF), "col", bit).astype(F32)
    back = back.astype(BF)
    home = [back[0]]
    for k in range(1, rows):
        home.append(swap(back[k], "row", k))
    home = jnp.concatenate(home, axis=0)
    tok = mm(place, home, ((0,), (0,)))
    expert_tok, grad_sent = tok[:, :width], tok[:, width:]

    mixed_out = (live_f * (hidden + gate_prob * expert_tok)).astype(BF)
    grad_gate = jnp.sum(grad_y * expert_tok, axis=-1, keepdims=True)
    grad_logits = grad_gate * gate_prob * (route_f - route_probs)
    grad_router = mm(normed_moe, grad_logits, ((0,), (0,)), precision=highest)
    grad_normed = grad_sent + mm(grad_logits, router_f, ((1,), (1,)), precision=highest)
    grad_gain_moe = jnp.sum(grad_normed * hat2, axis=0)
    scaled = grad_normed * gain_moe_f
    grad_hidden = grad_y + rms2 * (scaled - hat2 * jnp.mean(scaled * hat2, axis=-1, keepdims=True))
    grad_mixed = grad_hidden.astype(BF)

    grad_out = mm(gated, grad_mixed, ((0,), (0,)))
    grad_gated = mm(grad_mixed, full_out, ((1,), (1,)))
    grad_ssm = grad_gated * gate_silu
    grad_z = (grad_gated * ssm_out * (gate_sig * (1.0 + gate_z * (1.0 - gate_sig)))).astype(BF)
    guc, gdt, gb, gc, grad_a_log, grad_dt_bias, grad_d_skip = scan_bwd(
        u_value, dt_pre, grad_ssm.reshape(seqs, length, inner), bT, cT, starts,
        dt_bias_f[None], a_neg, d_skip_f[None])
    gdt = gdt.reshape(count, inner).astype(BF)
    grad_dt = mm(dt_low, gdt, ((0,), (0,)))
    grad_proj = jnp.concatenate([mm(gdt, full_dt, ((1,), (1,))), gb.reshape(count, NS), gc.reshape(count, NS)],
                                axis=1).astype(BF)
    grad_xproj = mm(u_low, grad_proj, ((0,), (0,)))
    grad_u = guc.reshape(count, inner) + mm(grad_proj, full_xproj, ((1,), (1,)))
    grad_conv = grad_u.reshape(seqs, length, inner) * (conv_sig * (1.0 + conv_out * (1.0 - conv_sig)))
    grad_conv_b = jnp.sum(grad_conv, axis=(0, 1))
    grad_conv_w = jnp.stack([jnp.sum(grad_conv * padded[:, k:k + length], axis=(0, 1)) for k in range(taps)])
    after = jnp.pad(grad_conv, ((0, 0), (0, taps - 1), (0, 0)))
    grad_inner = sum(conv_w_f[k] * after[:, taps - 1 - k:taps - 1 - k + length] for k in range(taps))
    grad_inner = grad_inner.reshape(count, inner).astype(BF)
    grad_in_x = mm(normed_mix, grad_inner, ((0,), (0,)))
    grad_in_z = mm(normed_mix, grad_z, ((0,), (0,)))
    grad_nm = mm(grad_inner, full_x, ((1,), (1,))) + mm(grad_z, full_z, ((1,), (1,)))
    grad_gain_mix = jnp.sum(grad_nm * hat1, axis=0)
    scaled = grad_nm * gain_mix_f
    grad_tokens = grad_hidden + rms1 * (scaled - hat1 * jnp.mean(scaled * hat1, axis=-1, keepdims=True))

    def blocks(g, like):
        r, c = like.shape
        return g.reshape(rows, r, cols, c).transpose(0, 2, 1, 3)
    grad_z_block = reduce_blocks(blocks(grad_in_z, w_in_z))
    grad_out_block = reduce_blocks(blocks(grad_out, w_out).reshape(rows, cols, -1, lanes)).reshape(w_out.shape)
    gsmall = jnp.concatenate([grad_conv_w, grad_conv_b[None], grad_dt_bias[None], grad_a_log, grad_d_skip[None]], axis=0)
    ggain = jnp.concatenate([grad_gain_mix.reshape(parts, 1, -1), grad_gain_moe.reshape(parts, 1, -1)], axis=2)
    gsmall = jnp.concatenate([gsmall.reshape(-1, parts, share).transpose(1, 0, 2), ggain], axis=1)
    gflat = jnp.concatenate([blocks(grad_xproj, w_xproj).reshape(rows, cols, -1),
                             blocks(grad_dt, w_dt).reshape(rows, cols, -1),
                             blocks(grad_router, w_router).reshape(rows, cols, -1),
                             gsmall.reshape(rows, cols, -1)], axis=2)
    gflat = jnp.pad(gflat, ((0, 0), (0, 0), (0, extra * lanes - sum(sizes)))).reshape(rows, cols, extra, lanes)
    done = reduce_blocks(jnp.concatenate([blocks(grad_in_x, w_in_x), gflat], axis=2))
    grad_x_block = done[:here]
    done = done[here:].reshape(-1)
    sm = done[cut[3]:cut[4]].reshape(-1, share)
    gm = gain_mix.shape[0]
    return (
        mixed_out.reshape(tokens.shape),
        grad_tokens.reshape(tokens.shape),
        grad_x_block,
        grad_z_block,
        sm[:taps],
        sm[taps],
        done[cut[0]:cut[1]].reshape(w_xproj.shape),
        done[cut[1]:cut[2]].reshape(w_dt.shape),
        sm[taps + 1],
        sm[taps + 2:taps + 2 + NS],
        sm[taps + 2 + NS],
        grad_out_block,
        sm[-1, :gm],
        sm[-1, gm:],
        done[cut[2]:cut[3]].reshape(w_router.shape),
        grad_w_up,
        grad_w_down,
    )


def solution(mesh):
    tok = P(("row", "col"), None, None)
    mat = P("row", "col")
    vec = P(("row", "col"))
    chan = P(None, ("row", "col"))
    up, down = P("row", None, "col"), P("row", "col", None)
    return jax.shard_map(
        on_device,
        mesh=mesh,
        in_specs=(tok, mat, mat, chan, vec, mat, mat, vec, chan, vec, mat, vec, vec, mat, up, down, tok, vec, tok),
        out_specs=(tok, tok, mat, mat, chan, vec, mat, mat, vec, chan, vec, mat, vec, vec, mat, up, down),
        check_vma=False,
    )
```

```python
import functools
import jax
import jax.numpy as jnp
from jax import lax
from jax.sharding import PartitionSpec as P
from jax.experimental import pallas as pl
from jax.experimental.pallas import tpu as pltpu
NS=16
F32=jnp.float32
SLOT_OF=[4*((i>>2)&1)+2*(1-((i>>1)&1))+(1-(i&1)) for i in range(8)]
def merge8(rows):
    idx=lax.broadcasted_iota(jnp.int32,(8,128),0)
    m4=idx<4; m2=(idx&2)!=0; m1=(idx&1)!=0
    p=[None]*8
    for i in range(8): p[SLOT_OF[i]]=rows[i]
    r=[jnp.where(m4,p[k],p[k+4])+pltpu.roll(jnp.where(m4,p[k+4],p[k]),4,0) for k in range(4)]
    def half(x,y,m,d):
        return jnp.where(m,x+pltpu.roll(x,d,0),y+pltpu.roll(y,8-d,0))
    v=[half(r[k],r[k+2],m2,2) for k in range(2)]
    return half(v[0],v[1],m1,1)
def softplus(v):
    e=jnp.exp(-jnp.abs(v))
    return jnp.maximum(v,0.)+jnp.log1p(e)
def spread(dst,src,T):
    for j in range(T):
        dst[j]=jnp.broadcast_to(src[0,0,:,j:j+1],(NS,128))
def fold(x): return x[0:8]+x[8:16]

def fwd_kernel(T,Q,u_ref,dtp_ref,bT_ref,cT_ref,bias_ref,a2_ref,skip_ref,y_ref,st_ref,state,bx,cx,dl,du):
    DI=u_ref.shape[-1]
    @pl.when(pl.program_id(1)==0)
    def _(): state[...]=jnp.zeros_like(state)
    st_ref[0,0]=state[...]
    spread(bx,bT_ref,T); spread(cx,cT_ref,T)
    d=softplus(dtp_ref[0]+bias_ref[...][None])
    dl[...]=d
    du[...]=d*u_ref[0]
    def grp(g,_):
        base=pl.multiple_of(g*(Q*128),128)
        lanes=[pl.ds(base+q*128,128) for q in range(Q)]
        a=[a2_ref[:,ln] for ln in lanes]
        sk=[skip_ref[:,ln] for ln in lanes]
        def tb(i,s):
            s=list(s)
            rows=[[] for _ in range(Q)]
            for k in range(8):
                t=i*8+k
                b=bx[t]; c=cx[t]
                for q in range(Q):
                    dd=dl[i,k:k+1,lanes[q]]; dub=du[i,k:k+1,lanes[q]]
                    s[q]=jnp.exp2(dd*a[q])*s[q]+b*dub
                    rows[q].append(fold(s[q]*c))
            for q in range(Q):
                y_ref[0,i,:,lanes[q]]=merge8(rows[q])+sk[q]*u_ref[0,i,:,lanes[q]]
            return tuple(s)
        s=lax.fori_loop(0,T//8,tb,tuple(state[:,ln] for ln in lanes))
        for q in range(Q): state[:,lanes[q]]=s[q]
        return 0
    lax.fori_loop(0,DI//(Q*128),grp,0)

def rows8(x):
    S,L,DI=x.shape
    return x.reshape(S,L//8,8,DI)
def scan_fwd(u,dtp,bT,cT,bias,a2,skip,Q=3):
    S,L,DI=u.shape
    C,T=bT.shape[1],bT.shape[3]
    row=lambda s,c:(s,c,0,0)
    big=pl.BlockSpec((1,T//8,8,DI),row)
    small=pl.BlockSpec((1,1,NS,T),row)
    par=lambda n:pl.BlockSpec((n,DI),lambda s,c:(0,0))
    y,st=pl.pallas_call(functools.partial(fwd_kernel,T,Q),
        grid=(S,C),
        in_specs=[big,big,small,small,par(1),par(NS),par(1)],
        out_specs=[big,pl.BlockSpec((1,1,NS,DI),row)],
        out_shape=[jax.ShapeDtypeStruct((S,L//8,8,DI),F32),jax.ShapeDtypeStruct((S,C,NS,DI),F32)],
        scratch_shapes=[pltpu.VMEM((NS,DI),F32),pltpu.VMEM((T,NS,128),F32),pltpu.VMEM((T,NS,128),F32),
                        pltpu.VMEM((T//8,8,DI),F32),pltpu.VMEM((T//8,8,DI),F32)],
        compiler_params=pltpu.CompilerParams(vmem_limit_bytes=32<<20),
    )(rows8(u),rows8(dtp),bT,cT,bias,a2,skip)
    return y.reshape(S,L,DI),st

def bwd_kernel(T,Q,Q2,u_ref,dtp_ref,gs_ref,bT_ref,cT_ref,st_ref,bias_ref,an_ref,skip_ref,
               guc_ref,gdt_ref,gb_ref,gc_ref,gal_ref,gbias_ref,gskip_ref,
               carry,bx,cx,dl,du,hs,ds,gbp,gcp):
    DI=u_ref.shape[-1]
    s_id,c_id=pl.program_id(0),pl.program_id(1)
    @pl.when(c_id==0)
    def _(): carry[...]=jnp.zeros_like(carry)
    @pl.when((c_id==0)&(s_id==0))
    def _():
        gal_ref[...]=jnp.zeros_like(gal_ref)
        gbias_ref[...]=jnp.zeros_like(gbias_ref)
        gskip_ref[...]=jnp.zeros_like(gskip_ref)
    spread(bx,bT_ref,T); spread(cx,cT_ref,T)
    d=softplus(dtp_ref[0]+bias_ref[...][None])
    dl[...]=d
    du[...]=d*u_ref[0]
    gbp[...]=jnp.zeros_like(gbp)
    gcp[...]=jnp.zeros_like(gcp)
    W=Q*128
    def grp(g,_):
        base=pl.multiple_of(g*W,128)
        lanes=[pl.ds(base+q*128,128) for q in range(Q)]
        loc=[slice(q*128,q*128+128) for q in range(Q)]
        an=[an_ref[:,ln] for ln in lanes]
        a2=[x*1.4426950408889634 for x in an]
        def tb(i,s):
            s=list(s)
            for k in range(8):
                t=i*8+k
                b=bx[t]; gc=gcp[t]
                for q in range(Q):
                    dd=dl[i,k:k+1,lanes[q]]; dub=du[i,k:k+1,lanes[q]]; gsr=gs_ref[0,i,k:k+1,lanes[q]]
                    dec=jnp.exp2(dd*a2[q])
                    h=dec*s[q]
                    ds[t,:,loc[q]]=dec
                    hs[t,:,loc[q]]=h
                    s[q]=h+b*dub
                    gc=gc+s[q]*gsr
                gcp[t]=gc
            return tuple(s)
        lax.fori_loop(0,T//8,tb,tuple(st_ref[0,0,:,ln] for ln in lanes))
        for q0 in range(0,Q,Q2):
            qs=range(q0,q0+Q2)
            sk={q:skip_ref[:,lanes[q]] for q in qs}
            def rb(j,cr):
                i=T//8-1-j
                g_,ga={q:cr[0][q-q0] for q in qs},{q:cr[1][q-q0] for q in qs}
                gbs,gsk=cr[2],cr[3]
                m1={q:[None]*8 for q in qs}; m2={q:[None]*8 for q in qs}
                for k in range(7,-1,-1):
                    t=i*8+k
                    b=bx[t]; c=cx[t]; gb=gbp[t]
                    for q in qs:
                        dd=dl[i,k:k+1,lanes[q]]; dub=du[i,k:k+1,lanes[q]]; gsr=gs_ref[0,i,k:k+1,lanes[q]]
                        dec=ds[t,:,loc[q]]; h=hs[t,:,loc[q]]
                        gg=gsr*c+g_[q]
                        g_[q]=gg*dec
                        qq=gg*h
                        m1[q][k]=fold(gg*b)
                        m2[q][k]=fold(qq*an[q])
                        ga[q]=ga[q]+qq*dd
                        gb=gb+gg*dub
                    gbp[t]=gb
                for q in qs:
                    s1=merge8(m1[q]); s2=merge8(m2[q])
                    u8=u_ref[0,i,:,lanes[q]]; d8=dl[i,:,lanes[q]]; gs8=gs_ref[0,i,:,lanes[q]]
                    guc_ref[0,i,:,lanes[q]]=d8*s1+sk[q]*gs8
                    gd=(s2+u8*s1)*jax.nn.sigmoid(dtp_ref[0,i,:,lanes[q]]+bias_ref[:,lanes[q]])
                    gdt_ref[0,i,:,lanes[q]]=gd
                    gbs=gbs[:q-q0]+(gbs[q-q0]+gd,)+gbs[q-q0+1:]
                    gsk=gsk[:q-q0]+(gsk[q-q0]+gs8*u8,)+gsk[q-q0+1:]
                return (tuple(g_[q] for q in qs),tuple(ga[q] for q in qs),gbs,gsk)
            z8=tuple(jnp.zeros((8,128),F32) for q in qs)
            cr=lax.fori_loop(0,T//8,rb,(tuple(carry[:,lanes[q]] for q in qs),tuple(jnp.zeros((NS,128),F32) for q in qs),z8,z8))
            for q in qs:
                carry[:,lanes[q]]=cr[0][q-q0]
                gal_ref[:,lanes[q]]+=cr[1][q-q0]*an[q]
                gbias_ref[:,lanes[q]]+=cr[2][q-q0]
                gskip_ref[:,lanes[q]]+=cr[3][q-q0]
        return 0
    lax.fori_loop(0,DI//W,grp,0)
    ones=jnp.ones((8,128),F32)
    nt=(((1,),(1,)),((),()))
    gb_ref[0,0]=lax.dot_general(ones,gbp[...].reshape(T*NS,128),nt,precision=lax.Precision.HIGHEST,preferred_element_type=F32)
    gc_ref[0,0]=lax.dot_general(ones,gcp[...].reshape(T*NS,128),nt,precision=lax.Precision.HIGHEST,preferred_element_type=F32)

def scan_bwd(u,dtp,gs,bT,cT,st,bias,an,skip,Q=3,Q2=1):
    S,L,DI=u.shape
    C,T=bT.shape[1],bT.shape[3]
    row=lambda s,c:(s,C-1-c,0,0)
    big=pl.BlockSpec((1,T//8,8,DI),row)
    small=pl.BlockSpec((1,1,NS,T),row)
    par=lambda n:pl.BlockSpec((n,DI),lambda s,c:(0,0))
    red=pl.BlockSpec((1,1,8,T*NS),row)
    guc,gdt,gb,gc,gal,gbias,gskip=pl.pallas_call(functools.partial(bwd_kernel,T,Q,Q2),
        grid=(S,C),
        in_specs=[big,big,big,small,small,pl.BlockSpec((1,1,NS,DI),row),par(1),par(NS),par(1)],
        out_specs=[big,big,red,red,par(NS),par(8),par(8)],
        out_shape=[jax.ShapeDtypeStruct((S,L//8,8,DI),F32)]*2+[jax.ShapeDtypeStruct((S,C,8,T*NS),F32)]*2+
                  [jax.ShapeDtypeStruct((NS,DI),F32)]+[jax.ShapeDtypeStruct((8,DI),F32)]*2,
        scratch_shapes=[pltpu.VMEM((NS,DI),F32),pltpu.VMEM((T,NS,128),F32),pltpu.VMEM((T,NS,128),F32),
                        pltpu.VMEM((T//8,8,DI),F32),pltpu.VMEM((T//8,8,DI),F32),
                        pltpu.VMEM((T,NS,Q*128),F32),pltpu.VMEM((T,NS,Q*128),F32),
                        pltpu.VMEM((T,NS,128),F32),pltpu.VMEM((T,NS,128),F32)],
        compiler_params=pltpu.CompilerParams(vmem_limit_bytes=40<<20),
    )(rows8(u),rows8(dtp),rows8(gs),bT,cT,st,bias,an,skip)
    gb=gb[:,:,0].reshape(S,L,NS); gc=gc[:,:,0].reshape(S,L,NS)
    return guc.reshape(S,L,DI),gdt.reshape(S,L,DI),gb,gc,gal,jnp.sum(gbias,0),jnp.sum(gskip,0)


R = 48
QB = 64
CAP = 13
BF = jnp.bfloat16
epsilon = 1e-05
highest = lax.Precision.HIGHEST
root_half = 0.7071067811865476
inv_root_two_pi = 0.3989422804014327
log2e = 1.4426950408889634


def mm(a, b, dims=((1,), (0,)), **kw):
    return lax.dot_general(a, b, (dims, ((), ())), preferred_element_type=F32, **kw)


def swap(x, axis, bit):
    n = lax.axis_size(axis)
    return lax.ppermute(x, axis, [(i, i ^ bit) for i in range(n)])


def bits_of(axis):
    n = lax.axis_size(axis)
    return [1 << k for k in range(n.bit_length() - 1)]


def exchange(x, mask):
    rm, cm = mask
    if rm == 0:
        return swap(x, "col", cm)
    if cm == 0:
        return swap(x, "row", rm)
    rows, cols = lax.axis_size("row"), lax.axis_size("col")
    pairs = [(r * cols + c, (r ^ rm) * cols + (c ^ cm)) for r in range(rows) for c in range(cols)]
    return lax.ppermute(x, ("row", "col"), pairs)


def combos(bits):
    out = [(0, 0)]
    for rb, cb in bits:
        out = out + [(r | rb, c | cb) for r, c in out]
    return out


def stages():
    row, col = bits_of("row"), bits_of("col")
    far = combos([(b, 0) for b in row[1:]])
    plane = combos([(row[0], 0)] + [(0, b) for b in col[1:]])
    return far, plane, (0, col[0])


def add(a, b):
    return (a[0] ^ b[0], a[1] ^ b[1])


def gather_list(x):
    far, plane, core = stages()
    mine = jnp.stack([x] + [exchange(x, m) for m in far[1:]])
    near = [([add(f, m) for f in far], mine if m == (0, 0) else exchange(mine, m)) for m in plane]
    return near + [([add(m, core) for m in ms], exchange(b, core)) for ms, b in near]


def assemble_kernel(masks, moves, count_in, *refs):
    r0, c0 = refs[0][0], refs[0][1]
    ins, outs = refs[1:1 + count_in], refs[1 + count_in:]
    for buf, ms in zip(ins, masks):
        for i, (rm, cm) in enumerate(ms):
            for (row, count, lanes), out, place in moves:
                place(outs[out], r0 ^ rm, c0 ^ cm, buf[i, row:row + count, :lanes])


def put_block(out, r, c, block):
    n, m = block.shape
    out[pl.ds(pl.multiple_of(r * n, n), n), pl.ds(pl.multiple_of(c * m, m), m)] = block


def put_pair(out, r, c, block):
    out[r, c] = block


def take_blocks(gathered):
    rows, cols = lax.axis_size("row"), lax.axis_size("col")
    order = [r * cols + c for ms, _ in gathered for r, c in ms]
    entry = jnp.asarray([order.index(i) for i in range(rows * cols)], jnp.int32)
    me = lax.axis_index("row") * cols + lax.axis_index("col")
    stacked = jnp.concatenate([b for _, b in gathered], axis=0)
    out = jnp.take(stacked, entry[jnp.arange(rows * cols, dtype=jnp.int32) ^ me], axis=0)
    return out.reshape((rows, cols) + stacked.shape[1:])


def assemble(gathered, moves, shapes):
    masks = [ms for ms, _ in gathered]
    bufs = [b for _, b in gathered]
    if any(lanes % 128 for (_, _, lanes), _, _ in moves):
        every = take_blocks(gathered)
        cut = [every[:, :, row:row + count, :lanes] for (row, count, lanes), _, _ in moves]
        return [v if place is put_pair else v.transpose(0, 2, 1, 3).reshape(shape)
                for v, shape, (_, _, place) in zip(cut, shapes, moves)]
    me = jnp.stack([lax.axis_index("row"), lax.axis_index("col")]).astype(jnp.int32)
    vmem = pl.BlockSpec(memory_space=pltpu.VMEM)
    return pl.pallas_call(
        functools.partial(assemble_kernel, masks, moves, len(bufs)),
        in_specs=[pl.BlockSpec(memory_space=pltpu.SMEM)] + [vmem] * len(bufs),
        out_specs=[vmem] * len(shapes),
        out_shape=[jax.ShapeDtypeStruct(s, BF) for s in shapes],
        compiler_params=pltpu.CompilerParams(vmem_limit_bytes=32 << 20),
        cost_estimate=pl.CostEstimate(flops=0, bytes_accessed=4 * sum(b.size for b in bufs), transcendentals=0),
    )(me, *bufs)


def reduce_list(parts):
    far, plane, core = stages()
    rows, cols = lax.axis_size("row"), lax.axis_size("col")
    r0 = lax.axis_index("row")
    near = [k for k in range(cols) if not k & core[1]]
    give = exchange(jnp.stack([parts[k | core[1]] for k in near]), core)
    sums = {k: parts[k].astype(F32) + give[i].astype(F32) for i, k in enumerate(near)}
    block = parts[0].shape[1:]

    def rows_of(k, rm):
        view = sums[k].reshape((rows // 2, 2) + block)
        return lax.dynamic_index_in_dim(view, (r0 ^ rm) & 1, 1, keepdims=False)
    total = rows_of(0, 0)
    for rm, cm in plane[1:]:
        total = total + exchange(rows_of(cm, rm).astype(BF), (rm, cm)).astype(F32)
    done = lax.dynamic_index_in_dim(total, r0 >> 1, 0, keepdims=False)
    for rm, cm in far[1:]:
        piece = lax.dynamic_index_in_dim(total, (r0 ^ rm) >> 1, 0, keepdims=False)
        done = done + exchange(piece.astype(BF), (rm, cm)).astype(F32)
    return done


def column_kernel(count, s_ref, *refs):
    total = mm(refs[0][...], refs[1][...], ((0,), (0,)))
    for k in range(1, count):
        total = total + mm(refs[2 * k][...], refs[2 * k + 1][...], ((0,), (0,)))
    refs[-1][0] = total.astype(BF)


def column_blocks(pairs, cols, my_col):
    n, m = pairs[0][0].shape
    w = pairs[0][1].shape[1] // cols
    count = len(pairs)
    if w % 128:
        total = sum(mm(a, b, ((0,), (0,))) for a, b in pairs).astype(BF).reshape(m, cols, w).transpose(1, 0, 2)
        return jnp.take(total, jnp.arange(cols, dtype=jnp.int32) ^ my_col, axis=0)
    return pl.pallas_call(
        functools.partial(column_kernel, count),
        grid_spec=pltpu.PrefetchScalarGridSpec(
            num_scalar_prefetch=1, grid=(cols,),
            in_specs=[pl.BlockSpec((n, m), lambda k, s: (0, 0)), pl.BlockSpec((n, w), lambda k, s: (0, s[0] ^ k))] * count,
            out_specs=pl.BlockSpec((1, m, w), lambda k, s: (k, 0, 0))),
        out_shape=jax.ShapeDtypeStruct((cols, m, w), BF),
        compiler_params=pltpu.CompilerParams(vmem_limit_bytes=32 << 20),
        cost_estimate=pl.CostEstimate(flops=2 * count * n * m * w * cols, bytes_accessed=2 * (count * (n * m + n * w * cols) + m * w * cols), transcendentals=0),
    )(my_col.reshape(1), *[v for p in pairs for v in p])


def gelu_parts(v):
    phi = 0.5 * (1.0 + lax.erf(v * root_half))
    return v * phi, phi + v * jnp.exp(-0.5 * v * v) * inv_root_two_pi


def expert_kernel(cols, *refs):
    both, up, down = refs[:cols], refs[cols], refs[cols + 1]
    outs, acts, gps = refs[cols + 2:2 * cols + 2], refs[2 * cols + 2], refs[2 * cols + 3]
    width = up.shape[1]
    n = both[0].shape[1]
    rows = jnp.concatenate([b[0] for b in both], axis=0)
    act, slope = gelu_parts(mm(rows[:, :width], up[0]))
    act = act.astype(BF)
    acts[0] = act
    gp = (mm(rows[:, width:], down[0], ((1,), (1,))) * slope).astype(BF)
    gps[0] = gp
    out = mm(act, down[0]).astype(BF)
    gin = mm(gp, up[0], ((1,), (1,))).astype(BF)
    for c in range(cols):
        outs[c][0, :, :width] = out[c * n:(c + 1) * n]
        outs[c][0, :, width:] = gin[c * n:(c + 1) * n]


def weights_kernel(cols, sets, *refs):
    up, down = refs[-2:]
    step = cols + 2
    gu = gd = None
    width = up.shape[1]
    for s in range(sets):
        both, act, gp = refs[s * step:s * step + cols], refs[s * step + cols][0], refs[s * step + cols + 1][0]
        rows = jnp.concatenate([b[0] for b in both], axis=0)
        a = mm(rows[:, :width], gp, ((0,), (0,)))
        b = mm(act, rows[:, width:], ((0,), (0,)))
        gu, gd = (a, b) if gu is None else (gu + a, gd + b)
    up[0] = gu
    down[0] = gd


def per_expert(kernel, ins, shapes, flops):
    tok = lambda a: pl.BlockSpec((1,) + a.shape[1:], lambda e: (e, 0, 0))
    size = sum(a.size * 2 for a in ins) + sum(s.size * s.dtype.itemsize for s in shapes)
    return list(pl.pallas_call(
        kernel, grid=(ins[0].shape[0],),
        in_specs=[tok(a) for a in ins], out_specs=[tok(s) for s in shapes], out_shape=shapes,
        compiler_params=pltpu.CompilerParams(vmem_limit_bytes=56 << 20),
        cost_estimate=pl.CostEstimate(flops=flops, bytes_accessed=size, transcendentals=0),
    )(*ins))


def expert_both(bufs, up, down):
    cols = len(bufs)
    experts, d, f = up.shape
    n = bufs[0].shape[1]
    shapes = ([jax.ShapeDtypeStruct((experts, n, 2 * d), BF)] * cols
              + [jax.ShapeDtypeStruct((experts, n * cols, f), BF)] * 2)
    outs = per_expert(functools.partial(expert_kernel, cols), bufs + [up, down], shapes, 8 * experts * cols * n * d * f)
    return outs[:cols], outs[cols:]


def expert_weights(sets, d, f):
    cols = len(sets[0]) - 2
    experts, n, _ = sets[0][0].shape
    if len(sets) > 1 and len(sets) * cols > 8:
        return [sum(v) for v in zip(*[expert_weights([s], d, f) for s in sets])]
    shapes = [jax.ShapeDtypeStruct((experts, d, f), F32), jax.ShapeDtypeStruct((experts, f, d), F32)]
    return per_expert(functools.partial(weights_kernel, cols, len(sets)), [v for s in sets for v in s], shapes,
                      4 * experts * cols * n * d * f * len(sets))


def to_chunks(b):
    s, length, n = b.shape
    return b.reshape(s, length // QB, QB, n).swapaxes(2, 3)


def on_device(tokens, w_in_x, w_in_z, conv_w, conv_b, w_xproj, w_dt, dt_bias, a_log, d_skip, w_out,
              gain_mix, gain_moe, w_router, w_up, w_down, routes, lengths, cotangent):
    rows, cols = lax.axis_size("row"), lax.axis_size("col")
    parts = rows * cols
    my_col = lax.axis_index("col")
    seqs, length, width = tokens.shape
    experts_here = w_up.shape[0]
    experts_all = experts_here * rows
    inner = w_in_x.shape[1] * cols
    count = seqs * length
    xp = w_xproj.shape[1] * cols
    share = inner // parts

    small = jnp.concatenate([conv_w, conv_b[None], dt_bias[None], a_log, d_skip[None],
                             jnp.concatenate([gain_mix, gain_moe])[None]], axis=0)
    flat = [w_xproj.reshape(-1), w_dt.reshape(-1), w_router.reshape(-1), small.reshape(-1)]
    sizes = [f.shape[0] for f in flat]
    lanes = w_in_x.shape[1]
    extra = -(-sum(sizes) // (16 * lanes)) * 16
    flat = jnp.pad(jnp.concatenate(flat), (0, extra * lanes - sum(sizes))).reshape(extra, lanes)
    here, out_rows, out_lanes = w_in_x.shape[0], w_out.shape[0], w_out.shape[1]
    wide = -(-out_lanes // 128) * 128
    first = gather_list(jnp.concatenate([w_in_x, flat], axis=0))
    full_x, rest = assemble(first, [((0, here, lanes), 0, put_block), ((here, extra, lanes), 1, put_pair)],
                            [(width, inner), (rows, cols, extra, lanes)])
    far_end = first[len(first) // 2 - 1][1]
    late_z, late_o, _ = lax.optimization_barrier((w_in_z, jnp.pad(w_out, ((0, 0), (0, wide - out_lanes))), far_end))
    (full_z,) = assemble(gather_list(late_z), [((0, here, lanes), 0, put_block)], [(width, inner)])
    (wide_out,) = assemble(gather_list(late_o), [((0, out_rows, wide), 0, put_block)], [(inner, cols * wide)])
    lane_of = jnp.arange(cols * wide, dtype=jnp.int32)
    narrow = jnp.where(lane_of % wide < out_lanes, lane_of // wide * out_lanes + lane_of % wide, -1)
    narrow = (narrow[:, None] == jnp.arange(width, dtype=jnp.int32)[None, :]).astype(BF)
    full_out = mm(wide_out, narrow).astype(BF)
    def whole(blocks):
        return blocks.transpose(0, 2, 1, 3).reshape(blocks.shape[0] * blocks.shape[2], -1)
    rest = rest.reshape(rows, cols, extra * lanes)
    cut = [0]
    for n in sizes:
        cut.append(cut[-1] + n)
    full_xproj = whole(rest[:, :, cut[0]:cut[1]].reshape((rows, cols) + w_xproj.shape))
    full_dt = whole(rest[:, :, cut[1]:cut[2]].reshape((rows, cols) + w_dt.shape))
    full_router = whole(rest[:, :, cut[2]:cut[3]].reshape((rows, cols) + w_router.shape))
    small = rest[:, :, cut[3]:cut[4]].reshape((parts,) + small.shape).transpose(1, 0, 2).astype(F32)
    chan = small[:-1].reshape(-1, inner)
    taps = conv_w.shape[0]
    conv_w_f, conv_b_f, dt_bias_f = chan[:taps], chan[taps], chan[taps + 1]
    a_log_f, d_skip_f = chan[taps + 2:taps + 2 + NS], chan[taps + 2 + NS]
    gain_mix_f = small[-1, :, :gain_mix.shape[0]].reshape(width)
    gain_moe_f = small[-1, :, gain_mix.shape[0]:].reshape(width)
    a_neg = -jnp.exp(a_log_f)

    shifted = jnp.where(lane_of % wide < out_lanes, (lane_of // wide ^ my_col) * out_lanes + lane_of % wide, -1)
    shifted = (jnp.arange(width, dtype=jnp.int32)[:, None] == shifted[None, :]).astype(BF)
    router_f = full_router.astype(F32)

    message = -(-experts_here * CAP // 8) * 8
    group = -(-rows * CAP // 16) * 16
    at = jnp.arange(experts_here * group, dtype=jnp.int32)
    there = at % group
    source = jnp.where(there < rows * CAP, there // CAP * message + at // group * CAP + there % CAP, -1)
    sort = (source[:, None] == jnp.arange(rows * message, dtype=jnp.int32)[None, :]).astype(BF)

    def forward(s, x, route, n_live, grad):
        out = {}
        route = route.reshape(length)
        live = jnp.arange(length, dtype=jnp.int32) < n_live
        live_f = live.astype(F32)[:, None]
        onehot = route[:, None] == jnp.arange(experts_all, dtype=jnp.int32)
        hits = (onehot & live[:, None]).astype(BF)
        before = jnp.arange(length)[:, None] > jnp.arange(length)[None, :]
        slot = jnp.sum(mm(before.astype(BF), hits) * hits.astype(F32), axis=-1).astype(jnp.int32)
        target = route // experts_here * message + route % experts_here * CAP + slot
        target = jnp.where(live & (slot < CAP), target, rows * message)
        place = (jnp.arange(rows * message, dtype=jnp.int32)[:, None] == target[None, :]).astype(BF)
        route_f = onehot.astype(F32)

        x = x.astype(F32)
        rms1 = lax.rsqrt(jnp.mean(x * x, axis=-1, keepdims=True) + epsilon)
        normed_mix = (x * rms1 * gain_mix_f).astype(BF)
        inner_x = mm(normed_mix, full_x)
        padded = jnp.pad(inner_x, ((taps - 1, 0), (0, 0)))
        conv_out = conv_b_f
        for k in range(taps):
            conv_out = conv_out + conv_w_f[k] * padded[k:k + length]
        u_value = conv_out * jax.nn.sigmoid(conv_out)
        u_low = u_value.astype(BF)
        projected = mm(u_low, full_xproj)
        dt_low = projected[:, :R].astype(BF)
        dt_pre = mm(dt_low, full_dt)
        bT = to_chunks(projected[None, :, R:R + NS])
        cT = to_chunks(projected[None, :, R + NS:])
        ssm_out, starts = scan_fwd(u_value[None], dt_pre[None], bT, cT, dt_bias_f[None], a_neg * log2e, d_skip_f[None])
        ssm_out = ssm_out[0]
        gate_z = mm(normed_mix, full_z)
        gated = (ssm_out * (gate_z * jax.nn.sigmoid(gate_z))).astype(BF)
        hidden = x + mm(gated, full_out)
        rms2 = lax.rsqrt(jnp.mean(hidden * hidden, axis=-1, keepdims=True) + epsilon)
        normed_moe = hidden * rms2 * gain_moe_f
        probs = jax.nn.softmax(mm(normed_moe, router_f, precision=highest), axis=-1)
        gate_prob = jnp.sum(probs * route_f, axis=-1, keepdims=True)
        grad_y = live_f * grad
        both = jnp.concatenate([normed_moe.astype(BF), (grad_y * gate_prob).astype(BF)], axis=1)
        outgoing = mm(place, both).astype(BF)
        kept = dict(x=x, rms1=rms1, normed_mix=normed_mix, inner_x=inner_x, conv_out=conv_out, u_value=u_value, u_low=u_low,
                    dt_low=dt_low, dt_pre=dt_pre, bT=bT, cT=cT, ssm_out=ssm_out, starts=starts, gate_z=gate_z, gated=gated,
                    hidden=hidden, rms2=rms2, normed_moe=normed_moe, probs=probs, gate_prob=gate_prob, grad_y=grad_y,
                    place=place, route_f=route_f, live_f=live_f)
        return outgoing, kept

    def to_experts(outgoing):
        got = lax.all_to_all(outgoing, "row", split_axis=0, concat_axis=0, tiled=True)
        bufs = [mm(sort, got).astype(BF).reshape(experts_here, group, 2 * width)]
        for bit in bits_of("col")[::-1]:
            bufs = bufs + [swap(v, "col", bit) for v in bufs]
        return bufs

    def from_experts(bufs):
        for bit in bits_of("col"):
            half = len(bufs) // 2
            bufs = [(a.astype(F32) + swap(b, "col", bit).astype(F32)).astype(BF) for a, b in zip(bufs[:half], bufs[half:])]
        got = mm(sort, bufs[0].reshape(experts_here * group, 2 * width), ((0,), (0,))).astype(BF)
        return lax.all_to_all(got, "row", split_axis=0, concat_axis=0, tiled=True)

    def backward(k, home):
        tok = mm(k["place"], home, ((0,), (0,)))
        expert_tok, grad_sent = tok[:, :width], tok[:, width:]
        g = {}
        hat2 = k["hidden"] * k["rms2"]
        mixed_out = (k["live_f"] * (k["hidden"] + k["gate_prob"] * expert_tok)).astype(BF)
        grad_gate = jnp.sum(k["grad_y"] * expert_tok, axis=-1, keepdims=True)
        grad_logits = grad_gate * k["gate_prob"] * (k["route_f"] - k["probs"])
        g["router"] = mm(k["normed_moe"], grad_logits, ((0,), (0,)), precision=highest)
        grad_normed = grad_sent + mm(grad_logits, router_f, ((1,), (1,)), precision=highest)
        g["gain_moe"] = jnp.sum(grad_normed * hat2, axis=0)
        scaled = grad_normed * gain_moe_f
        grad_hidden = k["grad_y"] + k["rms2"] * (scaled - hat2 * jnp.mean(scaled * hat2, axis=-1, keepdims=True))
        grad_mixed = grad_hidden.astype(BF)
        spread_mixed = mm(grad_mixed, shifted).astype(BF)
        grad_gated = mm(grad_mixed, full_out, ((1,), (1,)))
        gate_sig = jax.nn.sigmoid(k["gate_z"])
        grad_ssm = grad_gated * (k["gate_z"] * gate_sig)
        grad_z = (grad_gated * k["ssm_out"] * (gate_sig * (1.0 + k["gate_z"] * (1.0 - gate_sig)))).astype(BF)
        guc, gdt, gb, gc, g["a_log"], g["dt_bias"], g["d_skip"] = scan_bwd(
            k["u_value"][None], k["dt_pre"][None], grad_ssm[None], k["bT"], k["cT"], k["starts"], dt_bias_f[None], a_neg, d_skip_f[None])
        gdt = gdt[0].astype(BF)
        g["dt"] = mm(k["dt_low"], gdt, ((0,), (0,)))
        grad_proj = jnp.concatenate([mm(gdt, full_dt, ((1,), (1,))), gb[0], gc[0]], axis=1).astype(BF)
        g["xproj"] = mm(k["u_low"], grad_proj, ((0,), (0,)))
        grad_u = guc[0] + mm(grad_proj, full_xproj, ((1,), (1,)))
        sig = jax.nn.sigmoid(k["conv_out"])
        grad_conv = grad_u * (sig * (1.0 + k["conv_out"] * (1.0 - sig)))
        g["conv_b"] = jnp.sum(grad_conv, axis=0)
        padded = jnp.pad(k["inner_x"], ((taps - 1, 0), (0, 0)))
        g["conv_w"] = jnp.stack([jnp.sum(grad_conv * padded[i:i + length], axis=0) for i in range(taps)])
        after = jnp.pad(grad_conv, ((0, taps - 1), (0, 0)))
        grad_inner = sum(conv_w_f[i] * after[taps - 1 - i:taps - 1 - i + length] for i in range(taps)).astype(BF)
        grad_nm = mm(grad_inner, full_x, ((1,), (1,))) + mm(grad_z, full_z, ((1,), (1,)))
        hat1 = k["x"] * k["rms1"]
        g["gain_mix"] = jnp.sum(grad_nm * hat1, axis=0)
        scaled = grad_nm * gain_mix_f
        grad_tokens = grad_hidden + k["rms1"] * (scaled - hat1 * jnp.mean(scaled * hat1, axis=-1, keepdims=True))
        return mixed_out, grad_tokens, g, spread_mixed, grad_z, grad_inner

    states, arrivals, last = [], [], None
    for s in range(seqs):
        x = tokens[s]
        if last is not None:
            x, last = lax.optimization_barrier((x, last))
            arrivals.append(to_experts(last))
        last, kept = forward(s, x, routes[s], lengths[s], cotangent[s])
        states.append(kept)
    arrivals.append(to_experts(last))
    homes, sets = [], []
    for bufs in arrivals:
        outs, more = expert_both(bufs, w_up, w_down)
        sets.append(bufs + more)
        homes.append(from_experts(outs))
    grad_w_up, grad_w_down = expert_weights(sets, width, w_up.shape[2])
    results = [backward(k, h) for k, h in zip(states, homes)]
    total = functools.reduce(lambda a, b: jax.tree.map(jnp.add, a, b), [r[2] for r in results])

    grad_out = sum(mm(k["gated"], r[3], ((0,), (0,))) for k, r in zip(states, results)).astype(BF)
    grad_out_block = reduce_list([grad_out[:, k * wide:(k + 1) * wide].reshape(rows, out_rows, wide) for k in range(cols)])
    grad_out_block = grad_out_block[:, :out_lanes]
    grad_in_z = column_blocks([(k["normed_mix"], r[4]) for k, r in zip(states, results)], cols, my_col)
    grad_z_block = reduce_list([grad_in_z[k].reshape(rows, here, lanes) for k in range(cols)])
    grad_in_x = column_blocks([(k["normed_mix"], r[5]) for k, r in zip(states, results)], cols, my_col)

    def blocks(g, like):
        r, c = like.shape
        return g.astype(BF).reshape(rows, r, cols, c).transpose(0, 2, 1, 3).reshape(rows, cols, -1)
    gsmall = jnp.concatenate([total["conv_w"], total["conv_b"][None], total["dt_bias"][None], total["a_log"],
                              total["d_skip"][None]], axis=0).astype(BF)
    ggain = jnp.concatenate([total["gain_mix"].reshape(parts, 1, -1), total["gain_moe"].reshape(parts, 1, -1)], axis=2)
    gsmall = jnp.concatenate([gsmall.reshape(-1, parts, share).transpose(1, 0, 2), ggain.astype(BF)], axis=1)
    gflat = jnp.concatenate([blocks(total["xproj"], w_xproj), blocks(total["dt"], w_dt), blocks(total["router"], w_router),
                             gsmall.reshape(rows, cols, -1)], axis=2)
    gflat = jnp.pad(gflat, ((0, 0), (0, 0), (0, extra * lanes - sum(sizes)))).reshape(rows, cols, extra, lanes)
    done = reduce_list([jnp.concatenate([grad_in_x[k].reshape(rows, here, lanes),
                                         lax.dynamic_index_in_dim(gflat, my_col ^ k, 1, keepdims=False)], axis=1)
                        for k in range(cols)])
    grad_x_block = done[:here]
    done = done[here:].reshape(-1)
    sm = done[cut[3]:cut[4]].reshape(-1, share)
    gm = gain_mix.shape[0]
    return (
        jnp.stack([r[0] for r in results]),
        jnp.stack([r[1] for r in results]),
        grad_x_block,
        grad_z_block,
        sm[:taps],
        sm[taps],
        done[cut[0]:cut[1]].reshape(w_xproj.shape),
        done[cut[1]:cut[2]].reshape(w_dt.shape),
        sm[taps + 1],
        sm[taps + 2:taps + 2 + NS],
        sm[taps + 2 + NS],
        grad_out_block,
        sm[-1, :gm],
        sm[-1, gm:],
        done[cut[2]:cut[3]].reshape(w_router.shape),
        grad_w_up,
        grad_w_down,
    )


def solution(mesh):
    tok = P(("row", "col"), None, None)
    mat = P("row", "col")
    vec = P(("row", "col"))
    chan = P(None, ("row", "col"))
    up, down = P("row", None, "col"), P("row", "col", None)
    return jax.shard_map(
        on_device,
        mesh=mesh,
        in_specs=(tok, mat, mat, chan, vec, mat, mat, vec, chan, vec, mat, vec, vec, mat, up, down, tok, vec, tok),
        out_specs=(tok, tok, mat, mat, chan, vec, mat, mat, vec, chan, vec, mat, vec, vec, mat, up, down),
        check_vma=False,
    )
```

```python
import functools
import jax
import jax.numpy as jnp
from jax import lax
from jax.sharding import PartitionSpec as P
from jax.experimental import pallas as pl
from jax.experimental.pallas import tpu as pltpu
NS = 16
F32 = jnp.float32
SLOT_OF=[4*((i>>2)&1)+2*(1-((i>>1)&1))+(1-(i&1)) for i in range(8)]
def merge8(rows):
    idx=lax.broadcasted_iota(jnp.int32,(8,128),0)
    m4=idx<4; m2=(idx&2)!=0; m1=(idx&1)!=0
    p=[None]*8
    for i in range(8): p[SLOT_OF[i]]=rows[i]
    r=[jnp.where(m4,p[k],p[k+4])+pltpu.roll(jnp.where(m4,p[k+4],p[k]),4,0) for k in range(4)]
    def half(x,y,m,d):
        return jnp.where(m,x+pltpu.roll(x,d,0),y+pltpu.roll(y,8-d,0))
    v=[half(r[k],r[k+2],m2,2) for k in range(2)]
    return half(v[0],v[1],m1,1)
def mm(a, b, dims=((1,), (0,)), **kw):
    return lax.dot_general(a, b, (dims, ((), ())), preferred_element_type=F32, **kw)


NT = ((1,), (1,))
TN = ((0,), (0,))


def softplus(v):
    e = jnp.exp(-jnp.abs(v))
    tiny = e * (1.0 - e * (0.5 - e * (1.0 / 3.0 - e * 0.25)))
    return jnp.maximum(v, 0.0) + jnp.where(e < 0.01, tiny, jnp.log(1.0 + e))


def sigmoid_of_softplus(d):
    tiny = d * (1.0 - d * (0.5 - d * (1.0 / 6.0 - d * (1.0 / 24.0))))
    return jnp.where(d < 0.03, tiny, 1.0 - jnp.exp(-d))


def sigmoid(v):
    return 1.0 / (1.0 + jnp.exp(-v))


def spread(dst, src, T):
    for j in range(T):
        dst[j] = jnp.broadcast_to(src[:, j:j + 1], (NS, 128))


def fold(x):
    return x[0:8] + x[8:16]


def convolve(ext, w, b, T):
    taps = w.shape[0]
    out = b
    for k in range(taps):
        out = out + w[k:k + 1] * ext[9 - taps + k:9 - taps + k + T]
    return out


def mixer_kernel(T, Q, R, x_ref, gain_ref, wx_ref, xpT_ref, wdt_ref, par_ref, a2_ref,
                 nm_ref, in_ref, u_ref, dl_ref, pT_ref, y_ref, st_ref, state, bx, cx, du):
    c = pl.program_id(0)
    L, DI = nm_ref.shape[0], wx_ref.shape[1]
    taps = par_ref.shape[0] - 3

    @pl.when(c == 0)
    def _():
        state[...] = jnp.zeros_like(state)
        x = x_ref[...].astype(F32)
        nm = (x * lax.rsqrt(jnp.mean(x * x, axis=-1, keepdims=True) + 1e-05) * gain_ref[...]).astype(jnp.bfloat16)
        nm_ref[...] = nm
        in_ref[0:8] = jnp.zeros((8, DI), F32)
        in_ref[8:] = mm(nm, wx_ref[...])
    st_ref[0] = state[...]
    par = par_ref[...]
    skip = par[taps + 2:taps + 3]
    conv = convolve(in_ref[pl.ds(pl.multiple_of(c * T, 8), T + 8)], par[:taps], par[taps:taps + 1], T)
    u = conv * sigmoid(conv)
    u_ref[0] = u.reshape(T // 8, 8, DI)
    pT = mm(xpT_ref[...], u.astype(jnp.bfloat16), NT)
    pT_ref[0] = pT
    d = softplus(mm(pT[:R].astype(jnp.bfloat16), wdt_ref[...], TN) + par[taps + 1:taps + 2])
    dl_ref[0] = d.reshape(T // 8, 8, DI)
    du[...] = (d * u).reshape(T // 8, 8, DI)
    spread(bx, pT[R:R + NS], T)
    spread(cx, pT[R + NS:R + 2 * NS], T)

    def grp(g, _):
        base = pl.multiple_of(g * (Q * 128), 128)
        lanes = [pl.ds(base + q * 128, 128) for q in range(Q)]
        a = [a2_ref[:, ln] for ln in lanes]
        sk = [par_ref[taps + 2:taps + 3, ln] for ln in lanes]

        def tb(i, s):
            s = list(s)
            rows = [[] for _ in range(Q)]
            for k in range(8):
                t = i * 8 + k
                b = bx[t]
                cc = cx[t]
                for q in range(Q):
                    dd = dl_ref[0, i, k:k + 1, lanes[q]]
                    dub = du[i, k:k + 1, lanes[q]]
                    s[q] = jnp.exp2(dd * a[q]) * s[q] + b * dub
                    rows[q].append(fold(s[q] * cc))
            for q in range(Q):
                y_ref[0, i, :, lanes[q]] = merge8(rows[q]) + sk[q] * u_ref[0, i, :, lanes[q]]
            return tuple(s)
        s = lax.fori_loop(0, T // 8, tb, tuple(state[:, ln] for ln in lanes))
        for q in range(Q):
            state[:, lanes[q]] = s[q]
        return 0
    lax.fori_loop(0, DI // (Q * 128), grp, 0)


def whole_spec(a):
    return pl.BlockSpec(a.shape, lambda *_: (0,) * len(a.shape))


def sds(shape, dtype=F32):
    return jax.ShapeDtypeStruct(shape, dtype)


def mixer_forward(x, gain, wx, xpT, wdt, par, a2, T, Q=3):
    L, D = x.shape
    DI = wx.shape[1]
    C, XP, R = L // T, xpT.shape[0], wdt.shape[0]
    ins = [x, gain, wx, xpT, wdt, par, a2]
    rows = pl.BlockSpec((1, T // 8, 8, DI), lambda c: (c, 0, 0, 0))
    big = sds((C, T // 8, 8, DI))
    nm, inner = sds((L, D), jnp.bfloat16), sds((L + 8, DI))
    return pl.pallas_call(
        functools.partial(mixer_kernel, T, Q, R), grid=(C,),
        in_specs=[whole_spec(a) for a in ins],
        out_specs=[whole_spec(nm), whole_spec(inner), rows, rows, pl.BlockSpec((1, XP, T), lambda c: (c, 0, 0)), rows,
                   pl.BlockSpec((1, NS, DI), lambda c: (c, 0, 0))],
        out_shape=[nm, inner, big, big, sds((C, XP, T)), big, sds((C, NS, DI))],
        scratch_shapes=[pltpu.VMEM((NS, DI), F32), pltpu.VMEM((T, NS, 128), F32), pltpu.VMEM((T, NS, 128), F32),
                        pltpu.VMEM((T // 8, 8, DI), F32)],
        compiler_params=pltpu.CompilerParams(vmem_limit_bytes=48 << 20),
        cost_estimate=pl.CostEstimate(flops=40000000000, bytes_accessed=16 * L * DI, transcendentals=0),
    )(*ins)


def scan_back_kernel(T, Q, Q2, R, u_ref, dl_ref, gs_ref, in_ref, pT_ref, st_ref, xpT_ref, wdt_ref, par_ref, an_ref,
                     gi_ref, gxp_ref, gwd_ref, gpar_ref, carry, later, bx, cx, du, guc, gdt, hs, ds, gbp, gcp, sums):
    j = pl.program_id(0)
    c = pl.num_programs(0) - 1 - j
    DI = wdt_ref.shape[1]
    taps = par_ref.shape[0] - 3

    @pl.when(j == 0)
    def _():
        for ref in (carry, later, gxp_ref, gwd_ref, gpar_ref, sums):
            ref[...] = jnp.zeros_like(ref)
    pT = pT_ref[0]
    spread(bx, pT[R:R + NS], T)
    spread(cx, pT[R + NS:R + 2 * NS], T)
    du[...] = dl_ref[0] * u_ref[0]
    gbp[...] = jnp.zeros_like(gbp)
    gcp[...] = jnp.zeros_like(gcp)
    W = Q * 128

    def grp(g, _):
        base = pl.multiple_of(g * W, 128)
        lanes = [pl.ds(base + q * 128, 128) for q in range(Q)]
        loc = [slice(q * 128, q * 128 + 128) for q in range(Q)]
        an = [an_ref[:, ln] for ln in lanes]
        a2 = [v * 1.4426950408889634 for v in an]

        def tb(i, s):
            s = list(s)
            for k in range(8):
                t = i * 8 + k
                b = bx[t]
                gc = gcp[t]
                for q in range(Q):
                    dd = dl_ref[0, i, k:k + 1, lanes[q]]
                    dub = du[i, k:k + 1, lanes[q]]
                    gsr = gs_ref[0, i, k:k + 1, lanes[q]]
                    dec = jnp.exp2(dd * a2[q])
                    h = dec * s[q]
                    ds[t, :, loc[q]] = dec
                    hs[t, :, loc[q]] = h
                    s[q] = h + b * dub
                    gc = gc + s[q] * gsr
                gcp[t] = gc
            return tuple(s)
        lax.fori_loop(0, T // 8, tb, tuple(st_ref[0, :, ln] for ln in lanes))
        for q0 in range(0, Q, Q2):
            qs = range(q0, q0 + Q2)
            sk = {q: par_ref[taps + 2:taps + 3, lanes[q]] for q in qs}

            def rb(jj, cr):
                i = T // 8 - 1 - jj
                g_, ga = {q: cr[0][q - q0] for q in qs}, {q: cr[1][q - q0] for q in qs}
                gbs, gsk = list(cr[2]), list(cr[3])
                m1, m2 = {q: [None] * 8 for q in qs}, {q: [None] * 8 for q in qs}
                for k in range(7, -1, -1):
                    t = i * 8 + k
                    b = bx[t]
                    cc = cx[t]
                    gb = gbp[t]
                    for q in qs:
                        dd = dl_ref[0, i, k:k + 1, lanes[q]]
                        dub = du[i, k:k + 1, lanes[q]]
                        gsr = gs_ref[0, i, k:k + 1, lanes[q]]
                        gg = gsr * cc + g_[q]
                        g_[q] = gg * ds[t, :, loc[q]]
                        qq = gg * hs[t, :, loc[q]]
                        m1[q][k] = fold(gg * b)
                        m2[q][k] = fold(qq * an[q])
                        ga[q] = ga[q] + qq * dd
                        gb = gb + gg * dub
                    gbp[t] = gb
                for q in qs:
                    s1 = merge8(m1[q])
                    s2 = merge8(m2[q])
                    u8, d8, gs8 = u_ref[0, i, :, lanes[q]], dl_ref[0, i, :, lanes[q]], gs_ref[0, i, :, lanes[q]]
                    guc[i, :, lanes[q]] = d8 * s1 + sk[q] * gs8
                    gd = (s2 + u8 * s1) * sigmoid_of_softplus(d8)
                    gdt[i, :, lanes[q]] = gd
                    gbs[q - q0] = gbs[q - q0] + gd
                    gsk[q - q0] = gsk[q - q0] + gs8 * u8
                return (tuple(g_[q] for q in qs), tuple(ga[q] for q in qs), tuple(gbs), tuple(gsk))
            z8 = tuple(jnp.zeros((8, 128), F32) for q in qs)
            cr = lax.fori_loop(0, T // 8, rb, (tuple(carry[:, lanes[q]] for q in qs),
                                               tuple(jnp.zeros((NS, 128), F32) for q in qs), z8, z8))
            for q in qs:
                carry[:, lanes[q]] = cr[0][q - q0]
                gpar_ref[taps + 2:taps + 2 + NS, lanes[q]] += cr[1][q - q0] * an[q]
                sums[taps + 1, :, lanes[q]] += cr[2][q - q0]
                sums[taps + 2, :, lanes[q]] += cr[3][q - q0]
        return 0
    lax.fori_loop(0, DI // W, grp, 0)

    gbT = jnp.sum(gbp[...], axis=2).T
    gcT = jnp.sum(gcp[...], axis=2).T
    gd = gdt[...].reshape(T, DI).astype(jnp.bfloat16)
    gpT = jnp.concatenate([mm(wdt_ref[...], gd, NT), gbT, gcT], axis=0).astype(jnp.bfloat16)
    gwd_ref[...] += mm(pT[:R].astype(jnp.bfloat16), gd)
    gxp_ref[...] += mm(gpT, u_ref[0].reshape(T, DI).astype(jnp.bfloat16))
    gu = guc[...].reshape(T, DI) + mm(gpT, xpT_ref[...], TN)
    par = par_ref[...]
    ext = in_ref[pl.ds(pl.multiple_of(c * T, 8), T + 8)]
    conv = convolve(ext, par[:taps], par[taps:taps + 1], T)
    sig = sigmoid(conv)
    gconv = gu * (sig * (1.0 + conv * (1.0 - sig)))
    part = lambda v: jnp.sum(v.reshape(T // 8, 8, DI), axis=0)
    sums[taps] += part(gconv)
    for k in range(taps):
        sums[k] += part(gconv * ext[9 - taps + k:9 - taps + k + T])
    both = jnp.concatenate([gconv, later[...]], axis=0)
    gi = par[0:1] * both[taps - 1:taps - 1 + T]
    for k in range(1, taps):
        gi = gi + par[k:k + 1] * both[taps - 1 - k:taps - 1 - k + T]
    gi_ref[...] = gi.astype(jnp.bfloat16)
    later[...] = gconv[:8]

    @pl.when(c == 0)
    def _():
        for k in range(taps + 2):
            gpar_ref[k:k + 1] = jnp.sum(sums[k], axis=0, keepdims=True)
        gpar_ref[taps + 2 + NS:taps + 3 + NS] = jnp.sum(sums[taps + 2], axis=0, keepdims=True)


def scan_backward(u, dl, gs, inner, pT, st, xpT, wdt, par, an, Q=2, Q2=2):
    C, T8, _, DI = u.shape
    T = T8 * 8
    XP, R = xpT.shape[0], wdt.shape[0]
    n = par.shape[0] + NS
    rev = lambda *shape: pl.BlockSpec((1,) + shape, lambda j: (C - 1 - j,) + (0,) * len(shape))
    rows = rev(T8, 8, DI)
    outs = [sds((C * T, DI), jnp.bfloat16), sds((XP, DI)), sds((R, DI)), sds((n, DI))]
    V = lambda *s: pltpu.VMEM(s, F32)
    return pl.pallas_call(
        functools.partial(scan_back_kernel, T, Q, Q2, R), grid=(C,),
        in_specs=[rows, rows, rows, whole_spec(inner), rev(XP, T), rev(NS, DI)] + [whole_spec(a) for a in (xpT, wdt, par, an)],
        out_specs=[pl.BlockSpec((T, DI), lambda j: (C - 1 - j, 0))] + [whole_spec(o) for o in outs[1:]],
        out_shape=outs,
        scratch_shapes=[V(NS, DI), V(8, DI), V(T, NS, 128), V(T, NS, 128), V(T8, 8, DI), V(T8, 8, DI), V(T8, 8, DI),
                        V(T, NS, Q * 128), V(T, NS, Q * 128), V(T, NS, 128), V(T, NS, 128), V(par.shape[0], 8, DI)],
        compiler_params=pltpu.CompilerParams(vmem_limit_bytes=52 << 20),
        cost_estimate=pl.CostEstimate(flops=80000000000, bytes_accessed=16 * C * T * DI, transcendentals=0),
    )(u, dl, gs, inner, pT, st, xpT, wdt, par, an)


def one_call(kernel, ins, outs, scalars=(), flops=0):
    smem = pl.BlockSpec(memory_space=pltpu.SMEM)
    vmem = pl.BlockSpec(memory_space=pltpu.VMEM)
    size = sum(a.size * a.dtype.itemsize for a in list(ins) + list(outs))
    return pl.pallas_call(
        kernel,
        in_specs=[smem] * len(scalars) + [vmem] * len(ins), out_specs=[vmem] * len(outs), out_shape=list(outs),
        compiler_params=pltpu.CompilerParams(vmem_limit_bytes=56 << 20),
        cost_estimate=pl.CostEstimate(flops=flops, bytes_accessed=size, transcendentals=0),
    )(*scalars, *ins)


def route_kernel(cap, here, message, live_ref, x_ref, nm_ref, y_ref, wz_ref, wo_ref, gain_ref, wr_ref, route_ref, cot_ref,
                 z_ref, gated_ref, hid_ref, place_ref, out_ref, prob_ref, gate_ref):
    bf = jnp.bfloat16
    L = x_ref.shape[0]
    E = wr_ref.shape[1]
    z = mm(nm_ref[...], wz_ref[...])
    z_ref[...] = z
    gated = (y_ref[...] * (z * sigmoid(z))).astype(bf)
    gated_ref[...] = gated
    hid = x_ref[...].astype(F32) + mm(gated, wo_ref[...])
    hid_ref[...] = hid
    nmoe = hid * lax.rsqrt(jnp.mean(hid * hid, axis=-1, keepdims=True) + 1e-05) * gain_ref[...]
    logits = mm(nmoe, wr_ref[...], precision=lax.Precision.HIGHEST)
    e = jnp.exp(logits - jnp.max(logits, axis=-1, keepdims=True))
    probs = e / jnp.sum(e, axis=-1, keepdims=True)
    prob_ref[...] = probs
    route = route_ref[...]
    hot = route == lax.broadcasted_iota(jnp.int32, (L, E), 1)
    gate = jnp.sum(jnp.where(hot, probs, 0.0), axis=-1, keepdims=True)
    gate_ref[...] = gate
    live = lax.broadcasted_iota(jnp.int32, (L, 1), 0) < live_ref[0]
    hits = jnp.where(hot & live, 1.0, 0.0)
    before = lax.broadcasted_iota(jnp.int32, (L, L), 0) > lax.broadcasted_iota(jnp.int32, (L, L), 1)
    slot = jnp.sum(mm(jnp.where(before, 1.0, 0.0).astype(bf), hits.astype(bf)) * hits, axis=-1, keepdims=True).astype(jnp.int32)
    slots = place_ref.shape[1]
    target = route // here * message + route % here * cap + slot
    target = jnp.where(live & (slot < cap), target, slots)
    place = jnp.where(target == lax.broadcasted_iota(jnp.int32, (L, slots), 1), 1.0, 0.0).astype(bf)
    place_ref[...] = place
    D = hid.shape[1]
    gy = jnp.where(live, cot_ref[...], 0.0)
    out_ref[:, :D] = mm(place, nmoe.astype(bf), TN).astype(bf)
    out_ref[:, D:] = mm(place, (gy * gate).astype(bf), TN).astype(bf)


def unroute_kernel(live_ref, home_ref, place_ref, hid_ref, prob_ref, gate_ref, route_ref, cot_ref, gain_ref, wr_ref, wo_ref, sh_ref,
                   z_ref, y_ref, mix_ref, gh_ref, gs_ref, gz_ref, gm_ref, gr_ref, gg_ref):
    bf = jnp.bfloat16
    high = lax.Precision.HIGHEST
    hid, gain = hid_ref[...], gain_ref[...]
    L, D = hid.shape
    E = wr_ref.shape[1]
    tok = mm(place_ref[...], home_ref[...])
    etok, gsent = tok[:, :D], tok[:, D:]
    live = lax.broadcasted_iota(jnp.int32, (L, 1), 0) < live_ref[0]
    gate, probs = gate_ref[...], prob_ref[...]
    mix_ref[...] = jnp.where(live, hid + gate * etok, 0.0).astype(bf)
    gy = jnp.where(live, cot_ref[...], 0.0)
    ggate = jnp.sum(gy * etok, axis=-1, keepdims=True)
    hot = jnp.where(route_ref[...] == lax.broadcasted_iota(jnp.int32, (L, E), 1), 1.0, 0.0)
    glog = ggate * gate * (hot - probs)
    rms = lax.rsqrt(jnp.mean(hid * hid, axis=-1, keepdims=True) + 1e-05)
    hat = hid * rms
    gr_ref[...] = mm(hat * gain, glog, TN, precision=high)
    gnorm = gsent + mm(glog, wr_ref[...], NT, precision=high)
    gg_ref[...] = jnp.sum(gnorm * hat, axis=0, keepdims=True)
    scaled = gnorm * gain
    gh = gy + rms * (scaled - hat * jnp.mean(scaled * hat, axis=-1, keepdims=True))
    gh_ref[...] = gh
    gmix = gh.astype(bf)
    gm_ref[...] = mm(gmix, sh_ref[...]).astype(bf)
    ggated = mm(gmix, wo_ref[...], NT)
    z = z_ref[...]
    sig = sigmoid(z)
    gs_ref[...] = ggated * (z * sig)
    gz_ref[...] = (ggated * y_ref[...] * (sig * (1.0 + z * (1.0 - sig)))).astype(bf)


def token_kernel(gi_ref, gz_ref, wx_ref, wz_ref, x_ref, gh_ref, gain_ref, gt_ref, gg_ref):
    gnm = mm(gi_ref[...], wx_ref[...], NT) + mm(gz_ref[...], wz_ref[...], NT)
    x = x_ref[...].astype(F32)
    rms = lax.rsqrt(jnp.mean(x * x, axis=-1, keepdims=True) + 1e-05)
    hat = x * rms
    gg_ref[...] = jnp.sum(gnm * hat, axis=0, keepdims=True)
    scaled = gnm * gain_ref[...]
    gt_ref[...] = gh_ref[...] + rms * (scaled - hat * jnp.mean(scaled * hat, axis=-1, keepdims=True))


QB = 64
CAP = 13
BF = jnp.bfloat16
root_half = 0.7071067811865476
inv_root_two_pi = 0.3989422804014327
log2e = 1.4426950408889634


def swap(x, axis, bit):
    n = lax.axis_size(axis)
    return lax.ppermute(x, axis, [(i, i ^ bit) for i in range(n)])


def bits_of(axis):
    n = lax.axis_size(axis)
    return [1 << k for k in range(n.bit_length() - 1)]


def exchange(x, mask):
    rm, cm = mask
    if rm == 0:
        return swap(x, "col", cm)
    if cm == 0:
        return swap(x, "row", rm)
    rows, cols = lax.axis_size("row"), lax.axis_size("col")
    pairs = [(r * cols + c, (r ^ rm) * cols + (c ^ cm)) for r in range(rows) for c in range(cols)]
    return lax.ppermute(x, ("row", "col"), pairs)


def combos(bits):
    out = [(0, 0)]
    for rb, cb in bits:
        out = out + [(r | rb, c | cb) for r, c in out]
    return out


def stages():
    row, col = bits_of("row"), bits_of("col")
    far = combos([(b, 0) for b in row[1:]])
    plane = combos([(row[0], 0)] + [(0, b) for b in col[1:]])
    return far, plane, (0, col[0])


def add(a, b):
    return (a[0] ^ b[0], a[1] ^ b[1])


def gather_far(x):
    return jnp.stack([x] + [exchange(x, m) for m in stages()[0][1:]])


def gather_plane(mine):
    return [mine] + [exchange(mine, m) for m in stages()[1][1:]]


def gather_core(near):
    far, plane, core = stages()
    near = [([add(f, m) for f in far], b) for m, b in zip(plane, near)]
    return near + [([add(m, core) for m in ms], exchange(b, core)) for ms, b in near]


def gather_list(x):
    return gather_core(gather_plane(gather_far(x)))


def assemble_kernel(masks, moves, count_in, *refs):
    r0, c0 = refs[0][0], refs[0][1]
    ins, outs = refs[1:1 + count_in], refs[1 + count_in:]
    for buf, ms in zip(ins, masks):
        for i, (rm, cm) in enumerate(ms):
            for (row, count, lanes), out, place in moves:
                place(outs[out], r0 ^ rm, c0 ^ cm, buf[i, row:row + count, :lanes])


def put_block(out, r, c, block):
    n, m = block.shape
    out[pl.ds(pl.multiple_of(r * n, n), n), pl.ds(pl.multiple_of(c * m, m), m)] = block


def put_pair(out, r, c, block):
    out[r, c] = block


def take_blocks(gathered):
    rows, cols = lax.axis_size("row"), lax.axis_size("col")
    order = [r * cols + c for ms, _ in gathered for r, c in ms]
    entry = jnp.asarray([order.index(i) for i in range(rows * cols)], jnp.int32)
    me = lax.axis_index("row") * cols + lax.axis_index("col")
    stacked = jnp.concatenate([b for _, b in gathered], axis=0)
    out = jnp.take(stacked, entry[jnp.arange(rows * cols, dtype=jnp.int32) ^ me], axis=0)
    return out.reshape((rows, cols) + stacked.shape[1:])


def assemble(gathered, moves, shapes):
    masks = [ms for ms, _ in gathered]
    bufs = [b for _, b in gathered]
    if any(lanes % 128 for (_, _, lanes), _, _ in moves):
        every = take_blocks(gathered)
        cut = [every[:, :, row:row + count, :lanes] for (row, count, lanes), _, _ in moves]
        return [v if place is put_pair else v.transpose(0, 2, 1, 3).reshape(shape)
                for v, shape, (_, _, place) in zip(cut, shapes, moves)]
    me = jnp.stack([lax.axis_index("row"), lax.axis_index("col")]).astype(jnp.int32)
    vmem = pl.BlockSpec(memory_space=pltpu.VMEM)
    return pl.pallas_call(
        functools.partial(assemble_kernel, masks, moves, len(bufs)),
        in_specs=[pl.BlockSpec(memory_space=pltpu.SMEM)] + [vmem] * len(bufs),
        out_specs=[vmem] * len(shapes),
        out_shape=[jax.ShapeDtypeStruct(s, BF) for s in shapes],
        compiler_params=pltpu.CompilerParams(vmem_limit_bytes=32 << 20),
        cost_estimate=pl.CostEstimate(flops=0, bytes_accessed=4 * sum(b.size for b in bufs), transcendentals=0),
    )(me, *bufs)


def between(work, give, got):
    result = work(give)
    return lax.optimization_barrier((got, result))


def reduce_core(parts, work=None):
    far, plane, core = stages()
    near = [k for k in range(lax.axis_size("col")) if not k & core[1]]
    give = jnp.stack([parts[k | core[1]] for k in near])
    got = exchange(give, core)
    result = None
    if work:
        got, result = between(work, give, got)
    return [parts[k].astype(F32) + got[i].astype(F32) for i, k in enumerate(near)], result


def reduce_plane_give(sums):
    far, plane, core = stages()
    near = [k for k in range(lax.axis_size("col")) if not k & core[1]]
    rows, r0 = lax.axis_size("row"), lax.axis_index("row")

    def rows_of(k, rm):
        v = sums[near.index(k)]
        return lax.dynamic_index_in_dim(v.reshape((rows // 2, 2) + v.shape[1:]), (r0 ^ rm) & 1, 1, keepdims=False)
    return rows_of(0, 0), [rows_of(cm, rm).astype(BF) for rm, cm in plane[1:]]


def reduce_plane(own, give, work=None):
    got = [exchange(g, m) for g, m in zip(give, stages()[1][1:])]
    result = None
    if work:
        got, result = between(work, give, got)
    return functools.reduce(lambda t, v: t + v.astype(F32), got, own), result


def reduce_far(total, work=None):
    far = stages()[0]
    r0 = lax.axis_index("row")
    give = [lax.dynamic_index_in_dim(total, (r0 ^ rm) >> 1, 0, keepdims=False).astype(BF) for rm, _ in far[1:]]
    got = [exchange(g, m) for g, m in zip(give, far[1:])]
    result = None
    if work:
        got, result = between(work, give, got)
    done = lax.dynamic_index_in_dim(total, r0 >> 1, 0, keepdims=False)
    return functools.reduce(lambda t, v: t + v.astype(F32), got, done), result


def reduce_list(parts):
    own, give = reduce_plane_give(reduce_core(parts)[0])
    return reduce_far(reduce_plane(own, give)[0])[0]


def column_kernel(count, s_ref, *refs):
    total = mm(refs[0][...], refs[1][...], ((0,), (0,)))
    for k in range(1, count):
        total = total + mm(refs[2 * k][...], refs[2 * k + 1][...], ((0,), (0,)))
    refs[-1][0] = total.astype(BF)


def column_blocks(pairs, cols, my_col):
    n, m = pairs[0][0].shape
    w = pairs[0][1].shape[1] // cols
    count = len(pairs)
    if w % 128:
        total = sum(mm(a, b, ((0,), (0,))) for a, b in pairs).astype(BF).reshape(m, cols, w).transpose(1, 0, 2)
        return jnp.take(total, jnp.arange(cols, dtype=jnp.int32) ^ my_col, axis=0)
    return pl.pallas_call(
        functools.partial(column_kernel, count),
        grid_spec=pltpu.PrefetchScalarGridSpec(
            num_scalar_prefetch=1, grid=(cols,),
            in_specs=[pl.BlockSpec((n, m), lambda k, s: (0, 0)), pl.BlockSpec((n, w), lambda k, s: (0, s[0] ^ k))] * count,
            out_specs=pl.BlockSpec((1, m, w), lambda k, s: (k, 0, 0))),
        out_shape=jax.ShapeDtypeStruct((cols, m, w), BF),
        compiler_params=pltpu.CompilerParams(vmem_limit_bytes=32 << 20),
        cost_estimate=pl.CostEstimate(flops=2 * count * n * m * w * cols, bytes_accessed=2 * (count * (n * m + n * w * cols) + m * w * cols), transcendentals=0),
    )(my_col.reshape(1), *[v for p in pairs for v in p])


def gelu_parts(v):
    phi = 0.5 * (1.0 + lax.erf(v * root_half))
    return v * phi, phi + v * jnp.exp(-0.5 * v * v) * inv_root_two_pi


def expert_kernel(cols, *refs):
    both, up, down = refs[:cols], refs[cols], refs[cols + 1]
    outs, acts, gps = refs[cols + 2:2 * cols + 2], refs[2 * cols + 2], refs[2 * cols + 3]
    width = up.shape[1]
    n = both[0].shape[1]
    rows = jnp.concatenate([b[0] for b in both], axis=0)
    act, slope = gelu_parts(mm(rows[:, :width], up[0]))
    act = act.astype(BF)
    acts[0] = act
    gp = (mm(rows[:, width:], down[0], ((1,), (1,))) * slope).astype(BF)
    gps[0] = gp
    out = mm(act, down[0]).astype(BF)
    gin = mm(gp, up[0], ((1,), (1,))).astype(BF)
    for c in range(cols):
        outs[c][0, :, :width] = out[c * n:(c + 1) * n]
        outs[c][0, :, width:] = gin[c * n:(c + 1) * n]


def weights_kernel(cols, sets, *refs):
    up, down = refs[-2:]
    step = cols + 2
    gu = gd = None
    width = up.shape[1]
    for s in range(sets):
        both, act, gp = refs[s * step:s * step + cols], refs[s * step + cols][0], refs[s * step + cols + 1][0]
        rows = jnp.concatenate([b[0] for b in both], axis=0)
        a = mm(rows[:, :width], gp, ((0,), (0,)))
        b = mm(act, rows[:, width:], ((0,), (0,)))
        gu, gd = (a, b) if gu is None else (gu + a, gd + b)
    up[0] = gu
    down[0] = gd


def per_expert(kernel, ins, shapes, flops):
    tok = lambda a: pl.BlockSpec((1,) + a.shape[1:], lambda e: (e, 0, 0))
    size = sum(a.size * 2 for a in ins) + sum(s.size * s.dtype.itemsize for s in shapes)
    return list(pl.pallas_call(
        kernel, grid=(ins[0].shape[0],),
        in_specs=[tok(a) for a in ins], out_specs=[tok(s) for s in shapes], out_shape=shapes,
        compiler_params=pltpu.CompilerParams(vmem_limit_bytes=56 << 20),
        cost_estimate=pl.CostEstimate(flops=flops, bytes_accessed=size, transcendentals=0),
    )(*ins))


def expert_both(bufs, up, down):
    cols = len(bufs)
    experts, d, f = up.shape
    n = bufs[0].shape[1]
    shapes = ([jax.ShapeDtypeStruct((experts, n, 2 * d), BF)] * cols
              + [jax.ShapeDtypeStruct((experts, n * cols, f), BF)] * 2)
    outs = per_expert(functools.partial(expert_kernel, cols), bufs + [up, down], shapes, 8 * experts * cols * n * d * f)
    return outs[:cols], outs[cols:]


def expert_weights(sets, d, f):
    cols = len(sets[0]) - 2
    experts, n, _ = sets[0][0].shape
    if len(sets) > 1 and len(sets) * cols > 8:
        return [sum(v) for v in zip(*[expert_weights([s], d, f) for s in sets])]
    shapes = [jax.ShapeDtypeStruct((experts, d, f), F32), jax.ShapeDtypeStruct((experts, f, d), F32)]
    return per_expert(functools.partial(weights_kernel, cols, len(sets)), [v for s in sets for v in s], shapes,
                      4 * experts * cols * n * d * f * len(sets))


def up_to(n, m):
    return -(-n // m) * m


def tiles_fit(w_in_x, w_xproj, w_out, conv_w):
    lanes = w_in_x.shape[1]
    return (lanes % 128 == 0 and w_in_x.shape[0] % 32 == 0 and up_to(w_xproj.shape[0], 128) + 128 == lanes
            and w_xproj.shape[1] <= 32 and conv_w.shape[1] <= 128 and w_out.shape[0] % 16 == 0
            and up_to(w_out.shape[1], 128) == 256)


def one_hot(shape, match):
    i = lax.broadcasted_iota(jnp.int32, shape, 0)
    j = lax.broadcasted_iota(jnp.int32, shape, 1)
    return jnp.where(match(i, j), 1.0, 0.0).astype(BF)


def pack_kernel(wx, wdt, xp, cw, cb, db, al, ds, gx, gm, wo, wr, first, other, s_dt, s_xp, s_sm, s_out, s_r):
    n = wx.shape[0]
    for s in (s_dt, s_xp, s_sm, s_out, s_r):
        s[...] = jnp.zeros_like(s)
    first[:n] = wx[...]
    s_dt[:wdt.shape[0]] = wdt[...].astype(F32)
    first[n:n + 16] = s_dt[...].astype(BF)
    s_xp[:xp.shape[1], :xp.shape[0]] = xp[...].astype(F32).T
    wide = s_xp.shape[1]
    first[n + 16:, :wide] = s_xp[...].astype(BF)
    at = 0
    for v in (cw, cb, db, al, ds, gx, gm):
        s_sm[at:at + v.shape[0], :v.shape[1]] = v[...].astype(F32)
        at += v.shape[0]
    first[n + 16:, wide:] = s_sm[...].astype(BF)
    s_out[:, :wo.shape[1]] = wo[...].astype(F32)
    other[:wo.shape[0]] = s_out[...].astype(BF)
    s_r[:, :wr.shape[1]] = wr[...].astype(F32)
    half = wr.shape[0] // 2
    other[wo.shape[0]:, :128] = s_r[:half].astype(BF)
    other[wo.shape[0]:, 128:] = s_r[half:].astype(BF)


def pack_params(w_in_x, w_dt, w_xproj, conv_w, conv_b, dt_bias, a_log, d_skip, gain_mix, gain_moe, w_out, w_router):
    n, lanes = w_in_x.shape
    ins = [w_in_x, w_dt, w_xproj, conv_w, conv_b[None], dt_bias[None], a_log, d_skip[None], gain_mix[None], gain_moe[None],
           w_out, w_router]
    vmem = pl.BlockSpec(memory_space=pltpu.VMEM)
    V = lambda *s: pltpu.VMEM(s, F32)
    return pl.pallas_call(
        pack_kernel, in_specs=[vmem] * len(ins), out_specs=[vmem] * 2,
        out_shape=[sds((n + 48, lanes), BF), sds((w_out.shape[0] + w_router.shape[0] // 2, 256), BF)],
        scratch_shapes=[V(16, lanes), V(32, lanes - 128), V(32, 128), V(w_out.shape[0], 256), V(w_router.shape[0], 128)],
    )(*ins)


def each_block(masks, bufs, r0, c0):
    for buf, ms in zip(bufs, masks):
        for i, (rm, cm) in enumerate(ms):
            yield buf, i, r0 ^ rm, c0 ^ cm


def span(i, n):
    return pl.ds(pl.multiple_of(i * n, n), n)


def unpack_first(masks, dims, me, *refs):
    dt_rows, xp_cols, xp_rows, share, gshare, taps, rows, cols = dims
    count = len(masks)
    bufs = refs[:count]
    fx, dt, xpT, par, an, a2, gx, gm, w_dt, w_xp, w_sm = refs[count:]
    n = bufs[0].shape[1] - 48
    lanes = bufs[0].shape[2]
    wide = lanes - 128
    for buf, i, r, c in each_block(masks, bufs, me[0], me[1]):
        fx[span(r, n), span(c, lanes)] = buf[i, :n]
        w_dt[span(r, 16), span(c, lanes)] = buf[i, n:n + 16]
        w_xp[span(c, 32), span(r, wide)] = buf[i, n + 16:, :wide]
        w_sm[:, span(r * cols + c, 128)] = buf[i, n + 16:, wide:]
    pick = one_hot((dt.shape[0], 16 * rows), lambda i, j: (j % 16 < dt_rows) & (j // 16 * dt_rows + j % 16 == i))
    dt[...] = mm(pick, w_dt[...]).astype(BF)
    pick = one_hot((xpT.shape[0], 32 * cols), lambda i, j: (j % 32 < xp_cols) & (j // 32 * xp_cols + j % 32 == i))
    t = mm(pick, w_xp[...])
    xpT[...] = jnp.concatenate([t[:, r * wide:r * wide + xp_rows] for r in range(rows)], axis=1).astype(BF)
    sm = w_sm[...].astype(F32)
    chan = jnp.concatenate([sm[:, p * 128:p * 128 + share] for p in range(rows * cols)], axis=1)
    par[:taps + 2] = chan[:taps + 2]
    par[taps + 2:] = chan[taps + 2 + NS:taps + 3 + NS]
    neg = -jnp.exp(chan[taps + 2:taps + 2 + NS])
    an[...] = neg
    a2[...] = neg * log2e
    gains = jnp.concatenate([sm[taps + 3 + NS:taps + 5 + NS, p * 128:p * 128 + gshare] for p in range(rows * cols)], axis=1)
    gx[...] = gains[:1]
    gm[...] = gains[1:]


def unpack_other(masks, dims, me, *refs):
    out_rows, out_lanes, r_cols, cols = dims
    count = len(masks)
    bufs = refs[:count]
    fo, router, w_out, w_r = refs[count:]
    half = bufs[0].shape[1] - out_rows
    for buf, i, r, c in each_block(masks, bufs, me[0], me[1]):
        w_out[span(r, out_rows), span(c, 256)] = buf[i, :out_rows]
        w_r[pl.ds(pl.multiple_of(r * (2 * half), half), half), span(c, 128)] = buf[i, out_rows:, :128]
        w_r[pl.ds(pl.multiple_of(r * (2 * half) + half, half), half), span(c, 128)] = buf[i, out_rows:, 128:]
    wide = w_out[...]
    fo[...] = jnp.concatenate([wide[:, c * 256:c * 256 + out_lanes] for c in range(cols)], axis=1)
    pick = one_hot((128 * cols, router.shape[1]), lambda i, j: (i % 128 < r_cols) & (i // 128 * r_cols + i % 128 == j))
    router[...] = mm(w_r[...], pick)


def unpack_call(kernel, gathered, dims, outs, scratch):
    masks = [ms for ms, _ in gathered]
    bufs = [b for _, b in gathered]
    me = jnp.stack([lax.axis_index("row"), lax.axis_index("col")]).astype(jnp.int32)
    vmem = pl.BlockSpec(memory_space=pltpu.VMEM)
    return pl.pallas_call(
        functools.partial(kernel, masks, dims),
        in_specs=[pl.BlockSpec(memory_space=pltpu.SMEM)] + [vmem] * len(bufs), out_specs=[vmem] * len(outs), out_shape=outs,
        scratch_shapes=[pltpu.VMEM(s, BF) for s in scratch],
        compiler_params=pltpu.CompilerParams(vmem_limit_bytes=48 << 20),
        cost_estimate=pl.CostEstimate(flops=0, bytes_accessed=4 * sum(b.size for b in bufs), transcendentals=0),
    )(me, *bufs)


def grad_x_kernel(count, dims, s_ref, *refs):
    dt_rows, xp_cols, xp_rows, share, gshare, rows, cols = dims
    pairs = refs[:2 * count]
    gwd, gxp, gpar, gmix, gmoe = (refs[(2 + i) * count:(3 + i) * count] for i in range(5))
    out, w_dt, w_xp, w_sm = refs[7 * count:]
    k = pl.program_id(0)
    c = s_ref[0] ^ k
    n, lanes = out.shape[2] - 48, out.shape[3]
    wide = lanes - 128
    total = lambda vs: functools.reduce(lambda a, b: a + b, [v[...] for v in vs])

    @pl.when(k == 0)
    def _():
        g = total(gwd).astype(BF)
        put = one_hot((16 * rows, g.shape[0]), lambda j, i: (j % 16 < dt_rows) & (j // 16 * dt_rows + j % 16 == i))
        w_dt[...] = mm(put, g).astype(BF)
        g = total(gxp).astype(BF)
        put = one_hot((32 * cols, g.shape[0]), lambda j, i: (j % 32 < xp_cols) & (j // 32 * xp_cols + j % 32 == i))
        t = mm(put, g)
        gap = jnp.zeros((t.shape[0], wide - xp_rows), F32)
        w_xp[...] = jnp.concatenate([v for r in range(rows) for v in (t[:, r * xp_rows:(r + 1) * xp_rows], gap)], axis=1).astype(BF)
        w_sm[...] = jnp.zeros_like(w_sm)
        par, mix, moe = total(gpar), total(gmix), total(gmoe)
        m = par.shape[0]
        for p in range(rows * cols):
            w_sm[:m, p * 128:p * 128 + share] = par[:, p * share:(p + 1) * share]
            w_sm[m:m + 1, p * 128:p * 128 + gshare] = mix[:, p * gshare:(p + 1) * gshare]
            w_sm[m + 1:m + 2, p * 128:p * 128 + gshare] = moe[:, p * gshare:(p + 1) * gshare]
    g = mm(pairs[0][...], pairs[1][...], TN)
    for i in range(1, count):
        g = g + mm(pairs[2 * i][...], pairs[2 * i + 1][...], TN)
    out[0, :, :n] = g.astype(BF).reshape(rows, n, lanes)
    for r in range(rows):
        out[0, r, n:n + 16] = w_dt[r * 16:(r + 1) * 16, span(c, lanes)]
        out[0, r, n + 16:, :wide] = w_xp[span(c, 32), r * wide:(r + 1) * wide]
        out[0, r, n + 16:, wide:] = w_sm[:, span(r * cols + c, 128)].astype(BF)


def grad_x_blocks(pairs, smalls, dims, my_col):
    rows, cols = dims[-2:]
    count = len(pairs)
    n, m = pairs[0][0].shape
    lanes = pairs[0][1].shape[1] // cols
    flat = [v for p in pairs for v in p]
    specs = [pl.BlockSpec((n, m), lambda k, s: (0, 0)), pl.BlockSpec((n, lanes), lambda k, s: (0, s[0] ^ k))] * count
    more = [g[name] for name in ("dt", "xproj", "chan", "gain_mix", "gain_moe") for g in smalls]
    block = m // rows + 48
    return pl.pallas_call(
        functools.partial(grad_x_kernel, count, dims),
        grid_spec=pltpu.PrefetchScalarGridSpec(
            num_scalar_prefetch=1, grid=(cols,), in_specs=specs + [whole_spec(v) for v in more],
            out_specs=pl.BlockSpec((1, rows, block, lanes), lambda k, s: (k, 0, 0, 0)),
            scratch_shapes=[pltpu.VMEM((16 * rows, lanes * cols), BF), pltpu.VMEM((32 * cols, (lanes - 128) * rows), BF),
                            pltpu.VMEM((32, 128 * rows * cols), F32)]),
        out_shape=sds((cols, rows, block, lanes), BF),
        compiler_params=pltpu.CompilerParams(vmem_limit_bytes=48 << 20),
        cost_estimate=pl.CostEstimate(flops=2 * count * n * m * lanes * cols, bytes_accessed=1 << 23, transcendentals=0),
    )(my_col.reshape(1), *flat, *more)


def grad_out_kernel(count, r_cols, s_ref, *refs):
    pairs, routers, out = refs[:2 * count], refs[2 * count:3 * count], refs[3 * count]
    c = s_ref[0] ^ pl.program_id(0)
    rows = out.shape[1]
    g = mm(pairs[0][...], pairs[1][...], TN)
    r = routers[0][...]
    for i in range(1, count):
        g = g + mm(pairs[2 * i][...], pairs[2 * i + 1][...], TN)
        r = r + routers[i][...]
    n = g.shape[0] // rows
    out[0, :, :n] = g.astype(BF).reshape(rows, n, 256)
    put = one_hot((r.shape[1], 128), lambda i, j: (j < r_cols) & (i == c * r_cols + j))
    w = mm(r.astype(BF), put).astype(BF).reshape(rows, r.shape[0] // rows, 128)
    half = w.shape[1] // 2
    out[0, :, n:, :128] = w[:, :half]
    out[0, :, n:, 128:] = w[:, half:]


def grad_out_blocks(pairs, routers, rows, cols, r_cols, my_col):
    count = len(pairs)
    n, m = pairs[0][0].shape
    flat = [v for p in pairs for v in p]
    specs = [pl.BlockSpec((n, m), lambda k, s: (0, 0)), pl.BlockSpec((n, 256), lambda k, s: (0, k))] * count
    block = m // rows + routers[0].shape[0] // rows // 2
    return pl.pallas_call(
        functools.partial(grad_out_kernel, count, r_cols),
        grid_spec=pltpu.PrefetchScalarGridSpec(
            num_scalar_prefetch=1, grid=(cols,), in_specs=specs + [whole_spec(v) for v in routers],
            out_specs=pl.BlockSpec((1, rows, block, 256), lambda k, s: (k, 0, 0, 0))),
        out_shape=sds((cols, rows, block, 256), BF),
        compiler_params=pltpu.CompilerParams(vmem_limit_bytes=48 << 20),
        cost_estimate=pl.CostEstimate(flops=2 * count * n * m * 256 * cols, bytes_accessed=1 << 23, transcendentals=0),
    )(my_col.reshape(1), *flat, *routers)


def weights_part_kernel(cols, sets, lead, *refs):
    out = refs[-1]
    step = cols + 1
    total = None
    for s in range(sets):
        both, other = refs[s * step:s * step + cols], refs[s * step + cols][0]
        width = both[0].shape[2] // 2
        rows = jnp.concatenate([b[0, :, :width] if lead else b[0, :, width:] for b in both], axis=0)
        v = mm(rows, other, TN) if lead else mm(other, rows, TN)
        total = v if total is None else total + v
    out[0] = total


def expert_weights_part(sets, lead, d, f):
    cols = len(sets[0]) - 1
    experts, n, _ = sets[0][0].shape
    if len(sets) > 1 and len(sets) * cols > 8:
        return sum(expert_weights_part([s], lead, d, f) for s in sets)
    shape = (experts, d, f) if lead else (experts, f, d)
    return per_expert(functools.partial(weights_part_kernel, cols, len(sets), lead), [v for s in sets for v in s],
                      [sds(shape)], 2 * experts * cols * n * d * f * len(sets))[0]


def params_generic(w_in_x, w_in_z, conv_w, conv_b, w_xproj, w_dt, dt_bias, a_log, d_skip, w_out, gain_mix, gain_moe, w_router):
    rows, cols = lax.axis_size("row"), lax.axis_size("col")
    parts = rows * cols
    inner, width = w_in_x.shape[1] * cols, w_in_x.shape[0] * rows
    small = jnp.concatenate([conv_w, conv_b[None], dt_bias[None], a_log, d_skip[None],
                             jnp.concatenate([gain_mix, gain_moe])[None]], axis=0)
    flat = [w_xproj.reshape(-1), w_dt.reshape(-1), w_router.reshape(-1), small.reshape(-1)]
    sizes = [f.shape[0] for f in flat]
    lanes = w_in_x.shape[1]
    extra = -(-sum(sizes) // (16 * lanes)) * 16
    flat = jnp.pad(jnp.concatenate(flat), (0, extra * lanes - sum(sizes))).reshape(extra, lanes)
    here, out_rows, out_lanes = w_in_x.shape[0], w_out.shape[0], w_out.shape[1]
    wide = -(-out_lanes // 128) * 128
    first = gather_list(jnp.concatenate([w_in_x, flat], axis=0))
    full_x, rest = assemble(first, [((0, here, lanes), 0, put_block), ((here, extra, lanes), 1, put_pair)],
                            [(width, inner), (rows, cols, extra, lanes)])
    far_end = first[len(first) // 2 - 1][1]
    late_z, late_o, _ = lax.optimization_barrier((w_in_z, jnp.pad(w_out, ((0, 0), (0, wide - out_lanes))), far_end))
    (full_z,) = assemble(gather_list(late_z), [((0, here, lanes), 0, put_block)], [(width, inner)])
    (wide_out,) = assemble(gather_list(late_o), [((0, out_rows, wide), 0, put_block)], [(inner, cols * wide)])
    lane_of = jnp.arange(cols * wide, dtype=jnp.int32)
    narrow = jnp.where(lane_of % wide < out_lanes, lane_of // wide * out_lanes + lane_of % wide, -1)
    narrow = (narrow[:, None] == jnp.arange(width, dtype=jnp.int32)[None, :]).astype(BF)
    full_out = mm(wide_out, narrow).astype(BF)
    def whole(blocks):
        return blocks.transpose(0, 2, 1, 3).reshape(blocks.shape[0] * blocks.shape[2], -1)
    rest = rest.reshape(rows, cols, extra * lanes)
    cut = [0]
    for n in sizes:
        cut.append(cut[-1] + n)
    full_xpT = whole(rest[:, :, cut[0]:cut[1]].reshape((rows, cols) + w_xproj.shape)).T
    full_dt = whole(rest[:, :, cut[1]:cut[2]].reshape((rows, cols) + w_dt.shape))
    router_f = whole(rest[:, :, cut[2]:cut[3]].reshape((rows, cols) + w_router.shape)).astype(F32)
    small = rest[:, :, cut[3]:cut[4]].reshape((parts,) + small.shape).transpose(1, 0, 2).astype(F32)
    chan = small[:-1].reshape(-1, inner)
    taps = conv_w.shape[0]
    par = jnp.concatenate([chan[:taps + 2], chan[taps + 2 + NS:]], axis=0)
    a_neg = -jnp.exp(chan[taps + 2:taps + 2 + NS])
    a_two = a_neg * log2e
    gain_mix_f = small[-1, :, :gain_mix.shape[0]].reshape(1, width)
    gain_moe_f = small[-1, :, gain_mix.shape[0]:].reshape(1, width)
    return lambda done: (full_z, full_out, router_f, done), full_x, full_xpT, full_dt, par, a_neg, a_two, gain_mix_f, gain_moe_f


def params_tiled(w_in_x, w_in_z, conv_w, conv_b, w_xproj, w_dt, dt_bias, a_log, d_skip, w_out, gain_mix, gain_moe, w_router):
    rows, cols = lax.axis_size("row"), lax.axis_size("col")
    here, lanes = w_in_x.shape
    inner, width = lanes * cols, here * rows
    taps, share = conv_w.shape
    packed, other = pack_params(w_in_x, w_dt, w_xproj, conv_w, conv_b, dt_bias, a_log, d_skip, gain_mix, gain_moe, w_out, w_router)
    mine = gather_far(packed)
    late_z, other, _ = lax.optimization_barrier((w_in_z, other, mine))
    mine_z, mine_o = gather_far(late_z), gather_far(other)
    near = gather_plane(mine)
    mine_z, mine_o, _ = lax.optimization_barrier((mine_z, mine_o, near[-1]))
    near_z, near_o = gather_plane(mine_z), gather_plane(mine_o)
    first = gather_core(near)
    dims = (w_dt.shape[0], w_xproj.shape[1], w_xproj.shape[0], share, gain_mix.shape[0], taps, rows, cols)
    full_x, full_dt, full_xpT, par, a_neg, a_two, gx, gm = unpack_call(
        unpack_first, first, dims,
        [sds((width, inner), BF), sds((w_dt.shape[0] * rows, inner), BF), sds((w_xproj.shape[1] * cols, inner), BF),
         sds((taps + 3, inner)), sds((NS, inner)), sds((NS, inner)), sds((1, width)), sds((1, width))],
        [(16 * rows, inner), (32 * cols, (lanes - 128) * rows), (32, 128 * rows * cols)])

    def rest(done):
        z, o, done = lax.optimization_barrier((near_z, near_o, done))
        (full_z,) = assemble(gather_core(z), [((0, here, lanes), 0, put_block)], [(width, inner)])
        full_out, router_f = unpack_call(
            unpack_other, gather_core(o), (w_out.shape[0], w_out.shape[1], w_router.shape[1], cols),
            [sds((inner, width), BF), sds((width, w_router.shape[1] * cols))], [(inner, 256 * cols), (width, 128 * cols)])
        return full_z, full_out, router_f, done
    return rest, full_x, full_xpT, full_dt, par, a_neg, a_two, gx, gm


def grads_generic(nms, gateds, gs, total, w_in_x, w_in_z, w_xproj, w_dt, w_out, w_router, gain_mix, conv_w):
    rows, cols = lax.axis_size("row"), lax.axis_size("col")
    parts = rows * cols
    my_col = lax.axis_index("col")
    here, lanes = w_in_x.shape
    out_rows, out_lanes = w_out.shape
    wide = up_to(out_lanes, 128)
    share = conv_w.shape[1]
    sizes = [w_xproj.size, w_dt.size, w_router.size, (conv_w.shape[0] + 4 + NS) * share]
    extra = up_to(-(-sum(sizes) // lanes), 16)
    cut = [sum(sizes[:i]) for i in range(5)]
    grad_out = sum(mm(k[1], r["gm"], TN) for k, r in zip(zip(nms, gateds), gs)).astype(BF)
    grad_out_block = reduce_list([grad_out[:, k * wide:(k + 1) * wide].reshape(rows, out_rows, wide) for k in range(cols)])
    grad_out_block = grad_out_block[:, :out_lanes]
    grad_in_z = column_blocks([(k[0], r["gz"]) for k, r in zip(zip(nms, gateds), gs)], cols, my_col)
    grad_z_block = reduce_list([grad_in_z[k].reshape(rows, here, lanes) for k in range(cols)])
    grad_in_x = column_blocks([(k[0], r["gi"]) for k, r in zip(zip(nms, gateds), gs)], cols, my_col)

    def blocks(g, like):
        r, c = like.shape
        return g.astype(BF).reshape(rows, r, cols, c).transpose(0, 2, 1, 3).reshape(rows, cols, -1)
    gsmall = total["chan"].astype(BF)
    ggain = jnp.concatenate([total["gain_mix"].reshape(parts, 1, -1), total["gain_moe"].reshape(parts, 1, -1)], axis=2)
    gsmall = jnp.concatenate([gsmall.reshape(-1, parts, share).transpose(1, 0, 2), ggain.astype(BF)], axis=1)
    gflat = jnp.concatenate([blocks(total["xproj"].T, w_xproj), blocks(total["dt"], w_dt), blocks(total["router"], w_router),
                             gsmall.reshape(rows, cols, -1)], axis=2)
    gflat = jnp.pad(gflat, ((0, 0), (0, 0), (0, extra * lanes - sum(sizes)))).reshape(rows, cols, extra, lanes)
    done = reduce_list([jnp.concatenate([grad_in_x[k].reshape(rows, here, lanes),
                                         lax.dynamic_index_in_dim(gflat, my_col ^ k, 1, keepdims=False)], axis=1)
                        for k in range(cols)])
    grad_x_block = done[:here]
    done = done[here:].reshape(-1)
    sm = done[cut[3]:cut[4]].reshape(-1, share)
    gm = gain_mix.shape[0]
    small = (done[cut[0]:cut[1]].reshape(w_xproj.shape), done[cut[1]:cut[2]].reshape(w_dt.shape), sm[:-1], sm[-1, :gm], sm[-1, gm:],
             done[cut[2]:cut[3]].reshape(w_router.shape))
    return (grad_x_block, grad_z_block, grad_out_block), small


def on_device(tokens, w_in_x, w_in_z, conv_w, conv_b, w_xproj, w_dt, dt_bias, a_log, d_skip, w_out,
              gain_mix, gain_moe, w_router, w_up, w_down, routes, lengths, cotangent):
    rows, cols = lax.axis_size("row"), lax.axis_size("col")
    parts = rows * cols
    my_col = lax.axis_index("col")
    seqs, length, width = tokens.shape
    experts_here = w_up.shape[0]
    experts_all = experts_here * rows
    inner = w_in_x.shape[1] * cols
    count = seqs * length
    xp = w_xproj.shape[1] * cols
    share = inner // parts

    tiled = tiles_fit(w_in_x, w_xproj, w_out, conv_w)
    here, lanes = w_in_x.shape
    out_rows, out_lanes = w_out.shape
    wide = up_to(out_lanes, 128)
    taps = conv_w.shape[0]
    rest_of, full_x, full_xpT, full_dt, par, a_neg, a_two, gain_mix_f, gain_moe_f = (
        params_tiled if tiled else params_generic)(
            w_in_x, w_in_z, conv_w, conv_b, w_xproj, w_dt, dt_bias, a_log, d_skip, w_out, gain_mix, gain_moe, w_router)
    lane_of = jnp.arange(cols * wide, dtype=jnp.int32)
    shifted = jnp.where(lane_of % wide < out_lanes, (lane_of // wide ^ my_col) * out_lanes + lane_of % wide, -1)
    shifted = (jnp.arange(width, dtype=jnp.int32)[:, None] == shifted[None, :]).astype(BF)

    message = -(-experts_here * CAP // 8) * 8
    group = -(-rows * CAP // 16) * 16
    at = jnp.arange(experts_here * group, dtype=jnp.int32)
    there = at % group
    source = jnp.where(there < rows * CAP, there // CAP * message + at // group * CAP + there % CAP, -1)
    sort = (source[:, None] == jnp.arange(rows * message, dtype=jnp.int32)[None, :]).astype(BF)

    def mixer(x):
        nm, inner_x, u, dl, pT, ssm, starts = mixer_forward(x, gain_mix_f, full_x, full_xpT, full_dt, par, a_two, QB)
        return dict(x=x, nm=nm, inner=inner_x, u=u, dl=dl, pT=pT, ssm=ssm.reshape(length, inner), starts=starts)

    def router(k, route, n_live, grad):
        n_live = n_live.reshape(1)
        slots = rows * message
        z, gated, hidden, place, outgoing, probs, gate = one_call(
            functools.partial(route_kernel, CAP, experts_here, message),
            [k["x"], k["nm"], k["ssm"], full_z, full_out, gain_moe_f, router_f, route, grad],
            [sds((length, inner)), sds((length, inner), BF), sds((length, width)), sds((length, slots), BF),
             sds((slots, 2 * width), BF), sds((length, experts_all)), sds((length, 1))],
            [n_live], 6 * length * inner * width)
        kept = dict(k, z=z, gated=gated, hidden=hidden, place=place, probs=probs, gate=gate, route=route, n_live=n_live, cot=grad)
        return outgoing, kept

    def home(rows_out):
        return lax.all_to_all(rows_out, "row", split_axis=0, concat_axis=0, tiled=True)

    def arrive(got):
        return mm(sort, got).astype(BF).reshape(experts_here, group, 2 * width)

    def gather_cols(own):
        bufs = [own]
        for bit in bits_of("col")[::-1]:
            bufs = bufs + [swap(v, "col", bit) for v in bufs]
        return bufs

    def from_experts(bufs):
        for bit in bits_of("col"):
            half = len(bufs) // 2
            bufs = [(a.astype(F32) + swap(b, "col", bit).astype(F32)).astype(BF) for a, b in zip(bufs[:half], bufs[half:])]
        return mm(sort, bufs[0].reshape(experts_here * group, 2 * width), ((0,), (0,))).astype(BF)

    def unroute(k, back):
        mixed_out, gh, gs, gz, gm, g_router, g_moe = one_call(
            unroute_kernel,
            [back, k["place"], k["hidden"], k["probs"], k["gate"], k["route"], k["cot"], gain_moe_f, router_f, full_out, shifted,
             k["z"], k["ssm"]],
            [sds((length, width), BF), sds((length, width)), sds((length, inner)), sds((length, inner), BF),
             sds((length, cols * wide), BF), sds((width, experts_all)), sds((1, width))],
            [k["n_live"]], 6 * length * inner * width)
        return dict(mixed_out=mixed_out, gh=gh, gs=gs.reshape(k["u"].shape), gz=gz, gm=gm, router=g_router, gain_moe=g_moe)

    def unscan(k, gs):
        gi, g_xp, g_dt, g_chan = scan_backward(k["u"], k["dl"], gs, k["inner"], k["pT"], k["starts"], full_xpT, full_dt, par, a_neg)
        return dict(gi=gi, xproj=g_xp, dt=g_dt, chan=g_chan)

    def unproject(k, g):
        grad_tokens, g_mix = one_call(
            token_kernel, [g["gi"], g["gz"], full_x, full_z, k["x"], g["gh"], gain_mix_f], [sds((length, width)), sds((1, width))], (),
            4 * length * inner * width)
        return dict(tokens=grad_tokens, gain_mix=g_mix)

    after = lax.optimization_barrier
    ks, owns, last = [], [], None
    for s in range(seqs):
        x = tokens[s]
        if last is not None:
            x, last = after((x, last))
        k = mixer(x)
        if s == 0:
            full_z, full_out, router_f, k["ssm"] = rest_of(k["ssm"])
        if last is not None:
            own = arrive(home(last))
            k["ssm"], own = after((k["ssm"], own))
            owns.append(own)
        last, k = router(k, routes[s], lengths[s], cotangent[s])
        ks.append(k)
    got = home(last)
    sets, sent = [], []
    for s in range(seqs):
        if s == seqs - 1:
            if sets:
                got, outs = after((got, outs))
                sent[-1] = from_experts(outs)
            owns.append(arrive(got))
        bufs = gather_cols(owns[s])
        outs, more = expert_both(bufs, w_up, w_down)
        sets.append((bufs, more))
        sent.append(from_experts(outs))
    backs = [home(v) for v in sent]
    gs_ = []
    for s in range(seqs):
        g = unroute(ks[s], backs[s])
        gs_.append(g)
        if s + 1 < seqs:
            g["gs"], sent[s + 1] = after((g["gs"], sent[s + 1]))
            g.update(unscan(ks[s], g["gs"]))
            g["gi"], backs[s + 1] = after((g["gi"], backs[s + 1]))
    g = gs_[-1]
    nms, gateds = [k["nm"] for k in ks], [k["gated"] for k in ks]
    if tiled:
        out_parts = grad_out_blocks([(v, q["gm"]) for v, q in zip(gateds, gs_)], [q["router"] for q in gs_], rows, cols,
                                    w_router.shape[1], my_col)
        z_parts = column_blocks([(v, q["gz"]) for v, q in zip(nms, gs_)], cols, my_col)
        z_sums, first = reduce_core([z_parts[k].reshape(rows, here, lanes) for k in range(cols)],
                                    lambda give: unproject(ks[0], dict(gs_[0], gi=after((gs_[0]["gi"], give))[0])))
        out_sums, _ = reduce_core([out_parts[k] for k in range(cols)])
        z_own, z_give = reduce_plane_give(z_sums)
        out_own, out_give = reduce_plane_give(out_sums)
        g["gs"], z_give, out_give = after((g["gs"], z_give, out_give))
        g.update(unscan(ks[-1], g["gs"]))
        z_total, _ = reduce_plane(z_own, z_give)
        out_total, _ = reduce_plane(out_own, out_give)
        z_total, out_total, g["gi"] = after((z_total, out_total, g["gi"]))
        z_done, _ = reduce_far(z_total)
        out_done, _ = reduce_far(out_total)
        gs_[0].update(first)
        for s in range(1, seqs - 1):
            gs_[s].update(unproject(ks[s], gs_[s]))
        dims = (w_dt.shape[0], w_xproj.shape[1], w_xproj.shape[0], conv_w.shape[1], gain_mix.shape[0], rows, cols)
        g.update(unproject(ks[-1], g))
        x_parts = grad_x_blocks([(v, q["gi"]) for v, q in zip(nms, gs_)], gs_, dims, my_col)

        def weights(lead):
            def work(give):
                ins, _ = after(([b + [m[1 if lead else 0]] for b, m in sets], give))
                return expert_weights_part(ins, lead, width, w_up.shape[2])
            return work
        x_sums, _ = reduce_core([x_parts[k] for k in range(cols)])
        x_own, x_give = reduce_plane_give(x_sums)
        x_total, grad_w_up = reduce_plane(x_own, x_give, weights(True))
        done, grad_w_down = reduce_far(x_total, weights(False))
        xp = up_to(w_xproj.shape[0], 128)
        sm = done[here + 16:, xp:]
        share = conv_w.shape[1]
        gm = gain_mix.shape[0]
        chan = sm[:taps + 3 + NS, :share]
        half = w_router.shape[0] // 2
        router_done = jnp.concatenate([out_done[out_rows:, :w_router.shape[1]], out_done[out_rows:, 128:128 + w_router.shape[1]]], axis=0)
        small = (done[here + 16:here + 16 + w_xproj.shape[1], :w_xproj.shape[0]].T, done[here:here + w_dt.shape[0]], chan,
                 sm[taps + 3 + NS, :gm], sm[taps + 4 + NS, :gm], router_done)
        blocks = (done[:here], z_done, out_done[:out_rows, :out_lanes])
    else:
        g.update(unscan(ks[-1], g["gs"]))
        for k, q in zip(ks, gs_):
            q.update(unproject(k, q))
        names = ("xproj", "dt", "chan", "gain_mix", "gain_moe", "router")
        total = {n: sum(q[n] for q in gs_) for n in names}
        blocks, small = grads_generic(nms, gateds, gs_, total, w_in_x, w_in_z, w_xproj, w_dt, w_out, w_router, gain_mix, conv_w)
        grad_w_up = expert_weights_part([b + [m[1]] for b, m in sets], True, width, w_up.shape[2])
        grad_w_down = expert_weights_part([b + [m[0]] for b, m in sets], False, width, w_up.shape[2])
    g_xproj, g_dt, chan, g_mix, g_moe, g_router = small
    return (
        jnp.stack([q["mixed_out"] for q in gs_]),
        jnp.stack([q["tokens"] for q in gs_]),
        blocks[0],
        blocks[1],
        chan[:taps],
        chan[taps],
        g_xproj,
        g_dt,
        chan[taps + 1],
        chan[taps + 2:taps + 2 + NS],
        chan[taps + 2 + NS],
        blocks[2],
        g_mix,
        g_moe,
        g_router,
        grad_w_up,
        grad_w_down,
    )


def solution(mesh):
    tok = P(("row", "col"), None, None)
    mat = P("row", "col")
    vec = P(("row", "col"))
    chan = P(None, ("row", "col"))
    up, down = P("row", None, "col"), P("row", "col", None)
    return jax.shard_map(
        on_device,
        mesh=mesh,
        in_specs=(tok, mat, mat, chan, vec, mat, mat, vec, chan, vec, mat, vec, vec, mat, up, down, tok, vec, tok),
        out_specs=(tok, tok, mat, mat, chan, vec, mat, mat, vec, chan, vec, mat, vec, vec, mat, up, down),
        check_vma=False,
    )
```

```python
import functools
import jax
import jax.numpy as jnp
from jax import lax
from jax.sharding import PartitionSpec as P
from jax.experimental import pallas as pl
from jax.experimental.pallas import tpu as pltpu
NS = 16
F32 = jnp.float32
SLOT_OF=[4*((i>>2)&1)+2*(1-((i>>1)&1))+(1-(i&1)) for i in range(8)]
def merge8(rows):
    idx=lax.broadcasted_iota(jnp.int32,(8,128),0)
    m4=idx<4; m2=(idx&2)!=0; m1=(idx&1)!=0
    p=[None]*8
    for i in range(8): p[SLOT_OF[i]]=rows[i]
    r=[jnp.where(m4,p[k],p[k+4])+pltpu.roll(jnp.where(m4,p[k+4],p[k]),4,0) for k in range(4)]
    def half(x,y,m,d):
        return jnp.where(m,x+pltpu.roll(x,d,0),y+pltpu.roll(y,8-d,0))
    v=[half(r[k],r[k+2],m2,2) for k in range(2)]
    return half(v[0],v[1],m1,1)
def mm(a, b, dims=((1,), (0,)), **kw):
    return lax.dot_general(a, b, (dims, ((), ())), preferred_element_type=F32, **kw)


NT = ((1,), (1,))
TN = ((0,), (0,))


def softplus(v):
    e = jnp.exp(-jnp.abs(v))
    tiny = e * (1.0 - e * (0.5 - e * (1.0 / 3.0 - e * 0.25)))
    return jnp.maximum(v, 0.0) + jnp.where(e < 0.01, tiny, jnp.log(1.0 + e))


def sigmoid_of_softplus(d):
    tiny = d * (1.0 - d * (0.5 - d * (1.0 / 6.0 - d * (1.0 / 24.0))))
    return jnp.where(d < 0.03, tiny, 1.0 - jnp.exp(-d))


def sigmoid(v):
    return 1.0 / (1.0 + jnp.exp(-v))


def spread(dst, src, T):
    for j in range(T):
        dst[j] = jnp.broadcast_to(src[:, j:j + 1], (NS, 128))


def fold(x):
    return x[0:8] + x[8:16]


def convolve(ext, w, b, T):
    taps = w.shape[0]
    out = b
    for k in range(taps):
        out = out + w[k:k + 1] * ext[9 - taps + k:9 - taps + k + T]
    return out


def mixer_kernel(T, Q, R, x_ref, gain_ref, wx_ref, xpT_ref, wdt_ref, par_ref, a2_ref,
                 nm_ref, in_ref, cv_ref, u_ref, dl_ref, pT_ref, y_ref, st_ref, state, bx, cx, du):
    c = pl.program_id(0)
    L, DI = nm_ref.shape[0], wx_ref.shape[1]
    taps = par_ref.shape[0] - 3

    @pl.when(c == 0)
    def _():
        state[...] = jnp.zeros_like(state)
        x = x_ref[...].astype(F32)
        nm = (x * lax.rsqrt(jnp.mean(x * x, axis=-1, keepdims=True) + 1e-05) * gain_ref[...]).astype(jnp.bfloat16)
        nm_ref[...] = nm
        in_ref[0:8] = jnp.zeros((8, DI), F32)
        in_ref[8:] = mm(nm, wx_ref[...])
    st_ref[0] = state[...]
    par = par_ref[...]
    skip = par[taps + 2:taps + 3]
    conv = convolve(in_ref[pl.ds(pl.multiple_of(c * T, 8), T + 8)], par[:taps], par[taps:taps + 1], T)
    cv_ref[0] = conv.reshape(T // 8, 8, DI)
    u = conv * sigmoid(conv)
    u_ref[0] = u.reshape(T // 8, 8, DI)
    pT = mm(xpT_ref[...], u.astype(jnp.bfloat16), NT)
    pT_ref[0] = pT
    d = softplus(mm(pT[:R].astype(jnp.bfloat16), wdt_ref[...], TN) + par[taps + 1:taps + 2])
    dl_ref[0] = d.reshape(T // 8, 8, DI)
    du[...] = (d * u).reshape(T // 8, 8, DI)
    spread(bx, pT[R:R + NS], T)
    spread(cx, pT[R + NS:R + 2 * NS], T)

    def grp(g, _):
        base = pl.multiple_of(g * (Q * 128), 128)
        lanes = [pl.ds(base + q * 128, 128) for q in range(Q)]
        a = [a2_ref[:, ln] for ln in lanes]
        sk = [par_ref[taps + 2:taps + 3, ln] for ln in lanes]

        def tb(i, s):
            s = list(s)
            rows = [[] for _ in range(Q)]
            for k in range(8):
                t = i * 8 + k
                b = bx[t]
                cc = cx[t]
                for q in range(Q):
                    dd = dl_ref[0, i, k:k + 1, lanes[q]]
                    dub = du[i, k:k + 1, lanes[q]]
                    s[q] = jnp.exp2(dd * a[q]) * s[q] + b * dub
                    rows[q].append(fold(s[q] * cc))
            for q in range(Q):
                y_ref[0, i, :, lanes[q]] = merge8(rows[q]) + sk[q] * u_ref[0, i, :, lanes[q]]
            return tuple(s)
        s = lax.fori_loop(0, T // 8, tb, tuple(state[:, ln] for ln in lanes))
        for q in range(Q):
            state[:, lanes[q]] = s[q]
        return 0
    lax.fori_loop(0, DI // (Q * 128), grp, 0)


def whole_spec(a):
    return pl.BlockSpec(a.shape, lambda *_: (0,) * len(a.shape))


def sds(shape, dtype=F32):
    return jax.ShapeDtypeStruct(shape, dtype)


def mixer_forward(x, gain, wx, xpT, wdt, par, a2, T, Q=6):
    L, D = x.shape
    DI = wx.shape[1]
    C, XP, R = L // T, xpT.shape[0], wdt.shape[0]
    ins = [x, gain, wx, xpT, wdt, par, a2]
    rows = pl.BlockSpec((1, T // 8, 8, DI), lambda c: (c, 0, 0, 0))
    big = sds((C, T // 8, 8, DI))
    nm, inner = sds((L, D), jnp.bfloat16), sds((L + 8, DI))
    return pl.pallas_call(
        functools.partial(mixer_kernel, T, Q, R), grid=(C,),
        in_specs=[whole_spec(a) for a in ins],
        out_specs=[whole_spec(nm), whole_spec(inner), rows, rows, rows, pl.BlockSpec((1, XP, T), lambda c: (c, 0, 0)), rows,
                   pl.BlockSpec((1, NS, DI), lambda c: (c, 0, 0))],
        out_shape=[nm, inner, big, big, big, sds((C, XP, T)), big, sds((C, NS, DI))],
        scratch_shapes=[pltpu.VMEM((NS, DI), F32), pltpu.VMEM((T, NS, 128), F32), pltpu.VMEM((T, NS, 128), F32),
                        pltpu.VMEM((T // 8, 8, DI), F32)],
        compiler_params=pltpu.CompilerParams(vmem_limit_bytes=48 << 20),
        cost_estimate=pl.CostEstimate(flops=40000000000, bytes_accessed=16 * L * DI, transcendentals=0),
    )(*ins)


def scan_back_kernel(T, Q, Q2, R, u_ref, dl_ref, gs_ref, cv_ref, in_ref, pT_ref, st_ref, xpT_ref, wdt_ref, par_ref, an_ref,
                     gi_ref, gxp_ref, gwd_ref, gpar_ref, carry, later, bx, cx, du, guc, gdt, hs, ds, gbp, gcp, sums):
    j = pl.program_id(0)
    c = pl.num_programs(0) - 1 - j
    DI = wdt_ref.shape[1]
    taps = par_ref.shape[0] - 3

    @pl.when(j == 0)
    def _():
        for ref in (carry, later, gxp_ref, gwd_ref, gpar_ref, sums):
            ref[...] = jnp.zeros_like(ref)
    pT = pT_ref[0]
    spread(bx, pT[R:R + NS], T)
    spread(cx, pT[R + NS:R + 2 * NS], T)
    du[...] = dl_ref[0] * u_ref[0]
    gbp[...] = jnp.zeros_like(gbp)
    gcp[...] = jnp.zeros_like(gcp)
    W = Q * 128

    def grp(g, _):
        base = pl.multiple_of(g * W, 128)
        lanes = [pl.ds(base + q * 128, 128) for q in range(Q)]
        loc = [slice(q * 128, q * 128 + 128) for q in range(Q)]
        an = [an_ref[:, ln] for ln in lanes]
        a2 = [v * 1.4426950408889634 for v in an]

        def tb(i, s):
            s = list(s)
            for k in range(8):
                t = i * 8 + k
                b = bx[t]
                gc = gcp[t]
                for q in range(Q):
                    dd = dl_ref[0, i, k:k + 1, lanes[q]]
                    dub = du[i, k:k + 1, lanes[q]]
                    gsr = gs_ref[0, i, k:k + 1, lanes[q]]
                    dec = jnp.exp2(dd * a2[q])
                    h = dec * s[q]
                    ds[t, :, loc[q]] = dec
                    hs[t, :, loc[q]] = h
                    s[q] = h + b * dub
                    gc = gc + s[q] * gsr
                gcp[t] = gc
            return tuple(s)
        lax.fori_loop(0, T // 8, tb, tuple(st_ref[0, :, ln] for ln in lanes))
        for q0 in range(0, Q, Q2):
            qs = range(q0, q0 + Q2)
            sk = {q: par_ref[taps + 2:taps + 3, lanes[q]] for q in qs}

            def rb(jj, cr):
                i = T // 8 - 1 - jj
                g_, ga = {q: cr[0][q - q0] for q in qs}, {q: cr[1][q - q0] for q in qs}
                gbs, gsk = list(cr[2]), list(cr[3])
                m1, m2 = {q: [None] * 8 for q in qs}, {q: [None] * 8 for q in qs}
                for k in range(7, -1, -1):
                    t = i * 8 + k
                    b = bx[t]
                    cc = cx[t]
                    gb = gbp[t]
                    for q in qs:
                        dd = dl_ref[0, i, k:k + 1, lanes[q]]
                        dub = du[i, k:k + 1, lanes[q]]
                        gsr = gs_ref[0, i, k:k + 1, lanes[q]]
                        gg = gsr * cc + g_[q]
                        g_[q] = gg * ds[t, :, loc[q]]
                        qq = gg * hs[t, :, loc[q]]
                        m1[q][k] = fold(gg * b)
                        m2[q][k] = fold(qq * an[q])
                        ga[q] = ga[q] + qq * dd
                        gb = gb + gg * dub
                    gbp[t] = gb
                for q in qs:
                    s1 = merge8(m1[q])
                    s2 = merge8(m2[q])
                    u8, d8, gs8 = u_ref[0, i, :, lanes[q]], dl_ref[0, i, :, lanes[q]], gs_ref[0, i, :, lanes[q]]
                    guc[i, :, lanes[q]] = d8 * s1 + sk[q] * gs8
                    gd = (s2 + u8 * s1) * sigmoid_of_softplus(d8)
                    gdt[i, :, lanes[q]] = gd
                    gbs[q - q0] = gbs[q - q0] + gd
                    gsk[q - q0] = gsk[q - q0] + gs8 * u8
                return (tuple(g_[q] for q in qs), tuple(ga[q] for q in qs), tuple(gbs), tuple(gsk))
            z8 = tuple(jnp.zeros((8, 128), F32) for q in qs)
            cr = lax.fori_loop(0, T // 8, rb, (tuple(carry[:, lanes[q]] for q in qs),
                                               tuple(jnp.zeros((NS, 128), F32) for q in qs), z8, z8), unroll=2)
            for q in qs:
                carry[:, lanes[q]] = cr[0][q - q0]
                gpar_ref[taps + 2:taps + 2 + NS, lanes[q]] += cr[1][q - q0] * an[q]
                sums[taps + 1, :, lanes[q]] += cr[2][q - q0]
                sums[taps + 2, :, lanes[q]] += cr[3][q - q0]
        return 0
    lax.fori_loop(0, DI // W, grp, 0)

    gbT = jnp.sum(gbp[...], axis=2).T
    gcT = jnp.sum(gcp[...], axis=2).T
    gd = gdt[...].reshape(T, DI).astype(jnp.bfloat16)
    gpT = jnp.concatenate([mm(wdt_ref[...], gd, NT), gbT, gcT], axis=0).astype(jnp.bfloat16)
    gwd_ref[...] += mm(pT[:R].astype(jnp.bfloat16), gd)
    gxp_ref[...] += mm(gpT, u_ref[0].reshape(T, DI).astype(jnp.bfloat16))
    gu = guc[...].reshape(T, DI) + mm(gpT, xpT_ref[...], TN)
    par = par_ref[...]
    conv = cv_ref[0].reshape(T, DI)
    sig = sigmoid(conv)
    gconv = gu * (sig * (1.0 + conv * (1.0 - sig)))
    part = lambda v: jnp.sum(v.reshape(T // 8, 8, DI), axis=0)
    sums[taps] += part(gconv)
    inner_x = in_ref[pl.ds(pl.multiple_of(c * T + 8, 8), T)]
    both = jnp.concatenate([gconv, later[...]], axis=0)
    gi = None
    for k in range(taps):
        ahead = both[taps - 1 - k:taps - 1 - k + T]
        sums[k] += part(ahead * inner_x)
        gi = par[k:k + 1] * ahead if gi is None else gi + par[k:k + 1] * ahead
    gi_ref[...] = gi.astype(jnp.bfloat16)
    later[...] = gconv[:8]

    @pl.when(c == 0)
    def _():
        for k in range(taps + 2):
            gpar_ref[k:k + 1] = jnp.sum(sums[k], axis=0, keepdims=True)
        gpar_ref[taps + 2 + NS:taps + 3 + NS] = jnp.sum(sums[taps + 2], axis=0, keepdims=True)


def scan_backward(u, dl, gs, conv, inner, pT, st, xpT, wdt, par, an, Q=3, Q2=3):
    C, T8, _, DI = u.shape
    T = T8 * 8
    XP, R = xpT.shape[0], wdt.shape[0]
    n = par.shape[0] + NS
    rev = lambda *shape: pl.BlockSpec((1,) + shape, lambda j: (C - 1 - j,) + (0,) * len(shape))
    rows = rev(T8, 8, DI)
    outs = [sds((C * T, DI), jnp.bfloat16), sds((XP, DI)), sds((R, DI)), sds((n, DI))]
    V = lambda *s: pltpu.VMEM(s, F32)
    return pl.pallas_call(
        functools.partial(scan_back_kernel, T, Q, Q2, R), grid=(C,),
        in_specs=[rows, rows, rows, rows, whole_spec(inner), rev(XP, T), rev(NS, DI)] + [whole_spec(a) for a in (xpT, wdt, par, an)],
        out_specs=[pl.BlockSpec((T, DI), lambda j: (C - 1 - j, 0))] + [whole_spec(o) for o in outs[1:]],
        out_shape=outs,
        scratch_shapes=[V(NS, DI), V(8, DI), V(T, NS, 128), V(T, NS, 128), V(T8, 8, DI), V(T8, 8, DI), V(T8, 8, DI),
                        V(T, NS, Q * 128), V(T, NS, Q * 128), V(T, NS, 128), V(T, NS, 128), V(par.shape[0], 8, DI)],
        compiler_params=pltpu.CompilerParams(vmem_limit_bytes=52 << 20),
        cost_estimate=pl.CostEstimate(flops=80000000000, bytes_accessed=16 * C * T * DI, transcendentals=0),
    )(u, dl, gs, conv, inner, pT, st, xpT, wdt, par, an)


def one_call(kernel, ins, outs, scalars=(), flops=0):
    smem = pl.BlockSpec(memory_space=pltpu.SMEM)
    vmem = pl.BlockSpec(memory_space=pltpu.VMEM)
    size = sum(a.size * a.dtype.itemsize for a in list(ins) + list(outs))
    return pl.pallas_call(
        kernel,
        in_specs=[smem] * len(scalars) + [vmem] * len(ins), out_specs=[vmem] * len(outs), out_shape=list(outs),
        compiler_params=pltpu.CompilerParams(vmem_limit_bytes=56 << 20),
        cost_estimate=pl.CostEstimate(flops=flops, bytes_accessed=size, transcendentals=0),
    )(*scalars, *ins)


def route_kernel(cap, here, message, live_ref, x_ref, nm_ref, y_ref, wz_ref, wo_ref, gain_ref, wr_ref, route_ref, cot_ref,
                 z_ref, gated_ref, hid_ref, place_ref, out_ref, prob_ref, gate_ref):
    bf = jnp.bfloat16
    L = x_ref.shape[0]
    E = wr_ref.shape[1]
    z = mm(nm_ref[...], wz_ref[...])
    z_ref[...] = z
    gated = (y_ref[...] * (z * sigmoid(z))).astype(bf)
    gated_ref[...] = gated
    hid = x_ref[...].astype(F32) + mm(gated, wo_ref[...])
    hid_ref[...] = hid
    nmoe = hid * lax.rsqrt(jnp.mean(hid * hid, axis=-1, keepdims=True) + 1e-05) * gain_ref[...]
    logits = mm(nmoe, wr_ref[...], precision=lax.Precision.HIGHEST)
    e = jnp.exp(logits - jnp.max(logits, axis=-1, keepdims=True))
    probs = e / jnp.sum(e, axis=-1, keepdims=True)
    prob_ref[...] = probs
    route = route_ref[...]
    hot = route == lax.broadcasted_iota(jnp.int32, (L, E), 1)
    gate = jnp.sum(jnp.where(hot, probs, 0.0), axis=-1, keepdims=True)
    gate_ref[...] = gate
    live = lax.broadcasted_iota(jnp.int32, (L, 1), 0) < live_ref[0]
    hits = jnp.where(hot & live, 1.0, 0.0)
    before = lax.broadcasted_iota(jnp.int32, (L, L), 0) > lax.broadcasted_iota(jnp.int32, (L, L), 1)
    slot = jnp.sum(mm(jnp.where(before, 1.0, 0.0).astype(bf), hits.astype(bf)) * hits, axis=-1, keepdims=True).astype(jnp.int32)
    slots = place_ref.shape[1]
    target = route // here * message + route % here * cap + slot
    target = jnp.where(live & (slot < cap), target, slots)
    place = jnp.where(target == lax.broadcasted_iota(jnp.int32, (L, slots), 1), 1.0, 0.0).astype(bf)
    place_ref[...] = place
    D = hid.shape[1]
    gy = jnp.where(live, cot_ref[...], 0.0)
    out_ref[:, :D] = mm(place, nmoe.astype(bf), TN).astype(bf)
    out_ref[:, D:] = mm(place, (gy * gate).astype(bf), TN).astype(bf)


def unroute_kernel(live_ref, home_ref, place_ref, hid_ref, prob_ref, gate_ref, route_ref, cot_ref, gain_ref, wr_ref, wo_ref, sh_ref,
                   z_ref, y_ref, mix_ref, gh_ref, gs_ref, gz_ref, gm_ref, gr_ref, gg_ref):
    bf = jnp.bfloat16
    high = lax.Precision.HIGHEST
    hid, gain = hid_ref[...], gain_ref[...]
    L, D = hid.shape
    E = wr_ref.shape[1]
    tok = mm(place_ref[...], home_ref[...])
    etok, gsent = tok[:, :D], tok[:, D:]
    live = lax.broadcasted_iota(jnp.int32, (L, 1), 0) < live_ref[0]
    gate, probs = gate_ref[...], prob_ref[...]
    mix_ref[...] = jnp.where(live, hid + gate * etok, 0.0).astype(bf)
    gy = jnp.where(live, cot_ref[...], 0.0)
    ggate = jnp.sum(gy * etok, axis=-1, keepdims=True)
    hot = jnp.where(route_ref[...] == lax.broadcasted_iota(jnp.int32, (L, E), 1), 1.0, 0.0)
    glog = ggate * gate * (hot - probs)
    rms = lax.rsqrt(jnp.mean(hid * hid, axis=-1, keepdims=True) + 1e-05)
    hat = hid * rms
    gr_ref[...] = mm(hat * gain, glog, TN, precision=high)
    gnorm = gsent + mm(glog, wr_ref[...], NT, precision=high)
    gg_ref[...] = jnp.sum(gnorm * hat, axis=0, keepdims=True)
    scaled = gnorm * gain
    gh = gy + rms * (scaled - hat * jnp.mean(scaled * hat, axis=-1, keepdims=True))
    gh_ref[...] = gh
    gmix = gh.astype(bf)
    gm_ref[...] = mm(gmix, sh_ref[...]).astype(bf)
    ggated = mm(gmix, wo_ref[...], NT)
    z = z_ref[...]
    sig = sigmoid(z)
    gs_ref[...] = ggated * (z * sig)
    gz_ref[...] = (ggated * y_ref[...] * (sig * (1.0 + z * (1.0 - sig)))).astype(bf)


def token_kernel(gi_ref, gz_ref, wx_ref, wz_ref, x_ref, gh_ref, gain_ref, gt_ref, gg_ref):
    gnm = mm(gi_ref[...], wx_ref[...], NT) + mm(gz_ref[...], wz_ref[...], NT)
    x = x_ref[...].astype(F32)
    rms = lax.rsqrt(jnp.mean(x * x, axis=-1, keepdims=True) + 1e-05)
    hat = x * rms
    gg_ref[...] = jnp.sum(gnm * hat, axis=0, keepdims=True)
    scaled = gnm * gain_ref[...]
    gt_ref[...] = gh_ref[...] + rms * (scaled - hat * jnp.mean(scaled * hat, axis=-1, keepdims=True))


QB = 64
CAP = 13
BF = jnp.bfloat16
root_half = 0.7071067811865476
inv_root_two_pi = 0.3989422804014327
log2e = 1.4426950408889634


def swap(x, axis, bit):
    n = lax.axis_size(axis)
    return lax.ppermute(x, axis, [(i, i ^ bit) for i in range(n)])


def bits_of(axis):
    n = lax.axis_size(axis)
    return [1 << k for k in range(n.bit_length() - 1)]


def exchange(x, mask):
    rm, cm = mask
    if rm == 0:
        return swap(x, "col", cm)
    if cm == 0:
        return swap(x, "row", rm)
    rows, cols = lax.axis_size("row"), lax.axis_size("col")
    pairs = [(r * cols + c, (r ^ rm) * cols + (c ^ cm)) for r in range(rows) for c in range(cols)]
    return lax.ppermute(x, ("row", "col"), pairs)


def combos(bits):
    out = [(0, 0)]
    for rb, cb in bits:
        out = out + [(r | rb, c | cb) for r, c in out]
    return out


def stages():
    row, col = bits_of("row"), bits_of("col")
    far = combos([(b, 0) for b in row[1:]])
    plane = combos([(row[0], 0)] + [(0, b) for b in col[1:]])
    return far, plane, (0, col[0])


def add(a, b):
    return (a[0] ^ b[0], a[1] ^ b[1])


def gather_far(x):
    return jnp.stack([x] + [exchange(x, m) for m in stages()[0][1:]])


def gather_plane(mine):
    return [mine] + [exchange(mine, m) for m in stages()[1][1:]]


def gather_core(near):
    far, plane, core = stages()
    near = [([add(f, m) for f in far], b) for m, b in zip(plane, near)]
    return near + [([add(m, core) for m in ms], exchange(b, core)) for ms, b in near]


def gather_list(x):
    return gather_core(gather_plane(gather_far(x)))


def assemble_kernel(masks, moves, count_in, *refs):
    r0, c0 = refs[0][0], refs[0][1]
    ins, outs = refs[1:1 + count_in], refs[1 + count_in:]
    for buf, ms in zip(ins, masks):
        for i, (rm, cm) in enumerate(ms):
            for (row, count, lanes), out, place in moves:
                place(outs[out], r0 ^ rm, c0 ^ cm, buf[i, row:row + count, :lanes])


def put_block(out, r, c, block):
    n, m = block.shape
    out[pl.ds(pl.multiple_of(r * n, n), n), pl.ds(pl.multiple_of(c * m, m), m)] = block


def put_pair(out, r, c, block):
    out[r, c] = block


def take_blocks(gathered):
    rows, cols = lax.axis_size("row"), lax.axis_size("col")
    order = [r * cols + c for ms, _ in gathered for r, c in ms]
    entry = jnp.asarray([order.index(i) for i in range(rows * cols)], jnp.int32)
    me = lax.axis_index("row") * cols + lax.axis_index("col")
    stacked = jnp.concatenate([b for _, b in gathered], axis=0)
    out = jnp.take(stacked, entry[jnp.arange(rows * cols, dtype=jnp.int32) ^ me], axis=0)
    return out.reshape((rows, cols) + stacked.shape[1:])


def assemble(gathered, moves, shapes):
    masks = [ms for ms, _ in gathered]
    bufs = [b for _, b in gathered]
    if any(lanes % 128 for (_, _, lanes), _, _ in moves):
        every = take_blocks(gathered)
        cut = [every[:, :, row:row + count, :lanes] for (row, count, lanes), _, _ in moves]
        return [v if place is put_pair else v.transpose(0, 2, 1, 3).reshape(shape)
                for v, shape, (_, _, place) in zip(cut, shapes, moves)]
    me = jnp.stack([lax.axis_index("row"), lax.axis_index("col")]).astype(jnp.int32)
    vmem = pl.BlockSpec(memory_space=pltpu.VMEM)
    return pl.pallas_call(
        functools.partial(assemble_kernel, masks, moves, len(bufs)),
        in_specs=[pl.BlockSpec(memory_space=pltpu.SMEM)] + [vmem] * len(bufs),
        out_specs=[vmem] * len(shapes),
        out_shape=[jax.ShapeDtypeStruct(s, BF) for s in shapes],
        compiler_params=pltpu.CompilerParams(vmem_limit_bytes=32 << 20),
        cost_estimate=pl.CostEstimate(flops=0, bytes_accessed=4 * sum(b.size for b in bufs), transcendentals=0),
    )(me, *bufs)


def between(work, give, got):
    result = work(give)
    return lax.optimization_barrier((got, result))


def reduce_core(parts, work=None):
    far, plane, core = stages()
    near = [k for k in range(lax.axis_size("col")) if not k & core[1]]
    give = jnp.stack([parts[k | core[1]] for k in near])
    got = exchange(give, core)
    result = None
    if work:
        got, result = between(work, give, got)
    return [parts[k].astype(F32) + got[i].astype(F32) for i, k in enumerate(near)], result


def reduce_plane_give(sums):
    far, plane, core = stages()
    near = [k for k in range(lax.axis_size("col")) if not k & core[1]]
    rows, r0 = lax.axis_size("row"), lax.axis_index("row")

    def rows_of(k, rm):
        v = sums[near.index(k)]
        return lax.dynamic_index_in_dim(v.reshape((rows // 2, 2) + v.shape[1:]), (r0 ^ rm) & 1, 1, keepdims=False)
    return rows_of(0, 0), [rows_of(cm, rm).astype(BF) for rm, cm in plane[1:]]


def reduce_plane(own, give, work=None):
    got = [exchange(g, m) for g, m in zip(give, stages()[1][1:])]
    result = None
    if work:
        got, result = between(work, give, got)
    return functools.reduce(lambda t, v: t + v.astype(F32), got, own), result


def reduce_far(total, work=None):
    far = stages()[0]
    r0 = lax.axis_index("row")
    give = [lax.dynamic_index_in_dim(total, (r0 ^ rm) >> 1, 0, keepdims=False).astype(BF) for rm, _ in far[1:]]
    got = [exchange(g, m) for g, m in zip(give, far[1:])]
    result = None
    if work:
        got, result = between(work, give, got)
    done = lax.dynamic_index_in_dim(total, r0 >> 1, 0, keepdims=False)
    return functools.reduce(lambda t, v: t + v.astype(F32), got, done), result


def reduce_list(parts):
    own, give = reduce_plane_give(reduce_core(parts)[0])
    return reduce_far(reduce_plane(own, give)[0])[0]


def column_kernel(count, s_ref, *refs):
    total = mm(refs[0][...], refs[1][...], ((0,), (0,)))
    for k in range(1, count):
        total = total + mm(refs[2 * k][...], refs[2 * k + 1][...], ((0,), (0,)))
    refs[-1][0] = total.astype(BF)


def column_blocks(pairs, cols, my_col):
    n, m = pairs[0][0].shape
    w = pairs[0][1].shape[1] // cols
    count = len(pairs)
    if w % 128:
        total = sum(mm(a, b, ((0,), (0,))) for a, b in pairs).astype(BF).reshape(m, cols, w).transpose(1, 0, 2)
        return jnp.take(total, jnp.arange(cols, dtype=jnp.int32) ^ my_col, axis=0)
    return pl.pallas_call(
        functools.partial(column_kernel, count),
        grid_spec=pltpu.PrefetchScalarGridSpec(
            num_scalar_prefetch=1, grid=(cols,),
            in_specs=[pl.BlockSpec((n, m), lambda k, s: (0, 0)), pl.BlockSpec((n, w), lambda k, s: (0, s[0] ^ k))] * count,
            out_specs=pl.BlockSpec((1, m, w), lambda k, s: (k, 0, 0))),
        out_shape=jax.ShapeDtypeStruct((cols, m, w), BF),
        compiler_params=pltpu.CompilerParams(vmem_limit_bytes=32 << 20),
        cost_estimate=pl.CostEstimate(flops=2 * count * n * m * w * cols, bytes_accessed=2 * (count * (n * m + n * w * cols) + m * w * cols), transcendentals=0),
    )(my_col.reshape(1), *[v for p in pairs for v in p])


def gelu_parts(v):
    phi = 0.5 * (1.0 + lax.erf(v * root_half))
    return v * phi, phi + v * jnp.exp(-0.5 * v * v) * inv_root_two_pi


def expert_kernel(cols, *refs):
    both, up, down = refs[:cols], refs[cols], refs[cols + 1]
    outs, acts, gps = refs[cols + 2:2 * cols + 2], refs[2 * cols + 2], refs[2 * cols + 3]
    width = up.shape[1]
    n = both[0].shape[1]
    rows = jnp.concatenate([b[0] for b in both], axis=0)
    act, slope = gelu_parts(mm(rows[:, :width], up[0]))
    act = act.astype(BF)
    acts[0] = act
    gp = (mm(rows[:, width:], down[0], ((1,), (1,))) * slope).astype(BF)
    gps[0] = gp
    out = mm(act, down[0]).astype(BF)
    gin = mm(gp, up[0], ((1,), (1,))).astype(BF)
    for c in range(cols):
        outs[c][0, :, :width] = out[c * n:(c + 1) * n]
        outs[c][0, :, width:] = gin[c * n:(c + 1) * n]


def weights_kernel(cols, sets, *refs):
    up, down = refs[-2:]
    step = cols + 2
    gu = gd = None
    width = up.shape[1]
    for s in range(sets):
        both, act, gp = refs[s * step:s * step + cols], refs[s * step + cols][0], refs[s * step + cols + 1][0]
        rows = jnp.concatenate([b[0] for b in both], axis=0)
        a = mm(rows[:, :width], gp, ((0,), (0,)))
        b = mm(act, rows[:, width:], ((0,), (0,)))
        gu, gd = (a, b) if gu is None else (gu + a, gd + b)
    up[0] = gu
    down[0] = gd


def per_expert(kernel, ins, shapes, flops):
    tok = lambda a: pl.BlockSpec((1,) + a.shape[1:], lambda e: (e, 0, 0))
    size = sum(a.size * 2 for a in ins) + sum(s.size * s.dtype.itemsize for s in shapes)
    return list(pl.pallas_call(
        kernel, grid=(ins[0].shape[0],),
        in_specs=[tok(a) for a in ins], out_specs=[tok(s) for s in shapes], out_shape=shapes,
        compiler_params=pltpu.CompilerParams(vmem_limit_bytes=56 << 20),
        cost_estimate=pl.CostEstimate(flops=flops, bytes_accessed=size, transcendentals=0),
    )(*ins))


def expert_both(bufs, up, down):
    cols = len(bufs)
    experts, d, f = up.shape
    n = bufs[0].shape[1]
    shapes = ([jax.ShapeDtypeStruct((experts, n, 2 * d), BF)] * cols
              + [jax.ShapeDtypeStruct((experts, n * cols, f), BF)] * 2)
    outs = per_expert(functools.partial(expert_kernel, cols), bufs + [up, down], shapes, 8 * experts * cols * n * d * f)
    return outs[:cols], outs[cols:]


def expert_weights(sets, d, f):
    cols = len(sets[0]) - 2
    experts, n, _ = sets[0][0].shape
    if len(sets) > 1 and len(sets) * cols > 8:
        return [sum(v) for v in zip(*[expert_weights([s], d, f) for s in sets])]
    shapes = [jax.ShapeDtypeStruct((experts, d, f), F32), jax.ShapeDtypeStruct((experts, f, d), F32)]
    return per_expert(functools.partial(weights_kernel, cols, len(sets)), [v for s in sets for v in s], shapes,
                      4 * experts * cols * n * d * f * len(sets))


def up_to(n, m):
    return -(-n // m) * m


def tiles_fit(w_in_x, w_xproj, w_out, conv_w):
    lanes = w_in_x.shape[1]
    return (lanes == 384 and w_in_x.shape[0] % 32 == 0 and up_to(w_xproj.shape[0], 128) + 128 == lanes
            and w_xproj.shape[1] <= 32 and conv_w.shape[1] <= 128 and w_out.shape[0] % 16 == 0
            and up_to(w_out.shape[1], 128) == 256)


def one_hot(shape, match):
    i = lax.broadcasted_iota(jnp.int32, shape, 0)
    j = lax.broadcasted_iota(jnp.int32, shape, 1)
    return jnp.where(match(i, j), 1.0, 0.0).astype(BF)


def pack_kernel(wx, wdt, xp, cw, cb, db, al, ds, gx, gm, wz, wo, wr, first, other, s_dt, s_xp, s_sm, s_out, s_r):
    n = wx.shape[0]
    for s in (s_dt, s_xp, s_sm, s_out, s_r):
        s[...] = jnp.zeros_like(s)
    first[:n] = wx[...]
    s_dt[:wdt.shape[0]] = wdt[...].astype(F32)
    first[n:n + 16] = s_dt[...].astype(BF)
    s_xp[:xp.shape[1], :xp.shape[0]] = xp[...].astype(F32).T
    wide = s_xp.shape[1]
    first[n + 16:, :wide] = s_xp[...].astype(BF)
    at = 0
    for v in (cw, cb, db, al, ds, gx, gm):
        s_sm[at:at + v.shape[0], :v.shape[1]] = v[...].astype(F32)
        at += v.shape[0]
    first[n + 16:, wide:] = s_sm[...].astype(BF)
    s_out[:, :wo.shape[1]] = wo[...].astype(F32)
    s_r[:, :wr.shape[1]] = wr[...].astype(F32)
    put_other(lambda at, lane, v: store(other, at, lane, v), wz[:, :256], wz[:, 256:], s_out[...].astype(BF), s_r[...].astype(BF))


def store(ref, at, lane, v):
    ref[at:at + v.shape[0], lane:lane + v.shape[1]] = v


def put_other(put, z_wide, z_rest, out, router):
    n = z_wide.shape[-2]
    put(0, 0, z_wide)
    put(n, 0, z_rest[..., :n // 2, :])
    put(n, 128, z_rest[..., n // 2:, :])
    at = n + n // 2
    put(at, 0, out)
    at += out.shape[-2]
    half = router.shape[-2] // 2
    put(at, 0, router[..., :half, :])
    put(at, 128, router[..., half:, :])


def pack_params(w_in_x, w_dt, w_xproj, conv_w, conv_b, dt_bias, a_log, d_skip, gain_mix, gain_moe, w_in_z, w_out, w_router):
    n, lanes = w_in_x.shape
    ins = [w_in_x, w_dt, w_xproj, conv_w, conv_b[None], dt_bias[None], a_log, d_skip[None], gain_mix[None], gain_moe[None],
           w_in_z, w_out, w_router]
    vmem = pl.BlockSpec(memory_space=pltpu.VMEM)
    V = lambda *s: pltpu.VMEM(s, F32)
    return pl.pallas_call(
        pack_kernel, in_specs=[vmem] * len(ins), out_specs=[vmem] * 2,
        out_shape=[sds((n + 48, lanes), BF), sds((n + n // 2 + w_out.shape[0] + w_router.shape[0] // 2, 256), BF)],
        scratch_shapes=[V(16, lanes), V(32, lanes - 128), V(32, 128), V(w_out.shape[0], 256), V(w_router.shape[0], 128)],
    )(*ins)


def each_block(masks, bufs, r0, c0):
    for buf, ms in zip(bufs, masks):
        for i, (rm, cm) in enumerate(ms):
            yield buf, i, r0 ^ rm, c0 ^ cm


def span(i, n):
    return pl.ds(pl.multiple_of(i * n, n), n)


def unpack_first(masks, dims, me, *refs):
    dt_rows, xp_cols, xp_rows, share, gshare, taps, rows, cols = dims
    count = len(masks)
    bufs = refs[:count]
    fx, dt, xpT, par, an, a2, gx, gm, w_dt, w_xp, w_sm = refs[count:]
    n = bufs[0].shape[1] - 48
    lanes = bufs[0].shape[2]
    wide = lanes - 128
    for buf, i, r, c in each_block(masks, bufs, me[0], me[1]):
        fx[span(r, n), span(c, lanes)] = buf[i, :n]
        w_dt[span(r, 16), span(c, lanes)] = buf[i, n:n + 16]
        w_xp[span(c, 32), span(r, wide)] = buf[i, n + 16:, :wide]
        w_sm[:, span(r * cols + c, 128)] = buf[i, n + 16:, wide:]
    pick = one_hot((dt.shape[0], 16 * rows), lambda i, j: (j % 16 < dt_rows) & (j // 16 * dt_rows + j % 16 == i))
    dt[...] = mm(pick, w_dt[...]).astype(BF)
    pick = one_hot((xpT.shape[0], 32 * cols), lambda i, j: (j % 32 < xp_cols) & (j // 32 * xp_cols + j % 32 == i))
    t = mm(pick, w_xp[...])
    xpT[...] = jnp.concatenate([t[:, r * wide:r * wide + xp_rows] for r in range(rows)], axis=1).astype(BF)
    sm = w_sm[...].astype(F32)
    chan = jnp.concatenate([sm[:, p * 128:p * 128 + share] for p in range(rows * cols)], axis=1)
    par[:taps + 2] = chan[:taps + 2]
    par[taps + 2:] = chan[taps + 2 + NS:taps + 3 + NS]
    neg = -jnp.exp(chan[taps + 2:taps + 2 + NS])
    an[...] = neg
    a2[...] = neg * log2e
    gains = jnp.concatenate([sm[taps + 3 + NS:taps + 5 + NS, p * 128:p * 128 + gshare] for p in range(rows * cols)], axis=1)
    gx[...] = gains[:1]
    gm[...] = gains[1:]


def unpack_other(masks, dims, me, *refs):
    n, out_rows, out_lanes, r_cols, cols = dims
    count = len(masks)
    bufs = refs[:count]
    fz, fo, router, w_out, w_r = refs[count:]
    half = n // 2
    at = n + half
    for buf, i, r, c in each_block(masks, bufs, me[0], me[1]):
        fz[span(r, n), pl.ds(pl.multiple_of(c * 384, 128), 256)] = buf[i, :n]
        for j in range(2):
            rows = pl.ds(pl.multiple_of(r * n + j * half, 16), half)
            fz[rows, pl.ds(pl.multiple_of(c * 384 + 256, 128), 128)] = buf[i, n:at, j * 128:(j + 1) * 128]
            w_r[rows, span(c, 128)] = buf[i, at + out_rows:, j * 128:(j + 1) * 128]
        w_out[span(r, out_rows), span(c, 256)] = buf[i, at:at + out_rows]
    wide = w_out[...]
    fo[...] = jnp.concatenate([wide[:, c * 256:c * 256 + out_lanes] for c in range(cols)], axis=1)
    pick = one_hot((128 * cols, router.shape[1]), lambda i, j: (i % 128 < r_cols) & (i // 128 * r_cols + i % 128 == j))
    router[...] = mm(w_r[...], pick)


def unpack_call(kernel, gathered, dims, outs, scratch):
    masks = [ms for ms, _ in gathered]
    bufs = [b for _, b in gathered]
    me = jnp.stack([lax.axis_index("row"), lax.axis_index("col")]).astype(jnp.int32)
    vmem = pl.BlockSpec(memory_space=pltpu.VMEM)
    return pl.pallas_call(
        functools.partial(kernel, masks, dims),
        in_specs=[pl.BlockSpec(memory_space=pltpu.SMEM)] + [vmem] * len(bufs), out_specs=[vmem] * len(outs), out_shape=outs,
        scratch_shapes=[pltpu.VMEM(s, BF) for s in scratch],
        compiler_params=pltpu.CompilerParams(vmem_limit_bytes=48 << 20),
        cost_estimate=pl.CostEstimate(flops=0, bytes_accessed=4 * sum(b.size for b in bufs), transcendentals=0),
    )(me, *bufs)


def grad_x_kernel(count, dims, s_ref, *refs):
    dt_rows, xp_cols, xp_rows, share, gshare, rows, cols = dims
    pairs = refs[:2 * count]
    gwd, gxp, gpar, gmix, gmoe = (refs[(2 + i) * count:(3 + i) * count] for i in range(5))
    keep, give, w_dt, w_xp, w_sm = refs[7 * count:]
    k = pl.program_id(0)
    n, lanes = keep.shape[2] - 48, keep.shape[3]
    wide = lanes - 128
    total = lambda vs: functools.reduce(lambda a, b: a + b, [v[...] for v in vs])

    @pl.when(k == 0)
    def _():
        g = total(gwd).astype(BF)
        put = one_hot((16 * rows, g.shape[0]), lambda j, i: (j % 16 < dt_rows) & (j // 16 * dt_rows + j % 16 == i))
        w_dt[...] = mm(put, g).astype(BF)
        g = total(gxp).astype(BF)
        put = one_hot((32 * cols, g.shape[0]), lambda j, i: (j % 32 < xp_cols) & (j // 32 * xp_cols + j % 32 == i))
        t = mm(put, g)
        gap = jnp.zeros((t.shape[0], wide - xp_rows), F32)
        w_xp[...] = jnp.concatenate([v for r in range(rows) for v in (t[:, r * xp_rows:(r + 1) * xp_rows], gap)], axis=1).astype(BF)
        w_sm[...] = jnp.zeros_like(w_sm)
        par, mix, moe = total(gpar), total(gmix), total(gmoe)
        m = par.shape[0]
        for p in range(rows * cols):
            w_sm[:m, p * 128:p * 128 + share] = par[:, p * share:(p + 1) * share]
            w_sm[m:m + 1, p * 128:p * 128 + gshare] = mix[:, p * gshare:(p + 1) * gshare]
            w_sm[m + 1:m + 2, p * 128:p * 128 + gshare] = moe[:, p * gshare:(p + 1) * gshare]
    for j, out in enumerate((keep, give)):
        c = s_ref[0] ^ (2 * k + j)
        g = sum_products(pairs, lambda r: r[:, span(c, lanes)])
        out[0, :, :n] = g.astype(BF).reshape(rows, n, lanes)
        for r in range(rows):
            out[0, r, n:n + 16] = w_dt[r * 16:(r + 1) * 16, span(c, lanes)]
            out[0, r, n + 16:, :wide] = w_xp[span(c, 32), r * wide:(r + 1) * wide]
            out[0, r, n + 16:, wide:] = w_sm[:, span(r * cols + c, 128)].astype(BF)


def sum_products(pairs, block):
    return functools.reduce(lambda a, b: a + b, [mm(pairs[i][...], block(pairs[i + 1]), TN) for i in range(0, len(pairs), 2)])


def grad_blocks(kernel, ins, scratch, block, rows, cols, my_col, flops):
    out = sds((cols // 2, rows) + block, BF)
    return list(pl.pallas_call(
        kernel,
        grid_spec=pltpu.PrefetchScalarGridSpec(
            num_scalar_prefetch=1, grid=(cols // 2,), in_specs=[whole_spec(v) for v in ins],
            out_specs=[pl.BlockSpec((1, rows) + block, lambda k, s: (k, 0, 0, 0))] * 2, scratch_shapes=scratch),
        out_shape=[out, out],
        compiler_params=pltpu.CompilerParams(vmem_limit_bytes=56 << 20),
        cost_estimate=pl.CostEstimate(flops=flops, bytes_accessed=1 << 23, transcendentals=0),
    )(my_col.reshape(1), *ins))


def grad_x_blocks(pairs, smalls, dims, my_col):
    rows, cols = dims[-2:]
    n, m = pairs[0][0].shape
    inner = pairs[0][1].shape[1]
    lanes = inner // cols
    ins = [v for p in pairs for v in p] + [g[name] for name in ("dt", "xproj", "chan", "gain_mix", "gain_moe") for g in smalls]
    scratch = [pltpu.VMEM((16 * rows, inner), BF), pltpu.VMEM((32 * cols, (lanes - 128) * rows), BF), pltpu.VMEM((32, 128 * rows * cols), F32)]
    return grad_blocks(functools.partial(grad_x_kernel, len(pairs), dims), ins, scratch, (m // rows + 48, lanes), rows, cols, my_col,
                       2 * len(pairs) * n * m * inner)


def grad_other_kernel(count, r_cols, s_ref, *refs):
    zs, outs, routers = refs[:2 * count], refs[2 * count:4 * count], refs[4 * count:5 * count]
    keep, give = refs[5 * count:]
    rows = keep.shape[1]
    k = pl.program_id(0)
    r = functools.reduce(lambda a, b: a + b, [v[...] for v in routers]).astype(BF)
    for j, out in enumerate((keep, give)):
        c = s_ref[0] ^ (2 * k + j)
        z = sum_products(zs, lambda v: v[:, pl.ds(pl.multiple_of(c * 384, 128), 384)]).astype(BF)
        o = sum_products(outs, lambda v: v[:, span(2 * k + j, 256)]).astype(BF)
        put = one_hot((r.shape[1], 128), lambda a, b: (b < r_cols) & (a == c * r_cols + b))
        w = mm(r, put).astype(BF)
        z, o, w = (v.reshape(rows, v.shape[0] // rows, v.shape[1]) for v in (z, o, w))

        def put_block(at, lane, v):
            out[0, :, at:at + v.shape[1], lane:lane + v.shape[2]] = v
        put_other(put_block, z[..., :256], z[..., 256:], o, w)


def grad_other_blocks(zs, outs, routers, block, rows, cols, r_cols, my_col):
    ins = [v for p in zs for v in p] + [v for p in outs for v in p] + list(routers)
    flops = 2 * sum(a.shape[0] * a.shape[1] * b.shape[1] for a, b in zs + outs)
    return grad_blocks(functools.partial(grad_other_kernel, len(zs), r_cols), ins, [], block, rows, cols, my_col, flops)


def split_near_kernel(plan, s_ref, keep, got, own, *gives):
    for out, (ki, rm) in zip((own,) + gives, plan):
        p = (s_ref[0] ^ rm) & 1
        v = keep[ki, 0, p].astype(F32) + got[ki, 0, p].astype(F32)
        out[0] = v.astype(out.dtype)


def split_near(keep, got):
    plane = stages()[1]
    near, rows, n, lanes = keep.shape
    plan = [(cm >> 1, rm) for rm, cm in plane]
    view = (near, rows // 2, 2, n, lanes)
    outs = [sds((rows // 2, n, lanes), F32 if i == 0 else BF) for i in range(len(plan))]
    res = pl.pallas_call(
        functools.partial(split_near_kernel, plan),
        grid_spec=pltpu.PrefetchScalarGridSpec(
            num_scalar_prefetch=1, grid=(rows // 2,),
            in_specs=[pl.BlockSpec((near, 1, 2, n, lanes), lambda z, s: (0, z, 0, 0, 0))] * 2,
            out_specs=[pl.BlockSpec((1, n, lanes), lambda z, s: (z, 0, 0))] * len(outs)),
        out_shape=outs,
        compiler_params=pltpu.CompilerParams(vmem_limit_bytes=32 << 20),
        cost_estimate=pl.CostEstimate(flops=0, bytes_accessed=6 * keep.size, transcendentals=0),
    )(lax.axis_index("row").reshape(1), keep.reshape(view), got.reshape(view))
    return res[0], list(res[1:])


def split_far_kernel(count, plan, s_ref, own, *refs):
    gots, mine, gives = refs[:count], refs[count], refs[count + 1:]
    for out, rm in zip((mine,) + gives, plan):
        i = (s_ref[0] ^ rm) >> 1
        v = own[i]
        for g in gots:
            v = v + g[i].astype(F32)
        out[...] = v.astype(out.dtype)


def split_far(own, gots):
    plan = [rm for rm, _ in stages()[0]]
    _, n, lanes = own.shape
    outs = [sds((n, lanes), F32 if i == 0 else BF) for i in range(len(plan))]
    res = one_call(functools.partial(split_far_kernel, len(gots), plan), [own] + gots, outs, [lax.axis_index("row").reshape(1)])
    return res[0], list(res[1:])


def total_of(refs):
    return functools.reduce(lambda a, b: a + b[...].astype(F32), refs[1:], refs[0][...])


def finish_x_kernel(count, *refs):
    gx, gxp, gdt, gcw, gcb, gdb, gal, gds, gmix, gmoe, s = refs[count:]
    s[...] = total_of(refs[:count])
    n, lanes = gx.shape
    gx[...] = s[:n]
    gdt[...] = s[n:n + gdt.shape[0]]
    wide = lanes - 128
    gxp[...] = s[n + 16:, :wide].T[:gxp.shape[0], :gxp.shape[1]]
    at = n + 16
    for ref in (gcw, gcb, gdb, gal, gds, gmix, gmoe):
        ref[...] = s[at:at + ref.shape[0], wide:wide + ref.shape[1]]
        at += ref.shape[0]


def finish_other_kernel(count, *refs):
    gz, go, gr, s = refs[count:]
    s[...] = total_of(refs[:count])
    n = gz.shape[0]
    half = n // 2
    gz[:, :256] = s[:n]
    gz[:half, 256:] = s[n:n + half, :128]
    gz[half:, 256:] = s[n:n + half, 128:]
    at = n + half
    go[...] = s[at:at + go.shape[0], :go.shape[1]]
    at += go.shape[0]
    gr[:half] = s[at:, :gr.shape[1]]
    gr[half:] = s[at:, 128:128 + gr.shape[1]]


def finish(kernel, mine, gots, shapes):
    ins = [mine] + gots
    vmem = pl.BlockSpec(memory_space=pltpu.VMEM)
    return pl.pallas_call(
        functools.partial(kernel, len(ins)), in_specs=[vmem] * len(ins), out_specs=[vmem] * len(shapes),
        out_shape=[sds(s) for s in shapes], scratch_shapes=[pltpu.VMEM(mine.shape, F32)],
    )(*ins)


def weights_part_kernel(cols, sets, lead, *refs):
    out = refs[-1]
    step = cols + 1
    total = None
    for s in range(sets):
        both, other = refs[s * step:s * step + cols], refs[s * step + cols][0]
        width = both[0].shape[2] // 2
        rows = jnp.concatenate([b[0, :, :width] if lead else b[0, :, width:] for b in both], axis=0)
        v = mm(rows, other, TN) if lead else mm(other, rows, TN)
        total = v if total is None else total + v
    out[0] = total


def expert_weights_part(sets, lead, d, f):
    cols = len(sets[0]) - 1
    experts, n, _ = sets[0][0].shape
    if len(sets) > 1 and len(sets) * cols > 8:
        return sum(expert_weights_part([s], lead, d, f) for s in sets)
    shape = (experts, d, f) if lead else (experts, f, d)
    return per_expert(functools.partial(weights_part_kernel, cols, len(sets), lead), [v for s in sets for v in s],
                      [sds(shape)], 2 * experts * cols * n * d * f * len(sets))[0]


def params_generic(w_in_x, w_in_z, conv_w, conv_b, w_xproj, w_dt, dt_bias, a_log, d_skip, w_out, gain_mix, gain_moe, w_router):
    rows, cols = lax.axis_size("row"), lax.axis_size("col")
    parts = rows * cols
    inner, width = w_in_x.shape[1] * cols, w_in_x.shape[0] * rows
    small = jnp.concatenate([conv_w, conv_b[None], dt_bias[None], a_log, d_skip[None],
                             jnp.concatenate([gain_mix, gain_moe])[None]], axis=0)
    flat = [w_xproj.reshape(-1), w_dt.reshape(-1), w_router.reshape(-1), small.reshape(-1)]
    sizes = [f.shape[0] for f in flat]
    lanes = w_in_x.shape[1]
    extra = -(-sum(sizes) // (16 * lanes)) * 16
    flat = jnp.pad(jnp.concatenate(flat), (0, extra * lanes - sum(sizes))).reshape(extra, lanes)
    here, out_rows, out_lanes = w_in_x.shape[0], w_out.shape[0], w_out.shape[1]
    wide = -(-out_lanes // 128) * 128
    first = gather_list(jnp.concatenate([w_in_x, flat], axis=0))
    full_x, rest = assemble(first, [((0, here, lanes), 0, put_block), ((here, extra, lanes), 1, put_pair)],
                            [(width, inner), (rows, cols, extra, lanes)])
    far_end = first[len(first) // 2 - 1][1]
    late_z, late_o, _ = lax.optimization_barrier((w_in_z, jnp.pad(w_out, ((0, 0), (0, wide - out_lanes))), far_end))
    (full_z,) = assemble(gather_list(late_z), [((0, here, lanes), 0, put_block)], [(width, inner)])
    (wide_out,) = assemble(gather_list(late_o), [((0, out_rows, wide), 0, put_block)], [(inner, cols * wide)])
    lane_of = jnp.arange(cols * wide, dtype=jnp.int32)
    narrow = jnp.where(lane_of % wide < out_lanes, lane_of // wide * out_lanes + lane_of % wide, -1)
    narrow = (narrow[:, None] == jnp.arange(width, dtype=jnp.int32)[None, :]).astype(BF)
    full_out = mm(wide_out, narrow).astype(BF)
    def whole(blocks):
        return blocks.transpose(0, 2, 1, 3).reshape(blocks.shape[0] * blocks.shape[2], -1)
    rest = rest.reshape(rows, cols, extra * lanes)
    cut = [0]
    for n in sizes:
        cut.append(cut[-1] + n)
    full_xpT = whole(rest[:, :, cut[0]:cut[1]].reshape((rows, cols) + w_xproj.shape)).T
    full_dt = whole(rest[:, :, cut[1]:cut[2]].reshape((rows, cols) + w_dt.shape))
    router_f = whole(rest[:, :, cut[2]:cut[3]].reshape((rows, cols) + w_router.shape)).astype(F32)
    small = rest[:, :, cut[3]:cut[4]].reshape((parts,) + small.shape).transpose(1, 0, 2).astype(F32)
    chan = small[:-1].reshape(-1, inner)
    taps = conv_w.shape[0]
    par = jnp.concatenate([chan[:taps + 2], chan[taps + 2 + NS:]], axis=0)
    a_neg = -jnp.exp(chan[taps + 2:taps + 2 + NS])
    a_two = a_neg * log2e
    gain_mix_f = small[-1, :, :gain_mix.shape[0]].reshape(1, width)
    gain_moe_f = small[-1, :, gain_mix.shape[0]:].reshape(1, width)
    return lambda done: (full_z, full_out, router_f, done), full_x, full_xpT, full_dt, par, a_neg, a_two, gain_mix_f, gain_moe_f


def params_tiled(w_in_x, w_in_z, conv_w, conv_b, w_xproj, w_dt, dt_bias, a_log, d_skip, w_out, gain_mix, gain_moe, w_router):
    rows, cols = lax.axis_size("row"), lax.axis_size("col")
    here, lanes = w_in_x.shape
    inner, width = lanes * cols, here * rows
    taps, share = conv_w.shape
    packed, other = pack_params(w_in_x, w_dt, w_xproj, conv_w, conv_b, dt_bias, a_log, d_skip, gain_mix, gain_moe, w_in_z,
                                w_out, w_router)
    mine = gather_far(packed)
    other, _ = lax.optimization_barrier((other, mine))
    mine_o = gather_far(other)
    near = gather_plane(mine)
    mine_o, _ = lax.optimization_barrier((mine_o, near[-1]))
    near_o = gather_plane(mine_o)
    first = gather_core(near)
    dims = (w_dt.shape[0], w_xproj.shape[1], w_xproj.shape[0], share, gain_mix.shape[0], taps, rows, cols)
    full_x, full_dt, full_xpT, par, a_neg, a_two, gx, gm = unpack_call(
        unpack_first, first, dims,
        [sds((width, inner), BF), sds((w_dt.shape[0] * rows, inner), BF), sds((w_xproj.shape[1] * cols, inner), BF),
         sds((taps + 3, inner)), sds((NS, inner)), sds((NS, inner)), sds((1, width)), sds((1, width))],
        [(16 * rows, inner), (32 * cols, (lanes - 128) * rows), (32, 128 * rows * cols)])

    def rest(done):
        o, done = lax.optimization_barrier((near_o, done))
        full_z, full_out, router_f = unpack_call(
            unpack_other, gather_core(o), (here, w_out.shape[0], w_out.shape[1], w_router.shape[1], cols),
            [sds((width, inner), BF), sds((inner, width), BF), sds((width, w_router.shape[1] * cols))],
            [(inner, 256 * cols), (width, 128 * cols)])
        return full_z, full_out, router_f, done
    return rest, full_x, full_xpT, full_dt, par, a_neg, a_two, gx, gm


def grads_generic(nms, gateds, gs, total, w_in_x, w_in_z, w_xproj, w_dt, w_out, w_router, gain_mix, conv_w):
    rows, cols = lax.axis_size("row"), lax.axis_size("col")
    parts = rows * cols
    my_col = lax.axis_index("col")
    here, lanes = w_in_x.shape
    out_rows, out_lanes = w_out.shape
    wide = up_to(out_lanes, 128)
    share = conv_w.shape[1]
    sizes = [w_xproj.size, w_dt.size, w_router.size, (conv_w.shape[0] + 4 + NS) * share]
    extra = up_to(-(-sum(sizes) // lanes), 16)
    cut = [sum(sizes[:i]) for i in range(5)]
    grad_out = sum(mm(k[1], r["gm"], TN) for k, r in zip(zip(nms, gateds), gs)).astype(BF)
    grad_out_block = reduce_list([grad_out[:, k * wide:(k + 1) * wide].reshape(rows, out_rows, wide) for k in range(cols)])
    grad_out_block = grad_out_block[:, :out_lanes]
    grad_in_z = column_blocks([(k[0], r["gz"]) for k, r in zip(zip(nms, gateds), gs)], cols, my_col)
    grad_z_block = reduce_list([grad_in_z[k].reshape(rows, here, lanes) for k in range(cols)])
    grad_in_x = column_blocks([(k[0], r["gi"]) for k, r in zip(zip(nms, gateds), gs)], cols, my_col)

    def blocks(g, like):
        r, c = like.shape
        return g.astype(BF).reshape(rows, r, cols, c).transpose(0, 2, 1, 3).reshape(rows, cols, -1)
    gsmall = total["chan"].astype(BF)
    ggain = jnp.concatenate([total["gain_mix"].reshape(parts, 1, -1), total["gain_moe"].reshape(parts, 1, -1)], axis=2)
    gsmall = jnp.concatenate([gsmall.reshape(-1, parts, share).transpose(1, 0, 2), ggain.astype(BF)], axis=1)
    gflat = jnp.concatenate([blocks(total["xproj"].T, w_xproj), blocks(total["dt"], w_dt), blocks(total["router"], w_router),
                             gsmall.reshape(rows, cols, -1)], axis=2)
    gflat = jnp.pad(gflat, ((0, 0), (0, 0), (0, extra * lanes - sum(sizes)))).reshape(rows, cols, extra, lanes)
    done = reduce_list([jnp.concatenate([grad_in_x[k].reshape(rows, here, lanes),
                                         lax.dynamic_index_in_dim(gflat, my_col ^ k, 1, keepdims=False)], axis=1)
                        for k in range(cols)])
    grad_x_block = done[:here]
    done = done[here:].reshape(-1)
    sm = done[cut[3]:cut[4]].reshape(-1, share)
    gm = gain_mix.shape[0]
    taps = conv_w.shape[0]
    chan = (sm[:taps], sm[taps], sm[taps + 1], sm[taps + 2:taps + 2 + NS], sm[taps + 2 + NS])
    small = (done[cut[0]:cut[1]].reshape(w_xproj.shape), done[cut[1]:cut[2]].reshape(w_dt.shape), chan, sm[-1, :gm], sm[-1, gm:],
             done[cut[2]:cut[3]].reshape(w_router.shape))
    return (grad_x_block, grad_z_block, grad_out_block), small


def on_device(tokens, w_in_x, w_in_z, conv_w, conv_b, w_xproj, w_dt, dt_bias, a_log, d_skip, w_out,
              gain_mix, gain_moe, w_router, w_up, w_down, routes, lengths, cotangent):
    rows, cols = lax.axis_size("row"), lax.axis_size("col")
    parts = rows * cols
    my_col = lax.axis_index("col")
    seqs, length, width = tokens.shape
    experts_here = w_up.shape[0]
    experts_all = experts_here * rows
    inner = w_in_x.shape[1] * cols
    count = seqs * length
    xp = w_xproj.shape[1] * cols
    share = inner // parts

    tiled = tiles_fit(w_in_x, w_xproj, w_out, conv_w)
    here, lanes = w_in_x.shape
    out_rows, out_lanes = w_out.shape
    wide = up_to(out_lanes, 128)
    taps = conv_w.shape[0]
    rest_of, full_x, full_xpT, full_dt, par, a_neg, a_two, gain_mix_f, gain_moe_f = (
        params_tiled if tiled else params_generic)(
            w_in_x, w_in_z, conv_w, conv_b, w_xproj, w_dt, dt_bias, a_log, d_skip, w_out, gain_mix, gain_moe, w_router)
    lane_of = jnp.arange(cols * wide, dtype=jnp.int32)
    shifted = jnp.where(lane_of % wide < out_lanes, (lane_of // wide ^ my_col) * out_lanes + lane_of % wide, -1)
    shifted = (jnp.arange(width, dtype=jnp.int32)[:, None] == shifted[None, :]).astype(BF)

    message = -(-experts_here * CAP // 8) * 8
    group = -(-rows * CAP // 16) * 16
    at = jnp.arange(experts_here * group, dtype=jnp.int32)
    there = at % group
    source = jnp.where(there < rows * CAP, there // CAP * message + at // group * CAP + there % CAP, -1)
    sort = (source[:, None] == jnp.arange(rows * message, dtype=jnp.int32)[None, :]).astype(BF)

    def mixer(x):
        nm, inner_x, conv, u, dl, pT, ssm, starts = mixer_forward(x, gain_mix_f, full_x, full_xpT, full_dt, par, a_two, QB)
        return dict(x=x, nm=nm, inner=inner_x, conv=conv, u=u, dl=dl, pT=pT, ssm=ssm.reshape(length, inner), starts=starts)

    def router(k, route, n_live, grad):
        n_live = n_live.reshape(1)
        slots = rows * message
        z, gated, hidden, place, outgoing, probs, gate = one_call(
            functools.partial(route_kernel, CAP, experts_here, message),
            [k["x"], k["nm"], k["ssm"], full_z, full_out, gain_moe_f, router_f, route, grad],
            [sds((length, inner)), sds((length, inner), BF), sds((length, width)), sds((length, slots), BF),
             sds((slots, 2 * width), BF), sds((length, experts_all)), sds((length, 1))],
            [n_live], 6 * length * inner * width)
        kept = dict(k, z=z, gated=gated, hidden=hidden, place=place, probs=probs, gate=gate, route=route, n_live=n_live, cot=grad)
        return outgoing, kept

    def home(rows_out):
        return lax.all_to_all(rows_out, "row", split_axis=0, concat_axis=0, tiled=True)

    def arrive(got):
        return mm(sort, got).astype(BF).reshape(experts_here, group, 2 * width)

    def gather_cols(own):
        bufs = [own]
        for bit in bits_of("col")[::-1]:
            bufs = bufs + [swap(v, "col", bit) for v in bufs]
        return bufs

    def from_experts(bufs):
        for bit in bits_of("col"):
            half = len(bufs) // 2
            bufs = [(a.astype(F32) + swap(b, "col", bit).astype(F32)).astype(BF) for a, b in zip(bufs[:half], bufs[half:])]
        return mm(sort, bufs[0].reshape(experts_here * group, 2 * width), ((0,), (0,))).astype(BF)

    def unroute(k, back):
        mixed_out, gh, gs, gz, gm, g_router, g_moe = one_call(
            unroute_kernel,
            [back, k["place"], k["hidden"], k["probs"], k["gate"], k["route"], k["cot"], gain_moe_f, router_f, full_out, shifted,
             k["z"], k["ssm"]],
            [sds((length, width), BF), sds((length, width)), sds((length, inner)), sds((length, inner), BF),
             sds((length, cols * wide), BF), sds((width, experts_all)), sds((1, width))],
            [k["n_live"]], 6 * length * inner * width)
        return dict(mixed_out=mixed_out, gh=gh, gs=gs.reshape(k["u"].shape), gz=gz, gm=gm, router=g_router, gain_moe=g_moe)

    def unscan(k, gs):
        gi, g_xp, g_dt, g_chan = scan_backward(k["u"], k["dl"], gs, k["conv"], k["inner"], k["pT"], k["starts"], full_xpT, full_dt, par, a_neg)
        return dict(gi=gi, xproj=g_xp, dt=g_dt, chan=g_chan)

    def unproject(k, g):
        grad_tokens, g_mix = one_call(
            token_kernel, [g["gi"], g["gz"], full_x, full_z, k["x"], g["gh"], gain_mix_f], [sds((length, width)), sds((1, width))], (),
            4 * length * inner * width)
        return dict(tokens=grad_tokens, gain_mix=g_mix)

    after = lax.optimization_barrier
    ks, owns, last = [], [], None
    for s in range(seqs):
        x = tokens[s]
        if last is not None:
            x, last = after((x, last))
        k = mixer(x)
        if s == 0:
            full_z, full_out, router_f, k["ssm"] = rest_of(k["ssm"])
        before, (last, k) = last, router(k, routes[s], lengths[s], cotangent[s])
        ks.append(k)
        if before is not None:
            got, last = after((home(before), last))
            owns.append(arrive(got))
    owns.append(arrive(home(last)))
    sets, sent = [], []
    for s in range(seqs):
        bufs = gather_cols(owns[s])
        if s == seqs - 2:
            bufs, owns[-1] = after((bufs, owns[-1]))
        outs, more = expert_both(bufs, w_up, w_down)
        sets.append((bufs, more))
        sent.append(from_experts(outs))
    backs = [home(v) for v in sent]
    grads_w = []
    for lead in (True, False):
        ins, sent[0], _ = after(([b + [v[1 if lead else 0]] for b, v in sets], sent[0], grads_w))
        grads_w.append(expert_weights_part(ins, lead, width, w_up.shape[2]))
    backs[0], (grad_w_up, grad_w_down) = after((backs[0], grads_w))
    gs_ = []
    for s in range(seqs):
        g = unroute(ks[s], backs[s])
        gs_.append(g)
        if s + 1 < seqs:
            g["gs"], sent[s + 1] = after((g["gs"], sent[s + 1]))
            g.update(unscan(ks[s], g["gs"]))
            g["gi"], backs[s + 1] = after((g["gi"], backs[s + 1]))
    g = gs_[-1]
    nms, gateds = [k["nm"] for k in ks], [k["gated"] for k in ks]
    if tiled:
        block = (here + here // 2 + out_rows + w_router.shape[0] // 2, 256)
        keep, give = grad_other_blocks([(v, q["gz"]) for v, q in zip(nms, gs_)], [(v, q["gm"]) for v, q in zip(gateds, gs_)],
                                       [q["router"] for q in gs_], block, rows, cols, w_router.shape[1], my_col)
        far, plane, core = stages()

        def first_tokens(v):
            return unproject(ks[0], dict(gs_[0], gi=after((gs_[0]["gi"], v))[0]))
        got, first = between(first_tokens, give, exchange(give, core))
        if seqs > 1:
            gs_[0].update(first)
        own, gives = split_near(keep, got)
        g["gs"], gives = after((g["gs"], gives))
        gots = [exchange(v, p) for v, p in zip(gives, plane[1:])]
        g.update(unscan(ks[-1], g["gs"]))
        gots, g["gi"] = after((gots, g["gi"]))
        mine, gives = split_far(own, gots)
        g["gi"], gives = after((g["gi"], gives))
        gots_o = [exchange(v, p) for v, p in zip(gives, far[1:])]
        mine_o = mine
        dims = (w_dt.shape[0], w_xproj.shape[1], w_xproj.shape[0], conv_w.shape[1], gain_mix.shape[0], rows, cols)
        for s in range(1, seqs):
            gs_[s].update(unproject(ks[s], gs_[s]))
        keep, give = grad_x_blocks([(v, q["gi"]) for v, q in zip(nms, gs_)], gs_, dims, my_col)
        own, gives = split_near(keep, exchange(give, core))
        gots = [exchange(v, p) for v, p in zip(gives, plane[1:])]
        gots_o, _ = after((gots_o, gives))
        gz, go, g_router = finish(finish_other_kernel, mine_o, gots_o, [w_in_z.shape, w_out.shape, w_router.shape])
        gots, gz, go, g_router = after((gots, gz, go, g_router))
        mine, gives = split_far(own, gots)
        gots = [exchange(v, p) for v, p in zip(gives, far[1:])]
        share, gshare = conv_w.shape[1], gain_mix.shape[0]
        gx, g_xproj, g_dt, gcw, gcb, gdb, gal, gds, g_mix, g_moe = finish(
            finish_x_kernel, mine, gots,
            [w_in_x.shape, w_xproj.shape, w_dt.shape, conv_w.shape, (1, share), (1, share), a_log.shape, (1, share), (1, gshare), (1, gshare)])
        blocks = (gx, gz, go)
        small = (g_xproj, g_dt, (gcw, gcb[0], gdb[0], gal, gds[0]), g_mix[0], g_moe[0], g_router)
    else:
        g.update(unscan(ks[-1], g["gs"]))
        for k, q in zip(ks, gs_):
            q.update(unproject(k, q))
        names = ("xproj", "dt", "chan", "gain_mix", "gain_moe", "router")
        total = {n: sum(q[n] for q in gs_) for n in names}
        blocks, small = grads_generic(nms, gateds, gs_, total, w_in_x, w_in_z, w_xproj, w_dt, w_out, w_router, gain_mix, conv_w)
    g_xproj, g_dt, (gcw, gcb, gdb, gal, gds), g_mix, g_moe, g_router = small
    return (
        jnp.stack([q["mixed_out"] for q in gs_]),
        jnp.stack([q["tokens"] for q in gs_]),
        blocks[0],
        blocks[1],
        gcw,
        gcb,
        g_xproj,
        g_dt,
        gdb,
        gal,
        gds,
        blocks[2],
        g_mix,
        g_moe,
        g_router,
        grad_w_up,
        grad_w_down,
    )


def solution(mesh):
    tok = P(("row", "col"), None, None)
    mat = P("row", "col")
    vec = P(("row", "col"))
    chan = P(None, ("row", "col"))
    up, down = P("row", None, "col"), P("row", "col", None)
    return jax.shard_map(
        on_device,
        mesh=mesh,
        in_specs=(tok, mat, mat, chan, vec, mat, mat, vec, chan, vec, mat, vec, vec, mat, up, down, tok, vec, tok),
        out_specs=(tok, tok, mat, mat, chan, vec, mat, mat, vec, chan, vec, mat, vec, vec, mat, up, down),
        check_vma=False,
    )
```

```python
import functools
import jax
import jax.numpy as jnp
from jax import lax
from jax.sharding import PartitionSpec as P
from jax.experimental import pallas as pl
from jax.experimental.pallas import tpu as pltpu
NS = 16
F32 = jnp.float32
SLOT_OF=[4*((i>>2)&1)+2*(1-((i>>1)&1))+(1-(i&1)) for i in range(8)]
def merge8(rows):
    idx=lax.broadcasted_iota(jnp.int32,(8,128),0)
    m4=idx<4; m2=(idx&2)!=0; m1=(idx&1)!=0
    p=[None]*8
    for i in range(8): p[SLOT_OF[i]]=rows[i]
    r=[jnp.where(m4,p[k],p[k+4])+pltpu.roll(jnp.where(m4,p[k+4],p[k]),4,0) for k in range(4)]
    def half(x,y,m,d):
        return jnp.where(m,x+pltpu.roll(x,d,0),y+pltpu.roll(y,8-d,0))
    v=[half(r[k],r[k+2],m2,2) for k in range(2)]
    return half(v[0],v[1],m1,1)
def mm(a, b, dims=((1,), (0,)), **kw):
    return lax.dot_general(a, b, (dims, ((), ())), preferred_element_type=F32, **kw)


NT = ((1,), (1,))
TN = ((0,), (0,))


def softplus(v):
    e = jnp.exp(-jnp.abs(v))
    tiny = e * (1.0 - e * (0.5 - e * (1.0 / 3.0 - e * 0.25)))
    return jnp.maximum(v, 0.0) + jnp.where(e < 0.01, tiny, jnp.log(1.0 + e))


def sigmoid_of_softplus(d):
    tiny = d * (1.0 - d * (0.5 - d * (1.0 / 6.0 - d * (1.0 / 24.0))))
    return jnp.where(d < 0.03, tiny, 1.0 - jnp.exp(-d))


def sigmoid(v):
    return 1.0 / (1.0 + jnp.exp(-v))


def spread(dst, src, T):
    for j in range(T):
        dst[j] = jnp.broadcast_to(src[:, j:j + 1], (NS, 128))


def fold(x):
    return x[0:8] + x[8:16]


def convolve(ext, w, b, T):
    taps = w.shape[0]
    out = b
    for k in range(taps):
        out = out + w[k:k + 1] * ext[9 - taps + k:9 - taps + k + T]
    return out


def mixer_kernel(T, Q, R, x_ref, gain_ref, wx_ref, xpT_ref, wdt_ref, par_ref, a2_ref,
                 nm_ref, in_ref, cv_ref, u_ref, dl_ref, pT_ref, y_ref, st_ref, state, bx, cx, du):
    c = pl.program_id(0)
    L, DI = nm_ref.shape[0], wx_ref.shape[1]
    taps = par_ref.shape[0] - 3

    @pl.when(c == 0)
    def _():
        state[...] = jnp.zeros_like(state)
        x = x_ref[...].astype(F32)
        nm = (x * lax.rsqrt(jnp.mean(x * x, axis=-1, keepdims=True) + 1e-05) * gain_ref[...]).astype(jnp.bfloat16)
        nm_ref[...] = nm
        in_ref[0:8] = jnp.zeros((8, DI), F32)
        in_ref[8:] = mm(nm, wx_ref[...])
    st_ref[0] = state[...]
    par = par_ref[...]
    skip = par[taps + 2:taps + 3]
    conv = convolve(in_ref[pl.ds(pl.multiple_of(c * T, 8), T + 8)], par[:taps], par[taps:taps + 1], T)
    cv_ref[0] = conv.reshape(T // 8, 8, DI)
    u = conv * sigmoid(conv)
    u_ref[0] = u.reshape(T // 8, 8, DI)
    pT = mm(xpT_ref[...], u.astype(jnp.bfloat16), NT)
    pT_ref[0] = pT
    d = softplus(mm(pT[:R].astype(jnp.bfloat16), wdt_ref[...], TN) + par[taps + 1:taps + 2])
    dl_ref[0] = d.reshape(T // 8, 8, DI)
    du[...] = (d * u).reshape(T // 8, 8, DI)
    spread(bx, pT[R:R + NS], T)
    spread(cx, pT[R + NS:R + 2 * NS], T)

    def grp(g, _):
        base = pl.multiple_of(g * (Q * 128), 128)
        lanes = [pl.ds(base + q * 128, 128) for q in range(Q)]
        a = [a2_ref[:, ln] for ln in lanes]
        sk = [par_ref[taps + 2:taps + 3, ln] for ln in lanes]

        def tb(i, s):
            s = list(s)
            rows = [[] for _ in range(Q)]
            for k in range(8):
                t = i * 8 + k
                b = bx[t]
                cc = cx[t]
                for q in range(Q):
                    dd = dl_ref[0, i, k:k + 1, lanes[q]]
                    dub = du[i, k:k + 1, lanes[q]]
                    s[q] = jnp.exp2(dd * a[q]) * s[q] + b * dub
                    rows[q].append(fold(s[q] * cc))
            for q in range(Q):
                y_ref[0, i, :, lanes[q]] = merge8(rows[q]) + sk[q] * u_ref[0, i, :, lanes[q]]
            return tuple(s)
        s = lax.fori_loop(0, T // 8, tb, tuple(state[:, ln] for ln in lanes))
        for q in range(Q):
            state[:, lanes[q]] = s[q]
        return 0
    lax.fori_loop(0, DI // (Q * 128), grp, 0)


def whole_spec(a):
    return pl.BlockSpec(a.shape, lambda *_: (0,) * len(a.shape))


def sds(shape, dtype=F32):
    return jax.ShapeDtypeStruct(shape, dtype)


def mixer_forward(x, gain, wx, xpT, wdt, par, a2, T, limit, Q=6):
    L, D = x.shape
    DI = wx.shape[1]
    C, XP, R = L // T, xpT.shape[0], wdt.shape[0]
    ins = [x, gain, wx, xpT, wdt, par, a2]
    rows = pl.BlockSpec((1, T // 8, 8, DI), lambda c: (c, 0, 0, 0))
    big = sds((C, T // 8, 8, DI))
    nm, inner = sds((L, D), jnp.bfloat16), sds((L + 8, DI))
    return pl.pallas_call(
        functools.partial(mixer_kernel, T, Q, R), grid=(C,),
        in_specs=[whole_spec(a) for a in ins],
        out_specs=[whole_spec(nm), whole_spec(inner), rows, rows, rows, pl.BlockSpec((1, XP, T), lambda c: (c, 0, 0)), rows,
                   pl.BlockSpec((1, NS, DI), lambda c: (c, 0, 0))],
        out_shape=[nm, inner, big, big, big, sds((C, XP, T)), big, sds((C, NS, DI))],
        scratch_shapes=[pltpu.VMEM((NS, DI), F32), pltpu.VMEM((T, NS, 128), F32), pltpu.VMEM((T, NS, 128), F32),
                        pltpu.VMEM((T // 8, 8, DI), F32)],
        compiler_params=pltpu.CompilerParams(vmem_limit_bytes=limit << 20),
        cost_estimate=pl.CostEstimate(flops=40000000000, bytes_accessed=16 * L * DI, transcendentals=0),
    )(*ins)


def scan_back_kernel(T, Q, Q2, R, u_ref, dl_ref, gs_ref, cv_ref, in_ref, pT_ref, st_ref, xpT_ref, wdt_ref, par_ref, an_ref,
                     gi_ref, gxp_ref, gwd_ref, gpar_ref, carry, later, bx, cx, du, guc, gdt, hs, ds, gbp, gcp, sums):
    j = pl.program_id(0)
    c = pl.num_programs(0) - 1 - j
    DI = wdt_ref.shape[1]
    taps = par_ref.shape[0] - 3

    @pl.when(j == 0)
    def _():
        for ref in (carry, later, gxp_ref, gwd_ref, gpar_ref, sums):
            ref[...] = jnp.zeros_like(ref)
    pT = pT_ref[0]
    spread(bx, pT[R:R + NS], T)
    spread(cx, pT[R + NS:R + 2 * NS], T)
    du[...] = dl_ref[0] * u_ref[0]
    gbp[...] = jnp.zeros_like(gbp)
    gcp[...] = jnp.zeros_like(gcp)
    W = Q * 128

    def grp(g, _):
        base = pl.multiple_of(g * W, 128)
        lanes = [pl.ds(base + q * 128, 128) for q in range(Q)]
        loc = [slice(q * 128, q * 128 + 128) for q in range(Q)]
        an = [an_ref[:, ln] for ln in lanes]
        a2 = [v * 1.4426950408889634 for v in an]

        def tb(i, s):
            s = list(s)
            for k in range(8):
                t = i * 8 + k
                b = bx[t]
                gc = gcp[t]
                for q in range(Q):
                    dd = dl_ref[0, i, k:k + 1, lanes[q]]
                    dub = du[i, k:k + 1, lanes[q]]
                    gsr = gs_ref[0, i, k:k + 1, lanes[q]]
                    dec = jnp.exp2(dd * a2[q])
                    h = dec * s[q]
                    ds[t, :, loc[q]] = dec
                    hs[t, :, loc[q]] = h
                    s[q] = h + b * dub
                    gc = gc + s[q] * gsr
                gcp[t] = gc
            return tuple(s)
        lax.fori_loop(0, T // 8, tb, tuple(st_ref[0, :, ln] for ln in lanes))
        for q0 in range(0, Q, Q2):
            qs = range(q0, q0 + Q2)
            sk = {q: par_ref[taps + 2:taps + 3, lanes[q]] for q in qs}

            def rb(jj, cr):
                i = T // 8 - 1 - jj
                g_, ga = {q: cr[0][q - q0] for q in qs}, {q: cr[1][q - q0] for q in qs}
                gbs, gsk = list(cr[2]), list(cr[3])
                m1, m2 = {q: [None] * 8 for q in qs}, {q: [None] * 8 for q in qs}
                for k in range(7, -1, -1):
                    t = i * 8 + k
                    b = bx[t]
                    cc = cx[t]
                    gb = gbp[t]
                    for q in qs:
                        dd = dl_ref[0, i, k:k + 1, lanes[q]]
                        dub = du[i, k:k + 1, lanes[q]]
                        gsr = gs_ref[0, i, k:k + 1, lanes[q]]
                        gg = gsr * cc + g_[q]
                        g_[q] = gg * ds[t, :, loc[q]]
                        qq = gg * hs[t, :, loc[q]]
                        m1[q][k] = fold(gg * b)
                        m2[q][k] = fold(qq * an[q])
                        ga[q] = ga[q] + qq * dd
                        gb = gb + gg * dub
                    gbp[t] = gb
                for q in qs:
                    s1 = merge8(m1[q])
                    s2 = merge8(m2[q])
                    u8, d8, gs8 = u_ref[0, i, :, lanes[q]], dl_ref[0, i, :, lanes[q]], gs_ref[0, i, :, lanes[q]]
                    guc[i, :, lanes[q]] = d8 * s1 + sk[q] * gs8
                    gd = (s2 + u8 * s1) * sigmoid_of_softplus(d8)
                    gdt[i, :, lanes[q]] = gd
                    gbs[q - q0] = gbs[q - q0] + gd
                    gsk[q - q0] = gsk[q - q0] + gs8 * u8
                return (tuple(g_[q] for q in qs), tuple(ga[q] for q in qs), tuple(gbs), tuple(gsk))
            z8 = tuple(jnp.zeros((8, 128), F32) for q in qs)
            cr = lax.fori_loop(0, T // 8, rb, (tuple(carry[:, lanes[q]] for q in qs),
                                               tuple(jnp.zeros((NS, 128), F32) for q in qs), z8, z8), unroll=2)
            for q in qs:
                carry[:, lanes[q]] = cr[0][q - q0]
                gpar_ref[taps + 2:taps + 2 + NS, lanes[q]] += cr[1][q - q0] * an[q]
                sums[taps + 1, :, lanes[q]] += cr[2][q - q0]
                sums[taps + 2, :, lanes[q]] += cr[3][q - q0]
        return 0
    lax.fori_loop(0, DI // W, grp, 0)

    gbT = jnp.sum(gbp[...], axis=2).T
    gcT = jnp.sum(gcp[...], axis=2).T
    gd = gdt[...].reshape(T, DI).astype(jnp.bfloat16)
    gpT = jnp.concatenate([mm(wdt_ref[...], gd, NT), gbT, gcT], axis=0).astype(jnp.bfloat16)
    gwd_ref[...] += mm(pT[:R].astype(jnp.bfloat16), gd)
    gxp_ref[...] += mm(gpT, u_ref[0].reshape(T, DI).astype(jnp.bfloat16))
    gu = guc[...].reshape(T, DI) + mm(gpT, xpT_ref[...], TN)
    par = par_ref[...]
    conv = cv_ref[0].reshape(T, DI)
    sig = sigmoid(conv)
    gconv = gu * (sig * (1.0 + conv * (1.0 - sig)))
    part = lambda v: jnp.sum(v.reshape(T // 8, 8, DI), axis=0)
    sums[taps] += part(gconv)
    inner_x = in_ref[pl.ds(pl.multiple_of(c * T + 8, 8), T)]
    both = jnp.concatenate([gconv, later[...]], axis=0)
    gi = None
    for k in range(taps):
        ahead = both[taps - 1 - k:taps - 1 - k + T]
        sums[k] += part(ahead * inner_x)
        gi = par[k:k + 1] * ahead if gi is None else gi + par[k:k + 1] * ahead
    gi_ref[...] = gi.astype(jnp.bfloat16)
    later[...] = gconv[:8]

    @pl.when(c == 0)
    def _():
        for k in range(taps + 2):
            gpar_ref[k:k + 1] = jnp.sum(sums[k], axis=0, keepdims=True)
        gpar_ref[taps + 2 + NS:taps + 3 + NS] = jnp.sum(sums[taps + 2], axis=0, keepdims=True)


def scan_backward(u, dl, gs, conv, inner, pT, st, xpT, wdt, par, an, limit, Q=3, Q2=3):
    C, T8, _, DI = u.shape
    T = T8 * 8
    XP, R = xpT.shape[0], wdt.shape[0]
    n = par.shape[0] + NS
    rev = lambda *shape: pl.BlockSpec((1,) + shape, lambda j: (C - 1 - j,) + (0,) * len(shape))
    rows = rev(T8, 8, DI)
    outs = [sds((C * T, DI), jnp.bfloat16), sds((XP, DI)), sds((R, DI)), sds((n, DI))]
    V = lambda *s: pltpu.VMEM(s, F32)
    return pl.pallas_call(
        functools.partial(scan_back_kernel, T, Q, Q2, R), grid=(C,),
        in_specs=[rows, rows, rows, rows, whole_spec(inner), rev(XP, T), rev(NS, DI)] + [whole_spec(a) for a in (xpT, wdt, par, an)],
        out_specs=[pl.BlockSpec((T, DI), lambda j: (C - 1 - j, 0))] + [whole_spec(o) for o in outs[1:]],
        out_shape=outs,
        scratch_shapes=[V(NS, DI), V(8, DI), V(T, NS, 128), V(T, NS, 128), V(T8, 8, DI), V(T8, 8, DI), V(T8, 8, DI),
                        V(T, NS, Q * 128), V(T, NS, Q * 128), V(T, NS, 128), V(T, NS, 128), V(par.shape[0], 8, DI)],
        compiler_params=pltpu.CompilerParams(vmem_limit_bytes=limit << 20),
        cost_estimate=pl.CostEstimate(flops=80000000000, bytes_accessed=16 * C * T * DI, transcendentals=0),
    )(u, dl, gs, conv, inner, pT, st, xpT, wdt, par, an)


def one_call(kernel, ins, outs, scalars=(), flops=0, limit=56):
    smem = pl.BlockSpec(memory_space=pltpu.SMEM)
    vmem = pl.BlockSpec(memory_space=pltpu.VMEM)
    size = sum(a.size * a.dtype.itemsize for a in list(ins) + list(outs))
    return pl.pallas_call(
        kernel,
        in_specs=[smem] * len(scalars) + [vmem] * len(ins), out_specs=[vmem] * len(outs), out_shape=list(outs),
        compiler_params=pltpu.CompilerParams(vmem_limit_bytes=limit << 20),
        cost_estimate=pl.CostEstimate(flops=flops, bytes_accessed=size, transcendentals=0),
    )(*scalars, *ins)


def route_kernel(cap, here, message, live_ref, x_ref, nm_ref, y_ref, wz_ref, wo_ref, gain_ref, wr_ref, route_ref, cot_ref,
                 z_ref, gated_ref, hid_ref, place_ref, out_ref, prob_ref, gate_ref):
    bf = jnp.bfloat16
    L = x_ref.shape[0]
    E = wr_ref.shape[0]
    z = mm(nm_ref[...], wz_ref[...])
    z_ref[...] = z
    gated = (y_ref[...] * (z * sigmoid(z))).astype(bf)
    gated_ref[...] = gated
    hid = x_ref[...].astype(F32) + mm(gated, wo_ref[...])
    hid_ref[...] = hid
    nmoe = hid * lax.rsqrt(jnp.mean(hid * hid, axis=-1, keepdims=True) + 1e-05) * gain_ref[...]
    logits = mm(nmoe, wr_ref[...], NT, precision=lax.Precision.HIGHEST)
    e = jnp.exp(logits - jnp.max(logits, axis=-1, keepdims=True))
    probs = e / jnp.sum(e, axis=-1, keepdims=True)
    prob_ref[...] = probs
    route = route_ref[...]
    hot = route == lax.broadcasted_iota(jnp.int32, (L, E), 1)
    gate = jnp.sum(jnp.where(hot, probs, 0.0), axis=-1, keepdims=True)
    gate_ref[...] = gate
    live = lax.broadcasted_iota(jnp.int32, (L, 1), 0) < live_ref[0]
    hits = jnp.where(hot & live, 1.0, 0.0)
    before = lax.broadcasted_iota(jnp.int32, (L, L), 0) > lax.broadcasted_iota(jnp.int32, (L, L), 1)
    slot = jnp.sum(mm(jnp.where(before, 1.0, 0.0).astype(bf), hits.astype(bf)) * hits, axis=-1, keepdims=True).astype(jnp.int32)
    slots = place_ref.shape[1]
    target = route // here * message + route % here * cap + slot
    target = jnp.where(live & (slot < cap), target, slots)
    place = jnp.where(target == lax.broadcasted_iota(jnp.int32, (L, slots), 1), 1.0, 0.0).astype(bf)
    place_ref[...] = place
    D = hid.shape[1]
    gy = jnp.where(live, cot_ref[...], 0.0)
    out_ref[:, :D] = mm(place, nmoe.astype(bf), TN).astype(bf)
    out_ref[:, D:] = mm(place, (gy * gate).astype(bf), TN).astype(bf)


def unroute_kernel(live_ref, home_ref, place_ref, hid_ref, prob_ref, gate_ref, route_ref, cot_ref, gain_ref, wr_ref, wo_ref, sh_ref,
                   z_ref, y_ref, mix_ref, gh_ref, gs_ref, gz_ref, gm_ref, gr_ref, gg_ref):
    bf = jnp.bfloat16
    high = lax.Precision.HIGHEST
    hid, gain = hid_ref[...], gain_ref[...]
    L, D = hid.shape
    E = wr_ref.shape[0]
    tok = mm(place_ref[...], home_ref[...])
    etok, gsent = tok[:, :D], tok[:, D:]
    live = lax.broadcasted_iota(jnp.int32, (L, 1), 0) < live_ref[0]
    gate, probs = gate_ref[...], prob_ref[...]
    mix_ref[...] = jnp.where(live, hid + gate * etok, 0.0).astype(bf)
    gy = jnp.where(live, cot_ref[...], 0.0)
    ggate = jnp.sum(gy * etok, axis=-1, keepdims=True)
    hot = jnp.where(route_ref[...] == lax.broadcasted_iota(jnp.int32, (L, E), 1), 1.0, 0.0)
    glog = ggate * gate * (hot - probs)
    rms = lax.rsqrt(jnp.mean(hid * hid, axis=-1, keepdims=True) + 1e-05)
    hat = hid * rms
    gr_ref[...] = mm(glog, hat * gain, TN, precision=high)
    gnorm = gsent + mm(glog, wr_ref[...], precision=high)
    gg_ref[...] = jnp.sum(gnorm * hat, axis=0, keepdims=True)
    scaled = gnorm * gain
    gh = gy + rms * (scaled - hat * jnp.mean(scaled * hat, axis=-1, keepdims=True))
    gh_ref[...] = gh
    gmix = gh.astype(bf)
    gm_ref[...] = mm(gmix, sh_ref[...]).astype(bf)
    ggated = mm(gmix, wo_ref[...], NT)
    z = z_ref[...]
    sig = sigmoid(z)
    gs_ref[...] = ggated * (z * sig)
    gz_ref[...] = (ggated * y_ref[...] * (sig * (1.0 + z * (1.0 - sig)))).astype(bf)


def token_kernel(gi_ref, gz_ref, wx_ref, wz_ref, x_ref, gh_ref, gain_ref, gt_ref, gg_ref):
    gnm = mm(gi_ref[...], wx_ref[...], NT) + mm(gz_ref[...], wz_ref[...], NT)
    x = x_ref[...].astype(F32)
    rms = lax.rsqrt(jnp.mean(x * x, axis=-1, keepdims=True) + 1e-05)
    hat = x * rms
    gg_ref[...] = jnp.sum(gnm * hat, axis=0, keepdims=True)
    scaled = gnm * gain_ref[...]
    gt_ref[...] = gh_ref[...] + rms * (scaled - hat * jnp.mean(scaled * hat, axis=-1, keepdims=True))


QB = 64
CAP = 13
BF = jnp.bfloat16
root_half = 0.7071067811865476
inv_root_two_pi = 0.3989422804014327
log2e = 1.4426950408889634


def swap(x, axis, bit):
    n = lax.axis_size(axis)
    return lax.ppermute(x, axis, [(i, i ^ bit) for i in range(n)])


def bits_of(axis):
    n = lax.axis_size(axis)
    return [1 << k for k in range(n.bit_length() - 1)]


def exchange(x, mask):
    rm, cm = mask
    if rm == 0:
        return swap(x, "col", cm)
    if cm == 0:
        return swap(x, "row", rm)
    rows, cols = lax.axis_size("row"), lax.axis_size("col")
    pairs = [(r * cols + c, (r ^ rm) * cols + (c ^ cm)) for r in range(rows) for c in range(cols)]
    return lax.ppermute(x, ("row", "col"), pairs)


def combos(bits):
    out = [(0, 0)]
    for rb, cb in bits:
        out = out + [(r | rb, c | cb) for r, c in out]
    return out


def stages():
    row, col = bits_of("row"), bits_of("col")
    far = combos([(b, 0) for b in row[1:]])
    plane = combos([(row[0], 0)] + [(0, b) for b in col[1:]])
    return far, plane, (0, col[0])


def add(a, b):
    return (a[0] ^ b[0], a[1] ^ b[1])


def gather_far(x):
    return jnp.stack([x] + [exchange(x, m) for m in stages()[0][1:]])


def gather_plane(mine):
    return [mine] + [exchange(mine, m) for m in stages()[1][1:]]


def gather_core(near):
    far, plane, core = stages()
    near = [([add(f, m) for f in far], b) for m, b in zip(plane, near)]
    return near + [([add(m, core) for m in ms], exchange(b, core)) for ms, b in near]


def gather_list(x):
    return gather_core(gather_plane(gather_far(x)))


def assemble_kernel(masks, moves, count_in, *refs):
    r0, c0 = refs[0][0], refs[0][1]
    ins, outs = refs[1:1 + count_in], refs[1 + count_in:]
    for buf, ms in zip(ins, masks):
        for i, (rm, cm) in enumerate(ms):
            for (row, count, lanes), out, place in moves:
                place(outs[out], r0 ^ rm, c0 ^ cm, buf[i, row:row + count, :lanes])


def put_block(out, r, c, block):
    n, m = block.shape
    out[pl.ds(pl.multiple_of(r * n, n), n), pl.ds(pl.multiple_of(c * m, m), m)] = block


def put_pair(out, r, c, block):
    out[r, c] = block


def take_blocks(gathered):
    rows, cols = lax.axis_size("row"), lax.axis_size("col")
    order = [r * cols + c for ms, _ in gathered for r, c in ms]
    entry = jnp.asarray([order.index(i) for i in range(rows * cols)], jnp.int32)
    me = lax.axis_index("row") * cols + lax.axis_index("col")
    stacked = jnp.concatenate([b for _, b in gathered], axis=0)
    out = jnp.take(stacked, entry[jnp.arange(rows * cols, dtype=jnp.int32) ^ me], axis=0)
    return out.reshape((rows, cols) + stacked.shape[1:])


def assemble(gathered, moves, shapes):
    masks = [ms for ms, _ in gathered]
    bufs = [b for _, b in gathered]
    if any(lanes % 128 for (_, _, lanes), _, _ in moves):
        every = take_blocks(gathered)
        cut = [every[:, :, row:row + count, :lanes] for (row, count, lanes), _, _ in moves]
        return [v if place is put_pair else v.transpose(0, 2, 1, 3).reshape(shape)
                for v, shape, (_, _, place) in zip(cut, shapes, moves)]
    me = jnp.stack([lax.axis_index("row"), lax.axis_index("col")]).astype(jnp.int32)
    vmem = pl.BlockSpec(memory_space=pltpu.VMEM)
    return pl.pallas_call(
        functools.partial(assemble_kernel, masks, moves, len(bufs)),
        in_specs=[pl.BlockSpec(memory_space=pltpu.SMEM)] + [vmem] * len(bufs),
        out_specs=[vmem] * len(shapes),
        out_shape=[jax.ShapeDtypeStruct(s, BF) for s in shapes],
        compiler_params=pltpu.CompilerParams(vmem_limit_bytes=32 << 20),
        cost_estimate=pl.CostEstimate(flops=0, bytes_accessed=4 * sum(b.size for b in bufs), transcendentals=0),
    )(me, *bufs)


def between(work, give, got):
    result = work(give)
    return lax.optimization_barrier((got, result))


def reduce_core(parts, work=None):
    far, plane, core = stages()
    near = [k for k in range(lax.axis_size("col")) if not k & core[1]]
    give = jnp.stack([parts[k | core[1]] for k in near])
    got = exchange(give, core)
    result = None
    if work:
        got, result = between(work, give, got)
    return [parts[k].astype(F32) + got[i].astype(F32) for i, k in enumerate(near)], result


def reduce_plane_give(sums):
    far, plane, core = stages()
    near = [k for k in range(lax.axis_size("col")) if not k & core[1]]
    rows, r0 = lax.axis_size("row"), lax.axis_index("row")

    def rows_of(k, rm):
        v = sums[near.index(k)]
        return lax.dynamic_index_in_dim(v.reshape((rows // 2, 2) + v.shape[1:]), (r0 ^ rm) & 1, 1, keepdims=False)
    return rows_of(0, 0), [rows_of(cm, rm).astype(BF) for rm, cm in plane[1:]]


def reduce_plane(own, give, work=None):
    got = [exchange(g, m) for g, m in zip(give, stages()[1][1:])]
    result = None
    if work:
        got, result = between(work, give, got)
    return functools.reduce(lambda t, v: t + v.astype(F32), got, own), result


def reduce_far(total, work=None):
    far = stages()[0]
    r0 = lax.axis_index("row")
    give = [lax.dynamic_index_in_dim(total, (r0 ^ rm) >> 1, 0, keepdims=False).astype(BF) for rm, _ in far[1:]]
    got = [exchange(g, m) for g, m in zip(give, far[1:])]
    result = None
    if work:
        got, result = between(work, give, got)
    done = lax.dynamic_index_in_dim(total, r0 >> 1, 0, keepdims=False)
    return functools.reduce(lambda t, v: t + v.astype(F32), got, done), result


def reduce_list(parts):
    own, give = reduce_plane_give(reduce_core(parts)[0])
    return reduce_far(reduce_plane(own, give)[0])[0]


def column_kernel(count, s_ref, *refs):
    total = mm(refs[0][...], refs[1][...], ((0,), (0,)))
    for k in range(1, count):
        total = total + mm(refs[2 * k][...], refs[2 * k + 1][...], ((0,), (0,)))
    refs[-1][0] = total.astype(BF)


def column_blocks(pairs, cols, my_col):
    n, m = pairs[0][0].shape
    w = pairs[0][1].shape[1] // cols
    count = len(pairs)
    if w % 128:
        total = sum(mm(a, b, ((0,), (0,))) for a, b in pairs).astype(BF).reshape(m, cols, w).transpose(1, 0, 2)
        return jnp.take(total, jnp.arange(cols, dtype=jnp.int32) ^ my_col, axis=0)
    return pl.pallas_call(
        functools.partial(column_kernel, count),
        grid_spec=pltpu.PrefetchScalarGridSpec(
            num_scalar_prefetch=1, grid=(cols,),
            in_specs=[pl.BlockSpec((n, m), lambda k, s: (0, 0)), pl.BlockSpec((n, w), lambda k, s: (0, s[0] ^ k))] * count,
            out_specs=pl.BlockSpec((1, m, w), lambda k, s: (k, 0, 0))),
        out_shape=jax.ShapeDtypeStruct((cols, m, w), BF),
        compiler_params=pltpu.CompilerParams(vmem_limit_bytes=32 << 20),
        cost_estimate=pl.CostEstimate(flops=2 * count * n * m * w * cols, bytes_accessed=2 * (count * (n * m + n * w * cols) + m * w * cols), transcendentals=0),
    )(my_col.reshape(1), *[v for p in pairs for v in p])


def gelu_parts(v):
    phi = 0.5 * (1.0 + lax.erf(v * root_half))
    return v * phi, phi + v * jnp.exp(-0.5 * v * v) * inv_root_two_pi


def expert_kernel(cols, *refs):
    both, up, down = refs[:cols], refs[cols], refs[cols + 1]
    outs, acts, gps = refs[cols + 2:2 * cols + 2], refs[2 * cols + 2], refs[2 * cols + 3]
    width = up.shape[1]
    n = both[0].shape[1]
    rows = jnp.concatenate([b[0] for b in both], axis=0)
    act, slope = gelu_parts(mm(rows[:, :width], up[0]))
    act = act.astype(BF)
    acts[0] = act
    gp = (mm(rows[:, width:], down[0], ((1,), (1,))) * slope).astype(BF)
    gps[0] = gp
    out = mm(act, down[0]).astype(BF)
    gin = mm(gp, up[0], ((1,), (1,))).astype(BF)
    for c in range(cols):
        outs[c][0, :, :width] = out[c * n:(c + 1) * n]
        outs[c][0, :, width:] = gin[c * n:(c + 1) * n]


def weights_kernel(cols, sets, *refs):
    up, down = refs[-2:]
    step = cols + 2
    gu = gd = None
    width = up.shape[1]
    for s in range(sets):
        both, act, gp = refs[s * step:s * step + cols], refs[s * step + cols][0], refs[s * step + cols + 1][0]
        rows = jnp.concatenate([b[0] for b in both], axis=0)
        a = mm(rows[:, :width], gp, ((0,), (0,)))
        b = mm(act, rows[:, width:], ((0,), (0,)))
        gu, gd = (a, b) if gu is None else (gu + a, gd + b)
    up[0] = gu
    down[0] = gd


def per_expert(kernel, ins, shapes, flops):
    tok = lambda a: pl.BlockSpec((1,) + a.shape[1:], lambda e: (e, 0, 0))
    size = sum(a.size * 2 for a in ins) + sum(s.size * s.dtype.itemsize for s in shapes)
    return list(pl.pallas_call(
        kernel, grid=(ins[0].shape[0],),
        in_specs=[tok(a) for a in ins], out_specs=[tok(s) for s in shapes], out_shape=shapes,
        compiler_params=pltpu.CompilerParams(vmem_limit_bytes=(44 if len(ins) <= 12 else 56) << 20),
        cost_estimate=pl.CostEstimate(flops=flops, bytes_accessed=size, transcendentals=0),
    )(*ins))


def expert_both(bufs, up, down):
    cols = len(bufs)
    experts, d, f = up.shape
    n = bufs[0].shape[1]
    shapes = ([jax.ShapeDtypeStruct((experts, n, 2 * d), BF)] * cols
              + [jax.ShapeDtypeStruct((experts, n * cols, f), BF)] * 2)
    outs = per_expert(functools.partial(expert_kernel, cols), bufs + [up, down], shapes, 8 * experts * cols * n * d * f)
    return outs[:cols], outs[cols:]


def expert_weights(sets, d, f):
    cols = len(sets[0]) - 2
    experts, n, _ = sets[0][0].shape
    if len(sets) > 1 and len(sets) * cols > 8:
        return [sum(v) for v in zip(*[expert_weights([s], d, f) for s in sets])]
    shapes = [jax.ShapeDtypeStruct((experts, d, f), F32), jax.ShapeDtypeStruct((experts, f, d), F32)]
    return per_expert(functools.partial(weights_kernel, cols, len(sets)), [v for s in sets for v in s], shapes,
                      4 * experts * cols * n * d * f * len(sets))


def up_to(n, m):
    return -(-n // m) * m


def tiles_fit(w_in_x, w_xproj, w_out, conv_w, w_dt, w_router):
    return (w_in_x.shape == (96, 384) and w_xproj.shape[0] == 192 and w_xproj.shape[1] <= 26 and w_dt.shape[0] <= 6
            and conv_w.shape[0] + NS + 5 <= 26 and conv_w.shape[1] <= 128 and w_out.shape == (192, 192)
            and w_router.shape[0] <= 128 and w_router.shape[1] <= 16)


def one_hot(shape, match):
    i = lax.broadcasted_iota(jnp.int32, shape, 0)
    j = lax.broadcasted_iota(jnp.int32, shape, 1)
    return jnp.where(match(i, j), 1.0, 0.0).astype(BF)


def pack_kernel(wx, wdt, xp, cw, cb, db, al, ds, gx, gm, wz, wo, wr, first, other, s_ex, s_r):
    n = wx.shape[0]
    s_ex[...] = jnp.zeros_like(s_ex)
    s_r[...] = jnp.zeros_like(s_r)
    first[:n] = wx[...]
    s_ex[:xp.shape[1], :xp.shape[0]] = xp[...].astype(F32).T
    wide = s_ex.shape[1] - 128
    at = 0
    for v in (cw, cb, db, al, ds, gx, gm):
        s_ex[at:at + v.shape[0], wide:wide + v.shape[1]] = v[...].astype(F32)
        at += v.shape[0]
    s_ex[26:26 + wdt.shape[0]] = wdt[...].astype(F32)
    first[n:] = s_ex[...].astype(BF)
    s_r[:wr.shape[1], :wr.shape[0]] = wr[...].astype(F32).T

    def put(at, lane, v):
        other[at:at + v.shape[0], lane:lane + v.shape[1]] = v
    put_other(put, wz[...], wo[...])
    other[other.shape[0] - 16:] = s_r[...].astype(BF)


def put_other(put, z, out):
    n, m = z.shape[-2], out.shape[-2]
    put(0, 0, z[..., :256])
    put(n, 0, z[..., :n // 2, 256:])
    put(n, 128, z[..., n // 2:, 256:])
    at = n + n // 2
    put(at, 0, out[..., :m // 2, :128])
    put(at, 128, out[..., m // 2:, :128])
    put(at + m // 2, 0, jnp.concatenate([out[..., j * m // 4:(j + 1) * m // 4, 128:192] for j in range(4)], axis=-1))


def pack_params(w_in_x, w_dt, w_xproj, conv_w, conv_b, dt_bias, a_log, d_skip, gain_mix, gain_moe, w_in_z, w_out, w_router):
    n, lanes = w_in_x.shape
    ins = [w_in_x, w_dt, w_xproj, conv_w, conv_b[None], dt_bias[None], a_log, d_skip[None], gain_mix[None], gain_moe[None],
           w_in_z, w_out, w_router]
    vmem = pl.BlockSpec(memory_space=pltpu.VMEM)
    V = lambda *s: pltpu.VMEM(s, F32)
    return pl.pallas_call(
        pack_kernel, in_specs=[vmem] * len(ins), out_specs=[vmem] * 2,
        out_shape=[sds((n + 32, lanes), BF), sds((n + n // 2 + w_out.shape[0] * 3 // 4 + 16, 256), BF)],
        scratch_shapes=[V(32, lanes), V(16, 256)],
    )(*ins)


def each_block(masks, bufs, r0, c0):
    for buf, ms in zip(bufs, masks):
        for i, (rm, cm) in enumerate(ms):
            yield buf, i, r0 ^ rm, c0 ^ cm


def span(i, n):
    return pl.ds(pl.multiple_of(i * n, n), n)


def dt_match(j, i, dt_rows):
    k = j % 32 - 26
    return (k >= 0) & (k < dt_rows) & (j // 32 * dt_rows + k == i)


def unpack_first(masks, dims, me, *refs):
    dt_rows, xp_cols, xp_rows, share, gshare, taps, rows, cols = dims
    count = len(masks)
    bufs = refs[:count]
    fx, dt, xpT, par, an, a2, gx, gm, w_dt, w_xp, w_sm = refs[count:]
    n = bufs[0].shape[1] - 32
    lanes = bufs[0].shape[2]
    wide = lanes - 128
    for buf, i, r, c in each_block(masks, bufs, me[0], me[1]):
        fx[span(r, n), span(c, lanes)] = buf[i, :n]
        w_dt[span(r, 32), span(c, lanes)] = buf[i, n:]
        w_xp[span(c, 32), span(r, wide)] = buf[i, n:, :wide]
        w_sm[:, span(r * cols + c, 128)] = buf[i, n:, wide:]
    pick = one_hot((dt.shape[0], 32 * rows), lambda i, j: dt_match(j, i, dt_rows))
    dt[...] = mm(pick, w_dt[...]).astype(BF)
    pick = one_hot((xpT.shape[0], 32 * cols), lambda i, j: (j % 32 < xp_cols) & (j // 32 * xp_cols + j % 32 == i))
    t = mm(pick, w_xp[...])
    xpT[...] = jnp.concatenate([t[:, r * wide:r * wide + xp_rows] for r in range(rows)], axis=1).astype(BF)
    sm = w_sm[...].astype(F32)
    chan = jnp.concatenate([sm[:, p * 128:p * 128 + share] for p in range(rows * cols)], axis=1)
    par[:taps + 2] = chan[:taps + 2]
    par[taps + 2:] = chan[taps + 2 + NS:taps + 3 + NS]
    neg = -jnp.exp(chan[taps + 2:taps + 2 + NS])
    an[...] = neg
    a2[...] = neg * log2e
    gains = jnp.concatenate([sm[taps + 3 + NS:taps + 5 + NS, p * 128:p * 128 + gshare] for p in range(rows * cols)], axis=1)
    gx[...] = gains[:1]
    gm[...] = gains[1:]


def unpack_other(masks, dims, me, *refs):
    n, out_rows, out_lanes, r_cols, cols = dims
    count = len(masks)
    bufs = refs[:count]
    fz, fo, router, w_out, w_r = refs[count:]
    half = n // 2
    at = n + half
    m = out_rows
    for buf, i, r, c in each_block(masks, bufs, me[0], me[1]):
        fz[span(r, n), pl.ds(pl.multiple_of(c * 384, 128), 256)] = buf[i, :n]
        for j in range(2):
            rows = pl.ds(pl.multiple_of(r * n + j * half, 16), half)
            fz[rows, pl.ds(pl.multiple_of(c * 384 + 256, 128), 128)] = buf[i, n:at, j * 128:(j + 1) * 128]
            rows = pl.ds(pl.multiple_of(r * m + j * (m // 2), 16), m // 2)
            w_out[rows, span(2 * c, 128)] = buf[i, at:at + m // 2, j * 128:(j + 1) * 128]
        for j in range(4):
            rows = pl.ds(pl.multiple_of(r * m + j * (m // 4), 16), m // 4)
            w_out[rows, pl.ds(pl.multiple_of(c * 256 + 128, 128), 64)] = buf[i, at + m // 2:at + m * 3 // 4, j * 64:(j + 1) * 64]
        w_r[span(c, 16), span(r, 128)] = buf[i, at + m * 3 // 4:, :128]
    wide = w_out[...]
    fo[...] = jnp.concatenate([wide[:, c * 256:c * 256 + out_lanes] for c in range(cols)], axis=1)
    pick = one_hot((router.shape[0], 16 * cols), lambda i, j: (j % 16 < r_cols) & (j // 16 * r_cols + j % 16 == i))
    t = mm(pick, w_r[...])
    r_rows = router.shape[1] // (t.shape[1] // 128)
    router[...] = jnp.concatenate([t[:, r * 128:r * 128 + r_rows] for r in range(t.shape[1] // 128)], axis=1)


def unpack_call(kernel, gathered, dims, outs, scratch):
    masks = [ms for ms, _ in gathered]
    bufs = [b for _, b in gathered]
    me = jnp.stack([lax.axis_index("row"), lax.axis_index("col")]).astype(jnp.int32)
    vmem = pl.BlockSpec(memory_space=pltpu.VMEM)
    return pl.pallas_call(
        functools.partial(kernel, masks, dims),
        in_specs=[pl.BlockSpec(memory_space=pltpu.SMEM)] + [vmem] * len(bufs), out_specs=[vmem] * len(outs), out_shape=outs,
        scratch_shapes=[pltpu.VMEM(s, BF) for s in scratch],
        compiler_params=pltpu.CompilerParams(vmem_limit_bytes=28 << 20),
        cost_estimate=pl.CostEstimate(flops=0, bytes_accessed=4 * sum(b.size for b in bufs), transcendentals=0),
    )(me, *bufs)


def grad_x_kernel(count, dims, s_ref, *refs):
    dt_rows, xp_cols, xp_rows, share, gshare, rows, cols = dims
    pairs = refs[:2 * count]
    gwd, gxp, gpar, gmix, gmoe = (refs[(2 + i) * count:(3 + i) * count] for i in range(5))
    keep, give, w_dt, w_xp, w_sm, full = refs[7 * count:]
    k = pl.program_id(0)
    n, lanes = keep.shape[2] - 32, keep.shape[3]
    wide = lanes - 128
    total = lambda vs: functools.reduce(lambda a, b: a + b, [v[...] for v in vs])

    @pl.when(k == 0)
    def _():
        g = total(gwd).astype(BF)
        full[...] = sum_products(pairs)
        put = one_hot((32 * rows, g.shape[0]), lambda j, i: dt_match(j, i, dt_rows))
        w_dt[...] = mm(put, g).astype(BF)
        g = total(gxp).astype(BF)
        put = one_hot((32 * cols, g.shape[0]), lambda j, i: (j % 32 < xp_cols) & (j // 32 * xp_cols + j % 32 == i))
        t = mm(put, g)
        gap = jnp.zeros((t.shape[0], wide - xp_rows), F32)
        w_xp[...] = jnp.concatenate([v for r in range(rows) for v in (t[:, r * xp_rows:(r + 1) * xp_rows], gap)], axis=1).astype(BF)
        w_sm[...] = jnp.zeros_like(w_sm)
        par, mix, moe = total(gpar), total(gmix), total(gmoe)
        m = par.shape[0]
        for p in range(rows * cols):
            w_sm[:m, p * 128:p * 128 + share] = par[:, p * share:(p + 1) * share]
            w_sm[m:m + 1, p * 128:p * 128 + gshare] = mix[:, p * gshare:(p + 1) * gshare]
            w_sm[m + 1:m + 2, p * 128:p * 128 + gshare] = moe[:, p * gshare:(p + 1) * gshare]
    for j, out in enumerate((keep, give)):
        c = s_ref[0] ^ (2 * k + j)
        out[0, :, :n] = full[:, span(c, lanes)].astype(BF).reshape(rows, n, lanes)
        for r in range(rows):
            d = w_dt[r * 32:(r + 1) * 32, span(c, lanes)]
            out[0, r, n:, :wide] = w_xp[span(c, 32), r * wide:(r + 1) * wide] + d[:, :wide]
            out[0, r, n:, wide:] = (w_sm[:, span(r * cols + c, 128)] + d[:, wide:].astype(F32)).astype(BF)


def sum_products(pairs):
    return functools.reduce(lambda a, b: a + b, [mm(pairs[i][...], pairs[i + 1][...], TN) for i in range(0, len(pairs), 2)])


def grad_blocks(kernel, ins, scratch, block, rows, cols, my_col, flops):
    out = sds((cols // 2, rows) + block, BF)
    return list(pl.pallas_call(
        kernel,
        grid_spec=pltpu.PrefetchScalarGridSpec(
            num_scalar_prefetch=1, grid=(cols // 2,), in_specs=[whole_spec(v) for v in ins],
            out_specs=[pl.BlockSpec((1, rows) + block, lambda k, s: (k, 0, 0, 0))] * 2, scratch_shapes=scratch),
        out_shape=[out, out],
        compiler_params=pltpu.CompilerParams(vmem_limit_bytes=44 << 20),
        cost_estimate=pl.CostEstimate(flops=flops, bytes_accessed=1 << 23, transcendentals=0),
    )(my_col.reshape(1), *ins))


def grad_x_blocks(pairs, smalls, dims, my_col):
    rows, cols = dims[-2:]
    n, m = pairs[0][0].shape
    inner = pairs[0][1].shape[1]
    lanes = inner // cols
    ins = [v for p in pairs for v in p] + [g[name] for name in ("dt", "xproj", "chan", "gain_mix", "gain_moe") for g in smalls]
    scratch = [pltpu.VMEM((32 * rows, inner), BF), pltpu.VMEM((32 * cols, (lanes - 128) * rows), BF), pltpu.VMEM((32, 128 * rows * cols), F32),
               pltpu.VMEM((m, inner), F32)]
    return grad_blocks(functools.partial(grad_x_kernel, len(pairs), dims), ins, scratch, (m // rows + 32, lanes), rows, cols, my_col,
                       2 * len(pairs) * n * m * inner)


def grad_other_kernel(count, r_cols, s_ref, *refs):
    zs, outs, routers = refs[:2 * count], refs[2 * count:4 * count], refs[4 * count:5 * count]
    keep, give, full_z, full_o = refs[5 * count:]
    rows = keep.shape[1]
    k = pl.program_id(0)

    @pl.when(k == 0)
    def _():
        full_z[...] = sum_products(zs)
        full_o[...] = sum_products(outs)
    r = functools.reduce(lambda a, b: a + b, [v[...] for v in routers]).astype(BF)
    r_rows = r.shape[1] // rows
    for j, out in enumerate((keep, give)):
        c = s_ref[0] ^ (2 * k + j)
        z = full_z[:, pl.ds(pl.multiple_of(c * 384, 128), 384)].astype(BF)
        o = full_o[:, span(2 * k + j, 256)].astype(BF)
        z, o = (v.reshape(rows, v.shape[0] // rows, v.shape[1]) for v in (z, o))

        def put_block(at, lane, v):
            out[0, :, at:at + v.shape[1], lane:lane + v.shape[2]] = v
        put_other(put_block, z, o)
        w = mm(one_hot((16, r.shape[0]), lambda a, b: (a < r_cols) & (b == c * r_cols + a)), r).astype(BF)
        at = out.shape[2] - 16
        out[0, :, at:] = jnp.zeros((rows, 16, 256), BF)
        for q in range(rows):
            out[0, q, at:, :r_rows] = w[:, q * r_rows:(q + 1) * r_rows]


def grad_other_blocks(zs, outs, routers, block, rows, cols, r_cols, my_col):
    ins = [v for p in zs for v in p] + [v for p in outs for v in p] + list(routers)
    flops = 2 * sum(a.shape[0] * a.shape[1] * b.shape[1] for a, b in zs + outs)
    scratch = [pltpu.VMEM((a.shape[1], b.shape[1]), F32) for a, b in (zs[0], outs[0])]
    return grad_blocks(functools.partial(grad_other_kernel, len(zs), r_cols), ins, scratch, block, rows, cols, my_col, flops)


def split_near_kernel(plan, s_ref, keep, got, own, *gives):
    for out, (ki, rm) in zip((own,) + gives, plan):
        p = (s_ref[0] ^ rm) & 1
        v = keep[ki, 0, p].astype(F32) + got[ki, 0, p].astype(F32)
        out[0] = v.astype(out.dtype)


def split_near(keep, got):
    plane = stages()[1]
    near, rows, n, lanes = keep.shape
    plan = [(cm >> 1, rm) for rm, cm in plane]
    view = (near, rows // 2, 2, n, lanes)
    outs = [sds((rows // 2, n, lanes), F32 if i == 0 else BF) for i in range(len(plan))]
    res = pl.pallas_call(
        functools.partial(split_near_kernel, plan),
        grid_spec=pltpu.PrefetchScalarGridSpec(
            num_scalar_prefetch=1, grid=(rows // 2,),
            in_specs=[pl.BlockSpec((near, 1, 2, n, lanes), lambda z, s: (0, z, 0, 0, 0))] * 2,
            out_specs=[pl.BlockSpec((1, n, lanes), lambda z, s: (z, 0, 0))] * len(outs)),
        out_shape=outs,
        compiler_params=pltpu.CompilerParams(vmem_limit_bytes=16 << 20),
        cost_estimate=pl.CostEstimate(flops=0, bytes_accessed=6 * keep.size, transcendentals=0),
    )(lax.axis_index("row").reshape(1), keep.reshape(view), got.reshape(view))
    return res[0], list(res[1:])


def split_far_kernel(count, plan, s_ref, own, *refs):
    gots, mine, gives = refs[:count], refs[count], refs[count + 1:]
    for out, rm in zip((mine,) + gives, plan):
        i = (s_ref[0] ^ rm) >> 1
        v = own[i]
        for g in gots:
            v = v + g[i].astype(F32)
        out[...] = v.astype(out.dtype)


def split_far(own, gots):
    plan = [rm for rm, _ in stages()[0]]
    _, n, lanes = own.shape
    outs = [sds((n, lanes), F32 if i == 0 else BF) for i in range(len(plan))]
    res = one_call(functools.partial(split_far_kernel, len(gots), plan), [own] + gots, outs, [lax.axis_index("row").reshape(1)])
    return res[0], list(res[1:])


def total_of(refs):
    return functools.reduce(lambda a, b: a + b[...].astype(F32), refs[1:], refs[0][...])


def finish_x_kernel(count, *refs):
    gx, gxp, gdt, gcw, gcb, gdb, gal, gds, gmix, gmoe, s = refs[count:]
    s[...] = total_of(refs[:count])
    n, lanes = gx.shape
    gx[...] = s[:n]
    gdt[...] = s[n + 26:n + 26 + gdt.shape[0]]
    wide = lanes - 128
    gxp[...] = s[n:, :wide].T[:gxp.shape[0], :gxp.shape[1]]
    at = n
    for ref in (gcw, gcb, gdb, gal, gds, gmix, gmoe):
        ref[...] = s[at:at + ref.shape[0], wide:wide + ref.shape[1]]
        at += ref.shape[0]


def finish_other_kernel(count, *refs):
    gz, go, gr, s = refs[count:]
    s[...] = total_of(refs[:count])
    n = gz.shape[0]
    half = n // 2
    gz[:, :256] = s[:n]
    gz[:half, 256:] = s[n:n + half, :128]
    gz[half:, 256:] = s[n:n + half, 128:]
    at = n + half
    m = go.shape[0]
    for j in range(2):
        go[j * m // 2:(j + 1) * m // 2, :128] = s[at:at + m // 2, j * 128:(j + 1) * 128]
    for j in range(4):
        go[j * m // 4:(j + 1) * m // 4, 128:] = s[at + m // 2:at + m * 3 // 4, j * 64:(j + 1) * 64]
    gr[...] = s[at + m * 3 // 4:, :128].T[:gr.shape[0], :gr.shape[1]]


def finish(kernel, mine, gots, shapes):
    ins = [mine] + gots
    vmem = pl.BlockSpec(memory_space=pltpu.VMEM)
    return pl.pallas_call(
        functools.partial(kernel, len(ins)), in_specs=[vmem] * len(ins), out_specs=[vmem] * len(shapes),
        out_shape=[sds(s) for s in shapes], scratch_shapes=[pltpu.VMEM(mine.shape, F32)],
    )(*ins)


def weights_part_kernel(cols, sets, lead, *refs):
    out = refs[-1]
    step = cols + 1
    total = None
    for s in range(sets):
        both, other = refs[s * step:s * step + cols], refs[s * step + cols][0]
        width = both[0].shape[2] // 2
        rows = jnp.concatenate([b[0, :, :width] if lead else b[0, :, width:] for b in both], axis=0)
        v = mm(rows, other, TN) if lead else mm(other, rows, TN)
        total = v if total is None else total + v
    out[0] = total


def expert_weights_part(sets, lead, d, f):
    cols = len(sets[0]) - 1
    experts, n, _ = sets[0][0].shape
    if len(sets) > 1 and len(sets) * cols > 8:
        return sum(expert_weights_part([s], lead, d, f) for s in sets)
    shape = (experts, d, f) if lead else (experts, f, d)
    return per_expert(functools.partial(weights_part_kernel, cols, len(sets), lead), [v for s in sets for v in s],
                      [sds(shape)], 2 * experts * cols * n * d * f * len(sets))[0]


def params_generic(w_in_x, w_in_z, conv_w, conv_b, w_xproj, w_dt, dt_bias, a_log, d_skip, w_out, gain_mix, gain_moe, w_router):
    rows, cols = lax.axis_size("row"), lax.axis_size("col")
    parts = rows * cols
    inner, width = w_in_x.shape[1] * cols, w_in_x.shape[0] * rows
    small = jnp.concatenate([conv_w, conv_b[None], dt_bias[None], a_log, d_skip[None],
                             jnp.concatenate([gain_mix, gain_moe])[None]], axis=0)
    flat = [w_xproj.reshape(-1), w_dt.reshape(-1), w_router.reshape(-1), small.reshape(-1)]
    sizes = [f.shape[0] for f in flat]
    lanes = w_in_x.shape[1]
    extra = -(-sum(sizes) // (16 * lanes)) * 16
    flat = jnp.pad(jnp.concatenate(flat), (0, extra * lanes - sum(sizes))).reshape(extra, lanes)
    here, out_rows, out_lanes = w_in_x.shape[0], w_out.shape[0], w_out.shape[1]
    wide = -(-out_lanes // 128) * 128
    first = gather_list(jnp.concatenate([w_in_x, flat], axis=0))
    full_x, rest = assemble(first, [((0, here, lanes), 0, put_block), ((here, extra, lanes), 1, put_pair)],
                            [(width, inner), (rows, cols, extra, lanes)])
    far_end = first[len(first) // 2 - 1][1]
    late_z, late_o, _ = lax.optimization_barrier((w_in_z, jnp.pad(w_out, ((0, 0), (0, wide - out_lanes))), far_end))
    (full_z,) = assemble(gather_list(late_z), [((0, here, lanes), 0, put_block)], [(width, inner)])
    (wide_out,) = assemble(gather_list(late_o), [((0, out_rows, wide), 0, put_block)], [(inner, cols * wide)])
    lane_of = jnp.arange(cols * wide, dtype=jnp.int32)
    narrow = jnp.where(lane_of % wide < out_lanes, lane_of // wide * out_lanes + lane_of % wide, -1)
    narrow = (narrow[:, None] == jnp.arange(width, dtype=jnp.int32)[None, :]).astype(BF)
    full_out = mm(wide_out, narrow).astype(BF)
    def whole(blocks):
        return blocks.transpose(0, 2, 1, 3).reshape(blocks.shape[0] * blocks.shape[2], -1)
    rest = rest.reshape(rows, cols, extra * lanes)
    cut = [0]
    for n in sizes:
        cut.append(cut[-1] + n)
    full_xpT = whole(rest[:, :, cut[0]:cut[1]].reshape((rows, cols) + w_xproj.shape)).T
    full_dt = whole(rest[:, :, cut[1]:cut[2]].reshape((rows, cols) + w_dt.shape))
    router_f = whole(rest[:, :, cut[2]:cut[3]].reshape((rows, cols) + w_router.shape)).astype(F32).T
    small = rest[:, :, cut[3]:cut[4]].reshape((parts,) + small.shape).transpose(1, 0, 2).astype(F32)
    chan = small[:-1].reshape(-1, inner)
    taps = conv_w.shape[0]
    par = jnp.concatenate([chan[:taps + 2], chan[taps + 2 + NS:]], axis=0)
    a_neg = -jnp.exp(chan[taps + 2:taps + 2 + NS])
    a_two = a_neg * log2e
    gain_mix_f = small[-1, :, :gain_mix.shape[0]].reshape(1, width)
    gain_moe_f = small[-1, :, gain_mix.shape[0]:].reshape(1, width)
    return lambda done: (full_z, full_out, router_f, done), full_x, full_xpT, full_dt, par, a_neg, a_two, gain_mix_f, gain_moe_f


def params_tiled(w_in_x, w_in_z, conv_w, conv_b, w_xproj, w_dt, dt_bias, a_log, d_skip, w_out, gain_mix, gain_moe, w_router):
    rows, cols = lax.axis_size("row"), lax.axis_size("col")
    here, lanes = w_in_x.shape
    inner, width = lanes * cols, here * rows
    taps, share = conv_w.shape
    packed, other = pack_params(w_in_x, w_dt, w_xproj, conv_w, conv_b, dt_bias, a_log, d_skip, gain_mix, gain_moe, w_in_z,
                                w_out, w_router)
    mine = gather_far(packed)
    other, _ = lax.optimization_barrier((other, mine))
    mine_o = gather_far(other)
    near = gather_plane(mine)
    mine_o, _ = lax.optimization_barrier((mine_o, near[-1]))
    near_o = gather_plane(mine_o)
    first = gather_core(near)
    dims = (w_dt.shape[0], w_xproj.shape[1], w_xproj.shape[0], share, gain_mix.shape[0], taps, rows, cols)
    full_x, full_dt, full_xpT, par, a_neg, a_two, gx, gm = unpack_call(
        unpack_first, first, dims,
        [sds((width, inner), BF), sds((w_dt.shape[0] * rows, inner), BF), sds((w_xproj.shape[1] * cols, inner), BF),
         sds((taps + 3, inner)), sds((NS, inner)), sds((NS, inner)), sds((1, width)), sds((1, width))],
        [(32 * rows, inner), (32 * cols, (lanes - 128) * rows), (32, 128 * rows * cols)])

    def rest(done):
        o, done = lax.optimization_barrier((near_o, done))
        full_z, full_out, router_f = unpack_call(
            unpack_other, gather_core(o), (here, w_out.shape[0], w_out.shape[1], w_router.shape[1], cols),
            [sds((width, inner), BF), sds((inner, width), BF), sds((w_router.shape[1] * cols, width))],
            [(inner, 256 * cols), (16 * cols, 128 * rows)])
        return full_z, full_out, router_f, done
    return rest, full_x, full_xpT, full_dt, par, a_neg, a_two, gx, gm


def grads_generic(nms, gateds, gs, total, w_in_x, w_in_z, w_xproj, w_dt, w_out, w_router, gain_mix, conv_w):
    rows, cols = lax.axis_size("row"), lax.axis_size("col")
    parts = rows * cols
    my_col = lax.axis_index("col")
    here, lanes = w_in_x.shape
    out_rows, out_lanes = w_out.shape
    wide = up_to(out_lanes, 128)
    share = conv_w.shape[1]
    sizes = [w_xproj.size, w_dt.size, w_router.size, (conv_w.shape[0] + 4 + NS) * share]
    extra = up_to(-(-sum(sizes) // lanes), 16)
    cut = [sum(sizes[:i]) for i in range(5)]
    grad_out = sum(mm(k[1], r["gm"], TN) for k, r in zip(zip(nms, gateds), gs)).astype(BF)
    grad_out_block = reduce_list([grad_out[:, k * wide:(k + 1) * wide].reshape(rows, out_rows, wide) for k in range(cols)])
    grad_out_block = grad_out_block[:, :out_lanes]
    grad_in_z = column_blocks([(k[0], r["gz"]) for k, r in zip(zip(nms, gateds), gs)], cols, my_col)
    grad_z_block = reduce_list([grad_in_z[k].reshape(rows, here, lanes) for k in range(cols)])
    grad_in_x = column_blocks([(k[0], r["gi"]) for k, r in zip(zip(nms, gateds), gs)], cols, my_col)

    def blocks(g, like):
        r, c = like.shape
        return g.astype(BF).reshape(rows, r, cols, c).transpose(0, 2, 1, 3).reshape(rows, cols, -1)
    gsmall = total["chan"].astype(BF)
    ggain = jnp.concatenate([total["gain_mix"].reshape(parts, 1, -1), total["gain_moe"].reshape(parts, 1, -1)], axis=2)
    gsmall = jnp.concatenate([gsmall.reshape(-1, parts, share).transpose(1, 0, 2), ggain.astype(BF)], axis=1)
    gflat = jnp.concatenate([blocks(total["xproj"].T, w_xproj), blocks(total["dt"], w_dt), blocks(total["router"].T, w_router),
                             gsmall.reshape(rows, cols, -1)], axis=2)
    gflat = jnp.pad(gflat, ((0, 0), (0, 0), (0, extra * lanes - sum(sizes)))).reshape(rows, cols, extra, lanes)
    done = reduce_list([jnp.concatenate([grad_in_x[k].reshape(rows, here, lanes),
                                         lax.dynamic_index_in_dim(gflat, my_col ^ k, 1, keepdims=False)], axis=1)
                        for k in range(cols)])
    grad_x_block = done[:here]
    done = done[here:].reshape(-1)
    sm = done[cut[3]:cut[4]].reshape(-1, share)
    gm = gain_mix.shape[0]
    taps = conv_w.shape[0]
    chan = (sm[:taps], sm[taps], sm[taps + 1], sm[taps + 2:taps + 2 + NS], sm[taps + 2 + NS])
    small = (done[cut[0]:cut[1]].reshape(w_xproj.shape), done[cut[1]:cut[2]].reshape(w_dt.shape), chan, sm[-1, :gm], sm[-1, gm:],
             done[cut[2]:cut[3]].reshape(w_router.shape))
    return (grad_x_block, grad_z_block, grad_out_block), small


def on_device(tokens, w_in_x, w_in_z, conv_w, conv_b, w_xproj, w_dt, dt_bias, a_log, d_skip, w_out,
              gain_mix, gain_moe, w_router, w_up, w_down, routes, lengths, cotangent):
    rows, cols = lax.axis_size("row"), lax.axis_size("col")
    parts = rows * cols
    my_col = lax.axis_index("col")
    seqs, length, width = tokens.shape
    experts_here = w_up.shape[0]
    experts_all = experts_here * rows
    inner = w_in_x.shape[1] * cols
    count = seqs * length
    xp = w_xproj.shape[1] * cols
    share = inner // parts

    tiled = tiles_fit(w_in_x, w_xproj, w_out, conv_w, w_dt, w_router)
    here, lanes = w_in_x.shape
    out_rows, out_lanes = w_out.shape
    wide = up_to(out_lanes, 128)
    taps = conv_w.shape[0]
    rest_of, full_x, full_xpT, full_dt, par, a_neg, a_two, gain_mix_f, gain_moe_f = (
        params_tiled if tiled else params_generic)(
            w_in_x, w_in_z, conv_w, conv_b, w_xproj, w_dt, dt_bias, a_log, d_skip, w_out, gain_mix, gain_moe, w_router)
    lane_of = jnp.arange(cols * wide, dtype=jnp.int32)
    shifted = jnp.where(lane_of % wide < out_lanes, (lane_of // wide ^ my_col) * out_lanes + lane_of % wide, -1)
    shifted = (jnp.arange(width, dtype=jnp.int32)[:, None] == shifted[None, :]).astype(BF)

    message = -(-experts_here * CAP // 8) * 8
    group = -(-rows * CAP // 16) * 16
    at = jnp.arange(experts_here * group, dtype=jnp.int32)
    there = at % group
    source = jnp.where(there < rows * CAP, there // CAP * message + at // group * CAP + there % CAP, -1)
    sort = (source[:, None] == jnp.arange(rows * message, dtype=jnp.int32)[None, :]).astype(BF)

    def mixer(x, limit):
        nm, inner_x, conv, u, dl, pT, ssm, starts = mixer_forward(x, gain_mix_f, full_x, full_xpT, full_dt, par, a_two, QB, limit)
        return dict(x=x, nm=nm, inner=inner_x, conv=conv, u=u, dl=dl, pT=pT, ssm=ssm.reshape(length, inner), starts=starts)

    def router(k, route, n_live, grad):
        n_live = n_live.reshape(1)
        slots = rows * message
        z, gated, hidden, place, outgoing, probs, gate = one_call(
            functools.partial(route_kernel, CAP, experts_here, message),
            [k["x"], k["nm"], k["ssm"], full_z, full_out, gain_moe_f, router_f, route, grad],
            [sds((length, inner)), sds((length, inner), BF), sds((length, width)), sds((length, slots), BF),
             sds((slots, 2 * width), BF), sds((length, experts_all)), sds((length, 1))],
            [n_live], 6 * length * inner * width)
        kept = dict(k, z=z, gated=gated, hidden=hidden, place=place, probs=probs, gate=gate, route=route, n_live=n_live, cot=grad)
        return outgoing, kept

    def home(rows_out):
        return lax.all_to_all(rows_out, "row", split_axis=0, concat_axis=0, tiled=True)

    def arrive(got):
        return mm(sort, got).astype(BF).reshape(experts_here, group, 2 * width)

    def gather_cols(own):
        bufs = [own]
        for bit in bits_of("col")[::-1]:
            bufs = bufs + [swap(v, "col", bit) for v in bufs]
        return bufs

    def from_experts(bufs):
        for bit in bits_of("col"):
            half = len(bufs) // 2
            bufs = [(a.astype(F32) + swap(b, "col", bit).astype(F32)).astype(BF) for a, b in zip(bufs[:half], bufs[half:])]
        return mm(sort, bufs[0].reshape(experts_here * group, 2 * width), ((0,), (0,))).astype(BF)

    def unroute(k, back):
        mixed_out, gh, gs, gz, gm, g_router, g_moe = one_call(
            unroute_kernel,
            [back, k["place"], k["hidden"], k["probs"], k["gate"], k["route"], k["cot"], gain_moe_f, router_f, full_out, shifted,
             k["z"], k["ssm"]],
            [sds((length, width), BF), sds((length, width)), sds((length, inner)), sds((length, inner), BF),
             sds((length, cols * wide), BF), sds((experts_all, width)), sds((1, width))],
            [k["n_live"]], 6 * length * inner * width)
        return dict(mixed_out=mixed_out, gh=gh, gs=gs.reshape(k["u"].shape), gz=gz, gm=gm, router=g_router, gain_moe=g_moe)

    def unscan(k, gs, limit):
        gi, g_xp, g_dt, g_chan = scan_backward(k["u"], k["dl"], gs, k["conv"], k["inner"], k["pT"], k["starts"], full_xpT, full_dt, par, a_neg, limit)
        return dict(gi=gi, xproj=g_xp, dt=g_dt, chan=g_chan)

    def unproject(k, g):
        grad_tokens, g_mix = one_call(
            token_kernel, [g["gi"], g["gz"], full_x, full_z, k["x"], g["gh"], gain_mix_f], [sds((length, width)), sds((1, width))], (),
            4 * length * inner * width, 24)
        return dict(tokens=grad_tokens, gain_mix=g_mix)

    after = lax.optimization_barrier
    ks, owns, last = [], [], None
    for s in range(seqs):
        x = tokens[s]
        if last is not None:
            x, last = after((x, last))
        k = mixer(x, 24 if s == 0 else 48)
        if s == 0:
            full_z, full_out, router_f, k["ssm"] = rest_of(k["ssm"])
        before, (last, k) = last, router(k, routes[s], lengths[s], cotangent[s])
        ks.append(k)
        if before is not None:
            got, last = after((home(before), last))
            owns.append(arrive(got))
    owns.append(arrive(home(last)))
    sets, sent = [], []
    for s in range(seqs):
        bufs = gather_cols(owns[s])
        if s == seqs - 2:
            bufs, owns[-1] = after((bufs, owns[-1]))
        outs, more = expert_both(bufs, w_up, w_down)
        sets.append((bufs, more))
        sent.append(from_experts(outs))
    backs = [home(v) for v in sent]
    grads_w = []
    for lead in (True, False):
        ins, sent[0], _ = after(([b + [v[1 if lead else 0]] for b, v in sets], sent[0], grads_w))
        grads_w.append(expert_weights_part(ins, lead, width, w_up.shape[2]))
    backs[0], (grad_w_up, grad_w_down) = after((backs[0], grads_w))
    gs_ = []
    for s in range(seqs):
        g = unroute(ks[s], backs[s])
        gs_.append(g)
        if s + 1 < seqs:
            g["gs"], sent[s + 1] = after((g["gs"], sent[s + 1]))
            g.update(unscan(ks[s], g["gs"], 52))
            g["gi"], backs[s + 1] = after((g["gi"], backs[s + 1]))
    g = gs_[-1]
    nms, gateds = [k["nm"] for k in ks], [k["gated"] for k in ks]
    if tiled:
        block = (here + here // 2 + out_rows * 3 // 4 + 16, 256)
        keep, give = grad_other_blocks([(v, q["gz"]) for v, q in zip(nms, gs_)], [(v, q["gm"]) for v, q in zip(gateds, gs_)],
                                       [q["router"] for q in gs_], block, rows, cols, w_router.shape[1], my_col)
        far, plane, core = stages()

        def first_tokens(v):
            return unproject(ks[0], dict(gs_[0], gi=after((gs_[0]["gi"], v))[0]))
        got, first = between(first_tokens, give, exchange(give, core))
        if seqs > 1:
            gs_[0].update(first)
        own, gives = split_near(keep, got)
        g["gs"], gives = after((g["gs"], gives))
        gots = [exchange(v, p) for v, p in zip(gives, plane[1:])]
        g.update(unscan(ks[-1], g["gs"], 24))
        gots, g["gi"] = after((gots, g["gi"]))
        mine, gives = split_far(own, gots)
        g["gi"], gives = after((g["gi"], gives))
        gots_o = [exchange(v, p) for v, p in zip(gives, far[1:])]
        mine_o = mine
        dims = (w_dt.shape[0], w_xproj.shape[1], w_xproj.shape[0], conv_w.shape[1], gain_mix.shape[0], rows, cols)
        for s in range(1, seqs):
            gs_[s].update(unproject(ks[s], gs_[s]))
        keep, give = grad_x_blocks([(v, q["gi"]) for v, q in zip(nms, gs_)], gs_, dims, my_col)
        own, gives = split_near(keep, exchange(give, core))
        gots = [exchange(v, p) for v, p in zip(gives, plane[1:])]
        gots_o, _ = after((gots_o, gives))
        gz, go, g_router = finish(finish_other_kernel, mine_o, gots_o, [w_in_z.shape, w_out.shape, w_router.shape])
        gots, gz, go, g_router = after((gots, gz, go, g_router))
        mine, gives = split_far(own, gots)
        gots = [exchange(v, p) for v, p in zip(gives, far[1:])]
        share, gshare = conv_w.shape[1], gain_mix.shape[0]
        gx, g_xproj, g_dt, gcw, gcb, gdb, gal, gds, g_mix, g_moe = finish(
            finish_x_kernel, mine, gots,
            [w_in_x.shape, w_xproj.shape, w_dt.shape, conv_w.shape, (1, share), (1, share), a_log.shape, (1, share), (1, gshare), (1, gshare)])
        blocks = (gx, gz, go)
        small = (g_xproj, g_dt, (gcw, gcb[0], gdb[0], gal, gds[0]), g_mix[0], g_moe[0], g_router)
    else:
        g.update(unscan(ks[-1], g["gs"], 24))
        for k, q in zip(ks, gs_):
            q.update(unproject(k, q))
        names = ("xproj", "dt", "chan", "gain_mix", "gain_moe", "router")
        total = {n: sum(q[n] for q in gs_) for n in names}
        blocks, small = grads_generic(nms, gateds, gs_, total, w_in_x, w_in_z, w_xproj, w_dt, w_out, w_router, gain_mix, conv_w)
    g_xproj, g_dt, (gcw, gcb, gdb, gal, gds), g_mix, g_moe, g_router = small
    return (
        jnp.stack([q["mixed_out"] for q in gs_]),
        jnp.stack([q["tokens"] for q in gs_]),
        blocks[0],
        blocks[1],
        gcw,
        gcb,
        g_xproj,
        g_dt,
        gdb,
        gal,
        gds,
        blocks[2],
        g_mix,
        g_moe,
        g_router,
        grad_w_up,
        grad_w_down,
    )


def solution(mesh):
    tok = P(("row", "col"), None, None)
    mat = P("row", "col")
    vec = P(("row", "col"))
    chan = P(None, ("row", "col"))
    up, down = P("row", None, "col"), P("row", "col", None)
    return jax.shard_map(
        on_device,
        mesh=mesh,
        in_specs=(tok, mat, mat, chan, vec, mat, mat, vec, chan, vec, mat, vec, vec, mat, up, down, tok, vec, tok),
        out_specs=(tok, tok, mat, mat, chan, vec, mat, mat, vec, chan, vec, mat, vec, vec, mat, up, down),
        check_vma=False,
    )
```

```python
import functools
import jax
import jax.numpy as jnp
from jax import lax
from jax.sharding import PartitionSpec as P
from jax.experimental import pallas as pl
from jax.experimental.pallas import tpu as pltpu
NS = 16
F32 = jnp.float32
SLOT_OF=[4*((i>>2)&1)+2*(1-((i>>1)&1))+(1-(i&1)) for i in range(8)]
def merge8(rows):
    idx=lax.broadcasted_iota(jnp.int32,(8,128),0)
    m4=idx<4; m2=(idx&2)!=0; m1=(idx&1)!=0
    p=[None]*8
    for i in range(8): p[SLOT_OF[i]]=rows[i]
    r=[jnp.where(m4,p[k],p[k+4])+pltpu.roll(jnp.where(m4,p[k+4],p[k]),4,0) for k in range(4)]
    def half(x,y,m,d):
        return jnp.where(m,x+pltpu.roll(x,d,0),y+pltpu.roll(y,8-d,0))
    v=[half(r[k],r[k+2],m2,2) for k in range(2)]
    return half(v[0],v[1],m1,1)
def mm(a, b, dims=((1,), (0,)), **kw):
    return lax.dot_general(a, b, (dims, ((), ())), preferred_element_type=F32, **kw)


NT = ((1,), (1,))
TN = ((0,), (0,))


def softplus(v):
    e = jnp.exp(-jnp.abs(v))
    tiny = e * (1.0 - e * (0.5 - e * (1.0 / 3.0 - e * 0.25)))
    return jnp.maximum(v, 0.0) + jnp.where(e < 0.01, tiny, jnp.log(1.0 + e))


def sigmoid_of_softplus(d):
    tiny = d * (1.0 - d * (0.5 - d * (1.0 / 6.0 - d * (1.0 / 24.0))))
    return jnp.where(d < 0.03, tiny, 1.0 - jnp.exp(-d))


def sigmoid(v):
    return 1.0 / (1.0 + jnp.exp(-v))


def spread(dst, src, T):
    for j in range(T):
        dst[j] = jnp.broadcast_to(src[:, j:j + 1], (NS, 128))


def fold(x):
    return x[0:8] + x[8:16]


def convolve(ext, w, b, T):
    taps = w.shape[0]
    out = b
    for k in range(taps):
        out = out + w[k:k + 1] * ext[9 - taps + k:9 - taps + k + T]
    return out


def mixer_kernel(T, Q, R, x_ref, gain_ref, wx_ref, xpT_ref, wdt_ref, par_ref, a2_ref,
                 nm_ref, in_ref, cv_ref, u_ref, dl_ref, pT_ref, y_ref, st_ref, state, bx, cx, du):
    c = pl.program_id(0)
    L, DI = nm_ref.shape[0], wx_ref.shape[1]
    taps = par_ref.shape[0] - 3

    @pl.when(c == 0)
    def _():
        state[...] = jnp.zeros_like(state)
        x = x_ref[...].astype(F32)
        nm = (x * lax.rsqrt(jnp.mean(x * x, axis=-1, keepdims=True) + 1e-05) * gain_ref[...]).astype(jnp.bfloat16)
        nm_ref[...] = nm
        in_ref[0:8] = jnp.zeros((8, DI), F32)
        in_ref[8:] = mm(nm, wx_ref[...])
    st_ref[0] = state[...]
    par = par_ref[...]
    skip = par[taps + 2:taps + 3]
    conv = convolve(in_ref[pl.ds(pl.multiple_of(c * T, 8), T + 8)], par[:taps], par[taps:taps + 1], T)
    cv_ref[0] = conv.reshape(T // 8, 8, DI)
    u = conv * sigmoid(conv)
    u_ref[0] = u.reshape(T // 8, 8, DI)
    pT = mm(xpT_ref[...], u.astype(jnp.bfloat16), NT)
    pT_ref[0] = pT
    d = softplus(mm(pT[:R].astype(jnp.bfloat16), wdt_ref[...], TN) + par[taps + 1:taps + 2])
    dl_ref[0] = d.reshape(T // 8, 8, DI)
    du[...] = (d * u).reshape(T // 8, 8, DI)
    spread(bx, pT[R:R + NS], T)
    spread(cx, pT[R + NS:R + 2 * NS], T)

    def grp(g, _):
        base = pl.multiple_of(g * (Q * 128), 128)
        lanes = [pl.ds(base + q * 128, 128) for q in range(Q)]
        a = [a2_ref[:, ln] for ln in lanes]
        sk = [par_ref[taps + 2:taps + 3, ln] for ln in lanes]

        def tb(i, s):
            s = list(s)
            rows = [[] for _ in range(Q)]
            for k in range(8):
                t = i * 8 + k
                b = bx[t]
                cc = cx[t]
                for q in range(Q):
                    dd = dl_ref[0, i, k:k + 1, lanes[q]]
                    dub = du[i, k:k + 1, lanes[q]]
                    s[q] = jnp.exp2(dd * a[q]) * s[q] + b * dub
                    rows[q].append(fold(s[q] * cc))
            for q in range(Q):
                y_ref[0, i, :, lanes[q]] = merge8(rows[q]) + sk[q] * u_ref[0, i, :, lanes[q]]
            return tuple(s)
        s = lax.fori_loop(0, T // 8, tb, tuple(state[:, ln] for ln in lanes))
        for q in range(Q):
            state[:, lanes[q]] = s[q]
        return 0
    lax.fori_loop(0, DI // (Q * 128), grp, 0)


def whole_spec(a):
    return pl.BlockSpec(a.shape, lambda *_: (0,) * len(a.shape))


def sds(shape, dtype=F32):
    return jax.ShapeDtypeStruct(shape, dtype)


def mixer_forward(x, gain, wx, xpT, wdt, par, a2, T, limit, Q=6):
    L, D = x.shape
    DI = wx.shape[1]
    C, XP, R = L // T, xpT.shape[0], wdt.shape[0]
    ins = [x, gain, wx, xpT, wdt, par, a2]
    rows = pl.BlockSpec((1, T // 8, 8, DI), lambda c: (c, 0, 0, 0))
    big = sds((C, T // 8, 8, DI))
    nm, inner = sds((L, D), jnp.bfloat16), sds((L + 8, DI))
    return pl.pallas_call(
        functools.partial(mixer_kernel, T, Q, R), grid=(C,),
        in_specs=[whole_spec(a) for a in ins],
        out_specs=[whole_spec(nm), whole_spec(inner), rows, rows, rows, pl.BlockSpec((1, XP, T), lambda c: (c, 0, 0)), rows,
                   pl.BlockSpec((1, NS, DI), lambda c: (c, 0, 0))],
        out_shape=[nm, inner, big, big, big, sds((C, XP, T)), big, sds((C, NS, DI))],
        scratch_shapes=[pltpu.VMEM((NS, DI), F32), pltpu.VMEM((T, NS, 128), F32), pltpu.VMEM((T, NS, 128), F32),
                        pltpu.VMEM((T // 8, 8, DI), F32)],
        compiler_params=pltpu.CompilerParams(vmem_limit_bytes=limit << 20),
        cost_estimate=pl.CostEstimate(flops=40000000000, bytes_accessed=16 * L * DI, transcendentals=0),
    )(*ins)


def scan_back_kernel(T, Q, Q2, R, u_ref, dl_ref, gs_ref, cv_ref, in_ref, pT_ref, st_ref, xpT_ref, wdt_ref, par_ref, an_ref,
                     gi_ref, gxp_ref, gwd_ref, gpar_ref, carry, later, bx, cx, du, guc, gdt, hs, ds, gbp, gcp, sums):
    j = pl.program_id(0)
    c = pl.num_programs(0) - 1 - j
    DI = wdt_ref.shape[1]
    taps = par_ref.shape[0] - 3

    @pl.when(j == 0)
    def _():
        for ref in (carry, later, gxp_ref, gwd_ref, gpar_ref, sums):
            ref[...] = jnp.zeros_like(ref)
    pT = pT_ref[0]
    spread(bx, pT[R:R + NS], T)
    spread(cx, pT[R + NS:R + 2 * NS], T)
    du[...] = dl_ref[0] * u_ref[0]
    gbp[...] = jnp.zeros_like(gbp)
    gcp[...] = jnp.zeros_like(gcp)
    W = Q * 128

    def grp(g, _):
        base = pl.multiple_of(g * W, 128)
        lanes = [pl.ds(base + q * 128, 128) for q in range(Q)]
        loc = [slice(q * 128, q * 128 + 128) for q in range(Q)]
        an = [an_ref[:, ln] for ln in lanes]
        a2 = [v * 1.4426950408889634 for v in an]

        def tb(i, s):
            s = list(s)
            for k in range(8):
                t = i * 8 + k
                b = bx[t]
                gc = gcp[t]
                for q in range(Q):
                    dd = dl_ref[0, i, k:k + 1, lanes[q]]
                    dub = du[i, k:k + 1, lanes[q]]
                    gsr = gs_ref[0, i, k:k + 1, lanes[q]]
                    dec = jnp.exp2(dd * a2[q])
                    h = dec * s[q]
                    ds[t, :, loc[q]] = dec
                    hs[t, :, loc[q]] = h
                    s[q] = h + b * dub
                    gc = gc + s[q] * gsr
                gcp[t] = gc
            return tuple(s)
        lax.fori_loop(0, T // 8, tb, tuple(st_ref[0, :, ln] for ln in lanes))
        for q0 in range(0, Q, Q2):
            qs = range(q0, q0 + Q2)
            sk = {q: par_ref[taps + 2:taps + 3, lanes[q]] for q in qs}

            def rb(jj, cr):
                i = T // 8 - 1 - jj
                g_, ga = {q: cr[0][q - q0] for q in qs}, {q: cr[1][q - q0] for q in qs}
                gbs, gsk = list(cr[2]), list(cr[3])
                m1, m2 = {q: [None] * 8 for q in qs}, {q: [None] * 8 for q in qs}
                for k in range(7, -1, -1):
                    t = i * 8 + k
                    b = bx[t]
                    cc = cx[t]
                    gb = gbp[t]
                    for q in qs:
                        dd = dl_ref[0, i, k:k + 1, lanes[q]]
                        dub = du[i, k:k + 1, lanes[q]]
                        gsr = gs_ref[0, i, k:k + 1, lanes[q]]
                        gg = gsr * cc + g_[q]
                        g_[q] = gg * ds[t, :, loc[q]]
                        qq = gg * hs[t, :, loc[q]]
                        m1[q][k] = fold(gg * b)
                        m2[q][k] = fold(qq * an[q])
                        ga[q] = ga[q] + qq * dd
                        gb = gb + gg * dub
                    gbp[t] = gb
                for q in qs:
                    s1 = merge8(m1[q])
                    s2 = merge8(m2[q])
                    u8, d8, gs8 = u_ref[0, i, :, lanes[q]], dl_ref[0, i, :, lanes[q]], gs_ref[0, i, :, lanes[q]]
                    guc[i, :, lanes[q]] = d8 * s1 + sk[q] * gs8
                    gd = (s2 + u8 * s1) * sigmoid_of_softplus(d8)
                    gdt[i, :, lanes[q]] = gd
                    gbs[q - q0] = gbs[q - q0] + gd
                    gsk[q - q0] = gsk[q - q0] + gs8 * u8
                return (tuple(g_[q] for q in qs), tuple(ga[q] for q in qs), tuple(gbs), tuple(gsk))
            z8 = tuple(jnp.zeros((8, 128), F32) for q in qs)
            cr = lax.fori_loop(0, T // 8, rb, (tuple(carry[:, lanes[q]] for q in qs),
                                               tuple(jnp.zeros((NS, 128), F32) for q in qs), z8, z8), unroll=2)
            for q in qs:
                carry[:, lanes[q]] = cr[0][q - q0]
                gpar_ref[taps + 2:taps + 2 + NS, lanes[q]] += cr[1][q - q0] * an[q]
                sums[taps + 1, :, lanes[q]] += cr[2][q - q0]
                sums[taps + 2, :, lanes[q]] += cr[3][q - q0]
        return 0
    lax.fori_loop(0, DI // W, grp, 0)

    gbT = jnp.sum(gbp[...], axis=2).T
    gcT = jnp.sum(gcp[...], axis=2).T
    gd = gdt[...].reshape(T, DI).astype(jnp.bfloat16)
    gpT = jnp.concatenate([mm(wdt_ref[...], gd, NT), gbT, gcT], axis=0).astype(jnp.bfloat16)
    gwd_ref[...] += mm(pT[:R].astype(jnp.bfloat16), gd)
    gxp_ref[...] += mm(gpT, u_ref[0].reshape(T, DI).astype(jnp.bfloat16))
    gu = guc[...].reshape(T, DI) + mm(gpT, xpT_ref[...], TN)
    par = par_ref[...]
    conv = cv_ref[0].reshape(T, DI)
    sig = sigmoid(conv)
    gconv = gu * (sig * (1.0 + conv * (1.0 - sig)))
    part = lambda v: jnp.sum(v.reshape(T // 8, 8, DI), axis=0)
    sums[taps] += part(gconv)
    inner_x = in_ref[pl.ds(pl.multiple_of(c * T + 8, 8), T)]
    both = jnp.concatenate([gconv, later[...]], axis=0)
    gi = None
    for k in range(taps):
        ahead = both[taps - 1 - k:taps - 1 - k + T]
        sums[k] += part(ahead * inner_x)
        gi = par[k:k + 1] * ahead if gi is None else gi + par[k:k + 1] * ahead
    gi_ref[...] = gi.astype(jnp.bfloat16)
    later[...] = gconv[:8]

    @pl.when(c == 0)
    def _():
        for k in range(taps + 2):
            gpar_ref[k:k + 1] = jnp.sum(sums[k], axis=0, keepdims=True)
        gpar_ref[taps + 2 + NS:taps + 3 + NS] = jnp.sum(sums[taps + 2], axis=0, keepdims=True)


def scan_backward(u, dl, gs, conv, inner, pT, st, xpT, wdt, par, an, limit, Q=3, Q2=3):
    C, T8, _, DI = u.shape
    T = T8 * 8
    XP, R = xpT.shape[0], wdt.shape[0]
    n = par.shape[0] + NS
    rev = lambda *shape: pl.BlockSpec((1,) + shape, lambda j: (C - 1 - j,) + (0,) * len(shape))
    rows = rev(T8, 8, DI)
    outs = [sds((C * T, DI), jnp.bfloat16), sds((XP, DI)), sds((R, DI)), sds((n, DI))]
    V = lambda *s: pltpu.VMEM(s, F32)
    return pl.pallas_call(
        functools.partial(scan_back_kernel, T, Q, Q2, R), grid=(C,),
        in_specs=[rows, rows, rows, rows, whole_spec(inner), rev(XP, T), rev(NS, DI)] + [whole_spec(a) for a in (xpT, wdt, par, an)],
        out_specs=[pl.BlockSpec((T, DI), lambda j: (C - 1 - j, 0))] + [whole_spec(o) for o in outs[1:]],
        out_shape=outs,
        scratch_shapes=[V(NS, DI), V(8, DI), V(T, NS, 128), V(T, NS, 128), V(T8, 8, DI), V(T8, 8, DI), V(T8, 8, DI),
                        V(T, NS, Q * 128), V(T, NS, Q * 128), V(T, NS, 128), V(T, NS, 128), V(par.shape[0], 8, DI)],
        compiler_params=pltpu.CompilerParams(vmem_limit_bytes=limit << 20),
        cost_estimate=pl.CostEstimate(flops=80000000000, bytes_accessed=16 * C * T * DI, transcendentals=0),
    )(u, dl, gs, conv, inner, pT, st, xpT, wdt, par, an)


def one_call(kernel, ins, outs, scalars=(), flops=0, limit=56):
    smem = pl.BlockSpec(memory_space=pltpu.SMEM)
    vmem = pl.BlockSpec(memory_space=pltpu.VMEM)
    size = sum(a.size * a.dtype.itemsize for a in list(ins) + list(outs))
    return pl.pallas_call(
        kernel,
        in_specs=[smem] * len(scalars) + [vmem] * len(ins), out_specs=[vmem] * len(outs), out_shape=list(outs),
        compiler_params=pltpu.CompilerParams(vmem_limit_bytes=limit << 20),
        cost_estimate=pl.CostEstimate(flops=flops, bytes_accessed=size, transcendentals=0),
    )(*scalars, *ins)


def route_kernel(cap, here, message, s, live_ref, x_ref, nm_ref, y_ref, wz_ref, wo_ref, gain_ref, wr_ref, route_ref, cot_ref,
                 z_ref, gated_ref, hid_ref, place_ref, out_ref, prob_ref, gate_ref):
    bf = jnp.bfloat16
    L = nm_ref.shape[0]
    E = wr_ref.shape[0]
    z = mm(nm_ref[...], wz_ref[...])
    z_ref[...] = z
    gated = (y_ref[...] * (z * sigmoid(z))).astype(bf)
    gated_ref[...] = gated
    hid = x_ref[...].astype(F32) + mm(gated, wo_ref[...])
    hid_ref[...] = hid
    nmoe = hid * lax.rsqrt(jnp.mean(hid * hid, axis=-1, keepdims=True) + 1e-05) * gain_ref[...]
    logits = mm(nmoe, wr_ref[...], NT, precision=lax.Precision.HIGHEST)
    e = jnp.exp(logits - jnp.max(logits, axis=-1, keepdims=True))
    probs = e / jnp.sum(e, axis=-1, keepdims=True)
    prob_ref[...] = probs
    route = route_ref[...]
    hot = route == lax.broadcasted_iota(jnp.int32, (L, E), 1)
    gate = jnp.sum(jnp.where(hot, probs, 0.0), axis=-1, keepdims=True)
    gate_ref[...] = gate
    live = lax.broadcasted_iota(jnp.int32, (L, 1), 0) < live_ref[0]
    hits = jnp.where(hot & live, 1.0, 0.0)
    before = lax.broadcasted_iota(jnp.int32, (L, L), 0) > lax.broadcasted_iota(jnp.int32, (L, L), 1)
    slot = jnp.sum(mm(jnp.where(before, 1.0, 0.0).astype(bf), hits.astype(bf)) * hits, axis=-1, keepdims=True).astype(jnp.int32)
    slots = place_ref.shape[1]
    target = route // here * message + route % here * cap + slot
    target = jnp.where(live & (slot < cap), target, slots)
    place = jnp.where(target == lax.broadcasted_iota(jnp.int32, (L, slots), 1), 1.0, 0.0).astype(bf)
    place_ref[...] = place
    D = hid.shape[1]
    gy = jnp.where(live, cot_ref[s], 0.0)
    out_ref[:, :D] = mm(place, nmoe.astype(bf), TN).astype(bf)
    out_ref[:, D:] = mm(place, (gy * gate).astype(bf), TN).astype(bf)


def unroute_kernel(s, live_ref, home_ref, place_ref, hid_ref, prob_ref, gate_ref, route_ref, cot_ref, gain_ref, wr_ref, wo_ref, sh_ref,
                   z_ref, y_ref, mix_ref, gh_ref, gs_ref, gz_ref, gm_ref, gr_ref, gg_ref):
    bf = jnp.bfloat16
    high = lax.Precision.HIGHEST
    hid, gain = hid_ref[...], gain_ref[...]
    L, D = hid.shape
    E = wr_ref.shape[0]
    tok = mm(place_ref[...], home_ref[...])
    etok, gsent = tok[:, :D], tok[:, D:]
    live = lax.broadcasted_iota(jnp.int32, (L, 1), 0) < live_ref[0]
    gate, probs = gate_ref[...], prob_ref[...]
    mix_ref[...] = jnp.where(live, hid + gate * etok, 0.0).astype(bf)
    gy = jnp.where(live, cot_ref[s], 0.0)
    ggate = jnp.sum(gy * etok, axis=-1, keepdims=True)
    hot = jnp.where(route_ref[...] == lax.broadcasted_iota(jnp.int32, (L, E), 1), 1.0, 0.0)
    glog = ggate * gate * (hot - probs)
    rms = lax.rsqrt(jnp.mean(hid * hid, axis=-1, keepdims=True) + 1e-05)
    hat = hid * rms
    gr_ref[...] = mm(glog, hat * gain, TN, precision=high)
    gnorm = gsent + mm(glog, wr_ref[...], precision=high)
    gg_ref[...] = jnp.sum(gnorm * hat, axis=0, keepdims=True)
    scaled = gnorm * gain
    gh = gy + rms * (scaled - hat * jnp.mean(scaled * hat, axis=-1, keepdims=True))
    gh_ref[...] = gh
    gmix = gh.astype(bf)
    gm_ref[...] = mm(gmix, sh_ref[...]).astype(bf)
    ggated = mm(gmix, wo_ref[...], NT)
    z = z_ref[...]
    sig = sigmoid(z)
    gs_ref[...] = ggated * (z * sig)
    gz_ref[...] = (ggated * y_ref[...] * (sig * (1.0 + z * (1.0 - sig)))).astype(bf)


def token_kernel(gi_ref, gz_ref, wx_ref, wz_ref, x_ref, gh_ref, gain_ref, gt_ref, gg_ref):
    gnm = mm(gi_ref[...], wx_ref[...], NT) + mm(gz_ref[...], wz_ref[...], NT)
    x = x_ref[...].astype(F32)
    rms = lax.rsqrt(jnp.mean(x * x, axis=-1, keepdims=True) + 1e-05)
    hat = x * rms
    gg_ref[...] = jnp.sum(gnm * hat, axis=0, keepdims=True)
    scaled = gnm * gain_ref[...]
    gt_ref[...] = gh_ref[...] + rms * (scaled - hat * jnp.mean(scaled * hat, axis=-1, keepdims=True))


QB = 64
CAP = 13
BF = jnp.bfloat16
root_half = 0.7071067811865476
inv_root_two_pi = 0.3989422804014327
log2e = 1.4426950408889634


def swap(x, axis, bit):
    n = lax.axis_size(axis)
    return lax.ppermute(x, axis, [(i, i ^ bit) for i in range(n)])


def bits_of(axis):
    n = lax.axis_size(axis)
    return [1 << k for k in range(n.bit_length() - 1)]


def exchange(x, mask):
    rm, cm = mask
    if rm == 0:
        return swap(x, "col", cm)
    if cm == 0:
        return swap(x, "row", rm)
    rows, cols = lax.axis_size("row"), lax.axis_size("col")
    pairs = [(r * cols + c, (r ^ rm) * cols + (c ^ cm)) for r in range(rows) for c in range(cols)]
    return lax.ppermute(x, ("row", "col"), pairs)


def combos(bits):
    out = [(0, 0)]
    for rb, cb in bits:
        out = out + [(r | rb, c | cb) for r, c in out]
    return out


def stages():
    row, col = bits_of("row"), bits_of("col")
    far = combos([(b, 0) for b in row[1:]])
    plane = combos([(row[0], 0)] + [(0, b) for b in col[1:]])
    return far, plane, (0, col[0])


def add(a, b):
    return (a[0] ^ b[0], a[1] ^ b[1])


def gather_far(x):
    return jnp.stack([x] + [exchange(x, m) for m in stages()[0][1:]])


def gather_plane(mine):
    return [mine] + [exchange(mine, m) for m in stages()[1][1:]]


def gather_core(near):
    far, plane, core = stages()
    near = [([add(f, m) for f in far], b) for m, b in zip(plane, near)]
    return near + [([add(m, core) for m in ms], exchange(b, core)) for ms, b in near]


def gather_list(x):
    return gather_core(gather_plane(gather_far(x)))


def assemble_kernel(masks, moves, count_in, *refs):
    r0, c0 = refs[0][0], refs[0][1]
    ins, outs = refs[1:1 + count_in], refs[1 + count_in:]
    for buf, ms in zip(ins, masks):
        for i, (rm, cm) in enumerate(ms):
            for (row, count, lanes), out, place in moves:
                place(outs[out], r0 ^ rm, c0 ^ cm, buf[i, row:row + count, :lanes])


def put_block(out, r, c, block):
    n, m = block.shape
    out[pl.ds(pl.multiple_of(r * n, n), n), pl.ds(pl.multiple_of(c * m, m), m)] = block


def put_pair(out, r, c, block):
    out[r, c] = block


def take_blocks(gathered):
    rows, cols = lax.axis_size("row"), lax.axis_size("col")
    order = [r * cols + c for ms, _ in gathered for r, c in ms]
    entry = jnp.asarray([order.index(i) for i in range(rows * cols)], jnp.int32)
    me = lax.axis_index("row") * cols + lax.axis_index("col")
    stacked = jnp.concatenate([b for _, b in gathered], axis=0)
    out = jnp.take(stacked, entry[jnp.arange(rows * cols, dtype=jnp.int32) ^ me], axis=0)
    return out.reshape((rows, cols) + stacked.shape[1:])


def assemble(gathered, moves, shapes):
    masks = [ms for ms, _ in gathered]
    bufs = [b for _, b in gathered]
    if any(lanes % 128 for (_, _, lanes), _, _ in moves):
        every = take_blocks(gathered)
        cut = [every[:, :, row:row + count, :lanes] for (row, count, lanes), _, _ in moves]
        return [v if place is put_pair else v.transpose(0, 2, 1, 3).reshape(shape)
                for v, shape, (_, _, place) in zip(cut, shapes, moves)]
    me = jnp.stack([lax.axis_index("row"), lax.axis_index("col")]).astype(jnp.int32)
    vmem = pl.BlockSpec(memory_space=pltpu.VMEM)
    return pl.pallas_call(
        functools.partial(assemble_kernel, masks, moves, len(bufs)),
        in_specs=[pl.BlockSpec(memory_space=pltpu.SMEM)] + [vmem] * len(bufs),
        out_specs=[vmem] * len(shapes),
        out_shape=[jax.ShapeDtypeStruct(s, BF) for s in shapes],
        compiler_params=pltpu.CompilerParams(vmem_limit_bytes=32 << 20),
        cost_estimate=pl.CostEstimate(flops=0, bytes_accessed=4 * sum(b.size for b in bufs), transcendentals=0),
    )(me, *bufs)


def between(work, give, got):
    result = work(give)
    return lax.optimization_barrier((got, result))


def reduce_core(parts, work=None):
    far, plane, core = stages()
    near = [k for k in range(lax.axis_size("col")) if not k & core[1]]
    give = jnp.stack([parts[k | core[1]] for k in near])
    got = exchange(give, core)
    result = None
    if work:
        got, result = between(work, give, got)
    return [parts[k].astype(F32) + got[i].astype(F32) for i, k in enumerate(near)], result


def reduce_plane_give(sums):
    far, plane, core = stages()
    near = [k for k in range(lax.axis_size("col")) if not k & core[1]]
    rows, r0 = lax.axis_size("row"), lax.axis_index("row")

    def rows_of(k, rm):
        v = sums[near.index(k)]
        return lax.dynamic_index_in_dim(v.reshape((rows // 2, 2) + v.shape[1:]), (r0 ^ rm) & 1, 1, keepdims=False)
    return rows_of(0, 0), [rows_of(cm, rm).astype(BF) for rm, cm in plane[1:]]


def reduce_plane(own, give, work=None):
    got = [exchange(g, m) for g, m in zip(give, stages()[1][1:])]
    result = None
    if work:
        got, result = between(work, give, got)
    return functools.reduce(lambda t, v: t + v.astype(F32), got, own), result


def reduce_far(total, work=None):
    far = stages()[0]
    r0 = lax.axis_index("row")
    give = [lax.dynamic_index_in_dim(total, (r0 ^ rm) >> 1, 0, keepdims=False).astype(BF) for rm, _ in far[1:]]
    got = [exchange(g, m) for g, m in zip(give, far[1:])]
    result = None
    if work:
        got, result = between(work, give, got)
    done = lax.dynamic_index_in_dim(total, r0 >> 1, 0, keepdims=False)
    return functools.reduce(lambda t, v: t + v.astype(F32), got, done), result


def reduce_list(parts):
    own, give = reduce_plane_give(reduce_core(parts)[0])
    return reduce_far(reduce_plane(own, give)[0])[0]


def column_kernel(count, s_ref, *refs):
    total = mm(refs[0][...], refs[1][...], ((0,), (0,)))
    for k in range(1, count):
        total = total + mm(refs[2 * k][...], refs[2 * k + 1][...], ((0,), (0,)))
    refs[-1][0] = total.astype(BF)


def column_blocks(pairs, cols, my_col):
    n, m = pairs[0][0].shape
    w = pairs[0][1].shape[1] // cols
    count = len(pairs)
    if w % 128:
        total = sum(mm(a, b, ((0,), (0,))) for a, b in pairs).astype(BF).reshape(m, cols, w).transpose(1, 0, 2)
        return jnp.take(total, jnp.arange(cols, dtype=jnp.int32) ^ my_col, axis=0)
    return pl.pallas_call(
        functools.partial(column_kernel, count),
        grid_spec=pltpu.PrefetchScalarGridSpec(
            num_scalar_prefetch=1, grid=(cols,),
            in_specs=[pl.BlockSpec((n, m), lambda k, s: (0, 0)), pl.BlockSpec((n, w), lambda k, s: (0, s[0] ^ k))] * count,
            out_specs=pl.BlockSpec((1, m, w), lambda k, s: (k, 0, 0))),
        out_shape=jax.ShapeDtypeStruct((cols, m, w), BF),
        compiler_params=pltpu.CompilerParams(vmem_limit_bytes=32 << 20),
        cost_estimate=pl.CostEstimate(flops=2 * count * n * m * w * cols, bytes_accessed=2 * (count * (n * m + n * w * cols) + m * w * cols), transcendentals=0),
    )(my_col.reshape(1), *[v for p in pairs for v in p])


def gelu_parts(v):
    phi = 0.5 * (1.0 + lax.erf(v * root_half))
    return v * phi, phi + v * jnp.exp(-0.5 * v * v) * inv_root_two_pi


def expert_kernel(cols, *refs):
    both, up, down = refs[:cols], refs[cols], refs[cols + 1]
    outs, acts, gps = refs[cols + 2:2 * cols + 2], refs[2 * cols + 2], refs[2 * cols + 3]
    width = up.shape[1]
    n = both[0].shape[1]
    rows = jnp.concatenate([b[0] for b in both], axis=0)
    act, slope = gelu_parts(mm(rows[:, :width], up[0]))
    act = act.astype(BF)
    acts[0] = act
    gp = (mm(rows[:, width:], down[0], ((1,), (1,))) * slope).astype(BF)
    gps[0] = gp
    out = mm(act, down[0]).astype(BF)
    gin = mm(gp, up[0], ((1,), (1,))).astype(BF)
    for c in range(cols):
        outs[c][0, :, :width] = out[c * n:(c + 1) * n]
        outs[c][0, :, width:] = gin[c * n:(c + 1) * n]


def weights_kernel(cols, sets, *refs):
    up, down = refs[-2:]
    step = cols + 2
    gu = gd = None
    width = up.shape[1]
    for s in range(sets):
        both, act, gp = refs[s * step:s * step + cols], refs[s * step + cols][0], refs[s * step + cols + 1][0]
        rows = jnp.concatenate([b[0] for b in both], axis=0)
        a = mm(rows[:, :width], gp, ((0,), (0,)))
        b = mm(act, rows[:, width:], ((0,), (0,)))
        gu, gd = (a, b) if gu is None else (gu + a, gd + b)
    up[0] = gu
    down[0] = gd


def per_expert(kernel, ins, shapes, flops):
    tok = lambda a: pl.BlockSpec((1,) + a.shape[1:], lambda e: (e, 0, 0))
    size = sum(a.size * 2 for a in ins) + sum(s.size * s.dtype.itemsize for s in shapes)
    return list(pl.pallas_call(
        kernel, grid=(ins[0].shape[0],),
        in_specs=[tok(a) for a in ins], out_specs=[tok(s) for s in shapes], out_shape=shapes,
        compiler_params=pltpu.CompilerParams(vmem_limit_bytes=(44 if len(ins) <= 12 else 56) << 20),
        cost_estimate=pl.CostEstimate(flops=flops, bytes_accessed=size, transcendentals=0),
    )(*ins))


def expert_both(bufs, up, down):
    cols = len(bufs)
    experts, d, f = up.shape
    n = bufs[0].shape[1]
    shapes = ([jax.ShapeDtypeStruct((experts, n, 2 * d), BF)] * cols
              + [jax.ShapeDtypeStruct((experts, n * cols, f), BF)] * 2)
    outs = per_expert(functools.partial(expert_kernel, cols), bufs + [up, down], shapes, 8 * experts * cols * n * d * f)
    return outs[:cols], outs[cols:]


def expert_weights(sets, d, f):
    cols = len(sets[0]) - 2
    experts, n, _ = sets[0][0].shape
    if len(sets) > 1 and len(sets) * cols > 8:
        return [sum(v) for v in zip(*[expert_weights([s], d, f) for s in sets])]
    shapes = [jax.ShapeDtypeStruct((experts, d, f), F32), jax.ShapeDtypeStruct((experts, f, d), F32)]
    return per_expert(functools.partial(weights_kernel, cols, len(sets)), [v for s in sets for v in s], shapes,
                      4 * experts * cols * n * d * f * len(sets))


def up_to(n, m):
    return -(-n // m) * m


def tiles_fit(w_in_x, w_xproj, w_out, conv_w, w_dt, w_router):
    return (w_in_x.shape == (96, 384) and w_xproj.shape[0] == 192 and w_xproj.shape[1] <= 26 and w_dt.shape[0] <= 6
            and conv_w.shape[0] + NS + 5 <= 26 and conv_w.shape[1] <= 128 and w_out.shape == (192, 192)
            and w_router.shape[0] <= 128 and w_router.shape[1] <= 16)


def one_hot(shape, match):
    i = lax.broadcasted_iota(jnp.int32, shape, 0)
    j = lax.broadcasted_iota(jnp.int32, shape, 1)
    return jnp.where(match(i, j), 1.0, 0.0).astype(BF)


def pack_kernel(wx, wdt, xp, cw, cb, db, al, ds, gx, gm, wz, wo, wr, first, other, s_ex, s_r):
    n = wx.shape[0]
    s_ex[...] = jnp.zeros_like(s_ex)
    s_r[...] = jnp.zeros_like(s_r)
    first[:n] = wx[...]
    s_ex[:xp.shape[0], :xp.shape[1]] = xp[...].astype(F32)
    wide = s_ex.shape[1] - 128
    at = 0
    for v in (cw, cb, db, al, ds, gx, gm):
        s_ex[at:at + v.shape[0], wide:wide + v.shape[1]] = v[...].astype(F32)
        at += v.shape[0]
    s_ex[26:26 + wdt.shape[0]] = wdt[...].astype(F32)
    first[n:] = s_ex[...].astype(BF)
    s_r[:wr.shape[0], :wr.shape[1]] = wr[...].astype(F32)

    def put(at, lane, v):
        other[at:at + v.shape[0], lane:lane + v.shape[1]] = v
    put_other(put, wz[...], wo[...])
    other[other.shape[0] - 16:] = s_r[...].astype(BF)


def put_other(put, z, out):
    n, m = z.shape[-2], out.shape[-2]
    put(0, 0, z[..., :256])
    put(n, 0, z[..., :n // 2, 256:])
    put(n, 128, z[..., n // 2:, 256:])
    at = n + n // 2
    put(at, 0, out[..., :m // 2, :128])
    put(at, 128, out[..., m // 2:, :128])
    put(at + m // 2, 0, jnp.concatenate([out[..., j * m // 4:(j + 1) * m // 4, 128:192] for j in range(4)], axis=-1))


def pack_params(w_in_x, w_dt, w_xproj, conv_w, conv_b, dt_bias, a_log, d_skip, gain_mix, gain_moe, w_in_z, w_out, w_router):
    n, lanes = w_in_x.shape
    ins = [w_in_x, w_dt, w_xproj.T, conv_w, conv_b[None], dt_bias[None], a_log, d_skip[None], gain_mix[None], gain_moe[None],
           w_in_z, w_out, w_router.T]
    vmem = pl.BlockSpec(memory_space=pltpu.VMEM)
    V = lambda *s: pltpu.VMEM(s, F32)
    return pl.pallas_call(
        pack_kernel, in_specs=[vmem] * len(ins), out_specs=[vmem] * 2,
        out_shape=[sds((n + 32, lanes), BF), sds((n + n // 2 + w_out.shape[0] * 3 // 4 + 16, 256), BF)],
        scratch_shapes=[V(32, lanes), V(16, 256)],
    )(*ins)


def each_block(masks, bufs, r0, c0):
    for buf, ms in zip(bufs, masks):
        for i, (rm, cm) in enumerate(ms):
            yield buf, i, r0 ^ rm, c0 ^ cm


def span(i, n):
    return pl.ds(pl.multiple_of(i * n, n), n)


def dt_match(j, i, dt_rows):
    k = j % 32 - 26
    return (k >= 0) & (k < dt_rows) & (j // 32 * dt_rows + k == i)


def unpack_first(masks, dims, me, *refs):
    dt_rows, xp_cols, xp_rows, share, gshare, taps, rows, cols = dims
    count = len(masks)
    bufs = refs[:count]
    fx, dt, xpT, par, an, a2, gx, gm, w_dt, w_xp, w_sm = refs[count:]
    n = bufs[0].shape[1] - 32
    lanes = bufs[0].shape[2]
    wide = lanes - 128
    for buf, i, r, c in each_block(masks, bufs, me[0], me[1]):
        fx[span(r, n), span(c, lanes)] = buf[i, :n]
        w_dt[span(r, 32), span(c, lanes)] = buf[i, n:]
        w_xp[span(c, 32), span(r, wide)] = buf[i, n:, :wide]
        w_sm[:, span(r * cols + c, 128)] = buf[i, n:, wide:]
    pick = one_hot((dt.shape[0], 32 * rows), lambda i, j: dt_match(j, i, dt_rows))
    dt[...] = mm(pick, w_dt[...]).astype(BF)
    pick = one_hot((xpT.shape[0], 32 * cols), lambda i, j: (j % 32 < xp_cols) & (j // 32 * xp_cols + j % 32 == i))
    t = mm(pick, w_xp[...])
    xpT[...] = jnp.concatenate([t[:, r * wide:r * wide + xp_rows] for r in range(rows)], axis=1).astype(BF)
    sm = w_sm[...].astype(F32)
    chan = jnp.concatenate([sm[:, p * 128:p * 128 + share] for p in range(rows * cols)], axis=1)
    par[:taps + 2] = chan[:taps + 2]
    par[taps + 2:] = chan[taps + 2 + NS:taps + 3 + NS]
    neg = -jnp.exp(chan[taps + 2:taps + 2 + NS])
    an[...] = neg
    a2[...] = neg * log2e
    gains = jnp.concatenate([sm[taps + 3 + NS:taps + 5 + NS, p * 128:p * 128 + gshare] for p in range(rows * cols)], axis=1)
    gx[...] = gains[:1]
    gm[...] = gains[1:]


def unpack_other(masks, dims, me, *refs):
    n, out_rows, out_lanes, r_cols, cols = dims
    count = len(masks)
    bufs = refs[:count]
    fz, fo, router, w_out, w_r = refs[count:]
    half = n // 2
    at = n + half
    m = out_rows
    for buf, i, r, c in each_block(masks, bufs, me[0], me[1]):
        fz[span(r, n), pl.ds(pl.multiple_of(c * 384, 128), 256)] = buf[i, :n]
        for j in range(2):
            rows = pl.ds(pl.multiple_of(r * n + j * half, 16), half)
            fz[rows, pl.ds(pl.multiple_of(c * 384 + 256, 128), 128)] = buf[i, n:at, j * 128:(j + 1) * 128]
            rows = pl.ds(pl.multiple_of(r * m + j * (m // 2), 16), m // 2)
            w_out[rows, span(2 * c, 128)] = buf[i, at:at + m // 2, j * 128:(j + 1) * 128]
        for j in range(4):
            rows = pl.ds(pl.multiple_of(r * m + j * (m // 4), 16), m // 4)
            w_out[rows, pl.ds(pl.multiple_of(c * 256 + 128, 128), 64)] = buf[i, at + m // 2:at + m * 3 // 4, j * 64:(j + 1) * 64]
        w_r[span(c, 16), span(r, 128)] = buf[i, at + m * 3 // 4:, :128]
    wide = w_out[...]
    fo[...] = jnp.concatenate([wide[:, c * 256:c * 256 + out_lanes] for c in range(cols)], axis=1)
    pick = one_hot((router.shape[0], 16 * cols), lambda i, j: (j % 16 < r_cols) & (j // 16 * r_cols + j % 16 == i))
    t = mm(pick, w_r[...])
    r_rows = router.shape[1] // (t.shape[1] // 128)
    router[...] = jnp.concatenate([t[:, r * 128:r * 128 + r_rows] for r in range(t.shape[1] // 128)], axis=1)


def unpack_call(kernel, gathered, dims, outs, scratch):
    masks = [ms for ms, _ in gathered]
    bufs = [b for _, b in gathered]
    me = jnp.stack([lax.axis_index("row"), lax.axis_index("col")]).astype(jnp.int32)
    vmem = pl.BlockSpec(memory_space=pltpu.VMEM)
    return pl.pallas_call(
        functools.partial(kernel, masks, dims),
        in_specs=[pl.BlockSpec(memory_space=pltpu.SMEM)] + [vmem] * len(bufs), out_specs=[vmem] * len(outs), out_shape=outs,
        scratch_shapes=[pltpu.VMEM(s, BF) for s in scratch],
        compiler_params=pltpu.CompilerParams(vmem_limit_bytes=28 << 20),
        cost_estimate=pl.CostEstimate(flops=0, bytes_accessed=4 * sum(b.size for b in bufs), transcendentals=0),
    )(me, *bufs)


def grad_x_kernel(count, dims, s_ref, *refs):
    dt_rows, xp_cols, xp_rows, share, gshare, rows, cols = dims
    pairs = refs[:2 * count]
    gwd, gxp, gpar, gmix, gmoe = (refs[(2 + i) * count:(3 + i) * count] for i in range(5))
    keep, give, w_dt, w_xp, w_sm, full = refs[7 * count:]
    k = pl.program_id(0)
    n, lanes = keep.shape[2] - 32, keep.shape[3]
    wide = lanes - 128
    total = lambda vs: functools.reduce(lambda a, b: a + b, [v[...] for v in vs])

    @pl.when(k == 0)
    def _():
        g = total(gwd).astype(BF)
        full[...] = sum_products(pairs)
        put = one_hot((32 * rows, g.shape[0]), lambda j, i: dt_match(j, i, dt_rows))
        w_dt[...] = mm(put, g).astype(BF)
        g = total(gxp).astype(BF)
        put = one_hot((32 * cols, g.shape[0]), lambda j, i: (j % 32 < xp_cols) & (j // 32 * xp_cols + j % 32 == i))
        t = mm(put, g)
        gap = jnp.zeros((t.shape[0], wide - xp_rows), F32)
        w_xp[...] = jnp.concatenate([v for r in range(rows) for v in (t[:, r * xp_rows:(r + 1) * xp_rows], gap)], axis=1).astype(BF)
        w_sm[...] = jnp.zeros_like(w_sm)
        par, mix, moe = total(gpar), total(gmix), total(gmoe)
        m = par.shape[0]
        for p in range(rows * cols):
            w_sm[:m, p * 128:p * 128 + share] = par[:, p * share:(p + 1) * share]
            w_sm[m:m + 1, p * 128:p * 128 + gshare] = mix[:, p * gshare:(p + 1) * gshare]
            w_sm[m + 1:m + 2, p * 128:p * 128 + gshare] = moe[:, p * gshare:(p + 1) * gshare]
    for j, out in enumerate((keep, give)):
        c = s_ref[0] ^ (2 * k + j)
        out[0, :, :n] = full[:, span(c, lanes)].astype(BF).reshape(rows, n, lanes)
        for r in range(rows):
            d = w_dt[r * 32:(r + 1) * 32, span(c, lanes)]
            out[0, r, n:, :wide] = w_xp[span(c, 32), r * wide:(r + 1) * wide] + d[:, :wide]
            out[0, r, n:, wide:] = (w_sm[:, span(r * cols + c, 128)] + d[:, wide:].astype(F32)).astype(BF)


def sum_products(pairs):
    return functools.reduce(lambda a, b: a + b, [mm(pairs[i][...], pairs[i + 1][...], TN) for i in range(0, len(pairs), 2)])


def grad_blocks(kernel, ins, scratch, block, rows, cols, my_col, flops, limit):
    out = sds((cols // 2, rows) + block, BF)
    return list(pl.pallas_call(
        kernel,
        grid_spec=pltpu.PrefetchScalarGridSpec(
            num_scalar_prefetch=1, grid=(cols // 2,), in_specs=[whole_spec(v) for v in ins],
            out_specs=[pl.BlockSpec((1, rows) + block, lambda k, s: (k, 0, 0, 0))] * 2, scratch_shapes=scratch),
        out_shape=[out, out],
        compiler_params=pltpu.CompilerParams(vmem_limit_bytes=limit << 20),
        cost_estimate=pl.CostEstimate(flops=flops, bytes_accessed=1 << 23, transcendentals=0),
    )(my_col.reshape(1), *ins))


def grad_x_blocks(pairs, smalls, dims, my_col):
    rows, cols = dims[-2:]
    n, m = pairs[0][0].shape
    inner = pairs[0][1].shape[1]
    lanes = inner // cols
    ins = [v for p in pairs for v in p] + [g[name] for name in ("dt", "xproj", "chan", "gain_mix", "gain_moe") for g in smalls]
    scratch = [pltpu.VMEM((32 * rows, inner), BF), pltpu.VMEM((32 * cols, (lanes - 128) * rows), BF), pltpu.VMEM((32, 128 * rows * cols), F32),
               pltpu.VMEM((m, inner), F32)]
    return grad_blocks(functools.partial(grad_x_kernel, len(pairs), dims), ins, scratch, (m // rows + 32, lanes), rows, cols, my_col,
                       2 * len(pairs) * n * m * inner, 44)


def grad_other_kernel(count, r_cols, s_ref, *refs):
    zs, outs, routers = refs[:2 * count], refs[2 * count:4 * count], refs[4 * count:5 * count]
    keep, give, full_z, full_o = refs[5 * count:]
    rows = keep.shape[1]
    k = pl.program_id(0)

    @pl.when(k == 0)
    def _():
        full_z[...] = sum_products(zs)
        full_o[...] = sum_products(outs)
    r = functools.reduce(lambda a, b: a + b, [v[...] for v in routers]).astype(BF)
    r_rows = r.shape[1] // rows
    for j, out in enumerate((keep, give)):
        c = s_ref[0] ^ (2 * k + j)
        z = full_z[:, pl.ds(pl.multiple_of(c * 384, 128), 384)].astype(BF)
        o = full_o[:, span(2 * k + j, 256)].astype(BF)
        z, o = (v.reshape(rows, v.shape[0] // rows, v.shape[1]) for v in (z, o))

        def put_block(at, lane, v):
            out[0, :, at:at + v.shape[1], lane:lane + v.shape[2]] = v
        put_other(put_block, z, o)
        w = mm(one_hot((16, r.shape[0]), lambda a, b: (a < r_cols) & (b == c * r_cols + a)), r).astype(BF)
        at = out.shape[2] - 16
        out[0, :, at:] = jnp.zeros((rows, 16, 256), BF)
        for q in range(rows):
            out[0, q, at:, :r_rows] = w[:, q * r_rows:(q + 1) * r_rows]


def grad_other_blocks(zs, outs, routers, block, rows, cols, r_cols, my_col):
    ins = [v for p in zs for v in p] + [v for p in outs for v in p] + list(routers)
    flops = 2 * sum(a.shape[0] * a.shape[1] * b.shape[1] for a, b in zs + outs)
    scratch = [pltpu.VMEM((a.shape[1], b.shape[1]), F32) for a, b in (zs[0], outs[0])]
    return grad_blocks(functools.partial(grad_other_kernel, len(zs), r_cols), ins, scratch, block, rows, cols, my_col, flops, 56)


def split_near_kernel(plan, s_ref, keep, got, own, *gives):
    for out, (ki, rm) in zip((own,) + gives, plan):
        p = (s_ref[0] ^ rm) & 1
        v = keep[ki, 0, p].astype(F32) + got[ki, 0, p].astype(F32)
        out[0] = v.astype(out.dtype)


def split_near(keep, got):
    plane = stages()[1]
    near, rows, n, lanes = keep.shape
    plan = [(cm >> 1, rm) for rm, cm in plane]
    view = (near, rows // 2, 2, n, lanes)
    outs = [sds((rows // 2, n, lanes), F32 if i == 0 else BF) for i in range(len(plan))]
    res = pl.pallas_call(
        functools.partial(split_near_kernel, plan),
        grid_spec=pltpu.PrefetchScalarGridSpec(
            num_scalar_prefetch=1, grid=(rows // 2,),
            in_specs=[pl.BlockSpec((near, 1, 2, n, lanes), lambda z, s: (0, z, 0, 0, 0))] * 2,
            out_specs=[pl.BlockSpec((1, n, lanes), lambda z, s: (z, 0, 0))] * len(outs)),
        out_shape=outs,
        compiler_params=pltpu.CompilerParams(vmem_limit_bytes=16 << 20),
        cost_estimate=pl.CostEstimate(flops=0, bytes_accessed=6 * keep.size, transcendentals=0),
    )(lax.axis_index("row").reshape(1), keep.reshape(view), got.reshape(view))
    return res[0], list(res[1:])


def split_far_kernel(count, plan, s_ref, own, *refs):
    gots, mine, gives = refs[:count], refs[count], refs[count + 1:]
    for out, rm in zip((mine,) + gives, plan):
        i = (s_ref[0] ^ rm) >> 1
        v = own[i]
        for g in gots:
            v = v + g[i].astype(F32)
        out[...] = v.astype(out.dtype)


def split_far(own, gots):
    plan = [rm for rm, _ in stages()[0]]
    _, n, lanes = own.shape
    outs = [sds((n, lanes), F32 if i == 0 else BF) for i in range(len(plan))]
    res = one_call(functools.partial(split_far_kernel, len(gots), plan), [own] + gots, outs, [lax.axis_index("row").reshape(1)])
    return res[0], list(res[1:])


def total_of(refs):
    return functools.reduce(lambda a, b: a + b[...].astype(F32), refs[1:], refs[0][...])


def finish_x_kernel(count, *refs):
    gx, gxp, gdt, gcw, gcb, gdb, gal, gds, gmix, gmoe, s = refs[count:]
    s[...] = total_of(refs[:count])
    n, lanes = gx.shape
    gx[...] = s[:n]
    gdt[...] = s[n + 26:n + 26 + gdt.shape[0]]
    wide = lanes - 128
    gxp[...] = s[n:n + gxp.shape[0], :gxp.shape[1]]
    at = n
    for ref in (gcw, gcb, gdb, gal, gds, gmix, gmoe):
        ref[...] = s[at:at + ref.shape[0], wide:wide + ref.shape[1]]
        at += ref.shape[0]


def finish_other_kernel(count, *refs):
    gz, go, gr, s = refs[count:]
    s[...] = total_of(refs[:count])
    n = gz.shape[0]
    half = n // 2
    gz[:, :256] = s[:n]
    gz[:half, 256:] = s[n:n + half, :128]
    gz[half:, 256:] = s[n:n + half, 128:]
    at = n + half
    m = go.shape[0]
    for j in range(2):
        go[j * m // 2:(j + 1) * m // 2, :128] = s[at:at + m // 2, j * 128:(j + 1) * 128]
    for j in range(4):
        go[j * m // 4:(j + 1) * m // 4, 128:] = s[at + m // 2:at + m * 3 // 4, j * 64:(j + 1) * 64]
    at += m * 3 // 4
    gr[...] = s[at:at + gr.shape[0], :gr.shape[1]]


def finish(kernel, mine, gots, shapes):
    ins = [mine] + gots
    vmem = pl.BlockSpec(memory_space=pltpu.VMEM)
    return pl.pallas_call(
        functools.partial(kernel, len(ins)), in_specs=[vmem] * len(ins), out_specs=[vmem] * len(shapes),
        out_shape=[sds(s) for s in shapes], scratch_shapes=[pltpu.VMEM(mine.shape, F32)],
    )(*ins)


def weights_part_kernel(cols, sets, lead, *refs):
    out = refs[-1]
    step = cols + 1
    total = None
    for s in range(sets):
        both, other = refs[s * step:s * step + cols], refs[s * step + cols][0]
        width = both[0].shape[2] // 2
        rows = jnp.concatenate([b[0, :, :width] if lead else b[0, :, width:] for b in both], axis=0)
        v = mm(rows, other, TN) if lead else mm(other, rows, TN)
        total = v if total is None else total + v
    out[0] = total


def expert_weights_part(sets, lead, d, f):
    cols = len(sets[0]) - 1
    experts, n, _ = sets[0][0].shape
    if len(sets) > 1 and len(sets) * cols > 8:
        return sum(expert_weights_part([s], lead, d, f) for s in sets)
    shape = (experts, d, f) if lead else (experts, f, d)
    return per_expert(functools.partial(weights_part_kernel, cols, len(sets), lead), [v for s in sets for v in s],
                      [sds(shape)], 2 * experts * cols * n * d * f * len(sets))[0]


def params_generic(w_in_x, w_in_z, conv_w, conv_b, w_xproj, w_dt, dt_bias, a_log, d_skip, w_out, gain_mix, gain_moe, w_router):
    rows, cols = lax.axis_size("row"), lax.axis_size("col")
    parts = rows * cols
    inner, width = w_in_x.shape[1] * cols, w_in_x.shape[0] * rows
    small = jnp.concatenate([conv_w, conv_b[None], dt_bias[None], a_log, d_skip[None],
                             jnp.concatenate([gain_mix, gain_moe])[None]], axis=0)
    flat = [w_xproj.reshape(-1), w_dt.reshape(-1), w_router.reshape(-1), small.reshape(-1)]
    sizes = [f.shape[0] for f in flat]
    lanes = w_in_x.shape[1]
    extra = -(-sum(sizes) // (16 * lanes)) * 16
    flat = jnp.pad(jnp.concatenate(flat), (0, extra * lanes - sum(sizes))).reshape(extra, lanes)
    here, out_rows, out_lanes = w_in_x.shape[0], w_out.shape[0], w_out.shape[1]
    wide = -(-out_lanes // 128) * 128
    first = gather_list(jnp.concatenate([w_in_x, flat], axis=0))
    full_x, rest = assemble(first, [((0, here, lanes), 0, put_block), ((here, extra, lanes), 1, put_pair)],
                            [(width, inner), (rows, cols, extra, lanes)])
    far_end = first[len(first) // 2 - 1][1]
    late_z, late_o, _ = lax.optimization_barrier((w_in_z, jnp.pad(w_out, ((0, 0), (0, wide - out_lanes))), far_end))
    (full_z,) = assemble(gather_list(late_z), [((0, here, lanes), 0, put_block)], [(width, inner)])
    (wide_out,) = assemble(gather_list(late_o), [((0, out_rows, wide), 0, put_block)], [(inner, cols * wide)])
    lane_of = jnp.arange(cols * wide, dtype=jnp.int32)
    narrow = jnp.where(lane_of % wide < out_lanes, lane_of // wide * out_lanes + lane_of % wide, -1)
    narrow = (narrow[:, None] == jnp.arange(width, dtype=jnp.int32)[None, :]).astype(BF)
    full_out = mm(wide_out, narrow).astype(BF)
    def whole(blocks):
        return blocks.transpose(0, 2, 1, 3).reshape(blocks.shape[0] * blocks.shape[2], -1)
    rest = rest.reshape(rows, cols, extra * lanes)
    cut = [0]
    for n in sizes:
        cut.append(cut[-1] + n)
    full_xpT = whole(rest[:, :, cut[0]:cut[1]].reshape((rows, cols) + w_xproj.shape)).T
    full_dt = whole(rest[:, :, cut[1]:cut[2]].reshape((rows, cols) + w_dt.shape))
    router_f = whole(rest[:, :, cut[2]:cut[3]].reshape((rows, cols) + w_router.shape)).astype(F32).T
    small = rest[:, :, cut[3]:cut[4]].reshape((parts,) + small.shape).transpose(1, 0, 2).astype(F32)
    chan = small[:-1].reshape(-1, inner)
    taps = conv_w.shape[0]
    par = jnp.concatenate([chan[:taps + 2], chan[taps + 2 + NS:]], axis=0)
    a_neg = -jnp.exp(chan[taps + 2:taps + 2 + NS])
    a_two = a_neg * log2e
    gain_mix_f = small[-1, :, :gain_mix.shape[0]].reshape(1, width)
    gain_moe_f = small[-1, :, gain_mix.shape[0]:].reshape(1, width)
    return lambda done: (full_z, full_out, router_f, done), full_x, full_xpT, full_dt, par, a_neg, a_two, gain_mix_f, gain_moe_f


def params_tiled(w_in_x, w_in_z, conv_w, conv_b, w_xproj, w_dt, dt_bias, a_log, d_skip, w_out, gain_mix, gain_moe, w_router):
    rows, cols = lax.axis_size("row"), lax.axis_size("col")
    here, lanes = w_in_x.shape
    inner, width = lanes * cols, here * rows
    taps, share = conv_w.shape
    packed, other = pack_params(w_in_x, w_dt, w_xproj, conv_w, conv_b, dt_bias, a_log, d_skip, gain_mix, gain_moe, w_in_z,
                                w_out, w_router)
    mine = gather_far(packed)
    other, _ = lax.optimization_barrier((other, mine))
    mine_o = gather_far(other)
    near = gather_plane(mine)
    mine_o, _ = lax.optimization_barrier((mine_o, near[-1]))
    near_o = gather_plane(mine_o)
    first = gather_core(near)
    dims = (w_dt.shape[0], w_xproj.shape[1], w_xproj.shape[0], share, gain_mix.shape[0], taps, rows, cols)
    full_x, full_dt, full_xpT, par, a_neg, a_two, gx, gm = unpack_call(
        unpack_first, first, dims,
        [sds((width, inner), BF), sds((w_dt.shape[0] * rows, inner), BF), sds((w_xproj.shape[1] * cols, inner), BF),
         sds((taps + 3, inner)), sds((NS, inner)), sds((NS, inner)), sds((1, width)), sds((1, width))],
        [(32 * rows, inner), (32 * cols, (lanes - 128) * rows), (32, 128 * rows * cols)])

    def rest(done):
        o, done = lax.optimization_barrier((near_o, done))
        full_z, full_out, router_f = unpack_call(
            unpack_other, gather_core(o), (here, w_out.shape[0], w_out.shape[1], w_router.shape[1], cols),
            [sds((width, inner), BF), sds((inner, width), BF), sds((w_router.shape[1] * cols, width))],
            [(inner, 256 * cols), (16 * cols, 128 * rows)])
        return full_z, full_out, router_f, done
    return rest, full_x, full_xpT, full_dt, par, a_neg, a_two, gx, gm


def grads_generic(nms, gateds, gs, total, w_in_x, w_in_z, w_xproj, w_dt, w_out, w_router, gain_mix, conv_w):
    rows, cols = lax.axis_size("row"), lax.axis_size("col")
    parts = rows * cols
    my_col = lax.axis_index("col")
    here, lanes = w_in_x.shape
    out_rows, out_lanes = w_out.shape
    wide = up_to(out_lanes, 128)
    share = conv_w.shape[1]
    sizes = [w_xproj.size, w_dt.size, w_router.size, (conv_w.shape[0] + 4 + NS) * share]
    extra = up_to(-(-sum(sizes) // lanes), 16)
    cut = [sum(sizes[:i]) for i in range(5)]
    grad_out = sum(mm(k[1], r["gm"], TN) for k, r in zip(zip(nms, gateds), gs)).astype(BF)
    grad_out_block = reduce_list([grad_out[:, k * wide:(k + 1) * wide].reshape(rows, out_rows, wide) for k in range(cols)])
    grad_out_block = grad_out_block[:, :out_lanes]
    grad_in_z = column_blocks([(k[0], r["gz"]) for k, r in zip(zip(nms, gateds), gs)], cols, my_col)
    grad_z_block = reduce_list([grad_in_z[k].reshape(rows, here, lanes) for k in range(cols)])
    grad_in_x = column_blocks([(k[0], r["gi"]) for k, r in zip(zip(nms, gateds), gs)], cols, my_col)

    def blocks(g, like):
        r, c = like.shape
        return g.astype(BF).reshape(rows, r, cols, c).transpose(0, 2, 1, 3).reshape(rows, cols, -1)
    gsmall = total["chan"].astype(BF)
    ggain = jnp.concatenate([total["gain_mix"].reshape(parts, 1, -1), total["gain_moe"].reshape(parts, 1, -1)], axis=2)
    gsmall = jnp.concatenate([gsmall.reshape(-1, parts, share).transpose(1, 0, 2), ggain.astype(BF)], axis=1)
    gflat = jnp.concatenate([blocks(total["xproj"].T, w_xproj), blocks(total["dt"], w_dt), blocks(total["router"].T, w_router),
                             gsmall.reshape(rows, cols, -1)], axis=2)
    gflat = jnp.pad(gflat, ((0, 0), (0, 0), (0, extra * lanes - sum(sizes)))).reshape(rows, cols, extra, lanes)
    done = reduce_list([jnp.concatenate([grad_in_x[k].reshape(rows, here, lanes),
                                         lax.dynamic_index_in_dim(gflat, my_col ^ k, 1, keepdims=False)], axis=1)
                        for k in range(cols)])
    grad_x_block = done[:here]
    done = done[here:].reshape(-1)
    sm = done[cut[3]:cut[4]].reshape(-1, share)
    gm = gain_mix.shape[0]
    taps = conv_w.shape[0]
    chan = (sm[:taps], sm[taps], sm[taps + 1], sm[taps + 2:taps + 2 + NS], sm[taps + 2 + NS])
    small = (done[cut[0]:cut[1]].reshape(w_xproj.shape), done[cut[1]:cut[2]].reshape(w_dt.shape), chan, sm[-1, :gm], sm[-1, gm:],
             done[cut[2]:cut[3]].reshape(w_router.shape))
    return (grad_x_block, grad_z_block, grad_out_block), small


def on_device(tokens, w_in_x, w_in_z, conv_w, conv_b, w_xproj, w_dt, dt_bias, a_log, d_skip, w_out,
              gain_mix, gain_moe, w_router, w_up, w_down, routes, lengths, cotangent):
    rows, cols = lax.axis_size("row"), lax.axis_size("col")
    parts = rows * cols
    my_col = lax.axis_index("col")
    seqs, length, width = tokens.shape
    experts_here = w_up.shape[0]
    experts_all = experts_here * rows
    inner = w_in_x.shape[1] * cols
    count = seqs * length
    xp = w_xproj.shape[1] * cols
    share = inner // parts

    tiled = tiles_fit(w_in_x, w_xproj, w_out, conv_w, w_dt, w_router)
    here, lanes = w_in_x.shape
    out_rows, out_lanes = w_out.shape
    wide = up_to(out_lanes, 128)
    taps = conv_w.shape[0]
    rest_of, full_x, full_xpT, full_dt, par, a_neg, a_two, gain_mix_f, gain_moe_f = (
        params_tiled if tiled else params_generic)(
            w_in_x, w_in_z, conv_w, conv_b, w_xproj, w_dt, dt_bias, a_log, d_skip, w_out, gain_mix, gain_moe, w_router)
    lane_of = jnp.arange(cols * wide, dtype=jnp.int32)
    shifted = jnp.where(lane_of % wide < out_lanes, (lane_of // wide ^ my_col) * out_lanes + lane_of % wide, -1)
    shifted = (jnp.arange(width, dtype=jnp.int32)[:, None] == shifted[None, :]).astype(BF)

    message = -(-experts_here * CAP // 8) * 8
    group = -(-rows * CAP // 16) * 16
    at = jnp.arange(experts_here * group, dtype=jnp.int32)
    there = at % group
    source = jnp.where(there < rows * CAP, there // CAP * message + at // group * CAP + there % CAP, -1)
    sort = (source[:, None] == jnp.arange(rows * message, dtype=jnp.int32)[None, :]).astype(BF)

    def mixer(s, x, limit):
        nm, inner_x, conv, u, dl, pT, ssm, starts = mixer_forward(x, gain_mix_f, full_x, full_xpT, full_dt, par, a_two, QB, limit)
        return dict(x=x, s=s, nm=nm, inner=inner_x, conv=conv, u=u, dl=dl, pT=pT, ssm=ssm.reshape(length, inner), starts=starts)

    def router(k, route, n_live, grad):
        n_live = n_live.reshape(1)
        slots = rows * message
        z, gated, hidden, place, outgoing, probs, gate = one_call(
            functools.partial(route_kernel, CAP, experts_here, message, k["s"]),
            [k["x"], k["nm"], k["ssm"], full_z, full_out, gain_moe_f, router_f, route, grad],
            [sds((length, inner)), sds((length, inner), BF), sds((length, width)), sds((length, slots), BF),
             sds((slots, 2 * width), BF), sds((length, experts_all)), sds((length, 1))],
            [n_live], 6 * length * inner * width)
        kept = dict(k, z=z, gated=gated, hidden=hidden, place=place, probs=probs, gate=gate, route=route, n_live=n_live, cot=grad)
        return outgoing, kept

    def home(rows_out):
        return lax.all_to_all(rows_out, "row", split_axis=0, concat_axis=0, tiled=True)

    def arrive(got):
        return mm(sort, got).astype(BF).reshape(experts_here, group, 2 * width)

    def gather_cols(own):
        bufs = [own]
        for bit in bits_of("col")[::-1]:
            bufs = bufs + [swap(v, "col", bit) for v in bufs]
        return bufs

    def from_experts(bufs):
        for bit in bits_of("col"):
            half = len(bufs) // 2
            bufs = [(a.astype(F32) + swap(b, "col", bit).astype(F32)).astype(BF) for a, b in zip(bufs[:half], bufs[half:])]
        return mm(sort, bufs[0].reshape(experts_here * group, 2 * width), ((0,), (0,))).astype(BF)

    def unroute(k, back):
        mixed_out, gh, gs, gz, gm, g_router, g_moe = one_call(
            functools.partial(unroute_kernel, k["s"]),
            [back, k["place"], k["hidden"], k["probs"], k["gate"], k["route"], k["cot"], gain_moe_f, router_f, full_out, shifted,
             k["z"], k["ssm"]],
            [sds((length, width), BF), sds((length, width)), sds((length, inner)), sds((length, inner), BF),
             sds((length, cols * wide), BF), sds((experts_all, width)), sds((1, width))],
            [k["n_live"]], 6 * length * inner * width)
        return dict(mixed_out=mixed_out, gh=gh, gs=gs.reshape(k["u"].shape), gz=gz, gm=gm, router=g_router, gain_moe=g_moe)

    def unscan(k, gs, limit):
        gi, g_xp, g_dt, g_chan = scan_backward(k["u"], k["dl"], gs, k["conv"], k["inner"], k["pT"], k["starts"], full_xpT, full_dt, par, a_neg, limit)
        return dict(gi=gi, xproj=g_xp, dt=g_dt, chan=g_chan)

    def unproject(k, g):
        grad_tokens, g_mix = one_call(
            token_kernel, [g["gi"], g["gz"], full_x, full_z, k["x"], g["gh"], gain_mix_f], [sds((length, width)), sds((1, width))], (),
            4 * length * inner * width, 24)
        return dict(tokens=grad_tokens, gain_mix=g_mix)

    after = lax.optimization_barrier
    ks, owns, last = [], [], None
    for s in range(seqs):
        x = tokens[s]
        if last is not None:
            x, last = after((x, last))
        k = mixer(s, x, 24 if s == 0 else 48)
        if s == 0:
            full_z, full_out, router_f, k["ssm"] = rest_of(k["ssm"])
        before, (last, k) = last, router(k, routes[s], lengths[s], cotangent)
        ks.append(k)
        if before is not None:
            got, last = after((home(before), last))
            owns.append(arrive(got))
    owns.append(arrive(home(last)))
    sets, sent = [], []
    for s in range(seqs):
        bufs = gather_cols(owns[s])
        if s == seqs - 2:
            bufs, owns[-1] = after((bufs, owns[-1]))
        outs, more = expert_both(bufs, w_up, w_down)
        sets.append((bufs, more))
        sent.append(from_experts(outs))
    backs = [home(v) for v in sent]
    grads_w = []
    for lead in (True, False):
        ins, sent[0], _ = after(([b + [v[1 if lead else 0]] for b, v in sets], sent[0], grads_w))
        grads_w.append(expert_weights_part(ins, lead, width, w_up.shape[2]))
    backs[0], (grad_w_up, grad_w_down) = after((backs[0], grads_w))
    gs_ = []
    for s in range(seqs):
        g = unroute(ks[s], backs[s])
        gs_.append(g)
        if s + 1 < seqs:
            g["gs"], sent[s + 1] = after((g["gs"], sent[s + 1]))
            g.update(unscan(ks[s], g["gs"], 52))
            g["gi"], backs[s + 1] = after((g["gi"], backs[s + 1]))
    g = gs_[-1]
    nms, gateds = [k["nm"] for k in ks], [k["gated"] for k in ks]
    if tiled:
        block = (here + here // 2 + out_rows * 3 // 4 + 16, 256)
        keep, give = grad_other_blocks([(v, q["gz"]) for v, q in zip(nms, gs_)], [(v, q["gm"]) for v, q in zip(gateds, gs_)],
                                       [q["router"] for q in gs_], block, rows, cols, w_router.shape[1], my_col)
        far, plane, core = stages()

        def first_tokens(v):
            return unproject(ks[0], dict(gs_[0], gi=after((gs_[0]["gi"], v))[0]))
        got, first = between(first_tokens, give, exchange(give, core))
        if seqs > 1:
            gs_[0].update(first)
        own, gives = split_near(keep, got)
        g["gs"], gives = after((g["gs"], gives))
        gots = [exchange(v, p) for v, p in zip(gives, plane[1:])]
        g.update(unscan(ks[-1], g["gs"], 24))
        gots, g["gi"] = after((gots, g["gi"]))
        mine, gives = split_far(own, gots)
        g["gi"], gives = after((g["gi"], gives))
        gots_o = [exchange(v, p) for v, p in zip(gives, far[1:])]
        mine_o = mine
        dims = (w_dt.shape[0], w_xproj.shape[1], w_xproj.shape[0], conv_w.shape[1], gain_mix.shape[0], rows, cols)
        for s in range(1, seqs):
            gs_[s].update(unproject(ks[s], gs_[s]))
        keep, give = grad_x_blocks([(v, q["gi"]) for v, q in zip(nms, gs_)], gs_, dims, my_col)
        own, gives = split_near(keep, exchange(give, core))
        gots = [exchange(v, p) for v, p in zip(gives, plane[1:])]
        gots_o, _ = after((gots_o, gives))
        gz, go, g_router = finish(finish_other_kernel, mine_o, gots_o, [w_in_z.shape, w_out.shape, w_router.shape[::-1]])
        gots, gz, go, g_router = after((gots, gz, go, g_router))
        mine, gives = split_far(own, gots)
        gots = [exchange(v, p) for v, p in zip(gives, far[1:])]
        share, gshare = conv_w.shape[1], gain_mix.shape[0]
        gx, g_xproj, g_dt, gcw, gcb, gdb, gal, gds, g_mix, g_moe = finish(
            finish_x_kernel, mine, gots,
            [w_in_x.shape, w_xproj.shape[::-1], w_dt.shape, conv_w.shape, (1, share), (1, share), a_log.shape, (1, share), (1, gshare), (1, gshare)])
        blocks = (gx, gz, go)
        small = (g_xproj.T, g_dt, (gcw, gcb[0], gdb[0], gal, gds[0]), g_mix[0], g_moe[0], g_router.T)
    else:
        g.update(unscan(ks[-1], g["gs"], 24))
        for k, q in zip(ks, gs_):
            q.update(unproject(k, q))
        names = ("xproj", "dt", "chan", "gain_mix", "gain_moe", "router")
        total = {n: sum(q[n] for q in gs_) for n in names}
        blocks, small = grads_generic(nms, gateds, gs_, total, w_in_x, w_in_z, w_xproj, w_dt, w_out, w_router, gain_mix, conv_w)
    g_xproj, g_dt, (gcw, gcb, gdb, gal, gds), g_mix, g_moe, g_router = small
    return (
        jnp.stack([q["mixed_out"] for q in gs_]),
        jnp.stack([q["tokens"] for q in gs_]),
        blocks[0],
        blocks[1],
        gcw,
        gcb,
        g_xproj,
        g_dt,
        gdb,
        gal,
        gds,
        blocks[2],
        g_mix,
        g_moe,
        g_router,
        grad_w_up,
        grad_w_down,
    )


def solution(mesh):
    tok = P(("row", "col"), None, None)
    mat = P("row", "col")
    vec = P(("row", "col"))
    chan = P(None, ("row", "col"))
    up, down = P("row", None, "col"), P("row", "col", None)
    return jax.shard_map(
        on_device,
        mesh=mesh,
        in_specs=(tok, mat, mat, chan, vec, mat, mat, vec, chan, vec, mat, vec, vec, mat, up, down, tok, vec, tok),
        out_specs=(tok, tok, mat, mat, chan, vec, mat, mat, vec, chan, vec, mat, vec, vec, mat, up, down),
        check_vma=False,
    )
```

```python
import functools
import jax
import jax.numpy as jnp
from jax import lax
from jax.sharding import PartitionSpec as P
from jax.experimental import pallas as pl
from jax.experimental.pallas import tpu as pltpu
NS = 16
F32 = jnp.float32
SLOT_OF=[4*((i>>2)&1)+2*(1-((i>>1)&1))+(1-(i&1)) for i in range(8)]
def merge8(rows):
    idx=lax.broadcasted_iota(jnp.int32,(8,128),0)
    m4=idx<4; m2=(idx&2)!=0; m1=(idx&1)!=0
    p=[None]*8
    for i in range(8): p[SLOT_OF[i]]=rows[i]
    r=[jnp.where(m4,p[k],p[k+4])+pltpu.roll(jnp.where(m4,p[k+4],p[k]),4,0) for k in range(4)]
    def half(x,y,m,d):
        return jnp.where(m,x+pltpu.roll(x,d,0),y+pltpu.roll(y,8-d,0))
    v=[half(r[k],r[k+2],m2,2) for k in range(2)]
    return half(v[0],v[1],m1,1)
def mm(a, b, dims=((1,), (0,)), **kw):
    return lax.dot_general(a, b, (dims, ((), ())), preferred_element_type=F32, **kw)


NT = ((1,), (1,))
TN = ((0,), (0,))


def softplus(v):
    e = jnp.exp(-jnp.abs(v))
    tiny = e * (1.0 - e * (0.5 - e * (1.0 / 3.0 - e * 0.25)))
    return jnp.maximum(v, 0.0) + jnp.where(e < 0.01, tiny, jnp.log(1.0 + e))


def sigmoid_of_softplus(d):
    tiny = d * (1.0 - d * (0.5 - d * (1.0 / 6.0 - d * (1.0 / 24.0))))
    return jnp.where(d < 0.03, tiny, 1.0 - jnp.exp(-d))


def sigmoid(v):
    return 1.0 / (1.0 + jnp.exp(-v))


def spread(dst, src, T):
    for j in range(T):
        dst[j] = jnp.broadcast_to(src[:, j:j + 1], (NS, 128))


def fold(x):
    return x[0:8] + x[8:16]


def convolve(ext, w, b, T):
    taps = w.shape[0]
    out = b
    for k in range(taps):
        out = out + w[k:k + 1] * ext[9 - taps + k:9 - taps + k + T]
    return out


def mixer_kernel(T, Q, R, x_ref, gain_ref, wx_ref, xpT_ref, wdt_ref, par_ref, a2_ref,
                 nm_ref, in_ref, cv_ref, u_ref, dl_ref, pT_ref, y_ref, st_ref, state, bx, cx, du):
    c = pl.program_id(0)
    L, DI = nm_ref.shape[0], wx_ref.shape[1]
    taps = par_ref.shape[0] - 3

    @pl.when(c == 0)
    def _():
        state[...] = jnp.zeros_like(state)
        x = x_ref[...].astype(F32)
        nm = (x * lax.rsqrt(jnp.mean(x * x, axis=-1, keepdims=True) + 1e-05) * gain_ref[...]).astype(jnp.bfloat16)
        nm_ref[...] = nm
        in_ref[0:8] = jnp.zeros((8, DI), F32)
        in_ref[8:] = mm(nm, wx_ref[...])
    st_ref[0] = state[...]
    par = par_ref[...]
    skip = par[taps + 2:taps + 3]
    conv = convolve(in_ref[pl.ds(pl.multiple_of(c * T, 8), T + 8)], par[:taps], par[taps:taps + 1], T)
    cv_ref[0] = conv.reshape(T // 8, 8, DI)
    u = conv * sigmoid(conv)
    u_ref[0] = u.reshape(T // 8, 8, DI)
    pT = mm(xpT_ref[...], u.astype(jnp.bfloat16), NT)
    pT_ref[0] = pT
    d = softplus(mm(pT[:R].astype(jnp.bfloat16), wdt_ref[...], TN) + par[taps + 1:taps + 2])
    dl_ref[0] = d.reshape(T // 8, 8, DI)
    du[...] = (d * u).reshape(T // 8, 8, DI)
    spread(bx, pT[R:R + NS], T)
    spread(cx, pT[R + NS:R + 2 * NS], T)

    def grp(g, _):
        base = pl.multiple_of(g * (Q * 128), 128)
        lanes = [pl.ds(base + q * 128, 128) for q in range(Q)]
        a = [a2_ref[:, ln] for ln in lanes]
        sk = [par_ref[taps + 2:taps + 3, ln] for ln in lanes]

        def tb(i, s):
            s = list(s)
            rows = [[] for _ in range(Q)]
            for k in range(8):
                t = i * 8 + k
                b = bx[t]
                cc = cx[t]
                for q in range(Q):
                    dd = dl_ref[0, i, k:k + 1, lanes[q]]
                    dub = du[i, k:k + 1, lanes[q]]
                    s[q] = jnp.exp2(dd * a[q]) * s[q] + b * dub
                    rows[q].append(fold(s[q] * cc))
            for q in range(Q):
                y_ref[0, i, :, lanes[q]] = merge8(rows[q]) + sk[q] * u_ref[0, i, :, lanes[q]]
            return tuple(s)
        s = lax.fori_loop(0, T // 8, tb, tuple(state[:, ln] for ln in lanes))
        for q in range(Q):
            state[:, lanes[q]] = s[q]
        return 0
    lax.fori_loop(0, DI // (Q * 128), grp, 0)


def whole_spec(a):
    return pl.BlockSpec(a.shape, lambda *_: (0,) * len(a.shape))


def sds(shape, dtype=F32):
    return jax.ShapeDtypeStruct(shape, dtype)


def mixer_forward(x, gain, wx, xpT, wdt, par, a2, T, limit, Q=6):
    L, D = x.shape
    DI = wx.shape[1]
    C, XP, R = L // T, xpT.shape[0], wdt.shape[0]
    ins = [x, gain, wx, xpT, wdt, par, a2]
    rows = pl.BlockSpec((1, T // 8, 8, DI), lambda c: (c, 0, 0, 0))
    big = sds((C, T // 8, 8, DI))
    nm, inner = sds((L, D), jnp.bfloat16), sds((L + 8, DI))
    return pl.pallas_call(
        functools.partial(mixer_kernel, T, Q, R), grid=(C,),
        in_specs=[whole_spec(a) for a in ins],
        out_specs=[whole_spec(nm), whole_spec(inner), rows, rows, rows, pl.BlockSpec((1, XP, T), lambda c: (c, 0, 0)), rows,
                   pl.BlockSpec((1, NS, DI), lambda c: (c, 0, 0))],
        out_shape=[nm, inner, big, big, big, sds((C, XP, T)), big, sds((C, NS, DI))],
        scratch_shapes=[pltpu.VMEM((NS, DI), F32), pltpu.VMEM((T, NS, 128), F32), pltpu.VMEM((T, NS, 128), F32),
                        pltpu.VMEM((T // 8, 8, DI), F32)],
        compiler_params=pltpu.CompilerParams(vmem_limit_bytes=limit << 20),
        cost_estimate=pl.CostEstimate(flops=40000000000, bytes_accessed=16 * L * DI, transcendentals=0),
    )(*ins)


def scan_back_kernel(T, Q, Q2, R, u_ref, dl_ref, gs_ref, cv_ref, in_ref, pT_ref, st_ref, xpT_ref, wdt_ref, par_ref, an_ref,
                     gi_ref, gxp_ref, gwd_ref, gpar_ref, carry, later, bx, cx, du, guc, gdt, hs, ds, gbp, gcp, sums):
    j = pl.program_id(0)
    c = pl.num_programs(0) - 1 - j
    DI = wdt_ref.shape[1]
    taps = par_ref.shape[0] - 3

    @pl.when(j == 0)
    def _():
        for ref in (carry, later, gxp_ref, gwd_ref, gpar_ref, sums):
            ref[...] = jnp.zeros_like(ref)
    pT = pT_ref[0]
    spread(bx, pT[R:R + NS], T)
    spread(cx, pT[R + NS:R + 2 * NS], T)
    du[...] = dl_ref[0] * u_ref[0]
    gbp[...] = jnp.zeros_like(gbp)
    gcp[...] = jnp.zeros_like(gcp)
    W = Q * 128

    def grp(g, _):
        base = pl.multiple_of(g * W, 128)
        lanes = [pl.ds(base + q * 128, 128) for q in range(Q)]
        loc = [slice(q * 128, q * 128 + 128) for q in range(Q)]
        an = [an_ref[:, ln] for ln in lanes]
        a2 = [v * 1.4426950408889634 for v in an]

        def tb(i, s):
            s = list(s)
            for k in range(8):
                t = i * 8 + k
                b = bx[t]
                gc = gcp[t]
                for q in range(Q):
                    dd = dl_ref[0, i, k:k + 1, lanes[q]]
                    dub = du[i, k:k + 1, lanes[q]]
                    gsr = gs_ref[0, i, k:k + 1, lanes[q]]
                    dec = jnp.exp2(dd * a2[q])
                    h = dec * s[q]
                    ds[t, :, loc[q]] = dec
                    hs[t, :, loc[q]] = h
                    s[q] = h + b * dub
                    gc = gc + s[q] * gsr
                gcp[t] = gc
            return tuple(s)
        lax.fori_loop(0, T // 8, tb, tuple(st_ref[0, :, ln] for ln in lanes))
        for q0 in range(0, Q, Q2):
            qs = range(q0, q0 + Q2)
            sk = {q: par_ref[taps + 2:taps + 3, lanes[q]] for q in qs}

            def rb(jj, cr):
                i = T // 8 - 1 - jj
                g_, ga = {q: cr[0][q - q0] for q in qs}, {q: cr[1][q - q0] for q in qs}
                gbs, gsk = list(cr[2]), list(cr[3])
                m1, m2 = {q: [None] * 8 for q in qs}, {q: [None] * 8 for q in qs}
                for k in range(7, -1, -1):
                    t = i * 8 + k
                    b = bx[t]
                    cc = cx[t]
                    gb = gbp[t]
                    for q in qs:
                        dd = dl_ref[0, i, k:k + 1, lanes[q]]
                        dub = du[i, k:k + 1, lanes[q]]
                        gsr = gs_ref[0, i, k:k + 1, lanes[q]]
                        gg = gsr * cc + g_[q]
                        g_[q] = gg * ds[t, :, loc[q]]
                        qq = gg * hs[t, :, loc[q]]
                        m1[q][k] = fold(gg * b)
                        m2[q][k] = fold(qq * an[q])
                        ga[q] = ga[q] + qq * dd
                        gb = gb + gg * dub
                    gbp[t] = gb
                for q in qs:
                    s1 = merge8(m1[q])
                    s2 = merge8(m2[q])
                    u8, d8, gs8 = u_ref[0, i, :, lanes[q]], dl_ref[0, i, :, lanes[q]], gs_ref[0, i, :, lanes[q]]
                    guc[i, :, lanes[q]] = d8 * s1 + sk[q] * gs8
                    gd = (s2 + u8 * s1) * sigmoid_of_softplus(d8)
                    gdt[i, :, lanes[q]] = gd
                    gbs[q - q0] = gbs[q - q0] + gd
                    gsk[q - q0] = gsk[q - q0] + gs8 * u8
                return (tuple(g_[q] for q in qs), tuple(ga[q] for q in qs), tuple(gbs), tuple(gsk))
            z8 = tuple(jnp.zeros((8, 128), F32) for q in qs)
            cr = lax.fori_loop(0, T // 8, rb, (tuple(carry[:, lanes[q]] for q in qs),
                                               tuple(jnp.zeros((NS, 128), F32) for q in qs), z8, z8), unroll=2)
            for q in qs:
                carry[:, lanes[q]] = cr[0][q - q0]
                gpar_ref[taps + 2:taps + 2 + NS, lanes[q]] += cr[1][q - q0] * an[q]
                sums[taps + 1, :, lanes[q]] += cr[2][q - q0]
                sums[taps + 2, :, lanes[q]] += cr[3][q - q0]
        return 0
    lax.fori_loop(0, DI // W, grp, 0)

    gbT = jnp.sum(gbp[...], axis=2).T
    gcT = jnp.sum(gcp[...], axis=2).T
    gd = gdt[...].reshape(T, DI).astype(jnp.bfloat16)
    gpT = jnp.concatenate([mm(wdt_ref[...], gd, NT), gbT, gcT], axis=0).astype(jnp.bfloat16)
    gwd_ref[...] += mm(pT[:R].astype(jnp.bfloat16), gd)
    gxp_ref[...] += mm(gpT, u_ref[0].reshape(T, DI).astype(jnp.bfloat16))
    gu = guc[...].reshape(T, DI) + mm(gpT, xpT_ref[...], TN)
    par = par_ref[...]
    conv = cv_ref[0].reshape(T, DI)
    sig = sigmoid(conv)
    gconv = gu * (sig * (1.0 + conv * (1.0 - sig)))
    part = lambda v: jnp.sum(v.reshape(T // 8, 8, DI), axis=0)
    sums[taps] += part(gconv)
    inner_x = in_ref[pl.ds(pl.multiple_of(c * T + 8, 8), T)]
    both = jnp.concatenate([gconv, later[...]], axis=0)
    gi = None
    for k in range(taps):
        ahead = both[taps - 1 - k:taps - 1 - k + T]
        sums[k] += part(ahead * inner_x)
        gi = par[k:k + 1] * ahead if gi is None else gi + par[k:k + 1] * ahead
    gi_ref[...] = gi.astype(jnp.bfloat16)
    later[...] = gconv[:8]

    @pl.when(c == 0)
    def _():
        for k in range(taps + 2):
            gpar_ref[k:k + 1] = jnp.sum(sums[k], axis=0, keepdims=True)
        gpar_ref[taps + 2 + NS:taps + 3 + NS] = jnp.sum(sums[taps + 2], axis=0, keepdims=True)


def scan_backward(u, dl, gs, conv, inner, pT, st, xpT, wdt, par, an, limit, Q=3, Q2=3):
    C, T8, _, DI = u.shape
    T = T8 * 8
    XP, R = xpT.shape[0], wdt.shape[0]
    n = par.shape[0] + NS
    rev = lambda *shape: pl.BlockSpec((1,) + shape, lambda j: (C - 1 - j,) + (0,) * len(shape))
    rows = rev(T8, 8, DI)
    outs = [sds((C * T, DI), jnp.bfloat16), sds((XP, DI)), sds((R, DI)), sds((n, DI))]
    V = lambda *s: pltpu.VMEM(s, F32)
    return pl.pallas_call(
        functools.partial(scan_back_kernel, T, Q, Q2, R), grid=(C,),
        in_specs=[rows, rows, rows, rows, whole_spec(inner), rev(XP, T), rev(NS, DI)] + [whole_spec(a) for a in (xpT, wdt, par, an)],
        out_specs=[pl.BlockSpec((T, DI), lambda j: (C - 1 - j, 0))] + [whole_spec(o) for o in outs[1:]],
        out_shape=outs,
        scratch_shapes=[V(NS, DI), V(8, DI), V(T, NS, 128), V(T, NS, 128), V(T8, 8, DI), V(T8, 8, DI), V(T8, 8, DI),
                        V(T, NS, Q * 128), V(T, NS, Q * 128), V(T, NS, 128), V(T, NS, 128), V(par.shape[0], 8, DI)],
        compiler_params=pltpu.CompilerParams(vmem_limit_bytes=limit << 20),
        cost_estimate=pl.CostEstimate(flops=80000000000, bytes_accessed=16 * C * T * DI, transcendentals=0),
    )(u, dl, gs, conv, inner, pT, st, xpT, wdt, par, an)


def one_call(kernel, ins, outs, scalars=(), flops=0, limit=56):
    smem = pl.BlockSpec(memory_space=pltpu.SMEM)
    vmem = pl.BlockSpec(memory_space=pltpu.VMEM)
    size = sum(a.size * a.dtype.itemsize for a in list(ins) + list(outs))
    return pl.pallas_call(
        kernel,
        in_specs=[smem] * len(scalars) + [vmem] * len(ins), out_specs=[vmem] * len(outs), out_shape=list(outs),
        compiler_params=pltpu.CompilerParams(vmem_limit_bytes=limit << 20),
        cost_estimate=pl.CostEstimate(flops=flops, bytes_accessed=size, transcendentals=0),
    )(*scalars, *ins)


def route_kernel(cap, here, message, s, live_ref, x_ref, nm_ref, y_ref, wz_ref, wo_ref, gain_ref, wr_ref, route_ref, cot_ref,
                 z_ref, gated_ref, hid_ref, target_ref, out_ref, prob_ref, gate_ref):
    bf = jnp.bfloat16
    L = nm_ref.shape[0]
    E = wr_ref.shape[0]
    z = mm(nm_ref[...], wz_ref[...])
    z_ref[...] = z
    gated = (y_ref[...] * (z * sigmoid(z))).astype(bf)
    gated_ref[...] = gated
    hid = x_ref[...].astype(F32) + mm(gated, wo_ref[...])
    hid_ref[...] = hid
    nmoe = hid * lax.rsqrt(jnp.mean(hid * hid, axis=-1, keepdims=True) + 1e-05) * gain_ref[...]
    logits = mm(nmoe, wr_ref[...], NT, precision=lax.Precision.HIGHEST)
    e = jnp.exp(logits - jnp.max(logits, axis=-1, keepdims=True))
    probs = e / jnp.sum(e, axis=-1, keepdims=True)
    prob_ref[...] = probs
    route = route_ref[...]
    hot = route == lax.broadcasted_iota(jnp.int32, (L, E), 1)
    gate = jnp.sum(jnp.where(hot, probs, 0.0), axis=-1, keepdims=True)
    gate_ref[...] = gate
    live = lax.broadcasted_iota(jnp.int32, (L, 1), 0) < live_ref[0]
    hits = jnp.where(hot & live, 1.0, 0.0)
    before = lax.broadcasted_iota(jnp.int32, (L, L), 0) > lax.broadcasted_iota(jnp.int32, (L, L), 1)
    slot = jnp.sum(mm(jnp.where(before, 1.0, 0.0).astype(bf), hits.astype(bf)) * hits, axis=-1, keepdims=True).astype(jnp.int32)
    slots = out_ref.shape[0]
    target = route // here * message + route % here * cap + slot
    target = jnp.where(live & (slot < cap), target, -slots)
    target_ref[...] = target
    gy = jnp.where(live, cot_ref[s], 0.0)
    first, second = places(target, slots, here * cap)
    out_ref[...] = (mm(first, nmoe.astype(bf), TN) + mm(second, (gy * gate).astype(bf), TN)).astype(bf)


def places(target, slots, half):
    at = lax.broadcasted_iota(jnp.int32, (target.shape[0], slots), 1)
    return (jnp.where(at == target, 1.0, 0.0).astype(jnp.bfloat16), jnp.where(at == target + half, 1.0, 0.0).astype(jnp.bfloat16))


def sort_kernel(cap, message, half, group, got_ref, out_ref):
    n, slots = out_ref.shape[0], got_ref.shape[0]
    i = lax.broadcasted_iota(jnp.int32, (n, 1), 0)
    there = i % group
    src = jnp.where(there < slots // message * cap, there // cap * message + i // group * cap + there % cap, -slots)
    at = lax.broadcasted_iota(jnp.int32, (n, slots), 1)
    got = got_ref[...]
    D = got.shape[1]
    out_ref[:, :D] = mm(jnp.where(at == src, 1.0, 0.0).astype(jnp.bfloat16), got).astype(jnp.bfloat16)
    out_ref[:, D:] = mm(jnp.where(at == src + half, 1.0, 0.0).astype(jnp.bfloat16), got).astype(jnp.bfloat16)


def unsort_kernel(cap, message, half, group, buf_ref, out_ref):
    slots, n = out_ref.shape[0], buf_ref.shape[0]
    q = lax.broadcasted_iota(jnp.int32, (slots, 1), 0)
    w = q % message
    second = w >= half
    v = jnp.where(second, w - half, w)
    dst = jnp.where(w < 2 * half, v // cap * group + q // message * cap + v % cap, -1)
    at = lax.broadcasted_iota(jnp.int32, (slots, n), 1)
    D = out_ref.shape[1]
    one = jnp.where(at == jnp.where(second, -1, dst), 1.0, 0.0).astype(jnp.bfloat16)
    two = jnp.where(at == jnp.where(second, dst, -1), 1.0, 0.0).astype(jnp.bfloat16)
    out_ref[...] = (mm(one, buf_ref[:, :D]) + mm(two, buf_ref[:, D:])).astype(jnp.bfloat16)


def unroute_kernel(s, half, live_ref, home_ref, target_ref, hid_ref, prob_ref, gate_ref, route_ref, cot_ref, gain_ref, wr_ref, wo_ref, sh_ref,
                   z_ref, y_ref, mix_ref, gh_ref, gs_ref, gz_ref, gm_ref, gr_ref, gg_ref):
    bf = jnp.bfloat16
    high = lax.Precision.HIGHEST
    hid, gain = hid_ref[...], gain_ref[...]
    L, D = hid.shape
    E = wr_ref.shape[0]
    first, second = places(target_ref[...], home_ref.shape[0], half)
    etok, gsent = mm(first, home_ref[...]), mm(second, home_ref[...])
    live = lax.broadcasted_iota(jnp.int32, (L, 1), 0) < live_ref[0]
    gate, probs = gate_ref[...], prob_ref[...]
    mix_ref[...] = jnp.where(live, hid + gate * etok, 0.0).astype(bf)
    gy = jnp.where(live, cot_ref[s], 0.0)
    ggate = jnp.sum(gy * etok, axis=-1, keepdims=True)
    hot = jnp.where(route_ref[...] == lax.broadcasted_iota(jnp.int32, (L, E), 1), 1.0, 0.0)
    glog = ggate * gate * (hot - probs)
    rms = lax.rsqrt(jnp.mean(hid * hid, axis=-1, keepdims=True) + 1e-05)
    hat = hid * rms
    gr_ref[...] = mm(glog, hat * gain, TN, precision=high)
    gnorm = gsent + mm(glog, wr_ref[...], precision=high)
    gg_ref[...] = jnp.sum(gnorm * hat, axis=0, keepdims=True)
    scaled = gnorm * gain
    gh = gy + rms * (scaled - hat * jnp.mean(scaled * hat, axis=-1, keepdims=True))
    gh_ref[...] = gh
    gmix = gh.astype(bf)
    gm_ref[...] = mm(gmix, sh_ref[...]).astype(bf)
    ggated = mm(gmix, wo_ref[...], NT)
    z = z_ref[...]
    sig = sigmoid(z)
    gs_ref[...] = ggated * (z * sig)
    gz_ref[...] = (ggated * y_ref[...] * (sig * (1.0 + z * (1.0 - sig)))).astype(bf)


def token_kernel(gi_ref, gz_ref, wx_ref, wz_ref, x_ref, gh_ref, gain_ref, gt_ref, gg_ref):
    gnm = mm(gi_ref[...], wx_ref[...], NT) + mm(gz_ref[...], wz_ref[...], NT)
    x = x_ref[...].astype(F32)
    rms = lax.rsqrt(jnp.mean(x * x, axis=-1, keepdims=True) + 1e-05)
    hat = x * rms
    gg_ref[...] = jnp.sum(gnm * hat, axis=0, keepdims=True)
    scaled = gnm * gain_ref[...]
    gt_ref[...] = gh_ref[...] + rms * (scaled - hat * jnp.mean(scaled * hat, axis=-1, keepdims=True))


QB = 64
CAP = 13
BF = jnp.bfloat16
root_half = 0.7071067811865476
inv_root_two_pi = 0.3989422804014327
log2e = 1.4426950408889634


def swap(x, axis, bit):
    n = lax.axis_size(axis)
    return lax.ppermute(x, axis, [(i, i ^ bit) for i in range(n)])


def bits_of(axis):
    n = lax.axis_size(axis)
    return [1 << k for k in range(n.bit_length() - 1)]


def exchange(x, mask):
    rm, cm = mask
    if rm == 0:
        return swap(x, "col", cm)
    if cm == 0:
        return swap(x, "row", rm)
    rows, cols = lax.axis_size("row"), lax.axis_size("col")
    pairs = [(r * cols + c, (r ^ rm) * cols + (c ^ cm)) for r in range(rows) for c in range(cols)]
    return lax.ppermute(x, ("row", "col"), pairs)


def combos(bits):
    out = [(0, 0)]
    for rb, cb in bits:
        out = out + [(r | rb, c | cb) for r, c in out]
    return out


def stages():
    row, col = bits_of("row"), bits_of("col")
    far = combos([(b, 0) for b in row[1:]])
    plane = combos([(row[0], 0)] + [(0, b) for b in col[1:]])
    return far, plane, (0, col[0])


def add(a, b):
    return (a[0] ^ b[0], a[1] ^ b[1])


def gather_far(x):
    return jnp.stack([x] + [exchange(x, m) for m in stages()[0][1:]])


def gather_plane(mine):
    return [mine] + [exchange(mine, m) for m in stages()[1][1:]]


def gather_core(near):
    far, plane, core = stages()
    near = [([add(f, m) for f in far], b) for m, b in zip(plane, near)]
    return near + [([add(m, core) for m in ms], exchange(b, core)) for ms, b in near]


def gather_list(x):
    return gather_core(gather_plane(gather_far(x)))


def assemble_kernel(masks, moves, count_in, *refs):
    r0, c0 = refs[0][0], refs[0][1]
    ins, outs = refs[1:1 + count_in], refs[1 + count_in:]
    for buf, ms in zip(ins, masks):
        for i, (rm, cm) in enumerate(ms):
            for (row, count, lanes), out, place in moves:
                place(outs[out], r0 ^ rm, c0 ^ cm, buf[i, row:row + count, :lanes])


def put_block(out, r, c, block):
    n, m = block.shape
    out[pl.ds(pl.multiple_of(r * n, n), n), pl.ds(pl.multiple_of(c * m, m), m)] = block


def put_pair(out, r, c, block):
    out[r, c] = block


def take_blocks(gathered):
    rows, cols = lax.axis_size("row"), lax.axis_size("col")
    order = [r * cols + c for ms, _ in gathered for r, c in ms]
    entry = jnp.asarray([order.index(i) for i in range(rows * cols)], jnp.int32)
    me = lax.axis_index("row") * cols + lax.axis_index("col")
    stacked = jnp.concatenate([b for _, b in gathered], axis=0)
    out = jnp.take(stacked, entry[jnp.arange(rows * cols, dtype=jnp.int32) ^ me], axis=0)
    return out.reshape((rows, cols) + stacked.shape[1:])


def assemble(gathered, moves, shapes):
    masks = [ms for ms, _ in gathered]
    bufs = [b for _, b in gathered]
    if any(lanes % 128 for (_, _, lanes), _, _ in moves):
        every = take_blocks(gathered)
        cut = [every[:, :, row:row + count, :lanes] for (row, count, lanes), _, _ in moves]
        return [v if place is put_pair else v.transpose(0, 2, 1, 3).reshape(shape)
                for v, shape, (_, _, place) in zip(cut, shapes, moves)]
    me = jnp.stack([lax.axis_index("row"), lax.axis_index("col")]).astype(jnp.int32)
    vmem = pl.BlockSpec(memory_space=pltpu.VMEM)
    return pl.pallas_call(
        functools.partial(assemble_kernel, masks, moves, len(bufs)),
        in_specs=[pl.BlockSpec(memory_space=pltpu.SMEM)] + [vmem] * len(bufs),
        out_specs=[vmem] * len(shapes),
        out_shape=[jax.ShapeDtypeStruct(s, BF) for s in shapes],
        compiler_params=pltpu.CompilerParams(vmem_limit_bytes=32 << 20),
        cost_estimate=pl.CostEstimate(flops=0, bytes_accessed=4 * sum(b.size for b in bufs), transcendentals=0),
    )(me, *bufs)


def between(work, give, got):
    result = work(give)
    return lax.optimization_barrier((got, result))


def reduce_core(parts, work=None):
    far, plane, core = stages()
    near = [k for k in range(lax.axis_size("col")) if not k & core[1]]
    give = jnp.stack([parts[k | core[1]] for k in near])
    got = exchange(give, core)
    result = None
    if work:
        got, result = between(work, give, got)
    return [parts[k].astype(F32) + got[i].astype(F32) for i, k in enumerate(near)], result


def reduce_plane_give(sums):
    far, plane, core = stages()
    near = [k for k in range(lax.axis_size("col")) if not k & core[1]]
    rows, r0 = lax.axis_size("row"), lax.axis_index("row")

    def rows_of(k, rm):
        v = sums[near.index(k)]
        return lax.dynamic_index_in_dim(v.reshape((rows // 2, 2) + v.shape[1:]), (r0 ^ rm) & 1, 1, keepdims=False)
    return rows_of(0, 0), [rows_of(cm, rm).astype(BF) for rm, cm in plane[1:]]


def reduce_plane(own, give, work=None):
    got = [exchange(g, m) for g, m in zip(give, stages()[1][1:])]
    result = None
    if work:
        got, result = between(work, give, got)
    return functools.reduce(lambda t, v: t + v.astype(F32), got, own), result


def reduce_far(total, work=None):
    far = stages()[0]
    r0 = lax.axis_index("row")
    give = [lax.dynamic_index_in_dim(total, (r0 ^ rm) >> 1, 0, keepdims=False).astype(BF) for rm, _ in far[1:]]
    got = [exchange(g, m) for g, m in zip(give, far[1:])]
    result = None
    if work:
        got, result = between(work, give, got)
    done = lax.dynamic_index_in_dim(total, r0 >> 1, 0, keepdims=False)
    return functools.reduce(lambda t, v: t + v.astype(F32), got, done), result


def reduce_list(parts):
    own, give = reduce_plane_give(reduce_core(parts)[0])
    return reduce_far(reduce_plane(own, give)[0])[0]


def column_kernel(count, s_ref, *refs):
    total = mm(refs[0][...], refs[1][...], ((0,), (0,)))
    for k in range(1, count):
        total = total + mm(refs[2 * k][...], refs[2 * k + 1][...], ((0,), (0,)))
    refs[-1][0] = total.astype(BF)


def column_blocks(pairs, cols, my_col):
    n, m = pairs[0][0].shape
    w = pairs[0][1].shape[1] // cols
    count = len(pairs)
    if w % 128:
        total = sum(mm(a, b, ((0,), (0,))) for a, b in pairs).astype(BF).reshape(m, cols, w).transpose(1, 0, 2)
        return jnp.take(total, jnp.arange(cols, dtype=jnp.int32) ^ my_col, axis=0)
    return pl.pallas_call(
        functools.partial(column_kernel, count),
        grid_spec=pltpu.PrefetchScalarGridSpec(
            num_scalar_prefetch=1, grid=(cols,),
            in_specs=[pl.BlockSpec((n, m), lambda k, s: (0, 0)), pl.BlockSpec((n, w), lambda k, s: (0, s[0] ^ k))] * count,
            out_specs=pl.BlockSpec((1, m, w), lambda k, s: (k, 0, 0))),
        out_shape=jax.ShapeDtypeStruct((cols, m, w), BF),
        compiler_params=pltpu.CompilerParams(vmem_limit_bytes=32 << 20),
        cost_estimate=pl.CostEstimate(flops=2 * count * n * m * w * cols, bytes_accessed=2 * (count * (n * m + n * w * cols) + m * w * cols), transcendentals=0),
    )(my_col.reshape(1), *[v for p in pairs for v in p])


def gelu_parts(v):
    phi = 0.5 * (1.0 + lax.erf(v * root_half))
    return v * phi, phi + v * jnp.exp(-0.5 * v * v) * inv_root_two_pi


def expert_kernel(cols, *refs):
    both, up, down = refs[:cols], refs[cols], refs[cols + 1]
    outs, acts, gps = refs[cols + 2:2 * cols + 2], refs[2 * cols + 2], refs[2 * cols + 3]
    width = up.shape[1]
    n = both[0].shape[1]
    rows = jnp.concatenate([b[0] for b in both], axis=0)
    act, slope = gelu_parts(mm(rows[:, :width], up[0]))
    act = act.astype(BF)
    acts[0] = act
    gp = (mm(rows[:, width:], down[0], ((1,), (1,))) * slope).astype(BF)
    gps[0] = gp
    out = mm(act, down[0]).astype(BF)
    gin = mm(gp, up[0], ((1,), (1,))).astype(BF)
    for c in range(cols):
        outs[c][0, :, :width] = out[c * n:(c + 1) * n]
        outs[c][0, :, width:] = gin[c * n:(c + 1) * n]


def weights_kernel(cols, sets, *refs):
    up, down = refs[-2:]
    step = cols + 2
    gu = gd = None
    width = up.shape[1]
    for s in range(sets):
        both, act, gp = refs[s * step:s * step + cols], refs[s * step + cols][0], refs[s * step + cols + 1][0]
        rows = jnp.concatenate([b[0] for b in both], axis=0)
        a = mm(rows[:, :width], gp, ((0,), (0,)))
        b = mm(act, rows[:, width:], ((0,), (0,)))
        gu, gd = (a, b) if gu is None else (gu + a, gd + b)
    up[0] = gu
    down[0] = gd


def per_expert(kernel, ins, shapes, flops):
    tok = lambda a: pl.BlockSpec((1,) + a.shape[1:], lambda e: (e, 0, 0))
    size = sum(a.size * 2 for a in ins) + sum(s.size * s.dtype.itemsize for s in shapes)
    return list(pl.pallas_call(
        kernel, grid=(ins[0].shape[0],),
        in_specs=[tok(a) for a in ins], out_specs=[tok(s) for s in shapes], out_shape=shapes,
        compiler_params=pltpu.CompilerParams(vmem_limit_bytes=(44 if len(ins) <= 12 else 56) << 20),
        cost_estimate=pl.CostEstimate(flops=flops, bytes_accessed=size, transcendentals=0),
    )(*ins))


def expert_both(bufs, up, down):
    cols = len(bufs)
    experts, d, f = up.shape
    n = bufs[0].shape[1]
    shapes = ([jax.ShapeDtypeStruct((experts, n, 2 * d), BF)] * cols
              + [jax.ShapeDtypeStruct((experts, n * cols, f), BF)] * 2)
    outs = per_expert(functools.partial(expert_kernel, cols), bufs + [up, down], shapes, 8 * experts * cols * n * d * f)
    return outs[:cols], outs[cols:]


def expert_weights(sets, d, f):
    cols = len(sets[0]) - 2
    experts, n, _ = sets[0][0].shape
    if len(sets) > 1 and len(sets) * cols > 8:
        return [sum(v) for v in zip(*[expert_weights([s], d, f) for s in sets])]
    shapes = [jax.ShapeDtypeStruct((experts, d, f), F32), jax.ShapeDtypeStruct((experts, f, d), F32)]
    return per_expert(functools.partial(weights_kernel, cols, len(sets)), [v for s in sets for v in s], shapes,
                      4 * experts * cols * n * d * f * len(sets))


def up_to(n, m):
    return -(-n // m) * m


def tiles_fit(w_in_x, w_xproj, w_out, conv_w, w_dt, w_router):
    return (w_in_x.shape == (96, 384) and w_xproj.shape[0] == 192 and w_xproj.shape[1] <= 26 and w_dt.shape[0] <= 6
            and conv_w.shape[0] + NS + 5 <= 26 and conv_w.shape[1] <= 128 and w_out.shape == (192, 192)
            and w_router.shape[0] <= 128 and w_router.shape[1] <= 16)


def one_hot(shape, match):
    i = lax.broadcasted_iota(jnp.int32, shape, 0)
    j = lax.broadcasted_iota(jnp.int32, shape, 1)
    return jnp.where(match(i, j), 1.0, 0.0).astype(BF)


def pack_kernel(wx, wdt, xp, cw, cb, db, al, ds, gx, gm, wz, wo, wr, first, other, s_ex, s_r):
    n = wx.shape[0]
    s_ex[...] = jnp.zeros_like(s_ex)
    s_r[...] = jnp.zeros_like(s_r)
    first[:n] = wx[...]
    s_ex[:xp.shape[0], :xp.shape[1]] = xp[...].astype(F32)
    wide = s_ex.shape[1] - 128
    at = 0
    for v in (cw, cb, db, al, ds, gx, gm):
        s_ex[at:at + v.shape[0], wide:wide + v.shape[1]] = v[...].astype(F32)
        at += v.shape[0]
    s_ex[26:26 + wdt.shape[0]] = wdt[...].astype(F32)
    first[n:] = s_ex[...].astype(BF)
    s_r[:wr.shape[0], :wr.shape[1]] = wr[...].astype(F32)

    def put(at, lane, v):
        other[at:at + v.shape[0], lane:lane + v.shape[1]] = v
    put_other(put, wz[...], wo[...])
    other[other.shape[0] - 16:] = s_r[...].astype(BF)


def put_other(put, z, out):
    n, m = z.shape[-2], out.shape[-2]
    put(0, 0, z[..., :256])
    put(n, 0, z[..., :n // 2, 256:])
    put(n, 128, z[..., n // 2:, 256:])
    at = n + n // 2
    put(at, 0, out[..., :m // 2, :128])
    put(at, 128, out[..., m // 2:, :128])
    put(at + m // 2, 0, jnp.concatenate([out[..., j * m // 4:(j + 1) * m // 4, 128:192] for j in range(4)], axis=-1))


def pack_params(w_in_x, w_dt, w_xproj, conv_w, conv_b, dt_bias, a_log, d_skip, gain_mix, gain_moe, w_in_z, w_out, w_router):
    n, lanes = w_in_x.shape
    ins = [w_in_x, w_dt, w_xproj.T, conv_w, conv_b[None], dt_bias[None], a_log, d_skip[None], gain_mix[None], gain_moe[None],
           w_in_z, w_out, w_router.T]
    vmem = pl.BlockSpec(memory_space=pltpu.VMEM)
    V = lambda *s: pltpu.VMEM(s, F32)
    return pl.pallas_call(
        pack_kernel, in_specs=[vmem] * len(ins), out_specs=[vmem] * 2,
        out_shape=[sds((n + 32, lanes), BF), sds((n + n // 2 + w_out.shape[0] * 3 // 4 + 16, 256), BF)],
        scratch_shapes=[V(32, lanes), V(16, 256)],
    )(*ins)


def each_block(masks, bufs, r0, c0):
    for buf, ms in zip(bufs, masks):
        for i, (rm, cm) in enumerate(ms):
            yield buf, i, r0 ^ rm, c0 ^ cm


def span(i, n):
    return pl.ds(pl.multiple_of(i * n, n), n)


def dt_match(j, i, dt_rows):
    k = j % 32 - 26
    return (k >= 0) & (k < dt_rows) & (j // 32 * dt_rows + k == i)


def unpack_first(masks, dims, me, *refs):
    dt_rows, xp_cols, xp_rows, share, gshare, taps, rows, cols = dims
    count = len(masks)
    bufs = refs[:count]
    fx, dt, xpT, par, an, a2, gx, gm, w_dt, w_xp, w_sm = refs[count:]
    n = bufs[0].shape[1] - 32
    lanes = bufs[0].shape[2]
    wide = lanes - 128
    for buf, i, r, c in each_block(masks, bufs, me[0], me[1]):
        fx[span(r, n), span(c, lanes)] = buf[i, :n]
        w_dt[span(r, 32), span(c, lanes)] = buf[i, n:]
        w_xp[span(c, 32), span(r, wide)] = buf[i, n:, :wide]
        w_sm[:, span(r * cols + c, 128)] = buf[i, n:, wide:]
    pick = one_hot((dt.shape[0], 32 * rows), lambda i, j: dt_match(j, i, dt_rows))
    dt[...] = mm(pick, w_dt[...]).astype(BF)
    pick = one_hot((xpT.shape[0], 32 * cols), lambda i, j: (j % 32 < xp_cols) & (j // 32 * xp_cols + j % 32 == i))
    t = mm(pick, w_xp[...])
    xpT[...] = jnp.concatenate([t[:, r * wide:r * wide + xp_rows] for r in range(rows)], axis=1).astype(BF)
    sm = w_sm[...].astype(F32)
    chan = jnp.concatenate([sm[:, p * 128:p * 128 + share] for p in range(rows * cols)], axis=1)
    par[:taps + 2] = chan[:taps + 2]
    par[taps + 2:] = chan[taps + 2 + NS:taps + 3 + NS]
    neg = -jnp.exp(chan[taps + 2:taps + 2 + NS])
    an[...] = neg
    a2[...] = neg * log2e
    gains = jnp.concatenate([sm[taps + 3 + NS:taps + 5 + NS, p * 128:p * 128 + gshare] for p in range(rows * cols)], axis=1)
    gx[...] = gains[:1]
    gm[...] = gains[1:]


def unpack_other(masks, dims, me, *refs):
    n, out_rows, out_lanes, r_cols, cols = dims
    count = len(masks)
    bufs = refs[:count]
    fz, fo, router, w_out, w_r = refs[count:]
    half = n // 2
    at = n + half
    m = out_rows
    for buf, i, r, c in each_block(masks, bufs, me[0], me[1]):
        fz[span(r, n), pl.ds(pl.multiple_of(c * 384, 128), 256)] = buf[i, :n]
        for j in range(2):
            rows = pl.ds(pl.multiple_of(r * n + j * half, 16), half)
            fz[rows, pl.ds(pl.multiple_of(c * 384 + 256, 128), 128)] = buf[i, n:at, j * 128:(j + 1) * 128]
            rows = pl.ds(pl.multiple_of(r * m + j * (m // 2), 16), m // 2)
            w_out[rows, span(2 * c, 128)] = buf[i, at:at + m // 2, j * 128:(j + 1) * 128]
        for j in range(4):
            rows = pl.ds(pl.multiple_of(r * m + j * (m // 4), 16), m // 4)
            w_out[rows, pl.ds(pl.multiple_of(c * 256 + 128, 128), 64)] = buf[i, at + m // 2:at + m * 3 // 4, j * 64:(j + 1) * 64]
        w_r[span(c, 16), span(r, 128)] = buf[i, at + m * 3 // 4:, :128]
    wide = w_out[...]
    fo[...] = jnp.concatenate([wide[:, c * 256:c * 256 + out_lanes] for c in range(cols)], axis=1)
    pick = one_hot((router.shape[0], 16 * cols), lambda i, j: (j % 16 < r_cols) & (j // 16 * r_cols + j % 16 == i))
    t = mm(pick, w_r[...])
    r_rows = router.shape[1] // (t.shape[1] // 128)
    router[...] = jnp.concatenate([t[:, r * 128:r * 128 + r_rows] for r in range(t.shape[1] // 128)], axis=1)


def unpack_call(kernel, gathered, dims, outs, scratch):
    masks = [ms for ms, _ in gathered]
    bufs = [b for _, b in gathered]
    me = jnp.stack([lax.axis_index("row"), lax.axis_index("col")]).astype(jnp.int32)
    vmem = pl.BlockSpec(memory_space=pltpu.VMEM)
    return pl.pallas_call(
        functools.partial(kernel, masks, dims),
        in_specs=[pl.BlockSpec(memory_space=pltpu.SMEM)] + [vmem] * len(bufs), out_specs=[vmem] * len(outs), out_shape=outs,
        scratch_shapes=[pltpu.VMEM(s, BF) for s in scratch],
        compiler_params=pltpu.CompilerParams(vmem_limit_bytes=28 << 20),
        cost_estimate=pl.CostEstimate(flops=0, bytes_accessed=4 * sum(b.size for b in bufs), transcendentals=0),
    )(me, *bufs)


def grad_x_kernel(count, dims, s_ref, *refs):
    dt_rows, xp_cols, xp_rows, share, gshare, rows, cols = dims
    pairs = refs[:2 * count]
    gwd, gxp, gpar, gmix, gmoe = (refs[(2 + i) * count:(3 + i) * count] for i in range(5))
    keep, give, w_dt, w_xp, w_sm, full = refs[7 * count:]
    k = pl.program_id(0)
    n, lanes = keep.shape[2] - 32, keep.shape[3]
    wide = lanes - 128
    total = lambda vs: functools.reduce(lambda a, b: a + b, [v[...] for v in vs])

    @pl.when(k == 0)
    def _():
        g = total(gwd).astype(BF)
        full[...] = sum_products(pairs)
        put = one_hot((32 * rows, g.shape[0]), lambda j, i: dt_match(j, i, dt_rows))
        w_dt[...] = mm(put, g).astype(BF)
        g = total(gxp).astype(BF)
        put = one_hot((32 * cols, g.shape[0]), lambda j, i: (j % 32 < xp_cols) & (j // 32 * xp_cols + j % 32 == i))
        t = mm(put, g)
        gap = jnp.zeros((t.shape[0], wide - xp_rows), F32)
        w_xp[...] = jnp.concatenate([v for r in range(rows) for v in (t[:, r * xp_rows:(r + 1) * xp_rows], gap)], axis=1).astype(BF)
        w_sm[...] = jnp.zeros_like(w_sm)
        par, mix, moe = total(gpar), total(gmix), total(gmoe)
        m = par.shape[0]
        for p in range(rows * cols):
            w_sm[:m, p * 128:p * 128 + share] = par[:, p * share:(p + 1) * share]
            w_sm[m:m + 1, p * 128:p * 128 + gshare] = mix[:, p * gshare:(p + 1) * gshare]
            w_sm[m + 1:m + 2, p * 128:p * 128 + gshare] = moe[:, p * gshare:(p + 1) * gshare]
    for j, out in enumerate((keep, give)):
        c = s_ref[0] ^ (2 * k + j)
        out[0, :, :n] = full[:, span(c, lanes)].astype(BF).reshape(rows, n, lanes)
        for r in range(rows):
            d = w_dt[r * 32:(r + 1) * 32, span(c, lanes)]
            out[0, r, n:, :wide] = w_xp[span(c, 32), r * wide:(r + 1) * wide] + d[:, :wide]
            out[0, r, n:, wide:] = (w_sm[:, span(r * cols + c, 128)] + d[:, wide:].astype(F32)).astype(BF)


def sum_products(pairs):
    return functools.reduce(lambda a, b: a + b, [mm(pairs[i][...], pairs[i + 1][...], TN) for i in range(0, len(pairs), 2)])


def grad_blocks(kernel, ins, scratch, block, rows, cols, my_col, flops, limit):
    out = sds((cols // 2, rows) + block, BF)
    return list(pl.pallas_call(
        kernel,
        grid_spec=pltpu.PrefetchScalarGridSpec(
            num_scalar_prefetch=1, grid=(cols // 2,), in_specs=[whole_spec(v) for v in ins],
            out_specs=[pl.BlockSpec((1, rows) + block, lambda k, s: (k, 0, 0, 0))] * 2, scratch_shapes=scratch),
        out_shape=[out, out],
        compiler_params=pltpu.CompilerParams(vmem_limit_bytes=limit << 20),
        cost_estimate=pl.CostEstimate(flops=flops, bytes_accessed=1 << 23, transcendentals=0),
    )(my_col.reshape(1), *ins))


def grad_x_blocks(pairs, smalls, dims, my_col):
    rows, cols = dims[-2:]
    n, m = pairs[0][0].shape
    inner = pairs[0][1].shape[1]
    lanes = inner // cols
    ins = [v for p in pairs for v in p] + [g[name] for name in ("dt", "xproj", "chan", "gain_mix", "gain_moe") for g in smalls]
    scratch = [pltpu.VMEM((32 * rows, inner), BF), pltpu.VMEM((32 * cols, (lanes - 128) * rows), BF), pltpu.VMEM((32, 128 * rows * cols), F32),
               pltpu.VMEM((m, inner), F32)]
    return grad_blocks(functools.partial(grad_x_kernel, len(pairs), dims), ins, scratch, (m // rows + 32, lanes), rows, cols, my_col,
                       2 * len(pairs) * n * m * inner, 44)


def grad_other_kernel(count, r_cols, s_ref, *refs):
    zs, outs, routers = refs[:2 * count], refs[2 * count:4 * count], refs[4 * count:5 * count]
    keep, give, full_z, full_o = refs[5 * count:]
    rows = keep.shape[1]
    k = pl.program_id(0)

    @pl.when(k == 0)
    def _():
        full_z[...] = sum_products(zs)
        full_o[...] = sum_products(outs)
    r = functools.reduce(lambda a, b: a + b, [v[...] for v in routers]).astype(BF)
    r_rows = r.shape[1] // rows
    for j, out in enumerate((keep, give)):
        c = s_ref[0] ^ (2 * k + j)
        z = full_z[:, pl.ds(pl.multiple_of(c * 384, 128), 384)].astype(BF)
        o = full_o[:, span(2 * k + j, 256)].astype(BF)
        z, o = (v.reshape(rows, v.shape[0] // rows, v.shape[1]) for v in (z, o))

        def put_block(at, lane, v):
            out[0, :, at:at + v.shape[1], lane:lane + v.shape[2]] = v
        put_other(put_block, z, o)
        w = mm(one_hot((16, r.shape[0]), lambda a, b: (a < r_cols) & (b == c * r_cols + a)), r).astype(BF)
        at = out.shape[2] - 16
        out[0, :, at:] = jnp.zeros((rows, 16, 256), BF)
        for q in range(rows):
            out[0, q, at:, :r_rows] = w[:, q * r_rows:(q + 1) * r_rows]


def grad_other_blocks(zs, outs, routers, block, rows, cols, r_cols, my_col):
    ins = [v for p in zs for v in p] + [v for p in outs for v in p] + list(routers)
    flops = 2 * sum(a.shape[0] * a.shape[1] * b.shape[1] for a, b in zs + outs)
    scratch = [pltpu.VMEM((a.shape[1], b.shape[1]), F32) for a, b in (zs[0], outs[0])]
    return grad_blocks(functools.partial(grad_other_kernel, len(zs), r_cols), ins, scratch, block, rows, cols, my_col, flops, 56)


def split_near_kernel(plan, s_ref, keep, got, own, *gives):
    for out, (ki, rm) in zip((own,) + gives, plan):
        p = (s_ref[0] ^ rm) & 1
        v = keep[ki, 0, p].astype(F32) + got[ki, 0, p].astype(F32)
        out[0] = v.astype(out.dtype)


def split_near(keep, got):
    plane = stages()[1]
    near, rows, n, lanes = keep.shape
    plan = [(cm >> 1, rm) for rm, cm in plane]
    view = (near, rows // 2, 2, n, lanes)
    outs = [sds((rows // 2, n, lanes), F32 if i == 0 else BF) for i in range(len(plan))]
    res = pl.pallas_call(
        functools.partial(split_near_kernel, plan),
        grid_spec=pltpu.PrefetchScalarGridSpec(
            num_scalar_prefetch=1, grid=(rows // 2,),
            in_specs=[pl.BlockSpec((near, 1, 2, n, lanes), lambda z, s: (0, z, 0, 0, 0))] * 2,
            out_specs=[pl.BlockSpec((1, n, lanes), lambda z, s: (z, 0, 0))] * len(outs)),
        out_shape=outs,
        compiler_params=pltpu.CompilerParams(vmem_limit_bytes=16 << 20),
        cost_estimate=pl.CostEstimate(flops=0, bytes_accessed=6 * keep.size, transcendentals=0),
    )(lax.axis_index("row").reshape(1), keep.reshape(view), got.reshape(view))
    return res[0], list(res[1:])


def split_far_kernel(count, plan, s_ref, own, *refs):
    gots, mine, gives = refs[:count], refs[count], refs[count + 1:]
    for out, rm in zip((mine,) + gives, plan):
        i = (s_ref[0] ^ rm) >> 1
        v = own[i]
        for g in gots:
            v = v + g[i].astype(F32)
        out[...] = v.astype(out.dtype)


def split_far(own, gots):
    plan = [rm for rm, _ in stages()[0]]
    _, n, lanes = own.shape
    outs = [sds((n, lanes), F32 if i == 0 else BF) for i in range(len(plan))]
    res = one_call(functools.partial(split_far_kernel, len(gots), plan), [own] + gots, outs, [lax.axis_index("row").reshape(1)])
    return res[0], list(res[1:])


def total_of(refs):
    return functools.reduce(lambda a, b: a + b[...].astype(F32), refs[1:], refs[0][...])


def finish_x_kernel(count, *refs):
    gx, gxp, gdt, gcw, gcb, gdb, gal, gds, gmix, gmoe, s = refs[count:]
    s[...] = total_of(refs[:count])
    n, lanes = gx.shape
    gx[...] = s[:n]
    gdt[...] = s[n + 26:n + 26 + gdt.shape[0]]
    wide = lanes - 128
    gxp[...] = s[n:n + gxp.shape[0], :gxp.shape[1]]
    at = n
    for ref in (gcw, gcb, gdb, gal, gds, gmix, gmoe):
        ref[...] = s[at:at + ref.shape[0], wide:wide + ref.shape[1]]
        at += ref.shape[0]


def finish_other_kernel(count, *refs):
    gz, go, gr, s = refs[count:]
    s[...] = total_of(refs[:count])
    n = gz.shape[0]
    half = n // 2
    gz[:, :256] = s[:n]
    gz[:half, 256:] = s[n:n + half, :128]
    gz[half:, 256:] = s[n:n + half, 128:]
    at = n + half
    m = go.shape[0]
    for j in range(2):
        go[j * m // 2:(j + 1) * m // 2, :128] = s[at:at + m // 2, j * 128:(j + 1) * 128]
    for j in range(4):
        go[j * m // 4:(j + 1) * m // 4, 128:] = s[at + m // 2:at + m * 3 // 4, j * 64:(j + 1) * 64]
    at += m * 3 // 4
    gr[...] = s[at:at + gr.shape[0], :gr.shape[1]]


def finish(kernel, mine, gots, shapes):
    ins = [mine] + gots
    vmem = pl.BlockSpec(memory_space=pltpu.VMEM)
    return pl.pallas_call(
        functools.partial(kernel, len(ins)), in_specs=[vmem] * len(ins), out_specs=[vmem] * len(shapes),
        out_shape=[sds(s) for s in shapes], scratch_shapes=[pltpu.VMEM(mine.shape, F32)],
    )(*ins)


def weights_part_kernel(cols, sets, lead, *refs):
    out = refs[-1]
    step = cols + 1
    total = None
    for s in range(sets):
        both, other = refs[s * step:s * step + cols], refs[s * step + cols][0]
        width = both[0].shape[2] // 2
        rows = jnp.concatenate([b[0, :, :width] if lead else b[0, :, width:] for b in both], axis=0)
        v = mm(rows, other, TN) if lead else mm(other, rows, TN)
        total = v if total is None else total + v
    out[0] = total


def expert_weights_part(sets, lead, d, f):
    cols = len(sets[0]) - 1
    experts, n, _ = sets[0][0].shape
    if len(sets) > 1 and len(sets) * cols > 8:
        return sum(expert_weights_part([s], lead, d, f) for s in sets)
    shape = (experts, d, f) if lead else (experts, f, d)
    return per_expert(functools.partial(weights_part_kernel, cols, len(sets), lead), [v for s in sets for v in s],
                      [sds(shape)], 2 * experts * cols * n * d * f * len(sets))[0]


def params_generic(w_in_x, w_in_z, conv_w, conv_b, w_xproj, w_dt, dt_bias, a_log, d_skip, w_out, gain_mix, gain_moe, w_router):
    rows, cols = lax.axis_size("row"), lax.axis_size("col")
    parts = rows * cols
    inner, width = w_in_x.shape[1] * cols, w_in_x.shape[0] * rows
    small = jnp.concatenate([conv_w, conv_b[None], dt_bias[None], a_log, d_skip[None],
                             jnp.concatenate([gain_mix, gain_moe])[None]], axis=0)
    flat = [w_xproj.reshape(-1), w_dt.reshape(-1), w_router.reshape(-1), small.reshape(-1)]
    sizes = [f.shape[0] for f in flat]
    lanes = w_in_x.shape[1]
    extra = -(-sum(sizes) // (16 * lanes)) * 16
    flat = jnp.pad(jnp.concatenate(flat), (0, extra * lanes - sum(sizes))).reshape(extra, lanes)
    here, out_rows, out_lanes = w_in_x.shape[0], w_out.shape[0], w_out.shape[1]
    wide = -(-out_lanes // 128) * 128
    first = gather_list(jnp.concatenate([w_in_x, flat], axis=0))
    full_x, rest = assemble(first, [((0, here, lanes), 0, put_block), ((here, extra, lanes), 1, put_pair)],
                            [(width, inner), (rows, cols, extra, lanes)])
    far_end = first[len(first) // 2 - 1][1]
    late_z, late_o, _ = lax.optimization_barrier((w_in_z, jnp.pad(w_out, ((0, 0), (0, wide - out_lanes))), far_end))
    (full_z,) = assemble(gather_list(late_z), [((0, here, lanes), 0, put_block)], [(width, inner)])
    (wide_out,) = assemble(gather_list(late_o), [((0, out_rows, wide), 0, put_block)], [(inner, cols * wide)])
    lane_of = jnp.arange(cols * wide, dtype=jnp.int32)
    narrow = jnp.where(lane_of % wide < out_lanes, lane_of // wide * out_lanes + lane_of % wide, -1)
    narrow = (narrow[:, None] == jnp.arange(width, dtype=jnp.int32)[None, :]).astype(BF)
    full_out = mm(wide_out, narrow).astype(BF)
    def whole(blocks):
        return blocks.transpose(0, 2, 1, 3).reshape(blocks.shape[0] * blocks.shape[2], -1)
    rest = rest.reshape(rows, cols, extra * lanes)
    cut = [0]
    for n in sizes:
        cut.append(cut[-1] + n)
    full_xpT = whole(rest[:, :, cut[0]:cut[1]].reshape((rows, cols) + w_xproj.shape)).T
    full_dt = whole(rest[:, :, cut[1]:cut[2]].reshape((rows, cols) + w_dt.shape))
    router_f = whole(rest[:, :, cut[2]:cut[3]].reshape((rows, cols) + w_router.shape)).astype(F32).T
    small = rest[:, :, cut[3]:cut[4]].reshape((parts,) + small.shape).transpose(1, 0, 2).astype(F32)
    chan = small[:-1].reshape(-1, inner)
    taps = conv_w.shape[0]
    par = jnp.concatenate([chan[:taps + 2], chan[taps + 2 + NS:]], axis=0)
    a_neg = -jnp.exp(chan[taps + 2:taps + 2 + NS])
    a_two = a_neg * log2e
    gain_mix_f = small[-1, :, :gain_mix.shape[0]].reshape(1, width)
    gain_moe_f = small[-1, :, gain_mix.shape[0]:].reshape(1, width)
    return lambda done: (full_z, full_out, router_f, done), full_x, full_xpT, full_dt, par, a_neg, a_two, gain_mix_f, gain_moe_f


def params_tiled(w_in_x, w_in_z, conv_w, conv_b, w_xproj, w_dt, dt_bias, a_log, d_skip, w_out, gain_mix, gain_moe, w_router):
    rows, cols = lax.axis_size("row"), lax.axis_size("col")
    here, lanes = w_in_x.shape
    inner, width = lanes * cols, here * rows
    taps, share = conv_w.shape
    packed, other = pack_params(w_in_x, w_dt, w_xproj, conv_w, conv_b, dt_bias, a_log, d_skip, gain_mix, gain_moe, w_in_z,
                                w_out, w_router)
    mine = gather_far(packed)
    other, _ = lax.optimization_barrier((other, mine))
    mine_o = gather_far(other)
    near = gather_plane(mine)
    mine_o, _ = lax.optimization_barrier((mine_o, near[-1]))
    near_o = gather_plane(mine_o)
    first = gather_core(near)
    dims = (w_dt.shape[0], w_xproj.shape[1], w_xproj.shape[0], share, gain_mix.shape[0], taps, rows, cols)
    full_x, full_dt, full_xpT, par, a_neg, a_two, gx, gm = unpack_call(
        unpack_first, first, dims,
        [sds((width, inner), BF), sds((w_dt.shape[0] * rows, inner), BF), sds((w_xproj.shape[1] * cols, inner), BF),
         sds((taps + 3, inner)), sds((NS, inner)), sds((NS, inner)), sds((1, width)), sds((1, width))],
        [(32 * rows, inner), (32 * cols, (lanes - 128) * rows), (32, 128 * rows * cols)])

    def rest(done):
        o, done = lax.optimization_barrier((near_o, done))
        full_z, full_out, router_f = unpack_call(
            unpack_other, gather_core(o), (here, w_out.shape[0], w_out.shape[1], w_router.shape[1], cols),
            [sds((width, inner), BF), sds((inner, width), BF), sds((w_router.shape[1] * cols, width))],
            [(inner, 256 * cols), (16 * cols, 128 * rows)])
        return full_z, full_out, router_f, done
    return rest, full_x, full_xpT, full_dt, par, a_neg, a_two, gx, gm


def grads_generic(nms, gateds, gs, total, w_in_x, w_in_z, w_xproj, w_dt, w_out, w_router, gain_mix, conv_w):
    rows, cols = lax.axis_size("row"), lax.axis_size("col")
    parts = rows * cols
    my_col = lax.axis_index("col")
    here, lanes = w_in_x.shape
    out_rows, out_lanes = w_out.shape
    wide = up_to(out_lanes, 128)
    share = conv_w.shape[1]
    sizes = [w_xproj.size, w_dt.size, w_router.size, (conv_w.shape[0] + 4 + NS) * share]
    extra = up_to(-(-sum(sizes) // lanes), 16)
    cut = [sum(sizes[:i]) for i in range(5)]
    grad_out = sum(mm(k[1], r["gm"], TN) for k, r in zip(zip(nms, gateds), gs)).astype(BF)
    grad_out_block = reduce_list([grad_out[:, k * wide:(k + 1) * wide].reshape(rows, out_rows, wide) for k in range(cols)])
    grad_out_block = grad_out_block[:, :out_lanes]
    grad_in_z = column_blocks([(k[0], r["gz"]) for k, r in zip(zip(nms, gateds), gs)], cols, my_col)
    grad_z_block = reduce_list([grad_in_z[k].reshape(rows, here, lanes) for k in range(cols)])
    grad_in_x = column_blocks([(k[0], r["gi"]) for k, r in zip(zip(nms, gateds), gs)], cols, my_col)

    def blocks(g, like):
        r, c = like.shape
        return g.astype(BF).reshape(rows, r, cols, c).transpose(0, 2, 1, 3).reshape(rows, cols, -1)
    gsmall = total["chan"].astype(BF)
    ggain = jnp.concatenate([total["gain_mix"].reshape(parts, 1, -1), total["gain_moe"].reshape(parts, 1, -1)], axis=2)
    gsmall = jnp.concatenate([gsmall.reshape(-1, parts, share).transpose(1, 0, 2), ggain.astype(BF)], axis=1)
    gflat = jnp.concatenate([blocks(total["xproj"].T, w_xproj), blocks(total["dt"], w_dt), blocks(total["router"].T, w_router),
                             gsmall.reshape(rows, cols, -1)], axis=2)
    gflat = jnp.pad(gflat, ((0, 0), (0, 0), (0, extra * lanes - sum(sizes)))).reshape(rows, cols, extra, lanes)
    done = reduce_list([jnp.concatenate([grad_in_x[k].reshape(rows, here, lanes),
                                         lax.dynamic_index_in_dim(gflat, my_col ^ k, 1, keepdims=False)], axis=1)
                        for k in range(cols)])
    grad_x_block = done[:here]
    done = done[here:].reshape(-1)
    sm = done[cut[3]:cut[4]].reshape(-1, share)
    gm = gain_mix.shape[0]
    taps = conv_w.shape[0]
    chan = (sm[:taps], sm[taps], sm[taps + 1], sm[taps + 2:taps + 2 + NS], sm[taps + 2 + NS])
    small = (done[cut[0]:cut[1]].reshape(w_xproj.shape), done[cut[1]:cut[2]].reshape(w_dt.shape), chan, sm[-1, :gm], sm[-1, gm:],
             done[cut[2]:cut[3]].reshape(w_router.shape))
    return (grad_x_block, grad_z_block, grad_out_block), small


def on_device(tokens, w_in_x, w_in_z, conv_w, conv_b, w_xproj, w_dt, dt_bias, a_log, d_skip, w_out,
              gain_mix, gain_moe, w_router, w_up, w_down, routes, lengths, cotangent):
    rows, cols = lax.axis_size("row"), lax.axis_size("col")
    parts = rows * cols
    my_col = lax.axis_index("col")
    seqs, length, width = tokens.shape
    experts_here = w_up.shape[0]
    experts_all = experts_here * rows
    inner = w_in_x.shape[1] * cols
    count = seqs * length
    xp = w_xproj.shape[1] * cols
    share = inner // parts

    tiled = tiles_fit(w_in_x, w_xproj, w_out, conv_w, w_dt, w_router)
    here, lanes = w_in_x.shape
    out_rows, out_lanes = w_out.shape
    wide = up_to(out_lanes, 128)
    taps = conv_w.shape[0]
    rest_of, full_x, full_xpT, full_dt, par, a_neg, a_two, gain_mix_f, gain_moe_f = (
        params_tiled if tiled else params_generic)(
            w_in_x, w_in_z, conv_w, conv_b, w_xproj, w_dt, dt_bias, a_log, d_skip, w_out, gain_mix, gain_moe, w_router)
    lane_of = jnp.arange(cols * wide, dtype=jnp.int32)
    shifted = jnp.where(lane_of % wide < out_lanes, (lane_of // wide ^ my_col) * out_lanes + lane_of % wide, -1)
    shifted = (jnp.arange(width, dtype=jnp.int32)[:, None] == shifted[None, :]).astype(BF)

    half = experts_here * CAP
    message = -(-2 * half // 8) * 8
    group = -(-rows * CAP // 16) * 16
    slots = rows * message

    def mixer(s, x, limit):
        nm, inner_x, conv, u, dl, pT, ssm, starts = mixer_forward(x, gain_mix_f, full_x, full_xpT, full_dt, par, a_two, QB, limit)
        return dict(x=x, s=s, nm=nm, inner=inner_x, conv=conv, u=u, dl=dl, pT=pT, ssm=ssm.reshape(length, inner), starts=starts)

    def router(k, route, n_live, grad):
        n_live = n_live.reshape(1)
        z, gated, hidden, target, outgoing, probs, gate = one_call(
            functools.partial(route_kernel, CAP, experts_here, message, k["s"]),
            [k["x"], k["nm"], k["ssm"], full_z, full_out, gain_moe_f, router_f, route, grad],
            [sds((length, inner)), sds((length, inner), BF), sds((length, width)), sds((length, 1), jnp.int32),
             sds((slots, width), BF), sds((length, experts_all)), sds((length, 1))],
            [n_live], 6 * length * inner * width)
        kept = dict(k, z=z, gated=gated, hidden=hidden, target=target, probs=probs, gate=gate, route=route, n_live=n_live, cot=grad)
        return outgoing, kept

    def home(rows_out):
        return lax.all_to_all(rows_out, "row", split_axis=0, concat_axis=0, tiled=True)

    def arrive(got):
        (out,) = one_call(functools.partial(sort_kernel, CAP, message, half, group), [got], [sds((experts_here * group, 2 * width), BF)],
                          (), 4 * slots * experts_here * group * width, 24)
        return out.reshape(experts_here, group, 2 * width)

    def gather_cols(own):
        bufs = [own]
        for bit in bits_of("col")[::-1]:
            bufs = bufs + [swap(v, "col", bit) for v in bufs]
        return bufs

    def from_experts(bufs):
        for bit in bits_of("col"):
            mid = len(bufs) // 2
            bufs = [(a.astype(F32) + swap(b, "col", bit).astype(F32)).astype(BF) for a, b in zip(bufs[:mid], bufs[mid:])]
        (out,) = one_call(functools.partial(unsort_kernel, CAP, message, half, group), [bufs[0].reshape(experts_here * group, 2 * width)],
                          [sds((slots, width), BF)], (), 4 * slots * experts_here * group * width, 24)
        return out

    def unroute(k, back):
        mixed_out, gh, gs, gz, gm, g_router, g_moe = one_call(
            functools.partial(unroute_kernel, k["s"], half),
            [back, k["target"], k["hidden"], k["probs"], k["gate"], k["route"], k["cot"], gain_moe_f, router_f, full_out, shifted,
             k["z"], k["ssm"]],
            [sds((length, width), BF), sds((length, width)), sds((length, inner)), sds((length, inner), BF),
             sds((length, cols * wide), BF), sds((experts_all, width)), sds((1, width))],
            [k["n_live"]], 6 * length * inner * width)
        return dict(mixed_out=mixed_out, gh=gh, gs=gs.reshape(k["u"].shape), gz=gz, gm=gm, router=g_router, gain_moe=g_moe)

    def unscan(k, gs, limit):
        gi, g_xp, g_dt, g_chan = scan_backward(k["u"], k["dl"], gs, k["conv"], k["inner"], k["pT"], k["starts"], full_xpT, full_dt, par, a_neg, limit)
        return dict(gi=gi, xproj=g_xp, dt=g_dt, chan=g_chan)

    def unproject(k, g):
        grad_tokens, g_mix = one_call(
            token_kernel, [g["gi"], g["gz"], full_x, full_z, k["x"], g["gh"], gain_mix_f], [sds((length, width)), sds((1, width))], (),
            4 * length * inner * width, 24)
        return dict(tokens=grad_tokens, gain_mix=g_mix)

    after = lax.optimization_barrier
    ks, owns, last = [], [], None
    for s in range(seqs):
        x = tokens[s]
        if last is not None:
            x, last = after((x, last))
        k = mixer(s, x, 24 if s == 0 else 48)
        if s == 0:
            full_z, full_out, router_f, k["ssm"] = rest_of(k["ssm"])
        before, (last, k) = last, router(k, routes[s], lengths[s], cotangent)
        ks.append(k)
        if before is not None:
            got, last = after((home(before), last))
            owns.append(arrive(got))
    owns.append(arrive(home(last)))
    sets, sent = [], []
    for s in range(seqs):
        bufs = gather_cols(owns[s])
        if s == seqs - 2:
            bufs, owns[-1] = after((bufs, owns[-1]))
        outs, more = expert_both(bufs, w_up, w_down)
        sets.append((bufs, more))
        sent.append(from_experts(outs))
    backs = [home(v) for v in sent]
    grads_w = []
    for lead in (True, False):
        ins, sent[0], _ = after(([b + [v[1 if lead else 0]] for b, v in sets], sent[0], grads_w))
        grads_w.append(expert_weights_part(ins, lead, width, w_up.shape[2]))
    backs[0], (grad_w_up, grad_w_down) = after((backs[0], grads_w))
    gs_ = []
    for s in range(seqs):
        g = unroute(ks[s], backs[s])
        gs_.append(g)
        if s + 1 < seqs:
            g["gs"], sent[s + 1] = after((g["gs"], sent[s + 1]))
            g.update(unscan(ks[s], g["gs"], 52))
            g["gi"], backs[s + 1] = after((g["gi"], backs[s + 1]))
    g = gs_[-1]
    nms, gateds = [k["nm"] for k in ks], [k["gated"] for k in ks]
    if tiled:
        block = (here + here // 2 + out_rows * 3 // 4 + 16, 256)
        keep, give = grad_other_blocks([(v, q["gz"]) for v, q in zip(nms, gs_)], [(v, q["gm"]) for v, q in zip(gateds, gs_)],
                                       [q["router"] for q in gs_], block, rows, cols, w_router.shape[1], my_col)
        far, plane, core = stages()

        def first_tokens(v):
            return unproject(ks[0], dict(gs_[0], gi=after((gs_[0]["gi"], v))[0]))
        got, first = between(first_tokens, give, exchange(give, core))
        if seqs > 1:
            gs_[0].update(first)
        own, gives = split_near(keep, got)
        g["gs"], gives = after((g["gs"], gives))
        gots = [exchange(v, p) for v, p in zip(gives, plane[1:])]
        g.update(unscan(ks[-1], g["gs"], 24))
        dims = (w_dt.shape[0], w_xproj.shape[1], w_xproj.shape[0], conv_w.shape[1], gain_mix.shape[0], rows, cols)
        for s in range(1, seqs):
            gs_[s].update(unproject(ks[s], gs_[s]))
        keep, give = grad_x_blocks([(v, q["gi"]) for v, q in zip(nms, gs_)], gs_, dims, my_col)
        gots, give = after((gots, give))
        got = exchange(give, core)
        mine_o, gives = split_far(own, gots)
        got, gives = after((got, gives))
        gots_o = [exchange(v, p) for v, p in zip(gives, far[1:])]
        own, gives = split_near(keep, got)
        gots = [exchange(v, p) for v, p in zip(gives, plane[1:])]
        gots_o, _ = after((gots_o, gives))
        gz, go, g_router = finish(finish_other_kernel, mine_o, gots_o, [w_in_z.shape, w_out.shape, w_router.shape[::-1]])
        gots, gz, go, g_router = after((gots, gz, go, g_router))
        mine, gives = split_far(own, gots)
        gots = [exchange(v, p) for v, p in zip(gives, far[1:])]
        share, gshare = conv_w.shape[1], gain_mix.shape[0]
        gx, g_xproj, g_dt, gcw, gcb, gdb, gal, gds, g_mix, g_moe = finish(
            finish_x_kernel, mine, gots,
            [w_in_x.shape, w_xproj.shape[::-1], w_dt.shape, conv_w.shape, (1, share), (1, share), a_log.shape, (1, share), (1, gshare), (1, gshare)])
        blocks = (gx, gz, go)
        small = (g_xproj.T, g_dt, (gcw, gcb[0], gdb[0], gal, gds[0]), g_mix[0], g_moe[0], g_router.T)
    else:
        g.update(unscan(ks[-1], g["gs"], 24))
        for k, q in zip(ks, gs_):
            q.update(unproject(k, q))
        names = ("xproj", "dt", "chan", "gain_mix", "gain_moe", "router")
        total = {n: sum(q[n] for q in gs_) for n in names}
        blocks, small = grads_generic(nms, gateds, gs_, total, w_in_x, w_in_z, w_xproj, w_dt, w_out, w_router, gain_mix, conv_w)
    g_xproj, g_dt, (gcw, gcb, gdb, gal, gds), g_mix, g_moe, g_router = small
    return (
        jnp.stack([q["mixed_out"] for q in gs_]),
        jnp.stack([q["tokens"] for q in gs_]),
        blocks[0],
        blocks[1],
        gcw,
        gcb,
        g_xproj,
        g_dt,
        gdb,
        gal,
        gds,
        blocks[2],
        g_mix,
        g_moe,
        g_router,
        grad_w_up,
        grad_w_down,
    )


def solution(mesh):
    tok = P(("row", "col"), None, None)
    mat = P("row", "col")
    vec = P(("row", "col"))
    chan = P(None, ("row", "col"))
    up, down = P("row", None, "col"), P("row", "col", None)
    return jax.shard_map(
        on_device,
        mesh=mesh,
        in_specs=(tok, mat, mat, chan, vec, mat, mat, vec, chan, vec, mat, vec, vec, mat, up, down, tok, vec, tok),
        out_specs=(tok, tok, mat, mat, chan, vec, mat, mat, vec, chan, vec, mat, vec, vec, mat, up, down),
        check_vma=False,
    )
```

```python
import functools
import jax
import jax.numpy as jnp
from jax import lax
from jax.sharding import PartitionSpec as P
from jax.experimental import pallas as pl
from jax.experimental.pallas import tpu as pltpu
NS = 16
F32 = jnp.float32
SLOT_OF=[4*((i>>2)&1)+2*(1-((i>>1)&1))+(1-(i&1)) for i in range(8)]
def merge8(rows):
    idx=lax.broadcasted_iota(jnp.int32,(8,128),0)
    m4=idx<4; m2=(idx&2)!=0; m1=(idx&1)!=0
    p=[None]*8
    for i in range(8): p[SLOT_OF[i]]=rows[i]
    r=[jnp.where(m4,p[k],p[k+4])+pltpu.roll(jnp.where(m4,p[k+4],p[k]),4,0) for k in range(4)]
    def half(x,y,m,d):
        return jnp.where(m,x+pltpu.roll(x,d,0),y+pltpu.roll(y,8-d,0))
    v=[half(r[k],r[k+2],m2,2) for k in range(2)]
    return half(v[0],v[1],m1,1)
def mm(a, b, dims=((1,), (0,)), **kw):
    return lax.dot_general(a, b, (dims, ((), ())), preferred_element_type=F32, **kw)


NT = ((1,), (1,))
TN = ((0,), (0,))


def softplus(v):
    e = jnp.exp(-jnp.abs(v))
    tiny = e * (1.0 - e * (0.5 - e * (1.0 / 3.0 - e * 0.25)))
    return jnp.maximum(v, 0.0) + jnp.where(e < 0.01, tiny, jnp.log(1.0 + e))


def sigmoid_of_softplus(d):
    tiny = d * (1.0 - d * (0.5 - d * (1.0 / 6.0 - d * (1.0 / 24.0))))
    return jnp.where(d < 0.03, tiny, 1.0 - jnp.exp(-d))


def sigmoid(v):
    return 1.0 / (1.0 + jnp.exp(-v))


def spread(dst, src, T):
    for j in range(T):
        dst[j] = jnp.broadcast_to(src[:, j:j + 1], (NS, 128))


def fold(x):
    return x[0:8] + x[8:16]


def convolve(ext, w, b, T):
    taps = w.shape[0]
    out = b
    for k in range(taps):
        out = out + w[k:k + 1] * ext[9 - taps + k:9 - taps + k + T]
    return out


def mixer_kernel(T, Q, R, x_ref, gain_ref, wx_ref, xpT_ref, wdt_ref, par_ref, a2_ref,
                 nm_ref, in_ref, cv_ref, u_ref, dl_ref, pT_ref, y_ref, st_ref, state, bx, cx, du):
    c = pl.program_id(0)
    L, DI = nm_ref.shape[0], wx_ref.shape[1]
    taps = par_ref.shape[0] - 3

    @pl.when(c == 0)
    def _():
        state[...] = jnp.zeros_like(state)
        x = x_ref[...].astype(F32)
        nm = (x * lax.rsqrt(jnp.mean(x * x, axis=-1, keepdims=True) + 1e-05) * gain_ref[...]).astype(jnp.bfloat16)
        nm_ref[...] = nm
        in_ref[0:8] = jnp.zeros((8, DI), F32)
        in_ref[8:] = mm(nm, wx_ref[...])
    st_ref[0] = state[...]
    par = par_ref[...]
    skip = par[taps + 2:taps + 3]
    conv = convolve(in_ref[pl.ds(pl.multiple_of(c * T, 8), T + 8)], par[:taps], par[taps:taps + 1], T)
    cv_ref[0] = conv.reshape(T // 8, 8, DI)
    u = conv * sigmoid(conv)
    u_ref[0] = u.reshape(T // 8, 8, DI)
    pT = mm(xpT_ref[...], u.astype(jnp.bfloat16), NT)
    pT_ref[0] = pT
    d = softplus(mm(pT[:R].astype(jnp.bfloat16), wdt_ref[...], TN) + par[taps + 1:taps + 2])
    dl_ref[0] = d.reshape(T // 8, 8, DI)
    du[...] = (d * u).reshape(T // 8, 8, DI)
    spread(bx, pT[R:R + NS], T)
    spread(cx, pT[R + NS:R + 2 * NS], T)

    def grp(g, _):
        base = pl.multiple_of(g * (Q * 128), 128)
        lanes = [pl.ds(base + q * 128, 128) for q in range(Q)]
        a = [a2_ref[:, ln] for ln in lanes]
        sk = [par_ref[taps + 2:taps + 3, ln] for ln in lanes]

        def tb(i, s):
            s = list(s)
            rows = [[] for _ in range(Q)]
            for k in range(8):
                t = i * 8 + k
                b = bx[t]
                cc = cx[t]
                for q in range(Q):
                    dd = dl_ref[0, i, k:k + 1, lanes[q]]
                    dub = du[i, k:k + 1, lanes[q]]
                    s[q] = jnp.exp2(dd * a[q]) * s[q] + b * dub
                    rows[q].append(fold(s[q] * cc))
            for q in range(Q):
                y_ref[0, i, :, lanes[q]] = merge8(rows[q]) + sk[q] * u_ref[0, i, :, lanes[q]]
            return tuple(s)
        s = lax.fori_loop(0, T // 8, tb, tuple(state[:, ln] for ln in lanes))
        for q in range(Q):
            state[:, lanes[q]] = s[q]
        return 0
    lax.fori_loop(0, DI // (Q * 128), grp, 0)


def whole_spec(a):
    return pl.BlockSpec(a.shape, lambda *_: (0,) * len(a.shape))


def sds(shape, dtype=F32):
    return jax.ShapeDtypeStruct(shape, dtype)


def mixer_forward(x, gain, wx, xpT, wdt, par, a2, T, limit, Q=6):
    L, D = x.shape
    DI = wx.shape[1]
    C, XP, R = L // T, xpT.shape[0], wdt.shape[0]
    ins = [x, gain, wx, xpT, wdt, par, a2]
    rows = pl.BlockSpec((1, T // 8, 8, DI), lambda c: (c, 0, 0, 0))
    big = sds((C, T // 8, 8, DI))
    nm, inner = sds((L, D), jnp.bfloat16), sds((L + 8, DI))
    return pl.pallas_call(
        functools.partial(mixer_kernel, T, Q, R), grid=(C,),
        in_specs=[whole_spec(a) for a in ins],
        out_specs=[whole_spec(nm), whole_spec(inner), rows, rows, rows, pl.BlockSpec((1, XP, T), lambda c: (c, 0, 0)), rows,
                   pl.BlockSpec((1, NS, DI), lambda c: (c, 0, 0))],
        out_shape=[nm, inner, big, big, big, sds((C, XP, T)), big, sds((C, NS, DI))],
        scratch_shapes=[pltpu.VMEM((NS, DI), F32), pltpu.VMEM((T, NS, 128), F32), pltpu.VMEM((T, NS, 128), F32),
                        pltpu.VMEM((T // 8, 8, DI), F32)],
        compiler_params=pltpu.CompilerParams(vmem_limit_bytes=limit << 20),
        cost_estimate=pl.CostEstimate(flops=40000000000, bytes_accessed=16 * L * DI, transcendentals=0),
    )(*ins)


def scan_back_kernel(T, Q, Q2, R, u_ref, dl_ref, gs_ref, cv_ref, in_ref, pT_ref, st_ref, xpT_ref, wdt_ref, par_ref, an_ref,
                     gi_ref, gxp_ref, gwd_ref, gpar_ref, carry, later, bx, cx, du, guc, gdt, hs, ds, gbp, gcp, sums):
    j = pl.program_id(0)
    c = pl.num_programs(0) - 1 - j
    DI = wdt_ref.shape[1]
    taps = par_ref.shape[0] - 3

    @pl.when(j == 0)
    def _():
        for ref in (carry, later, gxp_ref, gwd_ref, gpar_ref, sums):
            ref[...] = jnp.zeros_like(ref)
    pT = pT_ref[0]
    spread(bx, pT[R:R + NS], T)
    spread(cx, pT[R + NS:R + 2 * NS], T)
    du[...] = dl_ref[0] * u_ref[0]
    gbp[...] = jnp.zeros_like(gbp)
    gcp[...] = jnp.zeros_like(gcp)
    W = Q * 128

    def grp(g, _):
        base = pl.multiple_of(g * W, 128)
        lanes = [pl.ds(base + q * 128, 128) for q in range(Q)]
        loc = [slice(q * 128, q * 128 + 128) for q in range(Q)]
        an = [an_ref[:, ln] for ln in lanes]
        a2 = [v * 1.4426950408889634 for v in an]

        def tb(i, s):
            s = list(s)
            for k in range(8):
                t = i * 8 + k
                b = bx[t]
                gc = gcp[t]
                for q in range(Q):
                    dd = dl_ref[0, i, k:k + 1, lanes[q]]
                    dub = du[i, k:k + 1, lanes[q]]
                    gsr = gs_ref[0, i, k:k + 1, lanes[q]]
                    dec = jnp.exp2(dd * a2[q])
                    h = dec * s[q]
                    ds[t, :, loc[q]] = dec
                    hs[t, :, loc[q]] = h
                    s[q] = h + b * dub
                    gc = gc + s[q] * gsr
                gcp[t] = gc
            return tuple(s)
        lax.fori_loop(0, T // 8, tb, tuple(st_ref[0, :, ln] for ln in lanes))
        for q0 in range(0, Q, Q2):
            qs = range(q0, q0 + Q2)
            sk = {q: par_ref[taps + 2:taps + 3, lanes[q]] for q in qs}

            def rb(jj, cr):
                i = T // 8 - 1 - jj
                g_, ga = {q: cr[0][q - q0] for q in qs}, {q: cr[1][q - q0] for q in qs}
                gbs, gsk = list(cr[2]), list(cr[3])
                m1, m2 = {q: [None] * 8 for q in qs}, {q: [None] * 8 for q in qs}
                for k in range(7, -1, -1):
                    t = i * 8 + k
                    b = bx[t]
                    cc = cx[t]
                    gb = gbp[t]
                    for q in qs:
                        dd = dl_ref[0, i, k:k + 1, lanes[q]]
                        dub = du[i, k:k + 1, lanes[q]]
                        gsr = gs_ref[0, i, k:k + 1, lanes[q]]
                        gg = gsr * cc + g_[q]
                        g_[q] = gg * ds[t, :, loc[q]]
                        qq = gg * hs[t, :, loc[q]]
                        m1[q][k] = fold(gg * b)
                        m2[q][k] = fold(qq * an[q])
                        ga[q] = ga[q] + qq * dd
                        gb = gb + gg * dub
                    gbp[t] = gb
                for q in qs:
                    s1 = merge8(m1[q])
                    s2 = merge8(m2[q])
                    u8, d8, gs8 = u_ref[0, i, :, lanes[q]], dl_ref[0, i, :, lanes[q]], gs_ref[0, i, :, lanes[q]]
                    guc[i, :, lanes[q]] = d8 * s1 + sk[q] * gs8
                    gd = (s2 + u8 * s1) * sigmoid_of_softplus(d8)
                    gdt[i, :, lanes[q]] = gd
                    gbs[q - q0] = gbs[q - q0] + gd
                    gsk[q - q0] = gsk[q - q0] + gs8 * u8
                return (tuple(g_[q] for q in qs), tuple(ga[q] for q in qs), tuple(gbs), tuple(gsk))
            z8 = tuple(jnp.zeros((8, 128), F32) for q in qs)
            cr = lax.fori_loop(0, T // 8, rb, (tuple(carry[:, lanes[q]] for q in qs),
                                               tuple(jnp.zeros((NS, 128), F32) for q in qs), z8, z8), unroll=4)
            for q in qs:
                carry[:, lanes[q]] = cr[0][q - q0]
                gpar_ref[taps + 2:taps + 2 + NS, lanes[q]] += cr[1][q - q0] * an[q]
                sums[taps + 1, :, lanes[q]] += cr[2][q - q0]
                sums[taps + 2, :, lanes[q]] += cr[3][q - q0]
        return 0
    lax.fori_loop(0, DI // W, grp, 0)

    gbT = jnp.sum(gbp[...], axis=2).T
    gcT = jnp.sum(gcp[...], axis=2).T
    gd = gdt[...].reshape(T, DI).astype(jnp.bfloat16)
    gpT = jnp.concatenate([mm(wdt_ref[...], gd, NT), gbT, gcT], axis=0).astype(jnp.bfloat16)
    gwd_ref[...] += mm(pT[:R].astype(jnp.bfloat16), gd)
    gxp_ref[...] += mm(gpT, u_ref[0].reshape(T, DI).astype(jnp.bfloat16))
    gu = guc[...].reshape(T, DI) + mm(gpT, xpT_ref[...], TN)
    par = par_ref[...]
    conv = cv_ref[0].reshape(T, DI)
    sig = sigmoid(conv)
    gconv = gu * (sig * (1.0 + conv * (1.0 - sig)))
    part = lambda v: jnp.sum(v.reshape(T // 8, 8, DI), axis=0)
    sums[taps] += part(gconv)
    inner_x = in_ref[pl.ds(pl.multiple_of(c * T + 8, 8), T)]
    both = jnp.concatenate([gconv, later[...]], axis=0)
    gi = None
    for k in range(taps):
        ahead = both[taps - 1 - k:taps - 1 - k + T]
        sums[k] += part(ahead * inner_x)
        gi = par[k:k + 1] * ahead if gi is None else gi + par[k:k + 1] * ahead
    gi_ref[...] = gi.astype(jnp.bfloat16)
    later[...] = gconv[:8]

    @pl.when(c == 0)
    def _():
        for k in range(taps + 2):
            gpar_ref[k:k + 1] = jnp.sum(sums[k], axis=0, keepdims=True)
        gpar_ref[taps + 2 + NS:taps + 3 + NS] = jnp.sum(sums[taps + 2], axis=0, keepdims=True)


def scan_backward(u, dl, gs, conv, inner, pT, st, xpT, wdt, par, an, limit, Q=3, Q2=3):
    C, T8, _, DI = u.shape
    T = T8 * 8
    XP, R = xpT.shape[0], wdt.shape[0]
    n = par.shape[0] + NS
    rev = lambda *shape: pl.BlockSpec((1,) + shape, lambda j: (C - 1 - j,) + (0,) * len(shape))
    rows = rev(T8, 8, DI)
    outs = [sds((C * T, DI), jnp.bfloat16), sds((XP, DI)), sds((R, DI)), sds((n, DI))]
    V = lambda *s: pltpu.VMEM(s, F32)
    return pl.pallas_call(
        functools.partial(scan_back_kernel, T, Q, Q2, R), grid=(C,),
        in_specs=[rows, rows, rows, rows, whole_spec(inner), rev(XP, T), rev(NS, DI)] + [whole_spec(a) for a in (xpT, wdt, par, an)],
        out_specs=[pl.BlockSpec((T, DI), lambda j: (C - 1 - j, 0))] + [whole_spec(o) for o in outs[1:]],
        out_shape=outs,
        scratch_shapes=[V(NS, DI), V(8, DI), V(T, NS, 128), V(T, NS, 128), V(T8, 8, DI), V(T8, 8, DI), V(T8, 8, DI),
                        V(T, NS, Q * 128), V(T, NS, Q * 128), V(T, NS, 128), V(T, NS, 128), V(par.shape[0], 8, DI)],
        compiler_params=pltpu.CompilerParams(vmem_limit_bytes=limit << 20),
        cost_estimate=pl.CostEstimate(flops=80000000000, bytes_accessed=16 * C * T * DI, transcendentals=0),
    )(u, dl, gs, conv, inner, pT, st, xpT, wdt, par, an)


def one_call(kernel, ins, outs, scalars=(), flops=0, limit=56):
    smem = pl.BlockSpec(memory_space=pltpu.SMEM)
    vmem = pl.BlockSpec(memory_space=pltpu.VMEM)
    size = sum(a.size * a.dtype.itemsize for a in list(ins) + list(outs))
    return pl.pallas_call(
        kernel,
        in_specs=[smem] * len(scalars) + [vmem] * len(ins), out_specs=[vmem] * len(outs), out_shape=list(outs),
        compiler_params=pltpu.CompilerParams(vmem_limit_bytes=limit << 20),
        cost_estimate=pl.CostEstimate(flops=flops, bytes_accessed=size, transcendentals=0),
    )(*scalars, *ins)


def route_kernel(cap, here, message, s, live_ref, x_ref, nm_ref, y_ref, wz_ref, wo_ref, gain_ref, wr_ref, route_ref, cot_ref,
                 z_ref, gated_ref, hid_ref, target_ref, out_ref, prob_ref, gate_ref):
    bf = jnp.bfloat16
    L = nm_ref.shape[0]
    E = wr_ref.shape[0]
    z = mm(nm_ref[...], wz_ref[...])
    z_ref[...] = z
    gated = (y_ref[...] * (z * sigmoid(z))).astype(bf)
    gated_ref[...] = gated
    hid = x_ref[...].astype(F32) + mm(gated, wo_ref[...])
    hid_ref[...] = hid
    nmoe = hid * lax.rsqrt(jnp.mean(hid * hid, axis=-1, keepdims=True) + 1e-05) * gain_ref[...]
    logits = mm(nmoe, wr_ref[...], NT, precision=lax.Precision.HIGHEST)
    e = jnp.exp(logits - jnp.max(logits, axis=-1, keepdims=True))
    probs = e / jnp.sum(e, axis=-1, keepdims=True)
    prob_ref[...] = probs
    route = route_ref[...]
    hot = route == lax.broadcasted_iota(jnp.int32, (L, E), 1)
    gate = jnp.sum(jnp.where(hot, probs, 0.0), axis=-1, keepdims=True)
    gate_ref[...] = gate
    live = lax.broadcasted_iota(jnp.int32, (L, 1), 0) < live_ref[0]
    hits = jnp.where(hot & live, 1.0, 0.0)
    before = lax.broadcasted_iota(jnp.int32, (L, L), 0) > lax.broadcasted_iota(jnp.int32, (L, L), 1)
    slot = jnp.sum(mm(jnp.where(before, 1.0, 0.0).astype(bf), hits.astype(bf)) * hits, axis=-1, keepdims=True).astype(jnp.int32)
    slots = out_ref.shape[0]
    target = route // here * message + route % here * cap + slot
    target = jnp.where(live & (slot < cap), target, -slots)
    target_ref[...] = target
    gy = jnp.where(live, cot_ref[s], 0.0)
    first, second = places(target, slots, here * cap)
    out_ref[...] = (mm(first, nmoe.astype(bf), TN) + mm(second, (gy * gate).astype(bf), TN)).astype(bf)


def places(target, slots, half):
    at = lax.broadcasted_iota(jnp.int32, (target.shape[0], slots), 1)
    return (jnp.where(at == target, 1.0, 0.0).astype(jnp.bfloat16), jnp.where(at == target + half, 1.0, 0.0).astype(jnp.bfloat16))


def sort_kernel(cap, message, half, group, got_ref, out_ref):
    n, slots = out_ref.shape[0], got_ref.shape[0]
    i = lax.broadcasted_iota(jnp.int32, (n, 1), 0)
    there = i % group
    src = jnp.where(there < slots // message * cap, there // cap * message + i // group * cap + there % cap, -slots)
    at = lax.broadcasted_iota(jnp.int32, (n, slots), 1)
    got = got_ref[...]
    D = got.shape[1]
    out_ref[:, :D] = mm(jnp.where(at == src, 1.0, 0.0).astype(jnp.bfloat16), got).astype(jnp.bfloat16)
    out_ref[:, D:] = mm(jnp.where(at == src + half, 1.0, 0.0).astype(jnp.bfloat16), got).astype(jnp.bfloat16)


def unsort_kernel(cap, message, half, group, buf_ref, out_ref):
    slots, n = out_ref.shape[0], buf_ref.shape[0]
    q = lax.broadcasted_iota(jnp.int32, (slots, 1), 0)
    w = q % message
    second = w >= half
    v = jnp.where(second, w - half, w)
    dst = jnp.where(w < 2 * half, v // cap * group + q // message * cap + v % cap, -1)
    at = lax.broadcasted_iota(jnp.int32, (slots, n), 1)
    D = out_ref.shape[1]
    one = jnp.where(at == jnp.where(second, -1, dst), 1.0, 0.0).astype(jnp.bfloat16)
    two = jnp.where(at == jnp.where(second, dst, -1), 1.0, 0.0).astype(jnp.bfloat16)
    out_ref[...] = (mm(one, buf_ref[:, :D]) + mm(two, buf_ref[:, D:])).astype(jnp.bfloat16)


def unroute_kernel(s, half, live_ref, home_ref, target_ref, hid_ref, prob_ref, gate_ref, route_ref, cot_ref, gain_ref, wr_ref, wo_ref, sh_ref,
                   z_ref, y_ref, mix_ref, gh_ref, gs_ref, gz_ref, gm_ref, gr_ref, gg_ref):
    bf = jnp.bfloat16
    high = lax.Precision.HIGHEST
    hid, gain = hid_ref[...], gain_ref[...]
    L, D = hid.shape
    E = wr_ref.shape[0]
    first, second = places(target_ref[...], home_ref.shape[0], half)
    etok, gsent = mm(first, home_ref[...]), mm(second, home_ref[...])
    live = lax.broadcasted_iota(jnp.int32, (L, 1), 0) < live_ref[0]
    gate, probs = gate_ref[...], prob_ref[...]
    mix_ref[...] = jnp.where(live, hid + gate * etok, 0.0).astype(bf)
    gy = jnp.where(live, cot_ref[s], 0.0)
    ggate = jnp.sum(gy * etok, axis=-1, keepdims=True)
    hot = jnp.where(route_ref[...] == lax.broadcasted_iota(jnp.int32, (L, E), 1), 1.0, 0.0)
    glog = ggate * gate * (hot - probs)
    rms = lax.rsqrt(jnp.mean(hid * hid, axis=-1, keepdims=True) + 1e-05)
    hat = hid * rms
    gr_ref[...] = mm(glog, hat * gain, TN, precision=high)
    gnorm = gsent + mm(glog, wr_ref[...], precision=high)
    gg_ref[...] = jnp.sum(gnorm * hat, axis=0, keepdims=True)
    scaled = gnorm * gain
    gh = gy + rms * (scaled - hat * jnp.mean(scaled * hat, axis=-1, keepdims=True))
    gh_ref[...] = gh
    gmix = gh.astype(bf)
    gm_ref[...] = mm(gmix, sh_ref[...]).astype(bf)
    ggated = mm(gmix, wo_ref[...], NT)
    z = z_ref[...]
    sig = sigmoid(z)
    gs_ref[...] = ggated * (z * sig)
    gz_ref[...] = (ggated * y_ref[...] * (sig * (1.0 + z * (1.0 - sig)))).astype(bf)


def token_kernel(gi_ref, gz_ref, wx_ref, wz_ref, x_ref, gh_ref, gain_ref, gt_ref, gg_ref):
    gnm = mm(gi_ref[...], wx_ref[...], NT) + mm(gz_ref[...], wz_ref[...], NT)
    x = x_ref[...].astype(F32)
    rms = lax.rsqrt(jnp.mean(x * x, axis=-1, keepdims=True) + 1e-05)
    hat = x * rms
    gg_ref[...] = jnp.sum(gnm * hat, axis=0, keepdims=True)
    scaled = gnm * gain_ref[...]
    gt_ref[...] = gh_ref[...] + rms * (scaled - hat * jnp.mean(scaled * hat, axis=-1, keepdims=True))


QB = 64
CAP = 13
BF = jnp.bfloat16
root_half = 0.7071067811865476
inv_root_two_pi = 0.3989422804014327
log2e = 1.4426950408889634


def swap(x, axis, bit):
    n = lax.axis_size(axis)
    return lax.ppermute(x, axis, [(i, i ^ bit) for i in range(n)])


def bits_of(axis):
    n = lax.axis_size(axis)
    return [1 << k for k in range(n.bit_length() - 1)]


def exchange(x, mask):
    rm, cm = mask
    if rm == 0:
        return swap(x, "col", cm)
    if cm == 0:
        return swap(x, "row", rm)
    rows, cols = lax.axis_size("row"), lax.axis_size("col")
    pairs = [(r * cols + c, (r ^ rm) * cols + (c ^ cm)) for r in range(rows) for c in range(cols)]
    return lax.ppermute(x, ("row", "col"), pairs)


def combos(bits):
    out = [(0, 0)]
    for rb, cb in bits:
        out = out + [(r | rb, c | cb) for r, c in out]
    return out


def stages():
    row, col = bits_of("row"), bits_of("col")
    far = combos([(b, 0) for b in row[1:]])
    plane = combos([(row[0], 0)] + [(0, b) for b in col[1:]])
    return far, plane, (0, col[0])


def add(a, b):
    return (a[0] ^ b[0], a[1] ^ b[1])


def gather_far(x):
    return jnp.stack([x] + [exchange(x, m) for m in stages()[0][1:]])


def gather_plane(mine):
    return [mine] + [exchange(mine, m) for m in stages()[1][1:]]


def gather_core(near):
    far, plane, core = stages()
    near = [([add(f, m) for f in far], b) for m, b in zip(plane, near)]
    return near + [([add(m, core) for m in ms], exchange(b, core)) for ms, b in near]


def gather_list(x):
    return gather_core(gather_plane(gather_far(x)))


def assemble_kernel(masks, moves, count_in, *refs):
    r0, c0 = refs[0][0], refs[0][1]
    ins, outs = refs[1:1 + count_in], refs[1 + count_in:]
    for buf, ms in zip(ins, masks):
        for i, (rm, cm) in enumerate(ms):
            for (row, count, lanes), out, place in moves:
                place(outs[out], r0 ^ rm, c0 ^ cm, buf[i, row:row + count, :lanes])


def put_block(out, r, c, block):
    n, m = block.shape
    out[pl.ds(pl.multiple_of(r * n, n), n), pl.ds(pl.multiple_of(c * m, m), m)] = block


def put_pair(out, r, c, block):
    out[r, c] = block


def take_blocks(gathered):
    rows, cols = lax.axis_size("row"), lax.axis_size("col")
    order = [r * cols + c for ms, _ in gathered for r, c in ms]
    entry = jnp.asarray([order.index(i) for i in range(rows * cols)], jnp.int32)
    me = lax.axis_index("row") * cols + lax.axis_index("col")
    stacked = jnp.concatenate([b for _, b in gathered], axis=0)
    out = jnp.take(stacked, entry[jnp.arange(rows * cols, dtype=jnp.int32) ^ me], axis=0)
    return out.reshape((rows, cols) + stacked.shape[1:])


def assemble(gathered, moves, shapes):
    masks = [ms for ms, _ in gathered]
    bufs = [b for _, b in gathered]
    if any(lanes % 128 for (_, _, lanes), _, _ in moves):
        every = take_blocks(gathered)
        cut = [every[:, :, row:row + count, :lanes] for (row, count, lanes), _, _ in moves]
        return [v if place is put_pair else v.transpose(0, 2, 1, 3).reshape(shape)
                for v, shape, (_, _, place) in zip(cut, shapes, moves)]
    me = jnp.stack([lax.axis_index("row"), lax.axis_index("col")]).astype(jnp.int32)
    vmem = pl.BlockSpec(memory_space=pltpu.VMEM)
    return pl.pallas_call(
        functools.partial(assemble_kernel, masks, moves, len(bufs)),
        in_specs=[pl.BlockSpec(memory_space=pltpu.SMEM)] + [vmem] * len(bufs),
        out_specs=[vmem] * len(shapes),
        out_shape=[jax.ShapeDtypeStruct(s, BF) for s in shapes],
        compiler_params=pltpu.CompilerParams(vmem_limit_bytes=32 << 20),
        cost_estimate=pl.CostEstimate(flops=0, bytes_accessed=4 * sum(b.size for b in bufs), transcendentals=0),
    )(me, *bufs)


def between(work, give, got):
    result = work(give)
    return lax.optimization_barrier((got, result))


def reduce_core(parts, work=None):
    far, plane, core = stages()
    near = [k for k in range(lax.axis_size("col")) if not k & core[1]]
    give = jnp.stack([parts[k | core[1]] for k in near])
    got = exchange(give, core)
    result = None
    if work:
        got, result = between(work, give, got)
    return [parts[k].astype(F32) + got[i].astype(F32) for i, k in enumerate(near)], result


def reduce_plane_give(sums):
    far, plane, core = stages()
    near = [k for k in range(lax.axis_size("col")) if not k & core[1]]
    rows, r0 = lax.axis_size("row"), lax.axis_index("row")

    def rows_of(k, rm):
        v = sums[near.index(k)]
        return lax.dynamic_index_in_dim(v.reshape((rows // 2, 2) + v.shape[1:]), (r0 ^ rm) & 1, 1, keepdims=False)
    return rows_of(0, 0), [rows_of(cm, rm).astype(BF) for rm, cm in plane[1:]]


def reduce_plane(own, give, work=None):
    got = [exchange(g, m) for g, m in zip(give, stages()[1][1:])]
    result = None
    if work:
        got, result = between(work, give, got)
    return functools.reduce(lambda t, v: t + v.astype(F32), got, own), result


def reduce_far(total, work=None):
    far = stages()[0]
    r0 = lax.axis_index("row")
    give = [lax.dynamic_index_in_dim(total, (r0 ^ rm) >> 1, 0, keepdims=False).astype(BF) for rm, _ in far[1:]]
    got = [exchange(g, m) for g, m in zip(give, far[1:])]
    result = None
    if work:
        got, result = between(work, give, got)
    done = lax.dynamic_index_in_dim(total, r0 >> 1, 0, keepdims=False)
    return functools.reduce(lambda t, v: t + v.astype(F32), got, done), result


def reduce_list(parts):
    own, give = reduce_plane_give(reduce_core(parts)[0])
    return reduce_far(reduce_plane(own, give)[0])[0]


def column_kernel(count, s_ref, *refs):
    total = mm(refs[0][...], refs[1][...], ((0,), (0,)))
    for k in range(1, count):
        total = total + mm(refs[2 * k][...], refs[2 * k + 1][...], ((0,), (0,)))
    refs[-1][0] = total.astype(BF)


def column_blocks(pairs, cols, my_col):
    n, m = pairs[0][0].shape
    w = pairs[0][1].shape[1] // cols
    count = len(pairs)
    if w % 128:
        total = sum(mm(a, b, ((0,), (0,))) for a, b in pairs).astype(BF).reshape(m, cols, w).transpose(1, 0, 2)
        return jnp.take(total, jnp.arange(cols, dtype=jnp.int32) ^ my_col, axis=0)
    return pl.pallas_call(
        functools.partial(column_kernel, count),
        grid_spec=pltpu.PrefetchScalarGridSpec(
            num_scalar_prefetch=1, grid=(cols,),
            in_specs=[pl.BlockSpec((n, m), lambda k, s: (0, 0)), pl.BlockSpec((n, w), lambda k, s: (0, s[0] ^ k))] * count,
            out_specs=pl.BlockSpec((1, m, w), lambda k, s: (k, 0, 0))),
        out_shape=jax.ShapeDtypeStruct((cols, m, w), BF),
        compiler_params=pltpu.CompilerParams(vmem_limit_bytes=32 << 20),
        cost_estimate=pl.CostEstimate(flops=2 * count * n * m * w * cols, bytes_accessed=2 * (count * (n * m + n * w * cols) + m * w * cols), transcendentals=0),
    )(my_col.reshape(1), *[v for p in pairs for v in p])


def gelu_parts(v):
    phi = 0.5 * (1.0 + lax.erf(v * root_half))
    return v * phi, phi + v * jnp.exp(-0.5 * v * v) * inv_root_two_pi


def expert_kernel(cols, *refs):
    both, up, down = refs[:cols], refs[cols], refs[cols + 1]
    outs, acts, gps = refs[cols + 2:2 * cols + 2], refs[2 * cols + 2], refs[2 * cols + 3]
    width = up.shape[1]
    n = both[0].shape[1]
    rows = jnp.concatenate([b[0] for b in both], axis=0)
    act, slope = gelu_parts(mm(rows[:, :width], up[0]))
    act = act.astype(BF)
    acts[0] = act
    gp = (mm(rows[:, width:], down[0], ((1,), (1,))) * slope).astype(BF)
    gps[0] = gp
    out = mm(act, down[0]).astype(BF)
    gin = mm(gp, up[0], ((1,), (1,))).astype(BF)
    for c in range(cols):
        outs[c][0, :, :width] = out[c * n:(c + 1) * n]
        outs[c][0, :, width:] = gin[c * n:(c + 1) * n]


def weights_kernel(cols, sets, *refs):
    up, down = refs[-2:]
    step = cols + 2
    gu = gd = None
    width = up.shape[1]
    for s in range(sets):
        both, act, gp = refs[s * step:s * step + cols], refs[s * step + cols][0], refs[s * step + cols + 1][0]
        rows = jnp.concatenate([b[0] for b in both], axis=0)
        a = mm(rows[:, :width], gp, ((0,), (0,)))
        b = mm(act, rows[:, width:], ((0,), (0,)))
        gu, gd = (a, b) if gu is None else (gu + a, gd + b)
    up[0] = gu
    down[0] = gd


def per_expert(kernel, ins, shapes, flops):
    tok = lambda a: pl.BlockSpec((1,) + a.shape[1:], lambda e: (e, 0, 0))
    size = sum(a.size * 2 for a in ins) + sum(s.size * s.dtype.itemsize for s in shapes)
    return list(pl.pallas_call(
        kernel, grid=(ins[0].shape[0],),
        in_specs=[tok(a) for a in ins], out_specs=[tok(s) for s in shapes], out_shape=shapes,
        compiler_params=pltpu.CompilerParams(vmem_limit_bytes=(44 if len(ins) <= 12 else 56) << 20),
        cost_estimate=pl.CostEstimate(flops=flops, bytes_accessed=size, transcendentals=0),
    )(*ins))


def expert_both(bufs, up, down):
    cols = len(bufs)
    experts, d, f = up.shape
    n = bufs[0].shape[1]
    shapes = ([jax.ShapeDtypeStruct((experts, n, 2 * d), BF)] * cols
              + [jax.ShapeDtypeStruct((experts, n * cols, f), BF)] * 2)
    outs = per_expert(functools.partial(expert_kernel, cols), bufs + [up, down], shapes, 8 * experts * cols * n * d * f)
    return outs[:cols], outs[cols:]


def expert_weights(sets, d, f):
    cols = len(sets[0]) - 2
    experts, n, _ = sets[0][0].shape
    if len(sets) > 1 and len(sets) * cols > 8:
        return [sum(v) for v in zip(*[expert_weights([s], d, f) for s in sets])]
    shapes = [jax.ShapeDtypeStruct((experts, d, f), F32), jax.ShapeDtypeStruct((experts, f, d), F32)]
    return per_expert(functools.partial(weights_kernel, cols, len(sets)), [v for s in sets for v in s], shapes,
                      4 * experts * cols * n * d * f * len(sets))


def up_to(n, m):
    return -(-n // m) * m


def tiles_fit(w_in_x, w_xproj, w_out, conv_w, w_dt, w_router):
    return (w_in_x.shape == (96, 384) and w_xproj.shape[0] == 192 and w_xproj.shape[1] <= 26 and w_dt.shape[0] <= 6
            and conv_w.shape[0] + NS + 5 <= 26 and conv_w.shape[1] <= 128 and w_out.shape == (192, 192)
            and w_router.shape[0] <= 128 and w_router.shape[1] <= 16)


def one_hot(shape, match):
    i = lax.broadcasted_iota(jnp.int32, shape, 0)
    j = lax.broadcasted_iota(jnp.int32, shape, 1)
    return jnp.where(match(i, j), 1.0, 0.0).astype(BF)


def pack_kernel(wx, wdt, xp, cw, cb, db, al, ds, gx, gm, wz, wo, wr, first, other, s_ex, s_r):
    n = wx.shape[0]
    s_ex[...] = jnp.zeros_like(s_ex)
    s_r[...] = jnp.zeros_like(s_r)
    first[:n] = wx[...]
    s_ex[:xp.shape[0], :xp.shape[1]] = xp[...].astype(F32)
    wide = s_ex.shape[1] - 128
    at = 0
    for v in (cw, cb, db, al, ds, gx, gm):
        s_ex[at:at + v.shape[0], wide:wide + v.shape[1]] = v[...].astype(F32)
        at += v.shape[0]
    s_ex[26:26 + wdt.shape[0]] = wdt[...].astype(F32)
    first[n:] = s_ex[...].astype(BF)
    s_r[:wr.shape[0], :wr.shape[1]] = wr[...].astype(F32)

    def put(at, lane, v):
        other[at:at + v.shape[0], lane:lane + v.shape[1]] = v
    put_other(put, wz[...], wo[...])
    other[other.shape[0] - 16:] = s_r[...].astype(BF)


def put_other(put, z, out):
    n, m = z.shape[-2], out.shape[-2]
    put(0, 0, z[..., :256])
    put(n, 0, z[..., :n // 2, 256:])
    put(n, 128, z[..., n // 2:, 256:])
    at = n + n // 2
    put(at, 0, out[..., :m // 2, :128])
    put(at, 128, out[..., m // 2:, :128])
    put(at + m // 2, 0, jnp.concatenate([out[..., j * m // 4:(j + 1) * m // 4, 128:192] for j in range(4)], axis=-1))


def pack_params(w_in_x, w_dt, w_xproj, conv_w, conv_b, dt_bias, a_log, d_skip, gain_mix, gain_moe, w_in_z, w_out, w_router):
    n, lanes = w_in_x.shape
    ins = [w_in_x, w_dt, w_xproj.T, conv_w, conv_b[None], dt_bias[None], a_log, d_skip[None], gain_mix[None], gain_moe[None],
           w_in_z, w_out, w_router.T]
    vmem = pl.BlockSpec(memory_space=pltpu.VMEM)
    V = lambda *s: pltpu.VMEM(s, F32)
    return pl.pallas_call(
        pack_kernel, in_specs=[vmem] * len(ins), out_specs=[vmem] * 2,
        out_shape=[sds((n + 32, lanes), BF), sds((n + n // 2 + w_out.shape[0] * 3 // 4 + 16, 256), BF)],
        scratch_shapes=[V(32, lanes), V(16, 256)],
    )(*ins)


def each_block(masks, bufs, r0, c0):
    for buf, ms in zip(bufs, masks):
        for i, (rm, cm) in enumerate(ms):
            yield buf, i, r0 ^ rm, c0 ^ cm


def span(i, n):
    return pl.ds(pl.multiple_of(i * n, n), n)


def dt_match(j, i, dt_rows):
    k = j % 32 - 26
    return (k >= 0) & (k < dt_rows) & (j // 32 * dt_rows + k == i)


def unpack_first(masks, dims, me, *refs):
    dt_rows, xp_cols, xp_rows, share, gshare, taps, rows, cols = dims
    count = len(masks)
    bufs = refs[:count]
    fx, dt, xpT, par, an, a2, gx, gm, w_dt, w_xp, w_sm = refs[count:]
    n = bufs[0].shape[1] - 32
    lanes = bufs[0].shape[2]
    wide = lanes - 128
    for buf, i, r, c in each_block(masks, bufs, me[0], me[1]):
        fx[span(r, n), span(c, lanes)] = buf[i, :n]
        w_dt[span(r, 32), span(c, lanes)] = buf[i, n:]
        w_xp[span(c, 32), span(r, wide)] = buf[i, n:, :wide]
        w_sm[:, span(r * cols + c, 128)] = buf[i, n:, wide:]
    pick = one_hot((dt.shape[0], 32 * rows), lambda i, j: dt_match(j, i, dt_rows))
    dt[...] = mm(pick, w_dt[...]).astype(BF)
    pick = one_hot((xpT.shape[0], 32 * cols), lambda i, j: (j % 32 < xp_cols) & (j // 32 * xp_cols + j % 32 == i))
    t = mm(pick, w_xp[...])
    xpT[...] = jnp.concatenate([t[:, r * wide:r * wide + xp_rows] for r in range(rows)], axis=1).astype(BF)
    sm = w_sm[...].astype(F32)
    chan = jnp.concatenate([sm[:, p * 128:p * 128 + share] for p in range(rows * cols)], axis=1)
    par[:taps + 2] = chan[:taps + 2]
    par[taps + 2:] = chan[taps + 2 + NS:taps + 3 + NS]
    neg = -jnp.exp(chan[taps + 2:taps + 2 + NS])
    an[...] = neg
    a2[...] = neg * log2e
    gains = jnp.concatenate([sm[taps + 3 + NS:taps + 5 + NS, p * 128:p * 128 + gshare] for p in range(rows * cols)], axis=1)
    gx[...] = gains[:1]
    gm[...] = gains[1:]


def unpack_other(masks, dims, me, *refs):
    n, out_rows, out_lanes, r_cols, cols = dims
    count = len(masks)
    bufs = refs[:count]
    fz, fo, router, w_out, w_r = refs[count:]
    half = n // 2
    at = n + half
    m = out_rows
    for buf, i, r, c in each_block(masks, bufs, me[0], me[1]):
        fz[span(r, n), pl.ds(pl.multiple_of(c * 384, 128), 256)] = buf[i, :n]
        for j in range(2):
            rows = pl.ds(pl.multiple_of(r * n + j * half, 16), half)
            fz[rows, pl.ds(pl.multiple_of(c * 384 + 256, 128), 128)] = buf[i, n:at, j * 128:(j + 1) * 128]
            rows = pl.ds(pl.multiple_of(r * m + j * (m // 2), 16), m // 2)
            w_out[rows, span(2 * c, 128)] = buf[i, at:at + m // 2, j * 128:(j + 1) * 128]
        for j in range(4):
            rows = pl.ds(pl.multiple_of(r * m + j * (m // 4), 16), m // 4)
            w_out[rows, pl.ds(pl.multiple_of(c * 256 + 128, 128), 64)] = buf[i, at + m // 2:at + m * 3 // 4, j * 64:(j + 1) * 64]
        w_r[span(c, 16), span(r, 128)] = buf[i, at + m * 3 // 4:, :128]
    wide = w_out[...]
    fo[...] = jnp.concatenate([wide[:, c * 256:c * 256 + out_lanes] for c in range(cols)], axis=1)
    pick = one_hot((router.shape[0], 16 * cols), lambda i, j: (j % 16 < r_cols) & (j // 16 * r_cols + j % 16 == i))
    t = mm(pick, w_r[...])
    r_rows = router.shape[1] // (t.shape[1] // 128)
    router[...] = jnp.concatenate([t[:, r * 128:r * 128 + r_rows] for r in range(t.shape[1] // 128)], axis=1)


def unpack_call(kernel, gathered, dims, outs, scratch):
    masks = [ms for ms, _ in gathered]
    bufs = [b for _, b in gathered]
    me = jnp.stack([lax.axis_index("row"), lax.axis_index("col")]).astype(jnp.int32)
    vmem = pl.BlockSpec(memory_space=pltpu.VMEM)
    return pl.pallas_call(
        functools.partial(kernel, masks, dims),
        in_specs=[pl.BlockSpec(memory_space=pltpu.SMEM)] + [vmem] * len(bufs), out_specs=[vmem] * len(outs), out_shape=outs,
        scratch_shapes=[pltpu.VMEM(s, BF) for s in scratch],
        compiler_params=pltpu.CompilerParams(vmem_limit_bytes=28 << 20),
        cost_estimate=pl.CostEstimate(flops=0, bytes_accessed=4 * sum(b.size for b in bufs), transcendentals=0),
    )(me, *bufs)


def grad_x_kernel(count, dims, s_ref, *refs):
    dt_rows, xp_cols, xp_rows, share, gshare, rows, cols = dims
    pairs = refs[:2 * count]
    gwd, gxp, gpar, gmix, gmoe = (refs[(2 + i) * count:(3 + i) * count] for i in range(5))
    keep, give, w_dt, w_xp, w_sm, full = refs[7 * count:]
    k = pl.program_id(0)
    n, lanes = keep.shape[2] - 32, keep.shape[3]
    wide = lanes - 128
    total = lambda vs: functools.reduce(lambda a, b: a + b, [v[...] for v in vs])

    @pl.when(k == 0)
    def _():
        g = total(gwd).astype(BF)
        full[...] = sum_products(pairs)
        put = one_hot((32 * rows, g.shape[0]), lambda j, i: dt_match(j, i, dt_rows))
        w_dt[...] = mm(put, g).astype(BF)
        g = total(gxp).astype(BF)
        put = one_hot((32 * cols, g.shape[0]), lambda j, i: (j % 32 < xp_cols) & (j // 32 * xp_cols + j % 32 == i))
        t = mm(put, g)
        gap = jnp.zeros((t.shape[0], wide - xp_rows), F32)
        w_xp[...] = jnp.concatenate([v for r in range(rows) for v in (t[:, r * xp_rows:(r + 1) * xp_rows], gap)], axis=1).astype(BF)
        w_sm[...] = jnp.zeros_like(w_sm)
        par, mix, moe = total(gpar), total(gmix), total(gmoe)
        m = par.shape[0]
        for p in range(rows * cols):
            w_sm[:m, p * 128:p * 128 + share] = par[:, p * share:(p + 1) * share]
            w_sm[m:m + 1, p * 128:p * 128 + gshare] = mix[:, p * gshare:(p + 1) * gshare]
            w_sm[m + 1:m + 2, p * 128:p * 128 + gshare] = moe[:, p * gshare:(p + 1) * gshare]
    for j, out in enumerate((keep, give)):
        c = s_ref[0] ^ (2 * k + j)
        out[0, :, :n] = full[:, span(c, lanes)].astype(BF).reshape(rows, n, lanes)
        for r in range(rows):
            d = w_dt[r * 32:(r + 1) * 32, span(c, lanes)]
            out[0, r, n:, :wide] = w_xp[span(c, 32), r * wide:(r + 1) * wide] + d[:, :wide]
            out[0, r, n:, wide:] = (w_sm[:, span(r * cols + c, 128)] + d[:, wide:].astype(F32)).astype(BF)


def sum_products(pairs):
    return functools.reduce(lambda a, b: a + b, [mm(pairs[i][...], pairs[i + 1][...], TN) for i in range(0, len(pairs), 2)])


def grad_blocks(kernel, ins, scratch, block, rows, cols, my_col, flops, limit):
    out = sds((cols // 2, rows) + block, BF)
    return list(pl.pallas_call(
        kernel,
        grid_spec=pltpu.PrefetchScalarGridSpec(
            num_scalar_prefetch=1, grid=(cols // 2,), in_specs=[whole_spec(v) for v in ins],
            out_specs=[pl.BlockSpec((1, rows) + block, lambda k, s: (k, 0, 0, 0))] * 2, scratch_shapes=scratch),
        out_shape=[out, out],
        compiler_params=pltpu.CompilerParams(vmem_limit_bytes=limit << 20),
        cost_estimate=pl.CostEstimate(flops=flops, bytes_accessed=1 << 23, transcendentals=0),
    )(my_col.reshape(1), *ins))


def grad_x_blocks(pairs, smalls, dims, my_col):
    rows, cols = dims[-2:]
    n, m = pairs[0][0].shape
    inner = pairs[0][1].shape[1]
    lanes = inner // cols
    ins = [v for p in pairs for v in p] + [g[name] for name in ("dt", "xproj", "chan", "gain_mix", "gain_moe") for g in smalls]
    scratch = [pltpu.VMEM((32 * rows, inner), BF), pltpu.VMEM((32 * cols, (lanes - 128) * rows), BF), pltpu.VMEM((32, 128 * rows * cols), F32),
               pltpu.VMEM((m, inner), F32)]
    return grad_blocks(functools.partial(grad_x_kernel, len(pairs), dims), ins, scratch, (m // rows + 32, lanes), rows, cols, my_col,
                       2 * len(pairs) * n * m * inner, 44)


def grad_other_kernel(count, r_cols, s_ref, *refs):
    zs, outs, routers = refs[:2 * count], refs[2 * count:4 * count], refs[4 * count:5 * count]
    keep, give, full_z, full_o = refs[5 * count:]
    rows = keep.shape[1]
    k = pl.program_id(0)

    @pl.when(k == 0)
    def _():
        full_z[...] = sum_products(zs)
        full_o[...] = sum_products(outs)
    r = functools.reduce(lambda a, b: a + b, [v[...] for v in routers]).astype(BF)
    r_rows = r.shape[1] // rows
    for j, out in enumerate((keep, give)):
        c = s_ref[0] ^ (2 * k + j)
        z = full_z[:, pl.ds(pl.multiple_of(c * 384, 128), 384)].astype(BF)
        o = full_o[:, span(2 * k + j, 256)].astype(BF)
        z, o = (v.reshape(rows, v.shape[0] // rows, v.shape[1]) for v in (z, o))

        def put_block(at, lane, v):
            out[0, :, at:at + v.shape[1], lane:lane + v.shape[2]] = v
        put_other(put_block, z, o)
        w = mm(one_hot((16, r.shape[0]), lambda a, b: (a < r_cols) & (b == c * r_cols + a)), r).astype(BF)
        at = out.shape[2] - 16
        out[0, :, at:] = jnp.zeros((rows, 16, 256), BF)
        for q in range(rows):
            out[0, q, at:, :r_rows] = w[:, q * r_rows:(q + 1) * r_rows]


def grad_other_blocks(zs, outs, routers, block, rows, cols, r_cols, my_col):
    ins = [v for p in zs for v in p] + [v for p in outs for v in p] + list(routers)
    flops = 2 * sum(a.shape[0] * a.shape[1] * b.shape[1] for a, b in zs + outs)
    scratch = [pltpu.VMEM((a.shape[1], b.shape[1]), F32) for a, b in (zs[0], outs[0])]
    return grad_blocks(functools.partial(grad_other_kernel, len(zs), r_cols), ins, scratch, block, rows, cols, my_col, flops, 56)


def split_near_kernel(plan, s_ref, keep, got, own, *gives):
    for out, (ki, rm) in zip((own,) + gives, plan):
        p = (s_ref[0] ^ rm) & 1
        v = keep[ki, 0, p].astype(F32) + got[ki, 0, p].astype(F32)
        out[0] = v.astype(out.dtype)


def split_near(keep, got):
    plane = stages()[1]
    near, rows, n, lanes = keep.shape
    plan = [(cm >> 1, rm) for rm, cm in plane]
    view = (near, rows // 2, 2, n, lanes)
    outs = [sds((rows // 2, n, lanes), F32 if i == 0 else BF) for i in range(len(plan))]
    res = pl.pallas_call(
        functools.partial(split_near_kernel, plan),
        grid_spec=pltpu.PrefetchScalarGridSpec(
            num_scalar_prefetch=1, grid=(rows // 2,),
            in_specs=[pl.BlockSpec((near, 1, 2, n, lanes), lambda z, s: (0, z, 0, 0, 0))] * 2,
            out_specs=[pl.BlockSpec((1, n, lanes), lambda z, s: (z, 0, 0))] * len(outs)),
        out_shape=outs,
        compiler_params=pltpu.CompilerParams(vmem_limit_bytes=16 << 20),
        cost_estimate=pl.CostEstimate(flops=0, bytes_accessed=6 * keep.size, transcendentals=0),
    )(lax.axis_index("row").reshape(1), keep.reshape(view), got.reshape(view))
    return res[0], list(res[1:])


def split_far_kernel(count, plan, s_ref, own, *refs):
    gots, mine, gives = refs[:count], refs[count], refs[count + 1:]
    for out, rm in zip((mine,) + gives, plan):
        i = (s_ref[0] ^ rm) >> 1
        v = own[i]
        for g in gots:
            v = v + g[i].astype(F32)
        out[...] = v.astype(out.dtype)


def split_far(own, gots):
    plan = [rm for rm, _ in stages()[0]]
    _, n, lanes = own.shape
    outs = [sds((n, lanes), F32 if i == 0 else BF) for i in range(len(plan))]
    res = one_call(functools.partial(split_far_kernel, len(gots), plan), [own] + gots, outs, [lax.axis_index("row").reshape(1)])
    return res[0], list(res[1:])


def total_of(refs):
    return functools.reduce(lambda a, b: a + b[...].astype(F32), refs[1:], refs[0][...])


def finish_x_kernel(count, *refs):
    gx, gxp, gdt, gcw, gcb, gdb, gal, gds, gmix, gmoe, s = refs[count:]
    s[...] = total_of(refs[:count])
    n, lanes = gx.shape
    gx[...] = s[:n]
    gdt[...] = s[n + 26:n + 26 + gdt.shape[0]]
    wide = lanes - 128
    gxp[...] = s[n:n + gxp.shape[0], :gxp.shape[1]]
    at = n
    for ref in (gcw, gcb, gdb, gal, gds, gmix, gmoe):
        ref[...] = s[at:at + ref.shape[0], wide:wide + ref.shape[1]]
        at += ref.shape[0]


def finish_other_kernel(count, *refs):
    gz, go, gr, s = refs[count:]
    s[...] = total_of(refs[:count])
    n = gz.shape[0]
    half = n // 2
    gz[:, :256] = s[:n]
    gz[:half, 256:] = s[n:n + half, :128]
    gz[half:, 256:] = s[n:n + half, 128:]
    at = n + half
    m = go.shape[0]
    for j in range(2):
        go[j * m // 2:(j + 1) * m // 2, :128] = s[at:at + m // 2, j * 128:(j + 1) * 128]
    for j in range(4):
        go[j * m // 4:(j + 1) * m // 4, 128:] = s[at + m // 2:at + m * 3 // 4, j * 64:(j + 1) * 64]
    at += m * 3 // 4
    gr[...] = s[at:at + gr.shape[0], :gr.shape[1]]


def finish(kernel, mine, gots, shapes):
    ins = [mine] + gots
    vmem = pl.BlockSpec(memory_space=pltpu.VMEM)
    return pl.pallas_call(
        functools.partial(kernel, len(ins)), in_specs=[vmem] * len(ins), out_specs=[vmem] * len(shapes),
        out_shape=[sds(s) for s in shapes], scratch_shapes=[pltpu.VMEM(mine.shape, F32)],
    )(*ins)


def weights_part_kernel(cols, sets, lead, *refs):
    out = refs[-1]
    step = cols + 1
    total = None
    for s in range(sets):
        both, other = refs[s * step:s * step + cols], refs[s * step + cols][0]
        width = both[0].shape[2] // 2
        rows = jnp.concatenate([b[0, :, :width] if lead else b[0, :, width:] for b in both], axis=0)
        v = mm(rows, other, TN) if lead else mm(other, rows, TN)
        total = v if total is None else total + v
    out[0] = total


def expert_weights_part(sets, lead, d, f):
    cols = len(sets[0]) - 1
    experts, n, _ = sets[0][0].shape
    if len(sets) > 1 and len(sets) * cols > 8:
        return sum(expert_weights_part([s], lead, d, f) for s in sets)
    shape = (experts, d, f) if lead else (experts, f, d)
    return per_expert(functools.partial(weights_part_kernel, cols, len(sets), lead), [v for s in sets for v in s],
                      [sds(shape)], 2 * experts * cols * n * d * f * len(sets))[0]


def params_generic(w_in_x, w_in_z, conv_w, conv_b, w_xproj, w_dt, dt_bias, a_log, d_skip, w_out, gain_mix, gain_moe, w_router):
    rows, cols = lax.axis_size("row"), lax.axis_size("col")
    parts = rows * cols
    inner, width = w_in_x.shape[1] * cols, w_in_x.shape[0] * rows
    small = jnp.concatenate([conv_w, conv_b[None], dt_bias[None], a_log, d_skip[None],
                             jnp.concatenate([gain_mix, gain_moe])[None]], axis=0)
    flat = [w_xproj.reshape(-1), w_dt.reshape(-1), w_router.reshape(-1), small.reshape(-1)]
    sizes = [f.shape[0] for f in flat]
    lanes = w_in_x.shape[1]
    extra = -(-sum(sizes) // (16 * lanes)) * 16
    flat = jnp.pad(jnp.concatenate(flat), (0, extra * lanes - sum(sizes))).reshape(extra, lanes)
    here, out_rows, out_lanes = w_in_x.shape[0], w_out.shape[0], w_out.shape[1]
    wide = -(-out_lanes // 128) * 128
    first = gather_list(jnp.concatenate([w_in_x, flat], axis=0))
    full_x, rest = assemble(first, [((0, here, lanes), 0, put_block), ((here, extra, lanes), 1, put_pair)],
                            [(width, inner), (rows, cols, extra, lanes)])
    far_end = first[len(first) // 2 - 1][1]
    late_z, late_o, _ = lax.optimization_barrier((w_in_z, jnp.pad(w_out, ((0, 0), (0, wide - out_lanes))), far_end))
    (full_z,) = assemble(gather_list(late_z), [((0, here, lanes), 0, put_block)], [(width, inner)])
    (wide_out,) = assemble(gather_list(late_o), [((0, out_rows, wide), 0, put_block)], [(inner, cols * wide)])
    lane_of = jnp.arange(cols * wide, dtype=jnp.int32)
    narrow = jnp.where(lane_of % wide < out_lanes, lane_of // wide * out_lanes + lane_of % wide, -1)
    narrow = (narrow[:, None] == jnp.arange(width, dtype=jnp.int32)[None, :]).astype(BF)
    full_out = mm(wide_out, narrow).astype(BF)
    def whole(blocks):
        return blocks.transpose(0, 2, 1, 3).reshape(blocks.shape[0] * blocks.shape[2], -1)
    rest = rest.reshape(rows, cols, extra * lanes)
    cut = [0]
    for n in sizes:
        cut.append(cut[-1] + n)
    full_xpT = whole(rest[:, :, cut[0]:cut[1]].reshape((rows, cols) + w_xproj.shape)).T
    full_dt = whole(rest[:, :, cut[1]:cut[2]].reshape((rows, cols) + w_dt.shape))
    router_f = whole(rest[:, :, cut[2]:cut[3]].reshape((rows, cols) + w_router.shape)).astype(F32).T
    small = rest[:, :, cut[3]:cut[4]].reshape((parts,) + small.shape).transpose(1, 0, 2).astype(F32)
    chan = small[:-1].reshape(-1, inner)
    taps = conv_w.shape[0]
    par = jnp.concatenate([chan[:taps + 2], chan[taps + 2 + NS:]], axis=0)
    a_neg = -jnp.exp(chan[taps + 2:taps + 2 + NS])
    a_two = a_neg * log2e
    gain_mix_f = small[-1, :, :gain_mix.shape[0]].reshape(1, width)
    gain_moe_f = small[-1, :, gain_mix.shape[0]:].reshape(1, width)
    return lambda done: (full_z, full_out, router_f, done), full_x, full_xpT, full_dt, par, a_neg, a_two, gain_mix_f, gain_moe_f


def params_tiled(w_in_x, w_in_z, conv_w, conv_b, w_xproj, w_dt, dt_bias, a_log, d_skip, w_out, gain_mix, gain_moe, w_router):
    rows, cols = lax.axis_size("row"), lax.axis_size("col")
    here, lanes = w_in_x.shape
    inner, width = lanes * cols, here * rows
    taps, share = conv_w.shape
    packed, other = pack_params(w_in_x, w_dt, w_xproj, conv_w, conv_b, dt_bias, a_log, d_skip, gain_mix, gain_moe, w_in_z,
                                w_out, w_router)
    mine = gather_far(packed)
    other, _ = lax.optimization_barrier((other, mine))
    mine_o = gather_far(other)
    near = gather_plane(mine)
    mine_o, _ = lax.optimization_barrier((mine_o, near[-1]))
    near_o = gather_plane(mine_o)
    first = gather_core(near)
    dims = (w_dt.shape[0], w_xproj.shape[1], w_xproj.shape[0], share, gain_mix.shape[0], taps, rows, cols)
    full_x, full_dt, full_xpT, par, a_neg, a_two, gx, gm = unpack_call(
        unpack_first, first, dims,
        [sds((width, inner), BF), sds((w_dt.shape[0] * rows, inner), BF), sds((w_xproj.shape[1] * cols, inner), BF),
         sds((taps + 3, inner)), sds((NS, inner)), sds((NS, inner)), sds((1, width)), sds((1, width))],
        [(32 * rows, inner), (32 * cols, (lanes - 128) * rows), (32, 128 * rows * cols)])

    def rest(done):
        o, done = lax.optimization_barrier((near_o, done))
        full_z, full_out, router_f = unpack_call(
            unpack_other, gather_core(o), (here, w_out.shape[0], w_out.shape[1], w_router.shape[1], cols),
            [sds((width, inner), BF), sds((inner, width), BF), sds((w_router.shape[1] * cols, width))],
            [(inner, 256 * cols), (16 * cols, 128 * rows)])
        return full_z, full_out, router_f, done
    return rest, full_x, full_xpT, full_dt, par, a_neg, a_two, gx, gm


def grads_generic(nms, gateds, gs, total, w_in_x, w_in_z, w_xproj, w_dt, w_out, w_router, gain_mix, conv_w):
    rows, cols = lax.axis_size("row"), lax.axis_size("col")
    parts = rows * cols
    my_col = lax.axis_index("col")
    here, lanes = w_in_x.shape
    out_rows, out_lanes = w_out.shape
    wide = up_to(out_lanes, 128)
    share = conv_w.shape[1]
    sizes = [w_xproj.size, w_dt.size, w_router.size, (conv_w.shape[0] + 4 + NS) * share]
    extra = up_to(-(-sum(sizes) // lanes), 16)
    cut = [sum(sizes[:i]) for i in range(5)]
    grad_out = sum(mm(k[1], r["gm"], TN) for k, r in zip(zip(nms, gateds), gs)).astype(BF)
    grad_out_block = reduce_list([grad_out[:, k * wide:(k + 1) * wide].reshape(rows, out_rows, wide) for k in range(cols)])
    grad_out_block = grad_out_block[:, :out_lanes]
    grad_in_z = column_blocks([(k[0], r["gz"]) for k, r in zip(zip(nms, gateds), gs)], cols, my_col)
    grad_z_block = reduce_list([grad_in_z[k].reshape(rows, here, lanes) for k in range(cols)])
    grad_in_x = column_blocks([(k[0], r["gi"]) for k, r in zip(zip(nms, gateds), gs)], cols, my_col)

    def blocks(g, like):
        r, c = like.shape
        return g.astype(BF).reshape(rows, r, cols, c).transpose(0, 2, 1, 3).reshape(rows, cols, -1)
    gsmall = total["chan"].astype(BF)
    ggain = jnp.concatenate([total["gain_mix"].reshape(parts, 1, -1), total["gain_moe"].reshape(parts, 1, -1)], axis=2)
    gsmall = jnp.concatenate([gsmall.reshape(-1, parts, share).transpose(1, 0, 2), ggain.astype(BF)], axis=1)
    gflat = jnp.concatenate([blocks(total["xproj"].T, w_xproj), blocks(total["dt"], w_dt), blocks(total["router"].T, w_router),
                             gsmall.reshape(rows, cols, -1)], axis=2)
    gflat = jnp.pad(gflat, ((0, 0), (0, 0), (0, extra * lanes - sum(sizes)))).reshape(rows, cols, extra, lanes)
    done = reduce_list([jnp.concatenate([grad_in_x[k].reshape(rows, here, lanes),
                                         lax.dynamic_index_in_dim(gflat, my_col ^ k, 1, keepdims=False)], axis=1)
                        for k in range(cols)])
    grad_x_block = done[:here]
    done = done[here:].reshape(-1)
    sm = done[cut[3]:cut[4]].reshape(-1, share)
    gm = gain_mix.shape[0]
    taps = conv_w.shape[0]
    chan = (sm[:taps], sm[taps], sm[taps + 1], sm[taps + 2:taps + 2 + NS], sm[taps + 2 + NS])
    small = (done[cut[0]:cut[1]].reshape(w_xproj.shape), done[cut[1]:cut[2]].reshape(w_dt.shape), chan, sm[-1, :gm], sm[-1, gm:],
             done[cut[2]:cut[3]].reshape(w_router.shape))
    return (grad_x_block, grad_z_block, grad_out_block), small


def on_device(tokens, w_in_x, w_in_z, conv_w, conv_b, w_xproj, w_dt, dt_bias, a_log, d_skip, w_out,
              gain_mix, gain_moe, w_router, w_up, w_down, routes, lengths, cotangent):
    rows, cols = lax.axis_size("row"), lax.axis_size("col")
    parts = rows * cols
    my_col = lax.axis_index("col")
    seqs, length, width = tokens.shape
    experts_here = w_up.shape[0]
    experts_all = experts_here * rows
    inner = w_in_x.shape[1] * cols
    count = seqs * length
    xp = w_xproj.shape[1] * cols
    share = inner // parts

    tiled = tiles_fit(w_in_x, w_xproj, w_out, conv_w, w_dt, w_router)
    here, lanes = w_in_x.shape
    out_rows, out_lanes = w_out.shape
    wide = up_to(out_lanes, 128)
    taps = conv_w.shape[0]
    rest_of, full_x, full_xpT, full_dt, par, a_neg, a_two, gain_mix_f, gain_moe_f = (
        params_tiled if tiled else params_generic)(
            w_in_x, w_in_z, conv_w, conv_b, w_xproj, w_dt, dt_bias, a_log, d_skip, w_out, gain_mix, gain_moe, w_router)
    lane_of = jnp.arange(cols * wide, dtype=jnp.int32)
    shifted = jnp.where(lane_of % wide < out_lanes, (lane_of // wide ^ my_col) * out_lanes + lane_of % wide, -1)
    shifted = (jnp.arange(width, dtype=jnp.int32)[:, None] == shifted[None, :]).astype(BF)

    half = experts_here * CAP
    message = -(-2 * half // 8) * 8
    group = -(-rows * CAP // 16) * 16
    slots = rows * message

    def mixer(s, x, limit):
        nm, inner_x, conv, u, dl, pT, ssm, starts = mixer_forward(x, gain_mix_f, full_x, full_xpT, full_dt, par, a_two, QB, limit)
        return dict(x=x, s=s, nm=nm, inner=inner_x, conv=conv, u=u, dl=dl, pT=pT, ssm=ssm.reshape(length, inner), starts=starts)

    def router(k, route, n_live, grad):
        n_live = n_live.reshape(1)
        z, gated, hidden, target, outgoing, probs, gate = one_call(
            functools.partial(route_kernel, CAP, experts_here, message, k["s"]),
            [k["x"], k["nm"], k["ssm"], full_z, full_out, gain_moe_f, router_f, route, grad],
            [sds((length, inner)), sds((length, inner), BF), sds((length, width)), sds((length, 1), jnp.int32),
             sds((slots, width), BF), sds((length, experts_all)), sds((length, 1))],
            [n_live], 6 * length * inner * width)
        kept = dict(k, z=z, gated=gated, hidden=hidden, target=target, probs=probs, gate=gate, route=route, n_live=n_live, cot=grad)
        return outgoing, kept

    def home(rows_out):
        return lax.all_to_all(rows_out, "row", split_axis=0, concat_axis=0, tiled=True)

    def arrive(got):
        (out,) = one_call(functools.partial(sort_kernel, CAP, message, half, group), [got], [sds((experts_here * group, 2 * width), BF)],
                          (), 4 * slots * experts_here * group * width, 24)
        return out.reshape(experts_here, group, 2 * width)

    def gather_cols(own):
        bufs = [own]
        for bit in bits_of("col")[::-1]:
            bufs = bufs + [swap(v, "col", bit) for v in bufs]
        return bufs

    def from_experts(bufs):
        for bit in bits_of("col"):
            mid = len(bufs) // 2
            bufs = [(a.astype(F32) + swap(b, "col", bit).astype(F32)).astype(BF) for a, b in zip(bufs[:mid], bufs[mid:])]
        (out,) = one_call(functools.partial(unsort_kernel, CAP, message, half, group), [bufs[0].reshape(experts_here * group, 2 * width)],
                          [sds((slots, width), BF)], (), 4 * slots * experts_here * group * width, 24)
        return out

    def unroute(k, back):
        mixed_out, gh, gs, gz, gm, g_router, g_moe = one_call(
            functools.partial(unroute_kernel, k["s"], half),
            [back, k["target"], k["hidden"], k["probs"], k["gate"], k["route"], k["cot"], gain_moe_f, router_f, full_out, shifted,
             k["z"], k["ssm"]],
            [sds((length, width), BF), sds((length, width)), sds((length, inner)), sds((length, inner), BF),
             sds((length, cols * wide), BF), sds((experts_all, width)), sds((1, width))],
            [k["n_live"]], 6 * length * inner * width)
        return dict(mixed_out=mixed_out, gh=gh, gs=gs.reshape(k["u"].shape), gz=gz, gm=gm, router=g_router, gain_moe=g_moe)

    def unscan(k, gs, limit):
        gi, g_xp, g_dt, g_chan = scan_backward(k["u"], k["dl"], gs, k["conv"], k["inner"], k["pT"], k["starts"], full_xpT, full_dt, par, a_neg, limit)
        return dict(gi=gi, xproj=g_xp, dt=g_dt, chan=g_chan)

    def unproject(k, g):
        grad_tokens, g_mix = one_call(
            token_kernel, [g["gi"], g["gz"], full_x, full_z, k["x"], g["gh"], gain_mix_f], [sds((length, width)), sds((1, width))], (),
            4 * length * inner * width, 24)
        return dict(tokens=grad_tokens, gain_mix=g_mix)

    after = lax.optimization_barrier
    ks, owns, last = [], [], None
    for s in range(seqs):
        x = tokens[s]
        if last is not None:
            x, last = after((x, last))
        k = mixer(s, x, 24 if s == 0 else 48)
        if s == 0:
            full_z, full_out, router_f, k["ssm"] = rest_of(k["ssm"])
        before, (last, k) = last, router(k, routes[s], lengths[s], cotangent)
        ks.append(k)
        if before is not None:
            got, last = after((home(before), last))
            owns.append(arrive(got))
    owns.append(arrive(home(last)))
    sets, sent = [], []
    for s in range(seqs):
        bufs = gather_cols(owns[s])
        if s == seqs - 2:
            bufs, owns[-1] = after((bufs, owns[-1]))
        outs, more = expert_both(bufs, w_up, w_down)
        sets.append((bufs, more))
        sent.append(from_experts(outs))
    backs = [home(v) for v in sent]
    grads_w = []
    for lead in (True, False):
        ins, sent[0], _ = after(([b + [v[1 if lead else 0]] for b, v in sets], sent[0], grads_w))
        grads_w.append(expert_weights_part(ins, lead, width, w_up.shape[2]))
    backs[0], (grad_w_up, grad_w_down) = after((backs[0], grads_w))
    gs_ = []
    for s in range(seqs):
        g = unroute(ks[s], backs[s])
        gs_.append(g)
        if s + 1 < seqs:
            g["gs"], sent[s + 1] = after((g["gs"], sent[s + 1]))
            g.update(unscan(ks[s], g["gs"], 52))
            g["gi"], backs[s + 1] = after((g["gi"], backs[s + 1]))
    g = gs_[-1]
    nms, gateds = [k["nm"] for k in ks], [k["gated"] for k in ks]
    if tiled:
        block = (here + here // 2 + out_rows * 3 // 4 + 16, 256)
        keep, give = grad_other_blocks([(v, q["gz"]) for v, q in zip(nms, gs_)], [(v, q["gm"]) for v, q in zip(gateds, gs_)],
                                       [q["router"] for q in gs_], block, rows, cols, w_router.shape[1], my_col)
        far, plane, core = stages()

        def first_tokens(v):
            return unproject(ks[0], dict(gs_[0], gi=after((gs_[0]["gi"], v))[0]))
        got, first = between(first_tokens, give, exchange(give, core))
        if seqs > 1:
            gs_[0].update(first)
        own, gives = split_near(keep, got)
        g["gs"], gives = after((g["gs"], gives))
        gots = [exchange(v, p) for v, p in zip(gives, plane[1:])]
        g.update(unscan(ks[-1], g["gs"], 24))
        dims = (w_dt.shape[0], w_xproj.shape[1], w_xproj.shape[0], conv_w.shape[1], gain_mix.shape[0], rows, cols)
        for s in range(1, seqs):
            gs_[s].update(unproject(ks[s], gs_[s]))
        keep, give = grad_x_blocks([(v, q["gi"]) for v, q in zip(nms, gs_)], gs_, dims, my_col)
        gots, give = after((gots, give))
        got = exchange(give, core)
        mine_o, gives = split_far(own, gots)
        got, gives = after((got, gives))
        gots_o = [exchange(v, p) for v, p in zip(gives, far[1:])]
        own, gives = split_near(keep, got)
        gots = [exchange(v, p) for v, p in zip(gives, plane[1:])]
        gots_o, _ = after((gots_o, gives))
        gz, go, g_router = finish(finish_other_kernel, mine_o, gots_o, [w_in_z.shape, w_out.shape, w_router.shape[::-1]])
        gots, gz, go, g_router = after((gots, gz, go, g_router))
        mine, gives = split_far(own, gots)
        gots = [exchange(v, p) for v, p in zip(gives, far[1:])]
        share, gshare = conv_w.shape[1], gain_mix.shape[0]
        gx, g_xproj, g_dt, gcw, gcb, gdb, gal, gds, g_mix, g_moe = finish(
            finish_x_kernel, mine, gots,
            [w_in_x.shape, w_xproj.shape[::-1], w_dt.shape, conv_w.shape, (1, share), (1, share), a_log.shape, (1, share), (1, gshare), (1, gshare)])
        blocks = (gx, gz, go)
        small = (g_xproj.T, g_dt, (gcw, gcb[0], gdb[0], gal, gds[0]), g_mix[0], g_moe[0], g_router.T)
    else:
        g.update(unscan(ks[-1], g["gs"], 24))
        for k, q in zip(ks, gs_):
            q.update(unproject(k, q))
        names = ("xproj", "dt", "chan", "gain_mix", "gain_moe", "router")
        total = {n: sum(q[n] for q in gs_) for n in names}
        blocks, small = grads_generic(nms, gateds, gs_, total, w_in_x, w_in_z, w_xproj, w_dt, w_out, w_router, gain_mix, conv_w)
    g_xproj, g_dt, (gcw, gcb, gdb, gal, gds), g_mix, g_moe, g_router = small
    return (
        jnp.stack([q["mixed_out"] for q in gs_]),
        jnp.stack([q["tokens"] for q in gs_]),
        blocks[0],
        blocks[1],
        gcw,
        gcb,
        g_xproj,
        g_dt,
        gdb,
        gal,
        gds,
        blocks[2],
        g_mix,
        g_moe,
        g_router,
        grad_w_up,
        grad_w_down,
    )


def solution(mesh):
    tok = P(("row", "col"), None, None)
    mat = P("row", "col")
    vec = P(("row", "col"))
    chan = P(None, ("row", "col"))
    up, down = P("row", None, "col"), P("row", "col", None)
    return jax.shard_map(
        on_device,
        mesh=mesh,
        in_specs=(tok, mat, mat, chan, vec, mat, mat, vec, chan, vec, mat, vec, vec, mat, up, down, tok, vec, tok),
        out_specs=(tok, tok, mat, mat, chan, vec, mat, mat, vec, chan, vec, mat, vec, vec, mat, up, down),
        check_vma=False,
    )
```
